32 devices in a mesh: dp: 4 (over y, x), ctx: 4 (over z), tp: 2 (over core).
Axes of the slice: x: 2, y: 2, z: 4, core: 2. Of those that a mesh axis runs over, the one named last changes fastest.
Arguments:
- q_proj: bfloat16 [4, 512, 4096], P('dp', 'ctx', 'tp'), may hold values from -6 to 6
- q_bias: bfloat16 [4096], P('tp'), may hold values from -3 to 3
- k_proj: bfloat16 [4, 512, 512], P('dp', 'ctx', 'tp'), may hold values from -6 to 6
- v_proj: bfloat16 [4, 512, 512], P('dp', 'ctx', 'tp'), may hold values from -6 to 6
- v_bias: bfloat16 [512], P('tp'), may hold values from -3 to 3
- dout: bfloat16 [4, 512, 4096], P('dp', 'ctx', 'tp'), may hold values from -6 to 6
- lengths: int32 [4, 8], P('dp'), may hold values from 1 to 384, 512 in all within a row
Outputs:
- attn_out: bfloat16 [4, 512, 4096], P('dp', 'ctx', 'tp')
- q_grad: bfloat16 [4, 512, 4096], P('dp', 'ctx', 'tp')
- k_grad: bfloat16 [4, 512, 512], P('dp', 'ctx', 'tp')
- v_grad: bfloat16 [4, 512, 512], P('dp', 'ctx', 'tp')
- q_bias_grad: float32 [4096], P('tp')
- v_bias_grad: float32 [512], P('tp')
The draws below stay inside these ranges and needn't reach their ends.
All inputs are finite; a program needn't handle non-finite values.
Results may differ from the reference program's by a relative error of at most 0.035.
Values may be sent and summed in bfloat16 or wider, within the bound.
No kernel may reach another device: no remote copies, remote signals or barrier semaphores. Data moves between devices by JAX's collectives and lax.ppermute only.
A program may use at most 64 MiB of HBM per device.

```python
import math
import jax
import jax.numpy as jnp
import numpy as np
from jax import lax

HEAD_DIM = 128
HEADS = 32
KV_HEADS = 4
DOCS = 8
TOKENS = 512
BATCH = 4
MOST = 384


def draw_q_proj(key, part):
    key = jax.random.fold_in(key, 1)
    shape = (BATCH, TOKENS, KV_HEADS, HEADS // KV_HEADS, HEAD_DIM)
    base = jnp.clip(1.5 * jax.random.normal(key, shape, jnp.float32), -6.0, 6.0)
    return base.reshape(BATCH, TOKENS, HEADS * HEAD_DIM).astype(jnp.bfloat16)


def draw_k_proj(key, part):
    key = jax.random.fold_in(key, 2)
    shape = (BATCH, TOKENS, KV_HEADS, HEAD_DIM)
    base = jnp.clip(1.3 * jax.random.normal(key, shape, jnp.float32), -6.0, 6.0)
    return base.reshape(BATCH, TOKENS, KV_HEADS * HEAD_DIM).astype(jnp.bfloat16)


def block_scale(key, extent, split, least, high):
    loudness = 1.0
    for axis_at, parts in split:
        steps = jax.random.uniform(jax.random.fold_in(jax.random.fold_in(key, 6), axis_at), (parts,), jnp.float32, least / len(split), high / len(split))
        loudness = loudness * jnp.repeat(jnp.exp(steps), extent[axis_at] // parts).reshape((-1,) + (1,) * (len(extent) - 1 - axis_at))
    return loudness


def length_profile(count, total, reach, skew):
    portions = [(1 << 20) // math.isqrt(grade ** skew) + 1 for grade in range(2, count + 1)]
    surplus, holding = total - reach - (count - 1), [1] * (count - 1)
    while surplus > 0:
        free = [i for i in range(count - 1) if holding[i] < reach]
        pool, remaining = sum([portions[i] for i in free]), surplus
        for i in free:
            more = min(reach - holding[i], max(1, remaining * portions[i] // pool), surplus)
            holding[i] = holding[i] + more
            surplus = surplus - more
    return np.array([reach] + holding)


def uneven_parts(own_key, number_of, total, bound, skew):
    if number_of == 2:
        one = jax.random.randint(own_key, (), max(1, total - bound), min(bound, total - 1) + 1)
        return jnp.stack([one, total - one])
    sizes = jnp.asarray(length_profile(number_of, total, bound, skew), jnp.int32)
    couples = (number_of - 1) // 2
    donor, receiver = sizes[1:1 + 2 * couples:2], sizes[2:2 + 2 * couples:2]
    margin = jnp.minimum(donor - 1, bound - receiver)
    shifted = jax.random.randint(jax.random.fold_in(own_key, 1), (couples,), 0, 1 << 20) % (margin + 1)
    sizes = sizes.at[1:1 + 2 * couples:2].set(donor - shifted).at[2:2 + 2 * couples:2].set(receiver + shifted)
    return sizes[jax.random.permutation(jax.random.fold_in(own_key, 2), number_of)]


def noise(rng, shape, deviation, most, shards=(), held_as=jnp.bfloat16):
    level = block_scale(rng, shape, shards, -0.22, 0.18) if shards else 1.0
    entries = jax.random.normal(rng, shape, jnp.float32) * deviation * level
    return jnp.minimum(jnp.maximum(entries, -most), most).astype(held_as)


def setup_inputs(seed: int = 0) -> dict:
    streams_of = jax.random.split(jax.random.key(seed), 8)
    q_proj = draw_q_proj(jax.random.fold_in(streams_of[7], 71), 0)
    q_bias = noise(streams_of[1], (HEADS * HEAD_DIM,), 0.5, 3.0, ((0, 2),))
    k_proj = draw_k_proj(jax.random.fold_in(streams_of[7], 71), 0)
    v_proj = noise(streams_of[3], (BATCH, TOKENS, KV_HEADS * HEAD_DIM), 1.0, 6.0, ((0, 4), (1, 4), (2, 2)))
    v_bias = noise(streams_of[4], (KV_HEADS * HEAD_DIM,), 0.5, 3.0, ((0, 2),))
    dout = noise(streams_of[5], (BATCH, TOKENS, HEADS * HEAD_DIM), 1.0, 6.0, ((0, 4), (1, 4), (2, 2)))
    lengths = jax.vmap(lambda own: uneven_parts(own, DOCS, TOKENS, MOST, 2))(jax.random.split(streams_of[6], BATCH)).reshape((BATCH, DOCS)).astype(jnp.int32)
    return dict(q_proj=q_proj, q_bias=q_bias, k_proj=k_proj, v_proj=v_proj, v_bias=v_bias, dout=dout, lengths=lengths)


def doc_index(lengths_row, positions):
    ends = jnp.cumsum(lengths_row).astype(jnp.int32)
    return jnp.sum((positions[:, None] >= ends[None, :]).astype(jnp.int32), axis=1)


def round_keep(array):
    return lax.optimization_barrier(array.astype(jnp.bfloat16)).astype(jnp.float32)


def head_group(queries, keys, values, grads, live):
    scale = HEAD_DIM ** -0.5
    score = jnp.einsum('gtd,sd->gts', queries, keys) * scale
    mask = live[None]
    row_max = jnp.max(jnp.where(mask, score, -1e30), axis=-1)
    weights = jnp.where(mask, jnp.exp(score - row_max[..., None]), 0.0)
    total = jnp.sum(weights, axis=-1)
    weights_b = round_keep(weights)
    attn = (jnp.einsum('gts,sd->gtd', weights_b, values) / total[..., None]).astype(jnp.bfloat16)
    lse = row_max + jnp.log(total)
    delta = jnp.sum(grads * attn.astype(jnp.float32), axis=-1)
    probs = jnp.where(mask, jnp.exp(score - lse[..., None]), 0.0)
    probs_b = round_keep(probs)
    value_grad = jnp.einsum('gts,gtd->sd', probs_b, grads)
    dprob = jnp.einsum('gtd,sd->gts', grads, values)
    dscore = round_keep(probs * (dprob - delta[..., None]))
    query_grad = jnp.einsum('gts,sd->gtd', dscore, keys) * scale
    key_grad = jnp.einsum('gts,gtd->sd', dscore, queries) * scale
    return attn, query_grad, key_grad, value_grad


def reference(q_proj, q_bias, k_proj, v_proj, v_bias, dout, lengths):
    group = HEADS // KV_HEADS
    positions = jnp.arange(TOKENS, dtype=jnp.int32)

    def one_batch(items):
        q_part, k_part, v_part, g_part, lens = items
        queries = round_keep(q_part.astype(jnp.float32) + q_bias.astype(jnp.float32))
        values = round_keep(v_part.astype(jnp.float32) + v_bias.astype(jnp.float32))
        keys = k_part.astype(jnp.float32)
        doc = doc_index(lens, positions)
        live = (positions[None, :] <= positions[:, None]) & (doc[None, :] == doc[:, None])
        q_heads = queries.reshape(TOKENS, KV_HEADS, group, HEAD_DIM)
        g_heads = g_part.astype(jnp.float32).reshape(TOKENS, KV_HEADS, group, HEAD_DIM)
        attn_list, qg_list, kg_list, vg_list = [], [], [], []
        for head in range(KV_HEADS):
            cols = slice(head * HEAD_DIM, (head + 1) * HEAD_DIM)
            attn, qg, kg, vg = head_group(q_heads[:, head].transpose(1, 0, 2), keys[:, cols], values[:, cols], g_heads[:, head].transpose(1, 0, 2), live)
            attn_list.append(attn.transpose(1, 0, 2))
            qg_list.append(qg.transpose(1, 0, 2))
            kg_list.append(kg)
            vg_list.append(vg)
        attn_all = jnp.stack(attn_list, axis=1).reshape(TOKENS, HEADS * HEAD_DIM)
        qg_all = jnp.stack(qg_list, axis=1).reshape(TOKENS, HEADS * HEAD_DIM)
        kg_all = jnp.concatenate(kg_list, axis=1)
        vg_all = jnp.concatenate(vg_list, axis=1)
        return (attn_all, qg_all.astype(jnp.bfloat16), kg_all.astype(jnp.bfloat16), vg_all.astype(jnp.bfloat16), jnp.sum(qg_all, axis=0), jnp.sum(vg_all, axis=0))

    attn_out, q_grad, k_grad, v_grad, q_sums, v_sums = lax.map(one_batch, (q_proj, k_proj, v_proj, dout, lengths))
    q_bias_grad = jnp.sum(q_sums, axis=0) / BATCH
    v_bias_grad = jnp.sum(v_sums, axis=0) / BATCH
    return (attn_out, q_grad, k_grad, v_grad, q_bias_grad, v_bias_grad)
```

```python
import functools

import jax
import jax.numpy as jnp
from jax import lax
from jax.experimental import pallas as pl
from jax.experimental.pallas import tpu as pltpu
from jax.sharding import PartitionSpec as P

HEAD_DIM = 128
HEADS = 32
KV_HEADS = 4
GROUP = HEADS // KV_HEADS
PAIR = 2
SCALE = HEAD_DIM ** (-0.5)
LOG2E = 1.4426950408889634
NEGATIVE = -1e30


def dot(left, right, left_dim, right_dim):
    return lax.dot_general(
        left, right, (((left_dim,), (right_dim,)), ((), ())), preferred_element_type=jnp.float32
    )


def attention_kernel(slots, *refs):
    len_ref, q_ref, qb_ref, vb_ref, g_ref, k_ref, v_ref = refs[:7]
    got_refs = refs[7 : 7 + slots - 1]
    refs = refs[7 + slots - 1 :]
    attn_ref, qg_ref, own_ref, sums_ref = refs[:4]
    out_refs = refs[4 : 4 + slots - 1]
    keys_ref, values_ref, live_ref = refs[4 + slots - 1 :]
    tok, width = q_ref.shape
    kv_width = k_ref.shape[1]
    kv_heads = kv_width // HEAD_DIM
    rank = lax.axis_index("ctx")

    query_pos = rank * tok + lax.broadcasted_iota(jnp.int32, (1, tok), 1)
    start = jnp.zeros((1, tok), jnp.int32)
    end = jnp.int32(0)
    for doc in range(len_ref.shape[1]):
        length = len_ref[0, doc]
        end = end + length
        start = start + jnp.where(query_pos >= end, length, 0)
    offsets = lax.broadcasted_iota(jnp.int32, (tok, tok), 0)
    bias = vb_ref[...].astype(jnp.float32)
    for slot in range(slots):
        rows = pl.ds(slot * tok, tok)
        key_pos = (rank - slot) * tok + offsets
        live = (key_pos >= start) & (key_pos <= query_pos)
        live_ref[rows, :] = jnp.where(live, 0.0, NEGATIVE)
        if slot == 0:
            keys, values = k_ref[...], v_ref[...]
        else:
            got = got_refs[slot - 1][...]
            keys, values = got[:, :kv_width], got[:, kv_width:]
        keys_ref[rows, :] = keys
        values_ref[rows, :] = (values.astype(jnp.float32) + bias).astype(jnp.bfloat16)

    for kv_head in range(kv_heads):
        kv_cols = slice(kv_head * HEAD_DIM, (kv_head + 1) * HEAD_DIM)
        keys = keys_ref[:, kv_cols]
        values = values_ref[:, kv_cols]
        keys_t = keys.T
        values_t = values.T
        key_term = jnp.zeros((slots * tok, HEAD_DIM), jnp.float32)
        value_term = jnp.zeros((slots * tok, HEAD_DIM), jnp.float32)
        for pair in range(GROUP // PAIR):
            first = kv_head * GROUP + pair * PAIR
            cols = [slice((first + n) * HEAD_DIM, (first + n + 1) * HEAD_DIM) for n in range(PAIR)]
            queries = jnp.concatenate(
                [
                    (q_ref[:, col].astype(jnp.float32) + qb_ref[:, col].astype(jnp.float32)).astype(
                        jnp.bfloat16
                    )
                    for col in cols
                ],
                axis=0,
            )
            grads = jnp.concatenate([g_ref[:, col] for col in cols], axis=0)
            live = jnp.concatenate([live_ref[...]] * PAIR, axis=1)
            score = dot(keys, queries, 1, 1) * (SCALE * LOG2E) + live
            row_max = jnp.max(score, axis=0, keepdims=True)
            weights = jnp.exp2(score - row_max)
            inverse = 1.0 / jnp.sum(weights, axis=0, keepdims=True)
            attn = dot(values_t, weights.astype(jnp.bfloat16), 1, 0) * inverse
            probs = weights * inverse
            dprob = dot(values, grads, 1, 1)
            delta = jnp.sum(probs * dprob, axis=0, keepdims=True)
            dscore = (probs * (dprob - delta)).astype(jnp.bfloat16)
            value_term = value_term + dot(probs.astype(jnp.bfloat16), grads, 1, 0)
            key_term = key_term + dot(dscore, queries, 1, 0)
            query_grad = dot(keys_t, dscore, 1, 0) * SCALE
            attn = attn.T
            query_grad = query_grad.T
            for n, col in enumerate(cols):
                rows = slice(n * tok, (n + 1) * tok)
                attn_ref[:, col] = attn[rows].astype(jnp.bfloat16)
                qg_ref[:, col] = query_grad[rows].astype(jnp.bfloat16)
                sums_ref[:, col] = jnp.sum(query_grad[rows], axis=0, keepdims=True)
        key_term = key_term * SCALE
        sum_cols = slice(width + kv_head * HEAD_DIM, width + (kv_head + 1) * HEAD_DIM)
        sums_ref[:, sum_cols] = jnp.sum(value_term, axis=0, keepdims=True)
        value_cols = slice(kv_width + kv_head * HEAD_DIM, kv_width + (kv_head + 1) * HEAD_DIM)
        own_ref[:, kv_cols] = key_term[:tok]
        own_ref[:, value_cols] = value_term[:tok]
        for slot in range(1, slots):
            rows = slice(slot * tok, (slot + 1) * tok)
            out_refs[slot - 1][:, kv_cols] = key_term[rows].astype(jnp.bfloat16)
            out_refs[slot - 1][:, value_cols] = value_term[rows].astype(jnp.bfloat16)


def attention(slots, lengths, q_proj, q_bias, v_bias, dout, k_proj, v_proj, got):
    tok, width = q_proj.shape
    kv_width = k_proj.shape[1]
    rows = slots * tok
    vmem = pl.BlockSpec(memory_space=pltpu.VMEM)
    shape = jax.ShapeDtypeStruct
    return pl.pallas_call(
        functools.partial(attention_kernel, slots),
        out_shape=[
            shape((tok, width), jnp.bfloat16),
            shape((tok, width), jnp.bfloat16),
            shape((tok, 2 * kv_width), jnp.float32),
            shape((1, width + kv_width), jnp.float32),
        ]
        + [shape((tok, 2 * kv_width), jnp.bfloat16)] * (slots - 1),
        in_specs=[pl.BlockSpec(memory_space=pltpu.SMEM)] + [vmem] * (6 + slots - 1),
        out_specs=[vmem] * (4 + slots - 1),
        scratch_shapes=[
            pltpu.VMEM((rows, kv_width), jnp.bfloat16),
            pltpu.VMEM((rows, kv_width), jnp.bfloat16),
            pltpu.VMEM((rows, tok), jnp.float32),
        ],
        compiler_params=pltpu.CompilerParams(vmem_limit_bytes=48 * 1024 * 1024),
        cost_estimate=pl.CostEstimate(
            flops=12 * rows * tok * width,
            bytes_accessed=8 * tok * width + 8 * rows * kv_width,
            transcendentals=rows * tok * width // HEAD_DIM,
        ),
        name="attention",
    )(lengths, q_proj, q_bias, v_bias, dout, k_proj, v_proj, *got)


def sum_over(axis, part):
    size = lax.axis_size(axis)
    terms = [
        lax.ppermute(part, axis, [(i, (i + shift) % size) for i in range(size)])
        for shift in range(1, size)
    ]
    return functools.reduce(lambda left, right: left + right, terms, part)


def shards(q_proj, q_bias, k_proj, v_proj, v_bias, dout, lengths):
    width = q_proj.shape[2]
    kv_width = k_proj.shape[2]
    ctx = lax.axis_size("ctx")
    batches = lax.axis_size("dp")
    pair = jnp.concatenate([k_proj[0], v_proj[0]], axis=1)
    got = [
        lax.ppermute(pair, "ctx", [(i, i + shift) for i in range(ctx - shift)])
        for shift in range(1, ctx)
    ]
    attn, q_grad, own, sums, *terms = attention(
        ctx, lengths, q_proj[0], q_bias[None], v_bias[None], dout[0], k_proj[0], v_proj[0], got
    )
    back = [
        lax.ppermute(term, "ctx", [(i, i - shift) for i in range(shift, ctx)])
        for shift, term in enumerate(terms, 1)
    ]
    sums = sum_over("dp", sum_over("ctx", sums)) / batches
    kv_grad = own
    for term in back:
        kv_grad = kv_grad + term.astype(jnp.float32)
    kv_grad = kv_grad.astype(jnp.bfloat16)
    return (
        attn[None],
        q_grad[None],
        kv_grad[None, :, :kv_width],
        kv_grad[None, :, kv_width:],
        sums[0, :width],
        sums[0, width:],
    )


def solution(mesh):
    tokens = P("dp", "ctx", "tp")
    return jax.shard_map(
        shards,
        mesh=mesh,
        in_specs=(tokens, P("tp"), tokens, tokens, P("tp"), tokens, P("dp", None)),
        out_specs=(tokens, tokens, tokens, tokens, P("tp"), P("tp")),
        check_vma=False,
    )
```

```python
import functools

import jax
import jax.numpy as jnp
from jax import lax
from jax.experimental import pallas as pl
from jax.experimental.pallas import tpu as pltpu
from jax.sharding import PartitionSpec as P

HEAD_DIM = 128
HEADS = 32
KV_HEADS = 4
GROUP = HEADS // KV_HEADS
PAIR = 2
SCALE = HEAD_DIM ** (-0.5)
LOG2E = 1.4426950408889634
NEGATIVE = -1e30
VMEM = pl.BlockSpec(memory_space=pltpu.VMEM)
SMEM = pl.BlockSpec(memory_space=pltpu.SMEM)


def dot(left, right, left_dim, right_dim):
    return lax.dot_general(
        left, right, (((left_dim,), (right_dim,)), ((), ())), preferred_element_type=jnp.float32
    )


def head_cols(head):
    return slice(head * HEAD_DIM, (head + 1) * HEAD_DIM)


def shape(dims, dtype):
    return jax.ShapeDtypeStruct(dims, dtype)


def params(mebibytes):
    return pltpu.CompilerParams(vmem_limit_bytes=mebibytes * 1024 * 1024)


def biased(values, bias):
    return (values.astype(jnp.float32) + bias.astype(jnp.float32)).astype(jnp.bfloat16)


def prepare_kernel(
    slots, len_ref, q_ref, qb_ref, vb_ref, g_ref, k_ref, v_ref, bias_ref, keys_ref, values_ref,
    queries_ref, grads_ref, score_ref, dprob_ref, live_ref,
):
    tok, width = q_ref.shape
    kv_heads = k_ref.shape[1] // HEAD_DIM
    rank = lax.axis_index("ctx")
    query_pos = rank * tok + lax.broadcasted_iota(jnp.int32, (1, tok), 1)
    start = jnp.zeros((1, tok), jnp.int32)
    end = jnp.int32(0)
    for doc in range(len_ref.shape[1]):
        length = len_ref[0, doc]
        end = end + length
        start = start + jnp.where(query_pos >= end, length, 0)
    offsets = lax.broadcasted_iota(jnp.int32, (tok, tok), 0)
    for slot in range(slots):
        key_pos = (rank - slot) * tok + offsets
        live = (key_pos >= start) & (key_pos <= query_pos)
        live_ref[slot * tok : (slot + 1) * tok, :] = jnp.where(live, 0.0, NEGATIVE)
    bias_ref[...] = vb_ref[...]
    keys_ref[...] = k_ref[...]
    values_ref[...] = biased(v_ref[...], vb_ref[...])
    for kv_head in range(kv_heads):
        cols = head_cols(kv_head)
        keys = k_ref[:, cols]
        values = values_ref[:, cols]
        for head in range(kv_head * GROUP, (kv_head + 1) * GROUP):
            at = head_cols(head)
            queries_ref[head * tok : (head + 1) * tok, :] = biased(q_ref[:, at], qb_ref[:, at])
            grads_ref[head * tok : (head + 1) * tok, :] = g_ref[:, at]
        rows = slice(kv_head * GROUP * tok, (kv_head + 1) * GROUP * tok)
        score_ref[:, rows] = dot(keys, queries_ref[rows, :], 1, 1)
        dprob_ref[:, rows] = dot(values, grads_ref[rows, :], 1, 1)


def attend_kernel(slots, *refs):
    bias_ref, k_ref, v_ref, queries_ref, grads_ref, score_ref, dprob_ref, live_ref = refs[:8]
    got_refs = refs[8 : 8 + slots - 1]
    refs = refs[8 + slots - 1 :]
    probs_ref, dscore_ref, keys_ref, values_ref, sums_ref, own_ref = refs[:6]
    out_refs = refs[6:]
    tok, kv_width = k_ref.shape
    kv_heads = kv_width // HEAD_DIM
    keys_ref[:tok, :] = k_ref[...]
    values_ref[:tok, :] = v_ref[...]
    for slot in range(1, slots):
        rows = slice(slot * tok, (slot + 1) * tok)
        keys_ref[rows, :] = got_refs[slot - 1][:, :kv_width]
        values_ref[rows, :] = biased(got_refs[slot - 1][:, kv_width:], bias_ref[...])
    for kv_head in range(kv_heads):
        cols = head_cols(kv_head)
        keys = keys_ref[tok:, cols]
        values = values_ref[tok:, cols]
        key_term = jnp.zeros((slots * tok, HEAD_DIM), jnp.float32)
        value_term = jnp.zeros((slots * tok, HEAD_DIM), jnp.float32)
        for pair in range(GROUP // PAIR):
            first = kv_head * GROUP + pair * PAIR
            at = slice(first * tok, (first + PAIR) * tok)
            queries = queries_ref[at, :]
            grads = grads_ref[at, :]
            live = jnp.concatenate([live_ref[...]] * PAIR, axis=1)
            score = jnp.concatenate([score_ref[:, at], dot(keys, queries, 1, 1)], axis=0)
            score = score * (SCALE * LOG2E) + live
            row_max = jnp.max(score, axis=0, keepdims=True)
            weights = jnp.exp2(score - row_max)
            probs = weights * (1.0 / jnp.sum(weights, axis=0, keepdims=True))
            dprob = jnp.concatenate([dprob_ref[:, at], dot(values, grads, 1, 1)], axis=0)
            delta = jnp.sum(probs * dprob, axis=0, keepdims=True)
            dscore = (probs * (dprob - delta)).astype(jnp.bfloat16)
            probs = probs.astype(jnp.bfloat16)
            probs_ref[:, at] = probs
            dscore_ref[:, at] = dscore
            value_term = value_term + dot(probs, grads, 1, 0)
            key_term = key_term + dot(dscore, queries, 1, 0)
        key_term = key_term * SCALE
        sums_ref[kv_head : kv_head + 1, :] = jnp.sum(value_term, axis=0, keepdims=True)
        value_cols = head_cols(kv_heads + kv_head)
        own_ref[:, cols] = key_term[:tok]
        own_ref[:, value_cols] = value_term[:tok]
        for slot in range(1, slots):
            rows = slice(slot * tok, (slot + 1) * tok)
            out_refs[slot - 1][:, cols] = key_term[rows].astype(jnp.bfloat16)
            out_refs[slot - 1][:, value_cols] = value_term[rows].astype(jnp.bfloat16)


def finish_kernel(
    probs_ref, dscore_ref, keys_ref, values_ref, vsums_ref, attn_ref, qg_ref, sums_ref
):
    tok, width = attn_ref.shape
    kv_heads = keys_ref.shape[1] // HEAD_DIM
    heads = width // HEAD_DIM
    copies = sums_ref.shape[0]
    for kv_head in range(kv_heads):
        cols = head_cols(kv_head)
        keys_t = keys_ref[:, cols].T
        values_t = values_ref[:, cols].T
        for pair in range(GROUP // PAIR):
            first = kv_head * GROUP + pair * PAIR
            at = slice(first * tok, (first + PAIR) * tok)
            attn = dot(values_t, probs_ref[:, at], 1, 0).T
            query_grad = (dot(keys_t, dscore_ref[:, at], 1, 0) * SCALE).T
            for n in range(PAIR):
                head = first + n
                rows = slice(n * tok, (n + 1) * tok)
                attn_ref[:, head_cols(head)] = attn[rows].astype(jnp.bfloat16)
                qg_ref[:, head_cols(head)] = query_grad[rows].astype(jnp.bfloat16)
                sums_ref[0, head : head + 1, :] = jnp.sum(query_grad[rows], axis=0, keepdims=True)
    sums_ref[0, heads:, :] = vsums_ref[...]
    sums = sums_ref[0]
    for copy in range(1, copies):
        sums_ref[copy] = sums


def shards(q_proj, q_bias, k_proj, v_proj, v_bias, dout, lengths):
    _, tok, width = q_proj.shape
    kv_width = k_proj.shape[2]
    heads = width // HEAD_DIM
    kv_heads = kv_width // HEAD_DIM
    ctx = lax.axis_size("ctx")
    batches = lax.axis_size("dp")
    rows = ctx * tok
    columns = heads * tok
    keys, values, v_bias = k_proj[0], v_proj[0], v_bias[None]
    pair = jnp.concatenate([keys, values], axis=1)
    got = [
        lax.ppermute(pair, "ctx", [(i, i + shift) for i in range(ctx - shift)])
        for shift in range(1, ctx)
    ]
    prepared = pl.pallas_call(
        functools.partial(prepare_kernel, ctx),
        out_shape=[
            shape((1, kv_width), jnp.bfloat16),
            shape((tok, kv_width), jnp.bfloat16),
            shape((tok, kv_width), jnp.bfloat16),
            shape((columns, HEAD_DIM), jnp.bfloat16),
            shape((columns, HEAD_DIM), jnp.bfloat16),
            shape((tok, columns), jnp.float32),
            shape((tok, columns), jnp.float32),
            shape((rows, tok), jnp.float32),
        ],
        in_specs=[SMEM] + [VMEM] * 6,
        out_specs=[VMEM] * 8,
        compiler_params=params(16),
        cost_estimate=pl.CostEstimate(
            flops=4 * tok * tok * width, bytes_accessed=16 * tok * width, transcendentals=0
        ),
        name="prepare",
    )(lengths, q_proj[0], q_bias[None], v_bias, dout[0], keys, values)
    term = shape((tok, 2 * kv_width), jnp.bfloat16)
    probs, dscore, all_keys, all_values, value_sums, own, *terms = pl.pallas_call(
        functools.partial(attend_kernel, ctx),
        out_shape=[
            shape((rows, columns), jnp.bfloat16),
            shape((rows, columns), jnp.bfloat16),
            shape((rows, kv_width), jnp.bfloat16),
            shape((rows, kv_width), jnp.bfloat16),
            shape((kv_heads, HEAD_DIM), jnp.float32),
            shape((tok, 2 * kv_width), jnp.float32),
        ]
        + [term] * (ctx - 1),
        in_specs=[VMEM] * (8 + ctx - 1),
        out_specs=[VMEM] * (6 + ctx - 1),
        compiler_params=params(40),
        cost_estimate=pl.CostEstimate(
            flops=8 * rows * tok * width,
            bytes_accessed=4 * rows * columns,
            transcendentals=rows * columns,
        ),
        name="attend",
    )(*prepared, *got)
    back = [
        lax.ppermute(term, "ctx", [(i, i - shift) for i in range(shift, ctx)])
        for shift, term in enumerate(terms, 1)
    ]
    attn, q_grad, sums = pl.pallas_call(
        finish_kernel,
        out_shape=[
            shape((tok, width), jnp.bfloat16),
            shape((tok, width), jnp.bfloat16),
            shape((batches * ctx, heads + kv_heads, HEAD_DIM), jnp.float32),
        ],
        in_specs=[VMEM] * 5,
        out_specs=[VMEM] * 3,
        compiler_params=params(24),
        cost_estimate=pl.CostEstimate(
            flops=4 * rows * tok * width, bytes_accessed=4 * rows * columns, transcendentals=0
        ),
        name="finish",
    )(probs, dscore, all_keys, all_values, value_sums)
    sums = lax.all_to_all(sums, ("dp", "ctx"), split_axis=0, concat_axis=0, tiled=True)
    sums = jnp.sum(sums, axis=0) / batches
    kv_grad = own
    for part in back:
        kv_grad = kv_grad + part.astype(jnp.float32)
    kv_grad = kv_grad.astype(jnp.bfloat16)
    return (
        attn[None],
        q_grad[None],
        kv_grad[None, :, :kv_width],
        kv_grad[None, :, kv_width:],
        sums[:heads].reshape(width),
        sums[heads:].reshape(kv_width),
    )


def solution(mesh):
    tokens = P("dp", "ctx", "tp")
    return jax.shard_map(
        shards,
        mesh=mesh,
        in_specs=(tokens, P("tp"), tokens, tokens, P("tp"), tokens, P("dp", None)),
        out_specs=(tokens, tokens, tokens, tokens, P("tp"), P("tp")),
        check_vma=False,
    )
```

```python
import functools

import jax
import jax.numpy as jnp
from jax import lax
from jax.experimental import pallas as pl
from jax.experimental.pallas import tpu as pltpu
from jax.sharding import PartitionSpec as P

HEAD_DIM = 128
HEADS = 32
KV_HEADS = 4
GROUP = HEADS // KV_HEADS
PAIR = 2
SCALE = HEAD_DIM ** (-0.5)
LOG2E = 1.4426950408889634
NEGATIVE = -1e30
VMEM = pl.BlockSpec(memory_space=pltpu.VMEM)
SMEM = pl.BlockSpec(memory_space=pltpu.SMEM)


def dot(left, right, left_dim, right_dim):
    return lax.dot_general(
        left, right, (((left_dim,), (right_dim,)), ((), ())), preferred_element_type=jnp.float32
    )


def head_cols(head):
    return slice(head * HEAD_DIM, (head + 1) * HEAD_DIM)


def shape(dims, dtype):
    return jax.ShapeDtypeStruct(dims, dtype)


def params(mebibytes):
    return pltpu.CompilerParams(vmem_limit_bytes=mebibytes * 1024 * 1024)


def biased(values, bias):
    return (values.astype(jnp.float32) + bias.astype(jnp.float32)).astype(jnp.bfloat16)


def prepare_kernel(
    slots, len_ref, pair_ref, qb_ref, vb_ref, q_ref, g_ref, bias_ref, queries_ref, grads_ref,
    score_ref, dprob_ref, live_ref,
):
    tok = q_ref.shape[0]
    kv_heads = vb_ref.shape[0]
    rank = lax.axis_index("ctx")
    query_pos = rank * tok + lax.broadcasted_iota(jnp.int32, (1, tok), 1)
    start = jnp.zeros((1, tok), jnp.int32)
    end = jnp.int32(0)
    for doc in range(len_ref.shape[1]):
        length = len_ref[0, doc]
        end = end + length
        start = start + jnp.where(query_pos >= end, length, 0)
    offsets = lax.broadcasted_iota(jnp.int32, (tok, tok), 0)
    for slot in range(slots):
        key_pos = (rank - slot) * tok + offsets
        live = (key_pos >= start) & (key_pos <= query_pos)
        live_ref[slot * tok : (slot + 1) * tok, :] = jnp.where(live, 0.0, NEGATIVE)
    bias_ref[...] = vb_ref[...]
    column = lax.broadcasted_iota(jnp.int32, (tok, HEAD_DIM), 1)
    for kv_head in range(kv_heads):
        keys = pair_ref[:, head_cols(kv_head)]
        values = biased(pair_ref[:, head_cols(kv_heads + kv_head)], vb_ref[kv_head : kv_head + 1, :])
        for head in range(kv_head * GROUP, (kv_head + 1) * GROUP):
            at = slice(head * tok, (head + 1) * tok)
            queries_ref[at, :HEAD_DIM] = biased(q_ref[:, head_cols(head)], qb_ref[head : head + 1, :])
            queries_ref[at, HEAD_DIM:] = (column == head).astype(jnp.bfloat16)
            grads_ref[at, :] = g_ref[:, head_cols(head)]
        rows = slice(kv_head * GROUP * tok, (kv_head + 1) * GROUP * tok)
        score_ref[:, rows] = dot(keys, queries_ref[rows, :HEAD_DIM], 1, 1)
        dprob_ref[:, rows] = dot(values, grads_ref[rows, :], 1, 1)


def attend_kernel(slots, *refs):
    bias_ref, queries_ref, grads_ref, score_ref, dprob_ref, live_ref = refs[:6]
    pair_refs = refs[6 : 6 + slots][::-1]
    refs = refs[6 + slots :]
    probs_ref, dscore_ref, keys_ref, values_ref, sums_ref, own_ref = refs[:6]
    out_refs = refs[6:]
    tok = pair_refs[0].shape[0]
    kv_heads = bias_ref.shape[0]
    kv_width = kv_heads * HEAD_DIM
    heads = kv_heads * GROUP
    for slot in range(slots):
        rows = slice(slot * tok, (slot + 1) * tok)
        keys_ref[rows, :] = pair_refs[slot][:, :kv_width]
        for kv_head in range(kv_heads):
            values_ref[rows, head_cols(kv_head)] = biased(
                pair_refs[slot][:, head_cols(kv_heads + kv_head)], bias_ref[kv_head : kv_head + 1, :]
            )
    for kv_head in range(kv_heads):
        cols = head_cols(kv_head)
        keys = keys_ref[tok:, cols]
        values = values_ref[tok:, cols]
        key_term = jnp.zeros((slots * tok, 2 * HEAD_DIM), jnp.float32)
        value_term = jnp.zeros((slots * tok, HEAD_DIM), jnp.float32)
        for pair in range(GROUP // PAIR):
            first = kv_head * GROUP + pair * PAIR
            at = slice(first * tok, (first + PAIR) * tok)
            queries = queries_ref[at, :]
            grads = grads_ref[at, :]
            live = jnp.concatenate([live_ref[...]] * PAIR, axis=1)
            score = jnp.concatenate(
                [score_ref[:, at], dot(keys, queries[:, :HEAD_DIM], 1, 1)], axis=0
            )
            score = score * (SCALE * LOG2E) + live
            row_max = jnp.max(score, axis=0, keepdims=True)
            weights = jnp.exp2(score - row_max)
            probs = weights * (1.0 / jnp.sum(weights, axis=0, keepdims=True))
            dprob = jnp.concatenate([dprob_ref[:, at], dot(values, grads, 1, 1)], axis=0)
            delta = jnp.sum(probs * dprob, axis=0, keepdims=True)
            dscore = (probs * (dprob - delta)).astype(jnp.bfloat16)
            probs = probs.astype(jnp.bfloat16)
            probs_ref[:, at] = probs
            dscore_ref[:, at] = dscore
            value_term = value_term + dot(probs, grads, 1, 0)
            key_term = key_term + dot(dscore, queries, 1, 0)
        over_queries = key_term[:, HEAD_DIM:]
        key_term = key_term[:, :HEAD_DIM] * SCALE
        high = over_queries.astype(jnp.bfloat16)
        low = (over_queries - high.astype(jnp.float32)).astype(jnp.bfloat16)
        all_keys = keys_ref[:, cols]
        query_sums = (dot(high, all_keys, 0, 0) + dot(low, all_keys, 0, 0)) * SCALE
        of_group = slice(kv_head * GROUP, (kv_head + 1) * GROUP)
        sums_ref[of_group, :] = query_sums[of_group]
        sums_ref[heads + kv_head : heads + kv_head + 1, :] = jnp.sum(
            value_term, axis=0, keepdims=True
        )
        value_cols = head_cols(kv_heads + kv_head)
        own_ref[:, cols] = key_term[:tok]
        own_ref[:, value_cols] = value_term[:tok]
        for slot in range(1, slots):
            rows = slice(slot * tok, (slot + 1) * tok)
            out_refs[slot - 1][:, cols] = key_term[rows].astype(jnp.bfloat16)
            out_refs[slot - 1][:, value_cols] = value_term[rows].astype(jnp.bfloat16)


def finish_kernel(probs_ref, dscore_ref, keys_ref, values_ref, attn_ref, qg_ref):
    tok = attn_ref.shape[0]
    kv_heads = keys_ref.shape[1] // HEAD_DIM
    for kv_head in range(kv_heads):
        cols = head_cols(kv_head)
        keys_t = keys_ref[:, cols].T
        values_t = values_ref[:, cols].T
        for pair in range(GROUP // PAIR):
            first = kv_head * GROUP + pair * PAIR
            at = slice(first * tok, (first + PAIR) * tok)
            attn = dot(values_t, probs_ref[:, at], 1, 0).T
            query_grad = (dot(keys_t, dscore_ref[:, at], 1, 0) * SCALE).T
            for n in range(PAIR):
                head = first + n
                rows = slice(n * tok, (n + 1) * tok)
                attn_ref[:, head_cols(head)] = attn[rows].astype(jnp.bfloat16)
                qg_ref[:, head_cols(head)] = query_grad[rows].astype(jnp.bfloat16)


def collect_kernel(batches, parts, kv_parts, *refs):
    sum_refs, refs = refs[:parts], refs[parts:]
    own_ref, refs = refs[0], refs[1:]
    back_refs, refs = refs[:kv_parts], refs[kv_parts:]
    kg_ref, vg_ref, qb_ref, vb_ref = refs
    heads = qb_ref.shape[0]
    kv_width = kg_ref.shape[1]
    total = sum_refs[0][...]
    for ref in sum_refs[1:]:
        total = total + ref[...]
    total = total * (1.0 / batches)
    qb_ref[...] = total[:heads]
    vb_ref[...] = total[heads:]
    term = own_ref[...]
    for ref in back_refs:
        term = term + ref[...].astype(jnp.float32)
    term = term.astype(jnp.bfloat16)
    kg_ref[...] = term[:, :kv_width]
    vg_ref[...] = term[:, kv_width:]


def total_of(parts):
    return functools.reduce(lambda left, right: left + right, parts)


def exchange(axis, part):
    size = lax.axis_size(axis)
    if size & (size - 1):
        return [part] + [
            lax.ppermute(part, axis, [(i, (i + shift) % size) for i in range(size)])
            for shift in range(1, size)
        ]
    parts, step = [part], 1
    while step < size:
        part = total_of(parts)
        parts = [part, lax.ppermute(part, axis, [(i, i ^ step) for i in range(size)])]
        step *= 2
    return parts


def shards(q_proj, q_bias, k_proj, v_proj, v_bias, dout, lengths):
    _, tok, width = q_proj.shape
    kv_width = k_proj.shape[2]
    heads = width // HEAD_DIM
    kv_heads = kv_width // HEAD_DIM
    ctx = lax.axis_size("ctx")
    batches = lax.axis_size("dp")
    rows = ctx * tok
    columns = heads * tok
    pair = jnp.concatenate([k_proj[0], v_proj[0]], axis=1)
    pairs = [
        lax.ppermute(pair, "ctx", [(i, i + shift) for i in range(ctx - shift)])
        for shift in range(ctx - 1, 0, -1)
    ] + [pair]
    prepared = pl.pallas_call(
        functools.partial(prepare_kernel, ctx),
        out_shape=[
            shape((kv_heads, HEAD_DIM), jnp.bfloat16),
            shape((columns, 2 * HEAD_DIM), jnp.bfloat16),
            shape((columns, HEAD_DIM), jnp.bfloat16),
            shape((tok, columns), jnp.float32),
            shape((tok, columns), jnp.float32),
            shape((rows, tok), jnp.float32),
        ],
        in_specs=[SMEM] + [VMEM] * 5,
        out_specs=[VMEM] * 6,
        compiler_params=params(16),
        cost_estimate=pl.CostEstimate(
            flops=4 * tok * tok * width, bytes_accessed=16 * tok * width, transcendentals=0
        ),
        name="prepare",
    )(
        lengths,
        pair,
        q_bias.reshape(heads, HEAD_DIM),
        v_bias.reshape(kv_heads, HEAD_DIM),
        q_proj[0],
        dout[0],
    )
    term = shape((tok, 2 * kv_width), jnp.bfloat16)
    probs, dscore, all_keys, all_values, sums, own, *terms = pl.pallas_call(
        functools.partial(attend_kernel, ctx),
        out_shape=[
            shape((rows, columns), jnp.bfloat16),
            shape((rows, columns), jnp.bfloat16),
            shape((rows, kv_width), jnp.bfloat16),
            shape((rows, kv_width), jnp.bfloat16),
            shape((heads + kv_heads, HEAD_DIM), jnp.float32),
            shape((tok, 2 * kv_width), jnp.float32),
        ]
        + [term] * (ctx - 1),
        in_specs=[VMEM] * (6 + ctx),
        out_specs=[VMEM] * (6 + ctx - 1),
        compiler_params=params(40),
        cost_estimate=pl.CostEstimate(
            flops=8 * rows * tok * width,
            bytes_accessed=4 * rows * columns,
            transcendentals=rows * columns,
        ),
        name="attend",
    )(*prepared, *pairs)
    back = [
        lax.ppermute(term, "ctx", [(i, i - shift) for i in range(shift, ctx)])
        for shift, term in enumerate(terms, 1)
    ]
    attn, q_grad = pl.pallas_call(
        finish_kernel,
        out_shape=[
            shape((tok, width), jnp.bfloat16),
            shape((tok, width), jnp.bfloat16),
        ],
        in_specs=[VMEM] * 4,
        out_specs=[VMEM] * 2,
        compiler_params=params(24),
        cost_estimate=pl.CostEstimate(
            flops=4 * rows * tok * width, bytes_accessed=4 * rows * columns, transcendentals=0
        ),
        name="finish",
    )(probs, dscore, all_keys, all_values)
    sums = exchange("ctx", total_of(exchange("dp", sums)))
    k_grad, v_grad, q_sum, v_sum = pl.pallas_call(
        functools.partial(collect_kernel, batches, len(sums), len(back)),
        out_shape=[
            shape((tok, kv_width), jnp.bfloat16),
            shape((tok, kv_width), jnp.bfloat16),
            shape((heads, HEAD_DIM), jnp.float32),
            shape((kv_heads, HEAD_DIM), jnp.float32),
        ],
        in_specs=[VMEM] * (len(sums) + 1 + len(back)),
        out_specs=[VMEM] * 4,
        compiler_params=params(8),
        cost_estimate=pl.CostEstimate(
            flops=8 * tok * kv_width, bytes_accessed=16 * tok * kv_width, transcendentals=0
        ),
        name="collect",
    )(*sums, own, *back)
    return (
        attn[None],
        q_grad[None],
        k_grad[None],
        v_grad[None],
        q_sum.reshape(width),
        v_sum.reshape(kv_width),
    )


def solution(mesh):
    tokens = P("dp", "ctx", "tp")
    return jax.shard_map(
        shards,
        mesh=mesh,
        in_specs=(tokens, P("tp"), tokens, tokens, P("tp"), tokens, P("dp", None)),
        out_specs=(tokens, tokens, tokens, tokens, P("tp"), P("tp")),
        check_vma=False,
    )
```

```python
import functools

import jax
import jax.numpy as jnp
from jax import lax
from jax.experimental import pallas as pl
from jax.experimental.pallas import tpu as pltpu
from jax.sharding import PartitionSpec as P

HEAD_DIM = 128
HEADS = 32
KV_HEADS = 4
GROUP = HEADS // KV_HEADS
PAIR = 2
SCALE = HEAD_DIM ** (-0.5)
LOG2E = 1.4426950408889634
NEGATIVE = -1e30
VMEM = pl.BlockSpec(memory_space=pltpu.VMEM)
SMEM = pl.BlockSpec(memory_space=pltpu.SMEM)


def dot(left, right, left_dim, right_dim):
    return lax.dot_general(
        left, right, (((left_dim,), (right_dim,)), ((), ())), preferred_element_type=jnp.float32
    )


def head_cols(head):
    return slice(head * HEAD_DIM, (head + 1) * HEAD_DIM)


def shape(dims, dtype):
    return jax.ShapeDtypeStruct(dims, dtype)


def params(mebibytes):
    return pltpu.CompilerParams(vmem_limit_bytes=mebibytes * 1024 * 1024)


def biased(values, bias):
    return (values.astype(jnp.float32) + bias.astype(jnp.float32)).astype(jnp.bfloat16)


def prepare_kernel(
    slots, len_ref, pair_ref, qb_ref, vb_ref, q_ref, g_ref, bias_ref, queries_ref, grads_ref,
    score_ref, dprob_ref, live_ref,
):
    tok = q_ref.shape[0]
    kv_heads = vb_ref.shape[0]
    rank = lax.axis_index("ctx")
    query_pos = rank * tok + lax.broadcasted_iota(jnp.int32, (1, tok), 1)
    start = jnp.zeros((1, tok), jnp.int32)
    end = jnp.int32(0)
    for doc in range(len_ref.shape[1]):
        length = len_ref[0, doc]
        end = end + length
        start = start + jnp.where(query_pos >= end, length, 0)
    offsets = lax.broadcasted_iota(jnp.int32, (tok, tok), 0)
    for slot in range(slots):
        key_pos = (rank - slot) * tok + offsets
        live = (key_pos >= start) & (key_pos <= query_pos)
        live_ref[slot * tok : (slot + 1) * tok, :] = jnp.where(live, 0.0, NEGATIVE)
    bias_ref[...] = vb_ref[...]
    column = lax.broadcasted_iota(jnp.int32, (tok, HEAD_DIM), 1)
    for kv_head in range(kv_heads):
        keys = pair_ref[:, head_cols(kv_head)]
        values = biased(pair_ref[:, head_cols(kv_heads + kv_head)], vb_ref[kv_head : kv_head + 1, :])
        for head in range(kv_head * GROUP, (kv_head + 1) * GROUP):
            at = slice(head * tok, (head + 1) * tok)
            queries_ref[at, :HEAD_DIM] = biased(q_ref[:, head_cols(head)], qb_ref[head : head + 1, :])
            queries_ref[at, HEAD_DIM:] = (column == head).astype(jnp.bfloat16)
            grads_ref[at, :] = g_ref[:, head_cols(head)]
        rows = slice(kv_head * GROUP * tok, (kv_head + 1) * GROUP * tok)
        score_ref[:, rows] = dot(keys, queries_ref[rows, :HEAD_DIM], 1, 1)
        dprob_ref[:, rows] = dot(values, grads_ref[rows, :], 1, 1)


def attend_kernel(slots, *refs):
    bias_ref, queries_ref, grads_ref, score_ref, dprob_ref, live_ref = refs[:6]
    pair_refs = refs[6 : 6 + slots][::-1]
    refs = refs[6 + slots :]
    probs_ref, dscore_ref, keys_ref, values_ref, sums_ref, own_ref = refs[:6]
    out_refs = refs[6:]
    tok = pair_refs[0].shape[0]
    kv_heads = bias_ref.shape[0]
    kv_width = kv_heads * HEAD_DIM
    heads = kv_heads * GROUP
    for slot in range(slots):
        rows = slice(slot * tok, (slot + 1) * tok)
        keys_ref[rows, :] = pair_refs[slot][:, :kv_width]
        for kv_head in range(kv_heads):
            values_ref[rows, head_cols(kv_head)] = biased(
                pair_refs[slot][:, head_cols(kv_heads + kv_head)], bias_ref[kv_head : kv_head + 1, :]
            )
    for kv_head in range(kv_heads):
        cols = head_cols(kv_head)
        keys = keys_ref[tok:, cols]
        values = values_ref[tok:, cols]
        key_term = jnp.zeros((slots * tok, 2 * HEAD_DIM), jnp.float32)
        value_term = jnp.zeros((slots * tok, HEAD_DIM), jnp.float32)
        for pair in range(GROUP // PAIR):
            first = kv_head * GROUP + pair * PAIR
            at = slice(first * tok, (first + PAIR) * tok)
            queries = queries_ref[at, :]
            grads = grads_ref[at, :]
            live = jnp.concatenate([live_ref[...]] * PAIR, axis=1)
            score = jnp.concatenate(
                [score_ref[:, at], dot(keys, queries[:, :HEAD_DIM], 1, 1)], axis=0
            )
            score = score * (SCALE * LOG2E) + live
            row_max = jnp.max(score, axis=0, keepdims=True)
            weights = jnp.exp2(score - row_max)
            probs = weights * (1.0 / jnp.sum(weights, axis=0, keepdims=True))
            dprob = jnp.concatenate([dprob_ref[:, at], dot(values, grads, 1, 1)], axis=0)
            delta = jnp.sum(probs * dprob, axis=0, keepdims=True)
            dscore = (probs * (dprob - delta)).astype(jnp.bfloat16)
            probs = probs.astype(jnp.bfloat16)
            probs_ref[:, at] = probs
            dscore_ref[:, at] = dscore
            value_term = value_term + dot(probs, grads, 1, 0)
            key_term = key_term + dot(dscore, queries, 1, 0)
        over_queries = key_term[:, HEAD_DIM:]
        key_term = key_term[:, :HEAD_DIM] * SCALE
        high = over_queries.astype(jnp.bfloat16)
        low = (over_queries - high.astype(jnp.float32)).astype(jnp.bfloat16)
        all_keys = keys_ref[:, cols]
        query_sums = (dot(high, all_keys, 0, 0) + dot(low, all_keys, 0, 0)) * SCALE
        of_group = slice(kv_head * GROUP, (kv_head + 1) * GROUP)
        sums_ref[of_group, :] = query_sums[of_group]
        sums_ref[heads + kv_head : heads + kv_head + 1, :] = jnp.sum(
            value_term, axis=0, keepdims=True
        )
        value_cols = head_cols(kv_heads + kv_head)
        own_ref[:, cols] = key_term[:tok]
        own_ref[:, value_cols] = value_term[:tok]
        for slot in range(1, slots):
            rows = slice(slot * tok, (slot + 1) * tok)
            out_refs[slot - 1][:, cols] = key_term[rows].astype(jnp.bfloat16)
            out_refs[slot - 1][:, value_cols] = value_term[rows].astype(jnp.bfloat16)


def finish_kernel(probs_ref, dscore_ref, keys_ref, values_ref, attn_ref, qg_ref):
    tok = attn_ref.shape[0]
    kv_heads = keys_ref.shape[1] // HEAD_DIM
    for kv_head in range(kv_heads):
        cols = head_cols(kv_head)
        keys_t = keys_ref[:, cols].T
        values_t = values_ref[:, cols].T
        for pair in range(GROUP // PAIR):
            first = kv_head * GROUP + pair * PAIR
            at = slice(first * tok, (first + PAIR) * tok)
            attn = dot(values_t, probs_ref[:, at], 1, 0).T
            query_grad = (dot(keys_t, dscore_ref[:, at], 1, 0) * SCALE).T
            for n in range(PAIR):
                head = first + n
                rows = slice(n * tok, (n + 1) * tok)
                attn_ref[:, head_cols(head)] = attn[rows].astype(jnp.bfloat16)
                qg_ref[:, head_cols(head)] = query_grad[rows].astype(jnp.bfloat16)


def collect_kernel(batches, kv_parts, sums_ref, own_ref, *refs):
    back_refs, refs = refs[:kv_parts], refs[kv_parts:]
    kg_ref, vg_ref, qb_ref, vb_ref = refs
    heads = qb_ref.shape[0]
    kv_width = kg_ref.shape[1]
    total = jnp.sum(sums_ref[...], axis=0) * (1.0 / batches)
    qb_ref[...] = total[:heads]
    vb_ref[...] = total[heads:]
    term = own_ref[...]
    for ref in back_refs:
        term = term + ref[...].astype(jnp.float32)
    term = term.astype(jnp.bfloat16)
    kg_ref[...] = term[:, :kv_width]
    vg_ref[...] = term[:, kv_width:]


def gathered(axis, part):
    copies = jnp.broadcast_to(part, (lax.axis_size(axis),) + part.shape)
    return lax.all_to_all(copies, axis, split_axis=0, concat_axis=0, tiled=True)


def shards(q_proj, q_bias, k_proj, v_proj, v_bias, dout, lengths):
    _, tok, width = q_proj.shape
    kv_width = k_proj.shape[2]
    heads = width // HEAD_DIM
    kv_heads = kv_width // HEAD_DIM
    ctx = lax.axis_size("ctx")
    batches = lax.axis_size("dp")
    rows = ctx * tok
    columns = heads * tok
    pair = jnp.concatenate([k_proj[0], v_proj[0]], axis=1)
    pairs = [
        lax.ppermute(pair, "ctx", [(i, i + shift) for i in range(ctx - shift)])
        for shift in range(ctx - 1, 0, -1)
    ] + [pair]
    prepared = pl.pallas_call(
        functools.partial(prepare_kernel, ctx),
        out_shape=[
            shape((kv_heads, HEAD_DIM), jnp.bfloat16),
            shape((columns, 2 * HEAD_DIM), jnp.bfloat16),
            shape((columns, HEAD_DIM), jnp.bfloat16),
            shape((tok, columns), jnp.float32),
            shape((tok, columns), jnp.float32),
            shape((rows, tok), jnp.float32),
        ],
        in_specs=[SMEM] + [VMEM] * 5,
        out_specs=[VMEM] * 6,
        compiler_params=params(16),
        cost_estimate=pl.CostEstimate(
            flops=4 * tok * tok * width, bytes_accessed=16 * tok * width, transcendentals=0
        ),
        name="prepare",
    )(
        lengths,
        pair,
        q_bias.reshape(heads, HEAD_DIM),
        v_bias.reshape(kv_heads, HEAD_DIM),
        q_proj[0],
        dout[0],
    )
    term = shape((tok, 2 * kv_width), jnp.bfloat16)
    probs, dscore, all_keys, all_values, sums, own, *terms = pl.pallas_call(
        functools.partial(attend_kernel, ctx),
        out_shape=[
            shape((rows, columns), jnp.bfloat16),
            shape((rows, columns), jnp.bfloat16),
            shape((rows, kv_width), jnp.bfloat16),
            shape((rows, kv_width), jnp.bfloat16),
            shape((heads + kv_heads, HEAD_DIM), jnp.float32),
            shape((tok, 2 * kv_width), jnp.float32),
        ]
        + [term] * (ctx - 1),
        in_specs=[VMEM] * (6 + ctx),
        out_specs=[VMEM] * (6 + ctx - 1),
        compiler_params=params(40),
        cost_estimate=pl.CostEstimate(
            flops=8 * rows * tok * width,
            bytes_accessed=4 * rows * columns,
            transcendentals=rows * columns,
        ),
        name="attend",
    )(*prepared, *pairs)
    back = [
        lax.ppermute(term, "ctx", [(i, i - shift) for i in range(shift, ctx)])
        for shift, term in enumerate(terms, 1)
    ]
    attn, q_grad = pl.pallas_call(
        finish_kernel,
        out_shape=[
            shape((tok, width), jnp.bfloat16),
            shape((tok, width), jnp.bfloat16),
        ],
        in_specs=[VMEM] * 4,
        out_specs=[VMEM] * 2,
        compiler_params=params(24),
        cost_estimate=pl.CostEstimate(
            flops=4 * rows * tok * width, bytes_accessed=4 * rows * columns, transcendentals=0
        ),
        name="finish",
    )(probs, dscore, all_keys, all_values)
    sums = gathered("ctx", jnp.sum(gathered("dp", sums), axis=0))
    k_grad, v_grad, q_sum, v_sum = pl.pallas_call(
        functools.partial(collect_kernel, batches, len(back)),
        out_shape=[
            shape((tok, kv_width), jnp.bfloat16),
            shape((tok, kv_width), jnp.bfloat16),
            shape((heads, HEAD_DIM), jnp.float32),
            shape((kv_heads, HEAD_DIM), jnp.float32),
        ],
        in_specs=[VMEM] * (2 + len(back)),
        out_specs=[VMEM] * 4,
        compiler_params=params(8),
        cost_estimate=pl.CostEstimate(
            flops=8 * tok * kv_width, bytes_accessed=16 * tok * kv_width, transcendentals=0
        ),
        name="collect",
    )(sums, own, *back)
    return (
        attn[None],
        q_grad[None],
        k_grad[None],
        v_grad[None],
        q_sum.reshape(width),
        v_sum.reshape(kv_width),
    )


def solution(mesh):
    tokens = P("dp", "ctx", "tp")
    return jax.shard_map(
        shards,
        mesh=mesh,
        in_specs=(tokens, P("tp"), tokens, tokens, P("tp"), tokens, P("dp", None)),
        out_specs=(tokens, tokens, tokens, tokens, P("tp"), P("tp")),
        check_vma=False,
    )
```

```python
import functools

import jax
import jax.numpy as jnp
from jax import lax
from jax.experimental import pallas as pl
from jax.experimental.pallas import tpu as pltpu
from jax.sharding import PartitionSpec as P

HEAD_DIM = 128
HEADS = 32
KV_HEADS = 4
GROUP = HEADS // KV_HEADS
PAIR = 2
SCALE = HEAD_DIM ** (-0.5)
LOG2E = 1.4426950408889634
NEGATIVE = -1e30
VMEM = pl.BlockSpec(memory_space=pltpu.VMEM)
SMEM = pl.BlockSpec(memory_space=pltpu.SMEM)


def dot(left, right, left_dim, right_dim):
    return lax.dot_general(
        left, right, (((left_dim,), (right_dim,)), ((), ())), preferred_element_type=jnp.float32
    )


def head_cols(head):
    return slice(head * HEAD_DIM, (head + 1) * HEAD_DIM)


def shape(dims, dtype):
    return jax.ShapeDtypeStruct(dims, dtype)


def params(mebibytes):
    return pltpu.CompilerParams(vmem_limit_bytes=mebibytes * 1024 * 1024)


def biased(values, bias):
    return (values.astype(jnp.float32) + bias.astype(jnp.float32)).astype(jnp.bfloat16)


def prepare_kernel(
    slots, len_ref, pair_ref, qb_ref, vb_ref, q_ref, g_ref, bias_ref, queries_ref, grads_ref,
    score_ref, dprob_ref, live_ref,
):
    tok = q_ref.shape[0]
    kv_heads = vb_ref.shape[0]
    rank = lax.axis_index("ctx")
    query_pos = rank * tok + lax.broadcasted_iota(jnp.int32, (1, tok), 1)
    start = jnp.zeros((1, tok), jnp.int32)
    end = jnp.int32(0)
    for doc in range(len_ref.shape[1]):
        length = len_ref[0, doc]
        end = end + length
        start = start + jnp.where(query_pos >= end, length, 0)
    offsets = lax.broadcasted_iota(jnp.int32, (tok, tok), 0)
    for slot in range(slots):
        key_pos = (rank - slot) * tok + offsets
        live = (key_pos >= start) & (key_pos <= query_pos)
        live_ref[slot * tok : (slot + 1) * tok, :] = jnp.where(live, 0.0, NEGATIVE)
    bias_ref[...] = vb_ref[...]
    column = lax.broadcasted_iota(jnp.int32, (tok, HEAD_DIM), 1)
    for kv_head in range(kv_heads):
        keys = pair_ref[:, head_cols(kv_head)]
        values = biased(pair_ref[:, head_cols(kv_heads + kv_head)], vb_ref[kv_head : kv_head + 1, :])
        for head in range(kv_head * GROUP, (kv_head + 1) * GROUP):
            at = slice(head * tok, (head + 1) * tok)
            queries_ref[at, :HEAD_DIM] = biased(q_ref[:, head_cols(head)], qb_ref[head : head + 1, :])
            queries_ref[at, HEAD_DIM:] = (column == head).astype(jnp.bfloat16)
            grads_ref[at, :] = g_ref[:, head_cols(head)]
        rows = slice(kv_head * GROUP * tok, (kv_head + 1) * GROUP * tok)
        score_ref[:, rows] = dot(keys, queries_ref[rows, :HEAD_DIM], 1, 1)
        dprob_ref[:, rows] = dot(values, grads_ref[rows, :], 1, 1)


def attend_kernel(slots, *refs):
    bias_ref, queries_ref, grads_ref, score_ref, dprob_ref, live_ref = refs[:6]
    pair_refs = refs[6 : 6 + slots][::-1]
    refs = refs[6 + slots :]
    probs_ref, dscore_ref, keys_ref, values_ref, sums_ref, own_ref = refs[:6]
    out_refs = refs[6:]
    tok = pair_refs[0].shape[0]
    kv_heads = bias_ref.shape[0]
    kv_width = kv_heads * HEAD_DIM
    heads = kv_heads * GROUP
    for slot in range(slots):
        rows = slice(slot * tok, (slot + 1) * tok)
        keys_ref[rows, :] = pair_refs[slot][:, :kv_width]
        for kv_head in range(kv_heads):
            values_ref[rows, head_cols(kv_head)] = biased(
                pair_refs[slot][:, head_cols(kv_heads + kv_head)], bias_ref[kv_head : kv_head + 1, :]
            )
    for kv_head in range(kv_heads):
        cols = head_cols(kv_head)
        keys = keys_ref[tok:, cols]
        values = values_ref[tok:, cols]
        key_term = jnp.zeros((slots * tok, 2 * HEAD_DIM), jnp.float32)
        value_term = jnp.zeros((slots * tok, HEAD_DIM), jnp.float32)
        for pair in range(GROUP // PAIR):
            first = kv_head * GROUP + pair * PAIR
            at = slice(first * tok, (first + PAIR) * tok)
            queries = queries_ref[at, :]
            grads = grads_ref[at, :]
            live = jnp.concatenate([live_ref[...]] * PAIR, axis=1)
            score = jnp.concatenate(
                [score_ref[:, at], dot(keys, queries[:, :HEAD_DIM], 1, 1)], axis=0
            )
            score = score * (SCALE * LOG2E) + live
            row_max = jnp.max(score, axis=0, keepdims=True)
            weights = jnp.exp2(score - row_max)
            probs = weights * (1.0 / jnp.sum(weights, axis=0, keepdims=True))
            dprob = jnp.concatenate([dprob_ref[:, at], dot(values, grads, 1, 1)], axis=0)
            delta = jnp.sum(probs * dprob, axis=0, keepdims=True)
            dscore = (probs * (dprob - delta)).astype(jnp.bfloat16)
            probs = probs.astype(jnp.bfloat16)
            probs_ref[:, at] = probs
            dscore_ref[:, at] = dscore
            value_term = value_term + dot(probs, grads, 1, 0)
            key_term = key_term + dot(dscore, queries, 1, 0)
        over_queries = key_term[:, HEAD_DIM:]
        key_term = key_term[:, :HEAD_DIM] * SCALE
        high = over_queries.astype(jnp.bfloat16)
        low = (over_queries - high.astype(jnp.float32)).astype(jnp.bfloat16)
        all_keys = keys_ref[:, cols]
        query_sums = (dot(high, all_keys, 0, 0) + dot(low, all_keys, 0, 0)) * SCALE
        of_group = slice(kv_head * GROUP, (kv_head + 1) * GROUP)
        sums_ref[of_group, :] = query_sums[of_group]
        sums_ref[heads + kv_head : heads + kv_head + 1, :] = jnp.sum(
            value_term, axis=0, keepdims=True
        )
        value_cols = head_cols(kv_heads + kv_head)
        own_ref[:, cols] = key_term[:tok]
        own_ref[:, value_cols] = value_term[:tok]
        for slot in range(1, slots):
            rows = slice(slot * tok, (slot + 1) * tok)
            out_refs[slot - 1][:, cols] = key_term[rows].astype(jnp.bfloat16)
            out_refs[slot - 1][:, value_cols] = value_term[rows].astype(jnp.bfloat16)


def finish_kernel(probs_ref, dscore_ref, keys_ref, values_ref, attn_ref, qg_ref):
    tok = attn_ref.shape[0]
    kv_heads = keys_ref.shape[1] // HEAD_DIM
    for kv_head in range(kv_heads):
        cols = head_cols(kv_head)
        keys_t = keys_ref[:, cols].T
        values_t = values_ref[:, cols].T
        for pair in range(GROUP // PAIR):
            first = kv_head * GROUP + pair * PAIR
            at = slice(first * tok, (first + PAIR) * tok)
            attn = dot(values_t, probs_ref[:, at], 1, 0).T
            query_grad = (dot(keys_t, dscore_ref[:, at], 1, 0) * SCALE).T
            for n in range(PAIR):
                head = first + n
                rows = slice(n * tok, (n + 1) * tok)
                attn_ref[:, head_cols(head)] = attn[rows].astype(jnp.bfloat16)
                qg_ref[:, head_cols(head)] = query_grad[rows].astype(jnp.bfloat16)


def collect_kernel(batches, parts, kv_parts, *refs):
    sum_refs, refs = refs[:parts], refs[parts:]
    own_ref, refs = refs[0], refs[1:]
    back_refs, refs = refs[:kv_parts], refs[kv_parts:]
    kg_ref, vg_ref, qb_ref, vb_ref = refs
    heads = qb_ref.shape[0]
    kv_width = kg_ref.shape[1]
    total = sum_refs[0][...]
    for ref in sum_refs[1:]:
        total = total + ref[...]
    total = total * (1.0 / batches)
    qb_ref[...] = total[:heads]
    vb_ref[...] = total[heads:]
    term = own_ref[...]
    for ref in back_refs:
        term = term + ref[...].astype(jnp.float32)
    term = term.astype(jnp.bfloat16)
    kg_ref[...] = term[:, :kv_width]
    vg_ref[...] = term[:, kv_width:]


def total_of(parts):
    return functools.reduce(lambda left, right: left + right, parts)


def exchange(axis, part):
    size = lax.axis_size(axis)
    return [part] + [
        lax.ppermute(part, axis, [(i, (i + shift) % size) for i in range(size)])
        for shift in range(1, size)
    ]


def shards(q_proj, q_bias, k_proj, v_proj, v_bias, dout, lengths):
    _, tok, width = q_proj.shape
    kv_width = k_proj.shape[2]
    heads = width // HEAD_DIM
    kv_heads = kv_width // HEAD_DIM
    ctx = lax.axis_size("ctx")
    batches = lax.axis_size("dp")
    rows = ctx * tok
    columns = heads * tok
    pair = jnp.concatenate([k_proj[0], v_proj[0]], axis=1)
    pairs = [
        lax.ppermute(pair, "ctx", [(i, i + shift) for i in range(ctx - shift)])
        for shift in range(ctx - 1, 0, -1)
    ] + [pair]
    prepared = pl.pallas_call(
        functools.partial(prepare_kernel, ctx),
        out_shape=[
            shape((kv_heads, HEAD_DIM), jnp.bfloat16),
            shape((columns, 2 * HEAD_DIM), jnp.bfloat16),
            shape((columns, HEAD_DIM), jnp.bfloat16),
            shape((tok, columns), jnp.float32),
            shape((tok, columns), jnp.float32),
            shape((rows, tok), jnp.float32),
        ],
        in_specs=[SMEM] + [VMEM] * 5,
        out_specs=[VMEM] * 6,
        compiler_params=params(16),
        cost_estimate=pl.CostEstimate(
            flops=4 * tok * tok * width, bytes_accessed=16 * tok * width, transcendentals=0
        ),
        name="prepare",
    )(
        lengths,
        pair,
        q_bias.reshape(heads, HEAD_DIM),
        v_bias.reshape(kv_heads, HEAD_DIM),
        q_proj[0],
        dout[0],
    )
    term = shape((tok, 2 * kv_width), jnp.bfloat16)
    probs, dscore, all_keys, all_values, sums, own, *terms = pl.pallas_call(
        functools.partial(attend_kernel, ctx),
        out_shape=[
            shape((rows, columns), jnp.bfloat16),
            shape((rows, columns), jnp.bfloat16),
            shape((rows, kv_width), jnp.bfloat16),
            shape((rows, kv_width), jnp.bfloat16),
            shape((heads + kv_heads, HEAD_DIM), jnp.float32),
            shape((tok, 2 * kv_width), jnp.float32),
        ]
        + [term] * (ctx - 1),
        in_specs=[VMEM] * (6 + ctx),
        out_specs=[VMEM] * (6 + ctx - 1),
        compiler_params=params(40),
        cost_estimate=pl.CostEstimate(
            flops=8 * rows * tok * width,
            bytes_accessed=4 * rows * columns,
            transcendentals=rows * columns,
        ),
        name="attend",
    )(*prepared, *pairs)
    back = [
        lax.ppermute(term, "ctx", [(i, i - shift) for i in range(shift, ctx)])
        for shift, term in enumerate(terms, 1)
    ]
    attn, q_grad = pl.pallas_call(
        finish_kernel,
        out_shape=[
            shape((tok, width), jnp.bfloat16),
            shape((tok, width), jnp.bfloat16),
        ],
        in_specs=[VMEM] * 4,
        out_specs=[VMEM] * 2,
        compiler_params=params(24),
        cost_estimate=pl.CostEstimate(
            flops=4 * rows * tok * width, bytes_accessed=4 * rows * columns, transcendentals=0
        ),
        name="finish",
    )(probs, dscore, all_keys, all_values)
    sums = exchange("ctx", total_of(exchange("dp", sums)))
    k_grad, v_grad, q_sum, v_sum = pl.pallas_call(
        functools.partial(collect_kernel, batches, len(sums), len(back)),
        out_shape=[
            shape((tok, kv_width), jnp.bfloat16),
            shape((tok, kv_width), jnp.bfloat16),
            shape((heads, HEAD_DIM), jnp.float32),
            shape((kv_heads, HEAD_DIM), jnp.float32),
        ],
        in_specs=[VMEM] * (len(sums) + 1 + len(back)),
        out_specs=[VMEM] * 4,
        compiler_params=params(8),
        cost_estimate=pl.CostEstimate(
            flops=8 * tok * kv_width, bytes_accessed=16 * tok * kv_width, transcendentals=0
        ),
        name="collect",
    )(*sums, own, *back)
    return (
        attn[None],
        q_grad[None],
        k_grad[None],
        v_grad[None],
        q_sum.reshape(width),
        v_sum.reshape(kv_width),
    )


def solution(mesh):
    tokens = P("dp", "ctx", "tp")
    return jax.shard_map(
        shards,
        mesh=mesh,
        in_specs=(tokens, P("tp"), tokens, tokens, P("tp"), tokens, P("dp", None)),
        out_specs=(tokens, tokens, tokens, tokens, P("tp"), P("tp")),
        check_vma=False,
    )
```

```python
import functools

import jax
import jax.numpy as jnp
from jax import lax
from jax.experimental import pallas as pl
from jax.experimental.pallas import tpu as pltpu
from jax.sharding import PartitionSpec as P

HEAD_DIM = 128
HEADS = 32
KV_HEADS = 4
GROUP = HEADS // KV_HEADS
PAIR = 2
BLOCK = 64
SCALE = HEAD_DIM ** (-0.5)
LOG2E = 1.4426950408889634
NEGATIVE = -1e30
VMEM = pl.BlockSpec(memory_space=pltpu.VMEM)
SMEM = pl.BlockSpec(memory_space=pltpu.SMEM)


def dot(left, right, left_dim, right_dim):
    return lax.dot_general(
        left, right, (((left_dim,), (right_dim,)), ((), ())), preferred_element_type=jnp.float32
    )


def head_cols(head):
    return slice(head * HEAD_DIM, (head + 1) * HEAD_DIM)


def shape(dims, dtype):
    return jax.ShapeDtypeStruct(dims, dtype)


def params(mebibytes):
    return pltpu.CompilerParams(vmem_limit_bytes=mebibytes * 1024 * 1024)


def biased(values, bias):
    return (values.astype(jnp.float32) + bias.astype(jnp.float32)).astype(jnp.bfloat16)


def prepare_kernel(
    slots, len_ref, pair_ref, qb_ref, vb_ref, q_ref, g_ref, bias_ref, queries_ref, grads_ref,
    score_ref, dprob_ref, live_ref,
):
    tok = q_ref.shape[0]
    kv_heads = vb_ref.shape[0]
    rank = lax.axis_index("ctx")
    query_pos = rank * tok + lax.broadcasted_iota(jnp.int32, (1, tok), 1)
    start = jnp.zeros((1, tok), jnp.int32)
    end = jnp.int32(0)
    for doc in range(len_ref.shape[1]):
        length = len_ref[0, doc]
        end = end + length
        start = start + jnp.where(query_pos >= end, length, 0)
    offsets = lax.broadcasted_iota(jnp.int32, (tok, tok), 0)
    for slot in range(slots):
        key_pos = (rank - slot) * tok + offsets
        live = (key_pos >= start) & (key_pos <= query_pos)
        live_ref[slot * tok : (slot + 1) * tok, :] = jnp.where(live, 0.0, NEGATIVE)
    bias_ref[...] = vb_ref[...]
    column = lax.broadcasted_iota(jnp.int32, (tok, HEAD_DIM), 1)
    for kv_head in range(kv_heads):
        keys = pair_ref[:, head_cols(kv_head)]
        values = biased(pair_ref[:, head_cols(kv_heads + kv_head)], vb_ref[kv_head : kv_head + 1, :])
        for head in range(kv_head * GROUP, (kv_head + 1) * GROUP):
            at = slice(head * tok, (head + 1) * tok)
            queries_ref[at, :HEAD_DIM] = biased(q_ref[:, head_cols(head)], qb_ref[head : head + 1, :])
            queries_ref[at, HEAD_DIM:] = (column == head).astype(jnp.bfloat16)
            grads_ref[at, :] = g_ref[:, head_cols(head)]
        rows = slice(kv_head * GROUP * tok, (kv_head + 1) * GROUP * tok)
        score_ref[:, rows] = dot(keys, queries_ref[rows, :HEAD_DIM], 1, 1)
        dprob_ref[:, rows] = dot(values, grads_ref[rows, :], 1, 1)


def attend_kernel(slots, *refs):
    bias_ref, queries_ref, grads_ref, score_ref, dprob_ref, live_ref = refs[:6]
    pair_refs = refs[6 : 6 + slots][::-1]
    refs = refs[6 + slots :]
    probs_ref, dscore_ref, keys_ref, values_ref, sums_ref, own_ref = refs[:6]
    out_refs = refs[6 : 6 + slots - 1]
    weights_ref, all_dprob_ref = refs[6 + slots - 1 :]
    tok = pair_refs[0].shape[0]
    kv_heads = bias_ref.shape[0]
    kv_width = kv_heads * HEAD_DIM
    heads = kv_heads * GROUP
    for slot in range(slots):
        rows = slice(slot * tok, (slot + 1) * tok)
        keys_ref[rows, :] = pair_refs[slot][:, :kv_width]
        for kv_head in range(kv_heads):
            values_ref[rows, head_cols(kv_head)] = biased(
                pair_refs[slot][:, head_cols(kv_heads + kv_head)], bias_ref[kv_head : kv_head + 1, :]
            )
    blocks = [slice(row, row + BLOCK) for row in range(0, slots * tok, BLOCK)]
    for kv_head in range(kv_heads):
        cols = head_cols(kv_head)
        group = slice(kv_head * GROUP * tok, (kv_head + 1) * GROUP * tok)
        weights_ref[tok:, group] = dot(keys_ref[tok:, cols], queries_ref[group, :HEAD_DIM], 1, 1)
        all_dprob_ref[tok:, group] = dot(values_ref[tok:, cols], grads_ref[group, :], 1, 1)
        for pair in range(GROUP // PAIR):
            first = kv_head * GROUP + pair * PAIR
            at = slice(first * tok, (first + PAIR) * tok)
            row_max = None
            for block in blocks:
                score = (score_ref if block.start < tok else weights_ref)[block, at]
                score = score + jnp.concatenate([live_ref[block, :]] * PAIR, axis=1)
                weights_ref[block, at] = score
                part = jnp.max(score.reshape(-1, 8, PAIR * tok), axis=0)
                row_max = part if row_max is None else jnp.maximum(row_max, part)
            row_max = jnp.max(row_max, axis=0, keepdims=True)
            total = jnp.zeros((8, PAIR * tok), jnp.float32)
            delta = jnp.zeros((8, PAIR * tok), jnp.float32)
            for block in blocks:
                dprob = (dprob_ref if block.start < tok else all_dprob_ref)[block, at]
                weights = jnp.exp2((weights_ref[block, at] - row_max) * (SCALE * LOG2E))
                weights_ref[block, at] = weights
                total = total + jnp.sum(weights.reshape(-1, 8, PAIR * tok), axis=0)
                delta = delta + jnp.sum((weights * dprob).reshape(-1, 8, PAIR * tok), axis=0)
            inverse = 1.0 / jnp.sum(total, axis=0, keepdims=True)
            delta = jnp.sum(delta, axis=0, keepdims=True) * inverse
            for block in blocks:
                dprob = (dprob_ref if block.start < tok else all_dprob_ref)[block, at]
                probs = weights_ref[block, at] * inverse
                probs_ref[block, at] = probs.astype(jnp.bfloat16)
                dscore_ref[block, at] = (probs * (dprob - delta)).astype(jnp.bfloat16)
        value_term = dot(probs_ref[:, group], grads_ref[group, :], 1, 0)
        key_term = dot(dscore_ref[:, group], queries_ref[group, :], 1, 0)
        over_queries = key_term[:, HEAD_DIM:]
        key_term = key_term[:, :HEAD_DIM] * SCALE
        high = over_queries.astype(jnp.bfloat16)
        low = (over_queries - high.astype(jnp.float32)).astype(jnp.bfloat16)
        all_keys = keys_ref[:, cols]
        query_sums = (dot(high, all_keys, 0, 0) + dot(low, all_keys, 0, 0)) * SCALE
        of_group = slice(kv_head * GROUP, (kv_head + 1) * GROUP)
        sums_ref[of_group, :] = query_sums[of_group]
        sums_ref[heads + kv_head : heads + kv_head + 1, :] = jnp.sum(
            value_term, axis=0, keepdims=True
        )
        value_cols = head_cols(kv_heads + kv_head)
        own_ref[:, cols] = key_term[:tok]
        own_ref[:, value_cols] = value_term[:tok]
        for slot in range(1, slots):
            rows = slice(slot * tok, (slot + 1) * tok)
            out_refs[slot - 1][:, cols] = key_term[rows].astype(jnp.bfloat16)
            out_refs[slot - 1][:, value_cols] = value_term[rows].astype(jnp.bfloat16)


def finish_kernel(probs_ref, dscore_ref, keys_ref, values_ref, attn_ref, qg_ref):
    tok = attn_ref.shape[0]
    kv_heads = keys_ref.shape[1] // HEAD_DIM
    for kv_head in range(kv_heads):
        cols = head_cols(kv_head)
        keys_t = keys_ref[:, cols].T
        values_t = values_ref[:, cols].T
        for pair in range(GROUP // PAIR):
            first = kv_head * GROUP + pair * PAIR
            at = slice(first * tok, (first + PAIR) * tok)
            attn = dot(values_t, probs_ref[:, at], 1, 0).T
            query_grad = (dot(keys_t, dscore_ref[:, at], 1, 0) * SCALE).T
            for n in range(PAIR):
                head = first + n
                rows = slice(n * tok, (n + 1) * tok)
                attn_ref[:, head_cols(head)] = attn[rows].astype(jnp.bfloat16)
                qg_ref[:, head_cols(head)] = query_grad[rows].astype(jnp.bfloat16)


def collect_kernel(batches, parts, kv_parts, *refs):
    sum_refs, refs = refs[:parts], refs[parts:]
    own_ref, refs = refs[0], refs[1:]
    back_refs, refs = refs[:kv_parts], refs[kv_parts:]
    kg_ref, vg_ref, qb_ref, vb_ref = refs
    heads = qb_ref.shape[0]
    kv_width = kg_ref.shape[1]
    total = sum_refs[0][...]
    for ref in sum_refs[1:]:
        total = total + ref[...]
    total = total * (1.0 / batches)
    qb_ref[...] = total[:heads]
    vb_ref[...] = total[heads:]
    term = own_ref[...]
    for ref in back_refs:
        term = term + ref[...].astype(jnp.float32)
    term = term.astype(jnp.bfloat16)
    kg_ref[...] = term[:, :kv_width]
    vg_ref[...] = term[:, kv_width:]


def total_of(parts):
    return functools.reduce(lambda left, right: left + right, parts)


def exchange(axis, part):
    size = lax.axis_size(axis)
    if axis == "ctx" and not size & (size - 1):
        step = 1
        while 2 * step < size:
            part = part + lax.ppermute(part, axis, [(i, i ^ step) for i in range(size)])
            step *= 2
        return [part, lax.ppermute(part, axis, [(i, i ^ step) for i in range(size)])]
    return [part] + [
        lax.ppermute(part, axis, [(i, (i + shift) % size) for i in range(size)])
        for shift in range(1, size)
    ]


def shards(q_proj, q_bias, k_proj, v_proj, v_bias, dout, lengths):
    _, tok, width = q_proj.shape
    kv_width = k_proj.shape[2]
    heads = width // HEAD_DIM
    kv_heads = kv_width // HEAD_DIM
    ctx = lax.axis_size("ctx")
    batches = lax.axis_size("dp")
    rows = ctx * tok
    columns = heads * tok
    pair = jnp.concatenate([k_proj[0], v_proj[0]], axis=1)
    pairs = [
        lax.ppermute(pair, "ctx", [(i, i + shift) for i in range(ctx - shift)])
        for shift in range(ctx - 1, 0, -1)
    ] + [pair]
    prepared = pl.pallas_call(
        functools.partial(prepare_kernel, ctx),
        out_shape=[
            shape((kv_heads, HEAD_DIM), jnp.bfloat16),
            shape((columns, 2 * HEAD_DIM), jnp.bfloat16),
            shape((columns, HEAD_DIM), jnp.bfloat16),
            shape((tok, columns), jnp.float32),
            shape((tok, columns), jnp.float32),
            shape((rows, tok), jnp.float32),
        ],
        in_specs=[SMEM] + [VMEM] * 5,
        out_specs=[VMEM] * 6,
        compiler_params=params(16),
        cost_estimate=pl.CostEstimate(
            flops=4 * tok * tok * width, bytes_accessed=16 * tok * width, transcendentals=0
        ),
        name="prepare",
    )(
        lengths,
        pair,
        q_bias.reshape(heads, HEAD_DIM),
        v_bias.reshape(kv_heads, HEAD_DIM),
        q_proj[0],
        dout[0],
    )
    term = shape((tok, 2 * kv_width), jnp.bfloat16)
    probs, dscore, all_keys, all_values, sums, own, *terms = pl.pallas_call(
        functools.partial(attend_kernel, ctx),
        out_shape=[
            shape((rows, columns), jnp.bfloat16),
            shape((rows, columns), jnp.bfloat16),
            shape((rows, kv_width), jnp.bfloat16),
            shape((rows, kv_width), jnp.bfloat16),
            shape((heads + kv_heads, HEAD_DIM), jnp.float32),
            shape((tok, 2 * kv_width), jnp.float32),
        ]
        + [term] * (ctx - 1),
        in_specs=[VMEM] * (6 + ctx),
        out_specs=[VMEM] * (6 + ctx - 1),
        scratch_shapes=[
            pltpu.VMEM((rows, columns), jnp.float32),
            pltpu.VMEM((rows, columns), jnp.float32),
        ],
        compiler_params=params(24 if ctx < 8 else 48),
        cost_estimate=pl.CostEstimate(
            flops=8 * rows * tok * width,
            bytes_accessed=4 * rows * columns,
            transcendentals=rows * columns,
        ),
        name="attend",
    )(*prepared, *pairs)
    back = [
        lax.ppermute(term, "ctx", [(i, i - shift) for i in range(shift, ctx)])
        for shift, term in enumerate(terms, 1)
    ]
    attn, q_grad = pl.pallas_call(
        finish_kernel,
        out_shape=[
            shape((tok, width), jnp.bfloat16),
            shape((tok, width), jnp.bfloat16),
        ],
        in_specs=[VMEM] * 4,
        out_specs=[VMEM] * 2,
        compiler_params=params(24),
        cost_estimate=pl.CostEstimate(
            flops=4 * rows * tok * width, bytes_accessed=4 * rows * columns, transcendentals=0
        ),
        name="finish",
    )(probs, dscore, all_keys, all_values)
    sums = exchange("ctx", total_of(exchange("dp", sums)))
    k_grad, v_grad, q_sum, v_sum = pl.pallas_call(
        functools.partial(collect_kernel, batches, len(sums), len(back)),
        out_shape=[
            shape((tok, kv_width), jnp.bfloat16),
            shape((tok, kv_width), jnp.bfloat16),
            shape((heads, HEAD_DIM), jnp.float32),
            shape((kv_heads, HEAD_DIM), jnp.float32),
        ],
        in_specs=[VMEM] * (len(sums) + 1 + len(back)),
        out_specs=[VMEM] * 4,
        compiler_params=params(8),
        cost_estimate=pl.CostEstimate(
            flops=8 * tok * kv_width, bytes_accessed=16 * tok * kv_width, transcendentals=0
        ),
        name="collect",
    )(*sums, own, *back)
    return (
        attn[None],
        q_grad[None],
        k_grad[None],
        v_grad[None],
        q_sum.reshape(width),
        v_sum.reshape(kv_width),
    )


def solution(mesh):
    tokens = P("dp", "ctx", "tp")
    return jax.shard_map(
        shards,
        mesh=mesh,
        in_specs=(tokens, P("tp"), tokens, tokens, P("tp"), tokens, P("dp", None)),
        out_specs=(tokens, tokens, tokens, tokens, P("tp"), P("tp")),
        check_vma=False,
    )
```

```python
import functools

import jax
import jax.numpy as jnp
from jax import lax
from jax.experimental import pallas as pl
from jax.experimental.pallas import tpu as pltpu
from jax.sharding import PartitionSpec as P

HEAD_DIM = 128
HEADS = 32
KV_HEADS = 4
GROUP = HEADS // KV_HEADS
PAIR = 2
BLOCK = 64
SCALE = HEAD_DIM ** (-0.5)
LOG2E = 1.4426950408889634
NEGATIVE = -1e30
VMEM = pl.BlockSpec(memory_space=pltpu.VMEM)
ANY = pl.BlockSpec(memory_space=pl.ANY)
SMEM = pl.BlockSpec(memory_space=pltpu.SMEM)


def dot(left, right, left_dim, right_dim):
    return lax.dot_general(
        left, right, (((left_dim,), (right_dim,)), ((), ())), preferred_element_type=jnp.float32
    )


def head_cols(head):
    return slice(head * HEAD_DIM, (head + 1) * HEAD_DIM)


def shape(dims, dtype):
    return jax.ShapeDtypeStruct(dims, dtype)


def params(mebibytes):
    return pltpu.CompilerParams(vmem_limit_bytes=mebibytes * 1024 * 1024)


def biased(values, bias):
    return (values.astype(jnp.float32) + bias.astype(jnp.float32)).astype(jnp.bfloat16)


def prepare_kernel(
    slots, len_ref, pair_ref, qb_ref, vb_ref, q_ref, g_ref, bias_ref, queries_ref, grads_ref,
    score_ref, dprob_ref, live_ref,
):
    tok = q_ref.shape[0]
    kv_heads = vb_ref.shape[0]
    rank = lax.axis_index("ctx")
    query_pos = rank * tok + lax.broadcasted_iota(jnp.int32, (1, tok), 1)
    start = jnp.zeros((1, tok), jnp.int32)
    end = jnp.int32(0)
    for doc in range(len_ref.shape[1]):
        length = len_ref[0, doc]
        end = end + length
        start = start + jnp.where(query_pos >= end, length, 0)
    offsets = lax.broadcasted_iota(jnp.int32, (tok, tok), 0)
    for slot in range(slots):
        key_pos = (rank - slot) * tok + offsets
        live = (key_pos >= start) & (key_pos <= query_pos)
        live_ref[slot * tok : (slot + 1) * tok, :] = jnp.where(live, 0.0, NEGATIVE)
    bias_ref[...] = vb_ref[...]
    column = lax.broadcasted_iota(jnp.int32, (tok, HEAD_DIM), 1)
    for kv_head in range(kv_heads):
        keys = pair_ref[:, head_cols(kv_head)]
        values = biased(pair_ref[:, head_cols(kv_heads + kv_head)], vb_ref[kv_head : kv_head + 1, :])
        for head in range(kv_head * GROUP, (kv_head + 1) * GROUP):
            at = slice(head * tok, (head + 1) * tok)
            queries_ref[at, :HEAD_DIM] = biased(q_ref[:, head_cols(head)], qb_ref[head : head + 1, :])
            queries_ref[at, HEAD_DIM:] = (column == head).astype(jnp.bfloat16)
            grads_ref[at, :] = g_ref[:, head_cols(head)]
        rows = slice(kv_head * GROUP * tok, (kv_head + 1) * GROUP * tok)
        score_ref[:, rows] = dot(keys, queries_ref[rows, :HEAD_DIM], 1, 1)
        dprob_ref[:, rows] = dot(values, grads_ref[rows, :], 1, 1)


def attend_kernel(slots, *refs):
    bias_ref, queries_ref, grads_ref, score_ref, dprob_ref, live_ref = refs[:6]
    pair_refs = refs[6 : 6 + slots][::-1]
    refs = refs[6 + slots :]
    probs_ref, dscore_ref, keys_ref, values_ref, sums_ref, own_ref = refs[:6]
    out_refs = refs[6 : 6 + slots - 1]
    weights_ref, all_dprob_ref = refs[6 + slots - 1 :]
    tok = pair_refs[0].shape[0]
    kv_heads = bias_ref.shape[0]
    kv_width = kv_heads * HEAD_DIM
    heads = kv_heads * GROUP
    for slot in range(slots):
        rows = slice(slot * tok, (slot + 1) * tok)
        keys_ref[rows, :] = pair_refs[slot][:, :kv_width]
        for kv_head in range(kv_heads):
            values_ref[rows, head_cols(kv_head)] = biased(
                pair_refs[slot][:, head_cols(kv_heads + kv_head)], bias_ref[kv_head : kv_head + 1, :]
            )
    blocks = [slice(row, row + BLOCK) for row in range(0, slots * tok, BLOCK)]
    for kv_head in range(kv_heads):
        cols = head_cols(kv_head)
        group = slice(kv_head * GROUP * tok, (kv_head + 1) * GROUP * tok)
        weights_ref[tok:, group] = dot(keys_ref[tok:, cols], queries_ref[group, :HEAD_DIM], 1, 1)
        all_dprob_ref[tok:, group] = dot(values_ref[tok:, cols], grads_ref[group, :], 1, 1)
        for pair in range(GROUP // PAIR):
            first = kv_head * GROUP + pair * PAIR
            at = slice(first * tok, (first + PAIR) * tok)
            row_max = None
            for block in blocks:
                score = (score_ref if block.start < tok else weights_ref)[block, at]
                score = score + jnp.concatenate([live_ref[block, :]] * PAIR, axis=1)
                weights_ref[block, at] = score
                part = jnp.max(score.reshape(-1, 8, PAIR * tok), axis=0)
                row_max = part if row_max is None else jnp.maximum(row_max, part)
            row_max = jnp.max(row_max, axis=0, keepdims=True)
            total = jnp.zeros((8, PAIR * tok), jnp.float32)
            delta = jnp.zeros((8, PAIR * tok), jnp.float32)
            for block in blocks:
                dprob = (dprob_ref if block.start < tok else all_dprob_ref)[block, at]
                weights = jnp.exp2((weights_ref[block, at] - row_max) * (SCALE * LOG2E))
                weights_ref[block, at] = weights
                total = total + jnp.sum(weights.reshape(-1, 8, PAIR * tok), axis=0)
                delta = delta + jnp.sum((weights * dprob).reshape(-1, 8, PAIR * tok), axis=0)
            inverse = 1.0 / jnp.sum(total, axis=0, keepdims=True)
            delta = jnp.sum(delta, axis=0, keepdims=True) * inverse
            for block in blocks:
                dprob = (dprob_ref if block.start < tok else all_dprob_ref)[block, at]
                probs = weights_ref[block, at] * inverse
                probs_ref[block, at] = probs.astype(jnp.bfloat16)
                dscore_ref[block, at] = (probs * (dprob - delta)).astype(jnp.bfloat16)
        value_term = dot(probs_ref[:, group], grads_ref[group, :], 1, 0)
        key_term = dot(dscore_ref[:, group], queries_ref[group, :], 1, 0)
        over_queries = key_term[:, HEAD_DIM:]
        key_term = key_term[:, :HEAD_DIM] * SCALE
        high = over_queries.astype(jnp.bfloat16)
        low = (over_queries - high.astype(jnp.float32)).astype(jnp.bfloat16)
        all_keys = keys_ref[:, cols]
        query_sums = (dot(high, all_keys, 0, 0) + dot(low, all_keys, 0, 0)) * SCALE
        of_group = slice(kv_head * GROUP, (kv_head + 1) * GROUP)
        sums_ref[of_group, :] = query_sums[of_group]
        sums_ref[heads + kv_head : heads + kv_head + 1, :] = jnp.sum(
            value_term, axis=0, keepdims=True
        )
        value_cols = head_cols(kv_heads + kv_head)
        own_ref[:, cols] = key_term[:tok]
        own_ref[:, value_cols] = value_term[:tok]
        for slot in range(1, slots):
            rows = slice(slot * tok, (slot + 1) * tok)
            out_refs[slot - 1][:, cols] = key_term[rows].astype(jnp.bfloat16)
            out_refs[slot - 1][:, value_cols] = value_term[rows].astype(jnp.bfloat16)


def finish_kernel(probs_ref, dscore_ref, keys_ref, values_ref, attn_ref, qg_ref):
    tok = attn_ref.shape[0]
    kv_heads = keys_ref.shape[1] // HEAD_DIM
    for kv_head in range(kv_heads):
        cols = head_cols(kv_head)
        keys_t = keys_ref[:, cols].T
        values_t = values_ref[:, cols].T
        for pair in range(GROUP // PAIR):
            first = kv_head * GROUP + pair * PAIR
            at = slice(first * tok, (first + PAIR) * tok)
            attn = dot(values_t, probs_ref[:, at], 1, 0).T
            query_grad = (dot(keys_t, dscore_ref[:, at], 1, 0) * SCALE).T
            for n in range(PAIR):
                head = first + n
                rows = slice(n * tok, (n + 1) * tok)
                attn_ref[:, head_cols(head)] = attn[rows].astype(jnp.bfloat16)
                qg_ref[:, head_cols(head)] = query_grad[rows].astype(jnp.bfloat16)


def collect_kernel(batches, parts, kv_parts, *refs):
    sum_refs, refs = refs[:parts], refs[parts:]
    own_ref, refs = refs[0], refs[1:]
    back_refs, refs = refs[:kv_parts], refs[kv_parts:]
    kg_ref, vg_ref, qb_ref, vb_ref = refs
    heads = qb_ref.shape[0]
    kv_width = kg_ref.shape[1]
    total = sum_refs[0][...]
    for ref in sum_refs[1:]:
        total = total + ref[...]
    total = total * (1.0 / batches)
    qb_ref[...] = total[:heads]
    vb_ref[...] = total[heads:]
    term = own_ref[...]
    for ref in back_refs:
        term = term + ref[...].astype(jnp.float32)
    term = term.astype(jnp.bfloat16)
    kg_ref[...] = term[:, :kv_width]
    vg_ref[...] = term[:, kv_width:]


def total_kernel(*refs):
    out_ref = refs[-2]
    total = refs[0][...]
    for ref in refs[1:-3]:
        total = total + ref[...]
    out_ref[...] = total


def total_after(parts, received):
    return pl.pallas_call(
        total_kernel,
        out_shape=[
            shape(parts[0].shape, parts[0].dtype),
            shape(received.shape, received.dtype),
        ],
        in_specs=[VMEM] * len(parts) + [ANY],
        out_specs=[VMEM, ANY],
        input_output_aliases={len(parts): 1},
        compiler_params=params(4),
        cost_estimate=pl.CostEstimate(flops=parts[0].size, bytes_accessed=0, transcendentals=0),
        name="total",
    )(*parts, received)


def exchange(axis, part):
    size = lax.axis_size(axis)
    return [part] + [
        lax.ppermute(part, axis, [(i, (i + shift) % size) for i in range(size)])
        for shift in range(1, size)
    ]


def shards(q_proj, q_bias, k_proj, v_proj, v_bias, dout, lengths):
    _, tok, width = q_proj.shape
    kv_width = k_proj.shape[2]
    heads = width // HEAD_DIM
    kv_heads = kv_width // HEAD_DIM
    ctx = lax.axis_size("ctx")
    batches = lax.axis_size("dp")
    rows = ctx * tok
    columns = heads * tok
    pair = jnp.concatenate([k_proj[0], v_proj[0]], axis=1)
    pairs = [
        lax.ppermute(pair, "ctx", [(i, i + shift) for i in range(ctx - shift)])
        for shift in range(ctx - 1, 0, -1)
    ] + [pair]
    prepared = pl.pallas_call(
        functools.partial(prepare_kernel, ctx),
        out_shape=[
            shape((kv_heads, HEAD_DIM), jnp.bfloat16),
            shape((columns, 2 * HEAD_DIM), jnp.bfloat16),
            shape((columns, HEAD_DIM), jnp.bfloat16),
            shape((tok, columns), jnp.float32),
            shape((tok, columns), jnp.float32),
            shape((rows, tok), jnp.float32),
        ],
        in_specs=[SMEM] + [VMEM] * 5,
        out_specs=[VMEM] * 6,
        compiler_params=params(16),
        cost_estimate=pl.CostEstimate(
            flops=4 * tok * tok * width, bytes_accessed=16 * tok * width, transcendentals=0
        ),
        name="prepare",
    )(
        lengths,
        pair,
        q_bias.reshape(heads, HEAD_DIM),
        v_bias.reshape(kv_heads, HEAD_DIM),
        q_proj[0],
        dout[0],
    )
    term = shape((tok, 2 * kv_width), jnp.bfloat16)
    probs, dscore, all_keys, all_values, sums, own, *terms = pl.pallas_call(
        functools.partial(attend_kernel, ctx),
        out_shape=[
            shape((rows, columns), jnp.bfloat16),
            shape((rows, columns), jnp.bfloat16),
            shape((rows, kv_width), jnp.bfloat16),
            shape((rows, kv_width), jnp.bfloat16),
            shape((heads + kv_heads, HEAD_DIM), jnp.float32),
            shape((tok, 2 * kv_width), jnp.float32),
        ]
        + [term] * (ctx - 1),
        in_specs=[VMEM] * (6 + ctx),
        out_specs=[VMEM] * (6 + ctx - 1),
        scratch_shapes=[
            pltpu.VMEM((rows, columns), jnp.float32),
            pltpu.VMEM((rows, columns), jnp.float32),
        ],
        compiler_params=params(24 if ctx < 8 else 48),
        cost_estimate=pl.CostEstimate(
            flops=8 * rows * tok * width,
            bytes_accessed=4 * rows * columns,
            transcendentals=rows * columns,
        ),
        name="attend",
    )(*prepared, *pairs)
    back = [
        lax.ppermute(term, "ctx", [(i, i - shift) for i in range(shift, ctx)])
        for shift, term in enumerate(terms, 1)
    ]
    attn, q_grad = pl.pallas_call(
        finish_kernel,
        out_shape=[
            shape((tok, width), jnp.bfloat16),
            shape((tok, width), jnp.bfloat16),
        ],
        in_specs=[VMEM] * 4,
        out_specs=[VMEM] * 2,
        compiler_params=params(24),
        cost_estimate=pl.CostEstimate(
            flops=4 * rows * tok * width, bytes_accessed=4 * rows * columns, transcendentals=0
        ),
        name="finish",
    )(probs, dscore, all_keys, all_values)
    sums, back[0] = total_after(exchange("dp", sums), back[0])
    sums = exchange("ctx", sums)
    k_grad, v_grad, q_sum, v_sum = pl.pallas_call(
        functools.partial(collect_kernel, batches, len(sums), len(back)),
        out_shape=[
            shape((tok, kv_width), jnp.bfloat16),
            shape((tok, kv_width), jnp.bfloat16),
            shape((heads, HEAD_DIM), jnp.float32),
            shape((kv_heads, HEAD_DIM), jnp.float32),
        ],
        in_specs=[VMEM] * (len(sums) + 1 + len(back)),
        out_specs=[VMEM] * 4,
        compiler_params=params(8),
        cost_estimate=pl.CostEstimate(
            flops=8 * tok * kv_width, bytes_accessed=16 * tok * kv_width, transcendentals=0
        ),
        name="collect",
    )(*sums, own, *back)
    return (
        attn[None],
        q_grad[None],
        k_grad[None],
        v_grad[None],
        q_sum.reshape(width),
        v_sum.reshape(kv_width),
    )


def solution(mesh):
    tokens = P("dp", "ctx", "tp")
    return jax.shard_map(
        shards,
        mesh=mesh,
        in_specs=(tokens, P("tp"), tokens, tokens, P("tp"), tokens, P("dp", None)),
        out_specs=(tokens, tokens, tokens, tokens, P("tp"), P("tp")),
        check_vma=False,
    )
```

```python
import functools

import jax
import jax.numpy as jnp
from jax import lax
from jax.experimental import pallas as pl
from jax.experimental.pallas import tpu as pltpu
from jax.sharding import PartitionSpec as P

HEAD_DIM = 128
HEADS = 32
KV_HEADS = 4
GROUP = HEADS // KV_HEADS
PAIR = 2
BLOCK = 64
SCALE = HEAD_DIM ** (-0.5)
LOG2E = 1.4426950408889634
NEGATIVE = -1e30
VMEM = pl.BlockSpec(memory_space=pltpu.VMEM)
HBM = pl.BlockSpec(memory_space=pltpu.HBM)


def dot(left, right, left_dim, right_dim):
    return lax.dot_general(
        left, right, (((left_dim,), (right_dim,)), ((), ())), preferred_element_type=jnp.float32
    )


def head_cols(head):
    return slice(head * HEAD_DIM, (head + 1) * HEAD_DIM)


def shape(dims, dtype):
    return jax.ShapeDtypeStruct(dims, dtype)


def params(mebibytes):
    return pltpu.CompilerParams(vmem_limit_bytes=mebibytes * 1024 * 1024)


def biased(values, bias):
    return (values.astype(jnp.float32) + bias.astype(jnp.float32)).astype(jnp.bfloat16)


def pack_kernel(
    q_ref, g_ref, k_ref, v_ref, qb_ref, vb_ref, len_ref, q_own, g_own, qb_own, vb_own, start_ref,
    *refs,
):
    pair_refs, len_own, sems = refs[:-2], refs[-2], refs[-1]
    moves = [(len_ref, len_own)]
    for kv_head, pair_ref in enumerate(pair_refs):
        at = pl.ds(kv_head * HEAD_DIM, HEAD_DIM)
        moves.append((k_ref.at[:, at], pair_ref.at[:, pl.ds(0, HEAD_DIM)]))
        moves.append((v_ref.at[:, at], pair_ref.at[:, pl.ds(HEAD_DIM, HEAD_DIM)]))
    moves += [(vb_ref, vb_own), (qb_ref, qb_own), (q_ref, q_own), (g_ref, g_own)]
    copies = [
        pltpu.make_async_copy(source, target, sems.at[n])
        for n, (source, target) in enumerate(moves)
    ]
    for copy in copies:
        copy.start()
    tok = start_ref.shape[1]
    rank = lax.axis_index("ctx")
    query_pos = rank * tok + lax.broadcasted_iota(jnp.int32, (1, tok), 1)
    start = jnp.zeros((1, tok), jnp.int32)
    end = jnp.int32(0)
    copies[0].wait()
    for doc in range(len_own.shape[1]):
        length = len_own[0, doc]
        end = end + length
        start = start + jnp.where(query_pos >= end, length, 0)
    start_ref[...] = start
    for copy in copies[1:]:
        copy.wait()


def prepare_kernel(
    slots, q_ref, g_ref, qb_ref, vb_ref, start_ref, *refs
):
    tok = q_ref.shape[0]
    kv_heads = vb_ref.shape[0]
    pair_refs = refs[:kv_heads]
    queries_ref, grads_ref, score_ref, dprob_ref, live_ref = refs[kv_heads:]
    rank = lax.axis_index("ctx")
    query_pos = rank * tok + lax.broadcasted_iota(jnp.int32, (1, tok), 1)
    start = start_ref[...]
    offsets = lax.broadcasted_iota(jnp.int32, (tok, tok), 0)
    for slot in range(slots):
        key_pos = (rank - slot) * tok + offsets
        live = (key_pos >= start) & (key_pos <= query_pos)
        live_ref[slot * tok : (slot + 1) * tok, :] = jnp.where(live, 0.0, NEGATIVE)
    column = lax.broadcasted_iota(jnp.int32, (tok, HEAD_DIM), 1)
    for kv_head in range(kv_heads):
        keys = pair_refs[kv_head][:, :HEAD_DIM]
        values = biased(pair_refs[kv_head][:, HEAD_DIM:], vb_ref[kv_head : kv_head + 1, :])
        for head in range(kv_head * GROUP, (kv_head + 1) * GROUP):
            at = slice(head * tok, (head + 1) * tok)
            queries_ref[at, :HEAD_DIM] = biased(q_ref[:, head_cols(head)], qb_ref[head : head + 1, :])
            queries_ref[at, HEAD_DIM:] = (column == head).astype(jnp.bfloat16)
            grads_ref[at, :] = g_ref[:, head_cols(head)]
        rows = slice(kv_head * GROUP * tok, (kv_head + 1) * GROUP * tok)
        score_ref[:, rows] = dot(keys, queries_ref[rows, :HEAD_DIM], 1, 1)
        dprob_ref[:, rows] = dot(values, grads_ref[rows, :], 1, 1)


def outputs_of_head(probs_ref, dscore_ref, keys_ref, values_ref, attn_ref, qg_ref, base):
    tok = attn_ref.shape[0]
    keys_t = keys_ref[...].T
    values_t = values_ref[...].T
    for pair in range(GROUP // PAIR):
        at = slice(pair * PAIR * tok, (pair + 1) * PAIR * tok)
        attn = dot(values_t, probs_ref[:, at], 1, 0).T
        query_grad = (dot(keys_t, dscore_ref[:, at], 1, 0) * SCALE).T
        for n in range(PAIR):
            cols = slice(base + (pair * PAIR + n) * HEAD_DIM, base + (pair * PAIR + n + 1) * HEAD_DIM)
            rows = slice(n * tok, (n + 1) * tok)
            attn_ref[:, cols] = attn[rows].astype(jnp.bfloat16)
            qg_ref[:, cols] = query_grad[rows].astype(jnp.bfloat16)


def attend_kernel(slots, kv_head, last, *refs):
    bias_ref, queries_ref, grads_ref, score_ref, dprob_ref, live_ref = refs[:6]
    pair_refs = refs[6 : 6 + slots][::-1]
    refs = refs[6 + slots :]
    if kv_head:
        filled_refs, refs = refs[: slots + 1], refs[slots + 1 :]
    sums_ref, own_ref = refs[:2]
    out_refs = refs[2 : 2 + slots - 1]
    refs = refs[2 + slots - 1 :]
    keys_ref, values_ref, probs_ref, dscore_ref = refs[:4] if last else refs[2:6]
    weights_ref, all_dprob_ref = refs[-2:]
    tok = pair_refs[0].shape[0]
    kv_heads = bias_ref.shape[0]
    heads = kv_heads * GROUP
    for slot in range(slots):
        rows = slice(slot * tok, (slot + 1) * tok)
        keys_ref[rows, :] = pair_refs[slot][:, :HEAD_DIM]
        values_ref[rows, :] = biased(
            pair_refs[slot][:, HEAD_DIM:], bias_ref[kv_head : kv_head + 1, :]
        )
    blocks = [slice(row, row + BLOCK) for row in range(0, slots * tok, BLOCK)]
    base = kv_head * GROUP * tok
    group = slice(base, base + GROUP * tok)
    weights_ref[tok:, :] = dot(keys_ref[tok:, :], queries_ref[group, :HEAD_DIM], 1, 1)
    all_dprob_ref[tok:, :] = dot(values_ref[tok:, :], grads_ref[group, :], 1, 1)
    for pair in range(GROUP // PAIR):
        at = slice(pair * PAIR * tok, (pair + 1) * PAIR * tok)
        of_all = slice(base + at.start, base + at.stop)
        row_max = None
        for block in blocks:
            own = block.start < tok
            score = score_ref[block, of_all] if own else weights_ref[block, at]
            score = score + jnp.concatenate([live_ref[block, :]] * PAIR, axis=1)
            weights_ref[block, at] = score
            part = jnp.max(score.reshape(-1, 8, PAIR * tok), axis=0)
            row_max = part if row_max is None else jnp.maximum(row_max, part)
        row_max = jnp.max(row_max, axis=0, keepdims=True)
        total = jnp.zeros((8, PAIR * tok), jnp.float32)
        delta = jnp.zeros((8, PAIR * tok), jnp.float32)
        for block in blocks:
            dprob = dprob_ref[block, of_all] if block.start < tok else all_dprob_ref[block, at]
            weights = jnp.exp2((weights_ref[block, at] - row_max) * (SCALE * LOG2E))
            weights_ref[block, at] = weights
            total = total + jnp.sum(weights.reshape(-1, 8, PAIR * tok), axis=0)
            delta = delta + jnp.sum((weights * dprob).reshape(-1, 8, PAIR * tok), axis=0)
        inverse = 1.0 / jnp.sum(total, axis=0, keepdims=True)
        delta = jnp.sum(delta, axis=0, keepdims=True) * inverse
        for block in blocks:
            dprob = dprob_ref[block, of_all] if block.start < tok else all_dprob_ref[block, at]
            probs = weights_ref[block, at] * inverse
            probs_ref[block, at] = probs.astype(jnp.bfloat16)
            dscore_ref[block, at] = (probs * (dprob - delta)).astype(jnp.bfloat16)
    value_term = dot(probs_ref[...], grads_ref[group, :], 1, 0)
    key_term = dot(dscore_ref[...], queries_ref[group, :], 1, 0)
    over_queries = key_term[:, HEAD_DIM:]
    key_term = key_term[:, :HEAD_DIM] * SCALE
    high = over_queries.astype(jnp.bfloat16)
    low = (over_queries - high.astype(jnp.float32)).astype(jnp.bfloat16)
    query_sums = (dot(high, keys_ref[...], 0, 0) + dot(low, keys_ref[...], 0, 0)) * SCALE
    of_group = slice(kv_head * GROUP, (kv_head + 1) * GROUP)
    sums_ref[of_group, :] = query_sums[of_group]
    sums_ref[heads + kv_head : heads + kv_head + 1, :] = jnp.sum(value_term, axis=0, keepdims=True)
    key_cols, value_cols = head_cols(kv_head), head_cols(kv_heads + kv_head)
    own_ref[:, key_cols] = key_term[:tok]
    own_ref[:, value_cols] = value_term[:tok]
    for slot in range(1, slots):
        rows = slice(slot * tok, (slot + 1) * tok)
        out_refs[slot - 1][:, key_cols] = key_term[rows].astype(jnp.bfloat16)
        out_refs[slot - 1][:, value_cols] = value_term[rows].astype(jnp.bfloat16)
    if kv_head:
        filled_sums_ref, *filled_refs = filled_refs
        sums_ref[: of_group.start, :] = filled_sums_ref[: of_group.start, :]
        sums_ref[heads : heads + kv_head, :] = filled_sums_ref[heads : heads + kv_head, :]
        for filled_ref, out_ref in zip(filled_refs, (own_ref, *out_refs)):
            for first in (0, kv_heads):
                cols = slice(first * HEAD_DIM, (first + kv_head) * HEAD_DIM)
                out_ref[:, cols] = filled_ref[:, cols]
    if not last:
        outputs_of_head(probs_ref, dscore_ref, keys_ref, values_ref, refs[0], refs[1], 0)


def attend(slots, kv_head, bias, prepared, pairs, filled):
    queries, _, _, _, live = prepared
    rows, tok = live.shape
    kv_heads = bias.shape[0]
    last = kv_head == kv_heads - 1
    width = GROUP * HEAD_DIM
    scores = (rows, GROUP * tok)
    outs = [
        shape((kv_heads * GROUP + kv_heads, HEAD_DIM), jnp.float32),
        shape((tok, 2 * kv_heads * HEAD_DIM), jnp.float32),
    ] + [shape((tok, 2 * kv_heads * HEAD_DIM), jnp.bfloat16)] * (slots - 1)
    held = [
        (shape((rows, HEAD_DIM), jnp.bfloat16), pltpu.VMEM((rows, HEAD_DIM), jnp.bfloat16)),
        (shape((rows, HEAD_DIM), jnp.bfloat16), pltpu.VMEM((rows, HEAD_DIM), jnp.bfloat16)),
        (shape(scores, jnp.bfloat16), pltpu.VMEM(scores, jnp.bfloat16)),
        (shape(scores, jnp.bfloat16), pltpu.VMEM(scores, jnp.bfloat16)),
    ]
    if last:
        more, scratch = [out for out, _ in held], []
    else:
        more, scratch = [shape((tok, width), jnp.bfloat16)] * 2, [kept for _, kept in held]
    results = pl.pallas_call(
        functools.partial(attend_kernel, slots, kv_head, last),
        out_shape=outs + more,
        in_specs=[VMEM] * (6 + slots + len(filled)),
        out_specs=[VMEM] * (len(outs) + len(more)),
        scratch_shapes=scratch + [pltpu.VMEM(scores, jnp.float32)] * 2,
        compiler_params=params(20 if slots < 8 else 36),
        cost_estimate=pl.CostEstimate(
            flops=8 * rows * tok * width,
            bytes_accessed=4 * rows * GROUP * tok,
            transcendentals=rows * GROUP * tok,
        ),
        name="attend",
    )(bias, *prepared, *pairs, *filled)
    return results[: len(outs)], results[len(outs) :]


def finish_kernel(done, *refs):
    held, before, (attn_ref, qg_ref) = refs[:4], refs[4 : 4 + 2 * done], refs[4 + 2 * done :]
    width = GROUP * HEAD_DIM
    for n in range(done):
        attn_ref[:, n * width : (n + 1) * width] = before[2 * n][...]
        qg_ref[:, n * width : (n + 1) * width] = before[2 * n + 1][...]
    outputs_of_head(*held, attn_ref, qg_ref, done * width)


def collect_kernel(batches, parts, kv_parts, *refs):
    sum_refs, refs = refs[:parts], refs[parts:]
    own_ref, refs = refs[0], refs[1:]
    back_refs, refs = refs[:kv_parts], refs[kv_parts:]
    kg_ref, vg_ref, qb_ref, vb_ref = refs
    heads = qb_ref.shape[0]
    kv_width = kg_ref.shape[1]
    total = sum_refs[0][...]
    for ref in sum_refs[1:]:
        total = total + ref[...]
    total = total * (1.0 / batches)
    qb_ref[...] = total[:heads]
    vb_ref[...] = total[heads:]
    term = own_ref[...]
    for ref in back_refs:
        term = term + ref[...].astype(jnp.float32)
    term = term.astype(jnp.bfloat16)
    kg_ref[...] = term[:, :kv_width]
    vg_ref[...] = term[:, kv_width:]


def total_of(parts):
    return functools.reduce(lambda left, right: left + right, parts)


def exchange(axis, part):
    size = lax.axis_size(axis)
    if axis == "ctx" and not size & (size - 1):
        step = 1
        while 2 * step < size:
            part = part + lax.ppermute(part, axis, [(i, i ^ step) for i in range(size)])
            step *= 2
        return [part, lax.ppermute(part, axis, [(i, i ^ step) for i in range(size)])]
    return [part] + [
        lax.ppermute(part, axis, [(i, (i + shift) % size) for i in range(size)])
        for shift in range(1, size)
    ]


def shards(q_proj, q_bias, k_proj, v_proj, v_bias, dout, lengths):
    _, tok, width = q_proj.shape
    kv_width = k_proj.shape[2]
    heads = width // HEAD_DIM
    kv_heads = kv_width // HEAD_DIM
    ctx = lax.axis_size("ctx")
    batches = lax.axis_size("dp")
    rows = ctx * tok
    columns = heads * tok
    q_own, g_own, qb_own, vb_own, start, *own_pairs = pl.pallas_call(
        pack_kernel,
        out_shape=[
            shape((tok, width), jnp.bfloat16),
            shape((tok, width), jnp.bfloat16),
            shape((heads, HEAD_DIM), jnp.bfloat16),
            shape((kv_heads, HEAD_DIM), jnp.bfloat16),
            shape((1, tok), jnp.int32),
        ]
        + [shape((tok, 2 * HEAD_DIM), jnp.bfloat16)] * kv_heads,
        in_specs=[HBM] * 7,
        out_specs=[VMEM] * (5 + kv_heads),
        scratch_shapes=[
            pltpu.SMEM(lengths.shape, jnp.int32),
            pltpu.SemaphoreType.DMA((5 + 2 * kv_heads,)),
        ],
        compiler_params=params(4),
        cost_estimate=pl.CostEstimate(flops=0, bytes_accessed=8 * tok * width, transcendentals=0),
        name="pack",
    )(
        *[
            pltpu.with_memory_space_constraint(array, pltpu.HBM)
            for array in (
                q_proj[0],
                dout[0],
                k_proj[0],
                v_proj[0],
                q_bias.reshape(heads, HEAD_DIM),
                v_bias.reshape(kv_heads, HEAD_DIM),
                lengths,
            )
        ]
    )
    pairs = [
        [
            lax.ppermute(pair, "ctx", [(i, i + shift) for i in range(ctx - shift)])
            for shift in range(ctx - 1, 0, -1)
        ]
        + [pair]
        for pair in own_pairs
    ]
    prepared = pl.pallas_call(
        functools.partial(prepare_kernel, ctx),
        out_shape=[
            shape((columns, 2 * HEAD_DIM), jnp.bfloat16),
            shape((columns, HEAD_DIM), jnp.bfloat16),
            shape((tok, columns), jnp.float32),
            shape((tok, columns), jnp.float32),
            shape((rows, tok), jnp.float32),
        ],
        in_specs=[VMEM] * (5 + kv_heads),
        out_specs=[VMEM] * 5,
        compiler_params=params(16),
        cost_estimate=pl.CostEstimate(
            flops=4 * tok * tok * width, bytes_accessed=16 * tok * width, transcendentals=0
        ),
        name="prepare",
    )(q_own, g_own, qb_own, vb_own, start, *own_pairs)
    filled, done = [], []
    for kv_head in range(kv_heads):
        filled, made = attend(ctx, kv_head, vb_own, prepared, pairs[kv_head], filled)
        done.append(made)
    sums, own, *terms = filled
    *before, last_made = done
    keys, values, probs, dscore = last_made
    before = [array for made in before for array in made]
    back = [
        lax.ppermute(term, "ctx", [(i, i - shift) for i in range(shift, ctx)])
        for shift, term in enumerate(terms, 1)
    ]
    attn, q_grad = pl.pallas_call(
        functools.partial(finish_kernel, kv_heads - 1),
        out_shape=[shape((tok, width), jnp.bfloat16)] * 2,
        in_specs=[VMEM] * (4 + len(before)),
        out_specs=[VMEM] * 2,
        compiler_params=params(16),
        cost_estimate=pl.CostEstimate(
            flops=4 * rows * tok * GROUP * HEAD_DIM,
            bytes_accessed=4 * tok * width,
            transcendentals=0,
        ),
        name="finish",
    )(probs, dscore, keys, values, *before)
    sums = exchange("ctx", total_of(exchange("dp", sums)))
    k_grad, v_grad, q_sum, v_sum = pl.pallas_call(
        functools.partial(collect_kernel, batches, len(sums), len(back)),
        out_shape=[
            shape((tok, kv_width), jnp.bfloat16),
            shape((tok, kv_width), jnp.bfloat16),
            shape((heads, HEAD_DIM), jnp.float32),
            shape((kv_heads, HEAD_DIM), jnp.float32),
        ],
        in_specs=[VMEM] * (len(sums) + 1 + len(back)),
        out_specs=[VMEM] * 4,
        compiler_params=params(8),
        cost_estimate=pl.CostEstimate(
            flops=8 * tok * kv_width, bytes_accessed=16 * tok * kv_width, transcendentals=0
        ),
        name="collect",
    )(*sums, own, *back)
    return (
        attn[None],
        q_grad[None],
        k_grad[None],
        v_grad[None],
        q_sum.reshape(width),
        v_sum.reshape(kv_width),
    )


def solution(mesh):
    tokens = P("dp", "ctx", "tp")
    return jax.shard_map(
        shards,
        mesh=mesh,
        in_specs=(tokens, P("tp"), tokens, tokens, P("tp"), tokens, P("dp", None)),
        out_specs=(tokens, tokens, tokens, tokens, P("tp"), P("tp")),
        check_vma=False,
    )
```

```python
import functools

import jax
import jax.numpy as jnp
from jax import lax
from jax.experimental import pallas as pl
from jax.experimental.pallas import tpu as pltpu
from jax.sharding import PartitionSpec as P

HEAD_DIM = 128
HEADS = 32
KV_HEADS = 4
GROUP = HEADS // KV_HEADS
PAIR = 2
BLOCK = 64
SCALE = HEAD_DIM ** (-0.5)
LOG2E = 1.4426950408889634
NEGATIVE = -1e30
VMEM = pl.BlockSpec(memory_space=pltpu.VMEM)
ANY = pl.BlockSpec(memory_space=pl.ANY)
SMEM = pl.BlockSpec(memory_space=pltpu.SMEM)


def dot(left, right, left_dim, right_dim):
    return lax.dot_general(
        left, right, (((left_dim,), (right_dim,)), ((), ())), preferred_element_type=jnp.float32
    )


def head_cols(head):
    return slice(head * HEAD_DIM, (head + 1) * HEAD_DIM)


def shape(dims, dtype):
    return jax.ShapeDtypeStruct(dims, dtype)


def params(mebibytes):
    return pltpu.CompilerParams(vmem_limit_bytes=mebibytes * 1024 * 1024)


def biased(values, bias):
    return (values.astype(jnp.float32) + bias.astype(jnp.float32)).astype(jnp.bfloat16)


def prepare_kernel(
    slots, len_ref, pair_ref, qb_ref, vb_ref, q_ref, g_ref, bias_ref, queries_ref, grads_ref,
    score_ref, dprob_ref, live_ref,
):
    tok = q_ref.shape[0]
    kv_heads = vb_ref.shape[0]
    rank = lax.axis_index("ctx")
    query_pos = rank * tok + lax.broadcasted_iota(jnp.int32, (1, tok), 1)
    start = jnp.zeros((1, tok), jnp.int32)
    end = jnp.int32(0)
    for doc in range(len_ref.shape[1]):
        length = len_ref[0, doc]
        end = end + length
        start = start + jnp.where(query_pos >= end, length, 0)
    offsets = lax.broadcasted_iota(jnp.int32, (tok, tok), 0)
    for slot in range(slots):
        key_pos = (rank - slot) * tok + offsets
        live = (key_pos >= start) & (key_pos <= query_pos)
        live_ref[slot * tok : (slot + 1) * tok, :] = jnp.where(live, 0.0, NEGATIVE)
    bias_ref[...] = vb_ref[...]
    column = lax.broadcasted_iota(jnp.int32, (tok, HEAD_DIM), 1)
    for kv_head in range(kv_heads):
        keys = pair_ref[:, head_cols(kv_head)]
        values = biased(pair_ref[:, head_cols(kv_heads + kv_head)], vb_ref[kv_head : kv_head + 1, :])
        for head in range(kv_head * GROUP, (kv_head + 1) * GROUP):
            at = slice(head * tok, (head + 1) * tok)
            queries_ref[at, :HEAD_DIM] = biased(q_ref[:, head_cols(head)], qb_ref[head : head + 1, :])
            queries_ref[at, HEAD_DIM:] = (column == head).astype(jnp.bfloat16)
            grads_ref[at, :] = g_ref[:, head_cols(head)]
        rows = slice(kv_head * GROUP * tok, (kv_head + 1) * GROUP * tok)
        score_ref[:, rows] = dot(keys, queries_ref[rows, :HEAD_DIM], 1, 1)
        dprob_ref[:, rows] = dot(values, grads_ref[rows, :], 1, 1)


def attend_kernel(slots, *refs):
    bias_ref, queries_ref, grads_ref, score_ref, dprob_ref, live_ref = refs[:6]
    pair_refs = refs[6 : 6 + slots][::-1]
    refs = refs[6 + slots :]
    probs_ref, dscore_ref, keys_ref, values_ref, sums_ref, own_ref = refs[:6]
    out_refs = refs[6 : 6 + slots - 1]
    weights_ref, all_dprob_ref = refs[6 + slots - 1 :]
    tok = pair_refs[0].shape[0]
    kv_heads = bias_ref.shape[0]
    kv_width = kv_heads * HEAD_DIM
    heads = kv_heads * GROUP
    for slot in range(slots):
        rows = slice(slot * tok, (slot + 1) * tok)
        keys_ref[rows, :] = pair_refs[slot][:, :kv_width]
        for kv_head in range(kv_heads):
            values_ref[rows, head_cols(kv_head)] = biased(
                pair_refs[slot][:, head_cols(kv_heads + kv_head)], bias_ref[kv_head : kv_head + 1, :]
            )
    blocks = [slice(row, row + BLOCK) for row in range(0, slots * tok, BLOCK)]
    for kv_head in range(kv_heads):
        cols = head_cols(kv_head)
        group = slice(kv_head * GROUP * tok, (kv_head + 1) * GROUP * tok)
        weights_ref[tok:, group] = dot(keys_ref[tok:, cols], queries_ref[group, :HEAD_DIM], 1, 1)
        all_dprob_ref[tok:, group] = dot(values_ref[tok:, cols], grads_ref[group, :], 1, 1)
        for pair in range(GROUP // PAIR):
            first = kv_head * GROUP + pair * PAIR
            at = slice(first * tok, (first + PAIR) * tok)
            row_max = None
            for block in blocks:
                score = (score_ref if block.start < tok else weights_ref)[block, at]
                score = score + jnp.concatenate([live_ref[block, :]] * PAIR, axis=1)
                weights_ref[block, at] = score
                part = jnp.max(score.reshape(-1, 8, PAIR * tok), axis=0)
                row_max = part if row_max is None else jnp.maximum(row_max, part)
            row_max = jnp.max(row_max, axis=0, keepdims=True)
            total = jnp.zeros((8, PAIR * tok), jnp.float32)
            delta = jnp.zeros((8, PAIR * tok), jnp.float32)
            for block in blocks:
                dprob = (dprob_ref if block.start < tok else all_dprob_ref)[block, at]
                weights = jnp.exp2((weights_ref[block, at] - row_max) * (SCALE * LOG2E))
                weights_ref[block, at] = weights
                total = total + jnp.sum(weights.reshape(-1, 8, PAIR * tok), axis=0)
                delta = delta + jnp.sum((weights * dprob).reshape(-1, 8, PAIR * tok), axis=0)
            inverse = 1.0 / jnp.sum(total, axis=0, keepdims=True)
            delta = jnp.sum(delta, axis=0, keepdims=True) * inverse
            for block in blocks:
                dprob = (dprob_ref if block.start < tok else all_dprob_ref)[block, at]
                probs = weights_ref[block, at] * inverse
                probs_ref[block, at] = probs.astype(jnp.bfloat16)
                dscore_ref[block, at] = (probs * (dprob - delta)).astype(jnp.bfloat16)
        value_term = dot(probs_ref[:, group], grads_ref[group, :], 1, 0)
        key_term = dot(dscore_ref[:, group], queries_ref[group, :], 1, 0)
        over_queries = key_term[:, HEAD_DIM:]
        key_term = key_term[:, :HEAD_DIM] * SCALE
        high = over_queries.astype(jnp.bfloat16)
        low = (over_queries - high.astype(jnp.float32)).astype(jnp.bfloat16)
        all_keys = keys_ref[:, cols]
        query_sums = (dot(high, all_keys, 0, 0) + dot(low, all_keys, 0, 0)) * SCALE
        of_group = slice(kv_head * GROUP, (kv_head + 1) * GROUP)
        sums_ref[of_group, :] = query_sums[of_group]
        sums_ref[heads + kv_head : heads + kv_head + 1, :] = jnp.sum(
            value_term, axis=0, keepdims=True
        )
        value_cols = head_cols(kv_heads + kv_head)
        own_ref[:, cols] = key_term[:tok]
        own_ref[:, value_cols] = value_term[:tok]
        for slot in range(1, slots):
            rows = slice(slot * tok, (slot + 1) * tok)
            out_refs[slot - 1][:, cols] = key_term[rows].astype(jnp.bfloat16)
            out_refs[slot - 1][:, value_cols] = value_term[rows].astype(jnp.bfloat16)


def finish_kernel(probs_ref, dscore_ref, keys_ref, values_ref, attn_ref, qg_ref):
    tok = attn_ref.shape[0]
    kv_heads = keys_ref.shape[1] // HEAD_DIM
    for kv_head in range(kv_heads):
        cols = head_cols(kv_head)
        keys_t = keys_ref[:, cols].T
        values_t = values_ref[:, cols].T
        for pair in range(GROUP // PAIR):
            first = kv_head * GROUP + pair * PAIR
            at = slice(first * tok, (first + PAIR) * tok)
            attn = dot(values_t, probs_ref[:, at], 1, 0).T
            query_grad = (dot(keys_t, dscore_ref[:, at], 1, 0) * SCALE).T
            for n in range(PAIR):
                head = first + n
                rows = slice(n * tok, (n + 1) * tok)
                attn_ref[:, head_cols(head)] = attn[rows].astype(jnp.bfloat16)
                qg_ref[:, head_cols(head)] = query_grad[rows].astype(jnp.bfloat16)


def collect_kernel(batches, parts, kv_parts, *refs):
    sum_refs, refs = refs[:parts], refs[parts:]
    own_ref, refs = refs[0], refs[1:]
    back_refs, refs = refs[:kv_parts], refs[kv_parts:]
    kg_ref, vg_ref, qb_ref, vb_ref = refs
    heads = qb_ref.shape[0]
    kv_width = kg_ref.shape[1]
    total = sum_refs[0][...]
    for ref in sum_refs[1:]:
        total = total + ref[...]
    total = total * (1.0 / batches)
    qb_ref[...] = total[:heads]
    vb_ref[...] = total[heads:]
    term = own_ref[...]
    for ref in back_refs:
        term = term + ref[...].astype(jnp.float32)
    term = term.astype(jnp.bfloat16)
    kg_ref[...] = term[:, :kv_width]
    vg_ref[...] = term[:, kv_width:]


def total_kernel(*refs):
    out_ref = refs[-2]
    total = refs[0][...]
    for ref in refs[1:-3]:
        total = total + ref[...]
    out_ref[...] = total


def total_after(parts, received):
    return pl.pallas_call(
        total_kernel,
        out_shape=[
            shape(parts[0].shape, parts[0].dtype),
            shape(received.shape, received.dtype),
        ],
        in_specs=[VMEM] * len(parts) + [ANY],
        out_specs=[VMEM, ANY],
        input_output_aliases={len(parts): 1},
        compiler_params=params(4),
        cost_estimate=pl.CostEstimate(flops=parts[0].size, bytes_accessed=0, transcendentals=0),
        name="total",
    )(*parts, received)


def exchange(axis, part):
    size = lax.axis_size(axis)
    return [part] + [
        lax.ppermute(part, axis, [(i, (i + shift) % size) for i in range(size)])
        for shift in range(1, size)
    ]


def shards(q_proj, q_bias, k_proj, v_proj, v_bias, dout, lengths):
    _, tok, width = q_proj.shape
    kv_width = k_proj.shape[2]
    heads = width // HEAD_DIM
    kv_heads = kv_width // HEAD_DIM
    ctx = lax.axis_size("ctx")
    batches = lax.axis_size("dp")
    rows = ctx * tok
    columns = heads * tok
    pair = jnp.concatenate([k_proj[0], v_proj[0]], axis=1)
    pairs = [
        lax.ppermute(pair, "ctx", [(i, (i + shift) % ctx) for i in range(ctx)])
        for shift in range(ctx - 1, 0, -1)
    ] + [pair]
    prepared = pl.pallas_call(
        functools.partial(prepare_kernel, ctx),
        out_shape=[
            shape((kv_heads, HEAD_DIM), jnp.bfloat16),
            shape((columns, 2 * HEAD_DIM), jnp.bfloat16),
            shape((columns, HEAD_DIM), jnp.bfloat16),
            shape((tok, columns), jnp.float32),
            shape((tok, columns), jnp.float32),
            shape((rows, tok), jnp.float32),
        ],
        in_specs=[SMEM] + [VMEM] * 5,
        out_specs=[VMEM] * 6,
        compiler_params=params(16),
        cost_estimate=pl.CostEstimate(
            flops=4 * tok * tok * width, bytes_accessed=16 * tok * width, transcendentals=0
        ),
        name="prepare",
    )(
        lengths,
        pair,
        q_bias.reshape(heads, HEAD_DIM),
        v_bias.reshape(kv_heads, HEAD_DIM),
        q_proj[0],
        dout[0],
    )
    term = shape((tok, 2 * kv_width), jnp.bfloat16)
    probs, dscore, all_keys, all_values, sums, own, *terms = pl.pallas_call(
        functools.partial(attend_kernel, ctx),
        out_shape=[
            shape((rows, columns), jnp.bfloat16),
            shape((rows, columns), jnp.bfloat16),
            shape((rows, kv_width), jnp.bfloat16),
            shape((rows, kv_width), jnp.bfloat16),
            shape((heads + kv_heads, HEAD_DIM), jnp.float32),
            shape((tok, 2 * kv_width), jnp.float32),
        ]
        + [term] * (ctx - 1),
        in_specs=[VMEM] * (6 + ctx),
        out_specs=[VMEM] * (6 + ctx - 1),
        scratch_shapes=[
            pltpu.VMEM((rows, columns), jnp.float32),
            pltpu.VMEM((rows, columns), jnp.float32),
        ],
        compiler_params=params(24 if ctx < 8 else 48),
        cost_estimate=pl.CostEstimate(
            flops=8 * rows * tok * width,
            bytes_accessed=4 * rows * columns,
            transcendentals=rows * columns,
        ),
        name="attend",
    )(*prepared, *pairs)
    back = [
        lax.ppermute(term, "ctx", [(i, (i - shift) % ctx) for i in range(ctx)])
        for shift, term in enumerate(terms, 1)
    ]
    attn, q_grad = pl.pallas_call(
        finish_kernel,
        out_shape=[
            shape((tok, width), jnp.bfloat16),
            shape((tok, width), jnp.bfloat16),
        ],
        in_specs=[VMEM] * 4,
        out_specs=[VMEM] * 2,
        compiler_params=params(24),
        cost_estimate=pl.CostEstimate(
            flops=4 * rows * tok * width, bytes_accessed=4 * rows * columns, transcendentals=0
        ),
        name="finish",
    )(probs, dscore, all_keys, all_values)
    sums, back[0] = total_after(exchange("dp", sums), back[0])
    sums = exchange("ctx", sums)
    k_grad, v_grad, q_sum, v_sum = pl.pallas_call(
        functools.partial(collect_kernel, batches, len(sums), len(back)),
        out_shape=[
            shape((tok, kv_width), jnp.bfloat16),
            shape((tok, kv_width), jnp.bfloat16),
            shape((heads, HEAD_DIM), jnp.float32),
            shape((kv_heads, HEAD_DIM), jnp.float32),
        ],
        in_specs=[VMEM] * (len(sums) + 1 + len(back)),
        out_specs=[VMEM] * 4,
        compiler_params=params(8),
        cost_estimate=pl.CostEstimate(
            flops=8 * tok * kv_width, bytes_accessed=16 * tok * kv_width, transcendentals=0
        ),
        name="collect",
    )(*sums, own, *back)
    return (
        attn[None],
        q_grad[None],
        k_grad[None],
        v_grad[None],
        q_sum.reshape(width),
        v_sum.reshape(kv_width),
    )


def solution(mesh):
    tokens = P("dp", "ctx", "tp")
    return jax.shard_map(
        shards,
        mesh=mesh,
        in_specs=(tokens, P("tp"), tokens, tokens, P("tp"), tokens, P("dp", None)),
        out_specs=(tokens, tokens, tokens, tokens, P("tp"), P("tp")),
        check_vma=False,
    )
```

```python
import functools

import jax
import jax.numpy as jnp
from jax import lax
from jax.experimental import pallas as pl
from jax.experimental.pallas import tpu as pltpu
from jax.sharding import PartitionSpec as P

HEAD_DIM = 128
HEADS = 32
KV_HEADS = 4
GROUP = HEADS // KV_HEADS
PAIR = 2
BLOCK = 64
SCALE = HEAD_DIM ** (-0.5)
LOG2E = 1.4426950408889634
NEGATIVE = -1e30
VMEM = pl.BlockSpec(memory_space=pltpu.VMEM)
ANY = pl.BlockSpec(memory_space=pl.ANY)
SMEM = pl.BlockSpec(memory_space=pltpu.SMEM)


def dot(left, right, left_dim, right_dim):
    return lax.dot_general(
        left, right, (((left_dim,), (right_dim,)), ((), ())), preferred_element_type=jnp.float32
    )


def head_cols(head):
    return slice(head * HEAD_DIM, (head + 1) * HEAD_DIM)


def shape(dims, dtype):
    return jax.ShapeDtypeStruct(dims, dtype)


def params(mebibytes):
    return pltpu.CompilerParams(vmem_limit_bytes=mebibytes * 1024 * 1024)


def biased(values, bias):
    return (values.astype(jnp.float32) + bias.astype(jnp.float32)).astype(jnp.bfloat16)


def prepare_kernel(
    slots, len_ref, pair_ref, qb_ref, vb_ref, q_ref, g_ref, bias_ref, queries_ref, grads_ref,
    score_ref, dprob_ref, live_ref,
):
    tok = q_ref.shape[0]
    kv_heads = vb_ref.shape[0]
    rank = lax.axis_index("ctx")
    query_pos = rank * tok + lax.broadcasted_iota(jnp.int32, (1, tok), 1)
    start = jnp.zeros((1, tok), jnp.int32)
    end = jnp.int32(0)
    for doc in range(len_ref.shape[1]):
        length = len_ref[0, doc]
        end = end + length
        start = start + jnp.where(query_pos >= end, length, 0)
    offsets = lax.broadcasted_iota(jnp.int32, (tok, tok), 0)
    for slot in range(slots):
        key_pos = (rank - slot) * tok + offsets
        live = (key_pos >= start) & (key_pos <= query_pos)
        live_ref[slot * tok : (slot + 1) * tok, :] = jnp.where(live, 0.0, NEGATIVE)
    bias_ref[...] = vb_ref[...]
    column = lax.broadcasted_iota(jnp.int32, (tok, HEAD_DIM), 1)
    for kv_head in range(kv_heads):
        keys = pair_ref[:, head_cols(kv_head)]
        values = biased(pair_ref[:, head_cols(kv_heads + kv_head)], vb_ref[kv_head : kv_head + 1, :])
        for head in range(kv_head * GROUP, (kv_head + 1) * GROUP):
            at = slice(head * tok, (head + 1) * tok)
            queries_ref[at, :HEAD_DIM] = biased(q_ref[:, head_cols(head)], qb_ref[head : head + 1, :])
            queries_ref[at, HEAD_DIM:] = (column == head).astype(jnp.bfloat16)
            grads_ref[at, :] = g_ref[:, head_cols(head)]
        rows = slice(kv_head * GROUP * tok, (kv_head + 1) * GROUP * tok)
        score_ref[:, rows] = dot(keys, queries_ref[rows, :HEAD_DIM], 1, 1)
        dprob_ref[:, rows] = dot(values, grads_ref[rows, :], 1, 1)


def attend_kernel(slots, *refs):
    bias_ref, queries_ref, grads_ref, score_ref, dprob_ref, live_ref = refs[:6]
    pair_refs = refs[6 : 6 + slots][::-1]
    refs = refs[6 + slots :]
    probs_ref, dscore_ref, keys_ref, values_ref, sums_ref, own_ref = refs[:6]
    out_refs = refs[6 : 6 + slots - 1]
    weights_ref, all_dprob_ref = refs[6 + slots - 1 :]
    tok = pair_refs[0].shape[0]
    kv_heads = bias_ref.shape[0]
    kv_width = kv_heads * HEAD_DIM
    heads = kv_heads * GROUP
    for slot in range(slots):
        rows = slice(slot * tok, (slot + 1) * tok)
        keys_ref[rows, :] = pair_refs[slot][:, :kv_width]
        for kv_head in range(kv_heads):
            values_ref[rows, head_cols(kv_head)] = biased(
                pair_refs[slot][:, head_cols(kv_heads + kv_head)], bias_ref[kv_head : kv_head + 1, :]
            )
    blocks = [slice(row, row + BLOCK) for row in range(0, slots * tok, BLOCK)]
    for kv_head in range(kv_heads):
        cols = head_cols(kv_head)
        group = slice(kv_head * GROUP * tok, (kv_head + 1) * GROUP * tok)
        weights_ref[tok:, group] = dot(keys_ref[tok:, cols], queries_ref[group, :HEAD_DIM], 1, 1)
        all_dprob_ref[tok:, group] = dot(values_ref[tok:, cols], grads_ref[group, :], 1, 1)
        for pair in range(GROUP // PAIR):
            first = kv_head * GROUP + pair * PAIR
            at = slice(first * tok, (first + PAIR) * tok)
            row_max = None
            for block in blocks:
                score = (score_ref if block.start < tok else weights_ref)[block, at]
                score = score + jnp.concatenate([live_ref[block, :]] * PAIR, axis=1)
                weights_ref[block, at] = score
                part = jnp.max(score.reshape(-1, 8, PAIR * tok), axis=0)
                row_max = part if row_max is None else jnp.maximum(row_max, part)
            row_max = jnp.max(row_max, axis=0, keepdims=True)
            total = jnp.zeros((8, PAIR * tok), jnp.float32)
            delta = jnp.zeros((8, PAIR * tok), jnp.float32)
            for block in blocks:
                dprob = (dprob_ref if block.start < tok else all_dprob_ref)[block, at]
                weights = jnp.exp2((weights_ref[block, at] - row_max) * (SCALE * LOG2E))
                weights_ref[block, at] = weights
                total = total + jnp.sum(weights.reshape(-1, 8, PAIR * tok), axis=0)
                delta = delta + jnp.sum((weights * dprob).reshape(-1, 8, PAIR * tok), axis=0)
            inverse = 1.0 / jnp.sum(total, axis=0, keepdims=True)
            delta = jnp.sum(delta, axis=0, keepdims=True) * inverse
            for block in blocks:
                dprob = (dprob_ref if block.start < tok else all_dprob_ref)[block, at]
                probs = weights_ref[block, at] * inverse
                probs_ref[block, at] = probs.astype(jnp.bfloat16)
                dscore_ref[block, at] = (probs * (dprob - delta)).astype(jnp.bfloat16)
        value_term = dot(probs_ref[:, group], grads_ref[group, :], 1, 0)
        key_term = dot(dscore_ref[:, group], queries_ref[group, :], 1, 0)
        over_queries = key_term[:, HEAD_DIM:]
        key_term = key_term[:, :HEAD_DIM] * SCALE
        high = over_queries.astype(jnp.bfloat16)
        low = (over_queries - high.astype(jnp.float32)).astype(jnp.bfloat16)
        all_keys = keys_ref[:, cols]
        query_sums = (dot(high, all_keys, 0, 0) + dot(low, all_keys, 0, 0)) * SCALE
        of_group = slice(kv_head * GROUP, (kv_head + 1) * GROUP)
        sums_ref[of_group, :] = query_sums[of_group]
        sums_ref[heads + kv_head : heads + kv_head + 1, :] = jnp.sum(
            value_term, axis=0, keepdims=True
        )
        value_cols = head_cols(kv_heads + kv_head)
        own_ref[:, cols] = key_term[:tok]
        own_ref[:, value_cols] = value_term[:tok]
        for slot in range(1, slots):
            rows = slice(slot * tok, (slot + 1) * tok)
            out_refs[slot - 1][:, cols] = key_term[rows].astype(jnp.bfloat16)
            out_refs[slot - 1][:, value_cols] = value_term[rows].astype(jnp.bfloat16)


def finish_kernel(probs_ref, dscore_ref, keys_ref, values_ref, attn_ref, qg_ref):
    tok = attn_ref.shape[0]
    kv_heads = keys_ref.shape[1] // HEAD_DIM
    for kv_head in range(kv_heads):
        cols = head_cols(kv_head)
        keys_t = keys_ref[:, cols].T
        values_t = values_ref[:, cols].T
        for pair in range(GROUP // PAIR):
            first = kv_head * GROUP + pair * PAIR
            at = slice(first * tok, (first + PAIR) * tok)
            attn = dot(values_t, probs_ref[:, at], 1, 0).T
            query_grad = (dot(keys_t, dscore_ref[:, at], 1, 0) * SCALE).T
            for n in range(PAIR):
                head = first + n
                rows = slice(n * tok, (n + 1) * tok)
                attn_ref[:, head_cols(head)] = attn[rows].astype(jnp.bfloat16)
                qg_ref[:, head_cols(head)] = query_grad[rows].astype(jnp.bfloat16)


def collect_kernel(batches, parts, kv_parts, *refs):
    sum_refs, refs = refs[:parts], refs[parts:]
    own_ref, refs = refs[0], refs[1:]
    back_refs, refs = refs[:kv_parts], refs[kv_parts:]
    kg_ref, vg_ref, qb_ref, vb_ref = refs
    heads = qb_ref.shape[0]
    kv_width = kg_ref.shape[1]
    total = sum_refs[0][...]
    for ref in sum_refs[1:]:
        total = total + ref[...]
    total = total * (1.0 / batches)
    qb_ref[...] = total[:heads]
    vb_ref[...] = total[heads:]
    term = own_ref[...]
    for ref in back_refs:
        term = term + ref[...].astype(jnp.float32)
    term = term.astype(jnp.bfloat16)
    kg_ref[...] = term[:, :kv_width]
    vg_ref[...] = term[:, kv_width:]


def total_kernel(count, *refs):
    total = refs[0][...]
    for ref in refs[1:count]:
        total = total + ref[...]
    refs[count + (len(refs) - count - 1) // 2][...] = total


def total_between(parts, passed):
    count = len(parts)
    total, *passed = pl.pallas_call(
        functools.partial(total_kernel, count),
        out_shape=[shape(array.shape, array.dtype) for array in (parts[0], *passed)],
        in_specs=[VMEM] * count + [ANY] * len(passed),
        out_specs=[VMEM] + [ANY] * len(passed),
        input_output_aliases={count + n: 1 + n for n in range(len(passed))},
        compiler_params=params(4),
        cost_estimate=pl.CostEstimate(flops=parts[0].size, bytes_accessed=0, transcendentals=0),
        name="total",
    )(*parts, *passed)
    return total, passed


def send_back(term, shift):
    size = lax.axis_size("ctx")
    return lax.ppermute(term, "ctx", [(i, (i - shift) % size) for i in range(size)])


def exchange(axis, part):
    size = lax.axis_size(axis)
    return [part] + [
        lax.ppermute(part, axis, [(i, (i + shift) % size) for i in range(size)])
        for shift in range(1, size)
    ]


def shards(q_proj, q_bias, k_proj, v_proj, v_bias, dout, lengths):
    _, tok, width = q_proj.shape
    kv_width = k_proj.shape[2]
    heads = width // HEAD_DIM
    kv_heads = kv_width // HEAD_DIM
    ctx = lax.axis_size("ctx")
    batches = lax.axis_size("dp")
    rows = ctx * tok
    columns = heads * tok
    pair = jnp.concatenate([k_proj[0], v_proj[0]], axis=1)
    pairs = [
        lax.ppermute(pair, "ctx", [(i, (i + shift) % ctx) for i in range(ctx)])
        for shift in range(ctx - 1, 0, -1)
    ] + [pair]
    prepared = pl.pallas_call(
        functools.partial(prepare_kernel, ctx),
        out_shape=[
            shape((kv_heads, HEAD_DIM), jnp.bfloat16),
            shape((columns, 2 * HEAD_DIM), jnp.bfloat16),
            shape((columns, HEAD_DIM), jnp.bfloat16),
            shape((tok, columns), jnp.float32),
            shape((tok, columns), jnp.float32),
            shape((rows, tok), jnp.float32),
        ],
        in_specs=[SMEM] + [VMEM] * 5,
        out_specs=[VMEM] * 6,
        compiler_params=params(16),
        cost_estimate=pl.CostEstimate(
            flops=4 * tok * tok * width, bytes_accessed=16 * tok * width, transcendentals=0
        ),
        name="prepare",
    )(
        lengths,
        pair,
        q_bias.reshape(heads, HEAD_DIM),
        v_bias.reshape(kv_heads, HEAD_DIM),
        q_proj[0],
        dout[0],
    )
    term = shape((tok, 2 * kv_width), jnp.bfloat16)
    probs, dscore, all_keys, all_values, sums, own, *terms = pl.pallas_call(
        functools.partial(attend_kernel, ctx),
        out_shape=[
            shape((rows, columns), jnp.bfloat16),
            shape((rows, columns), jnp.bfloat16),
            shape((rows, kv_width), jnp.bfloat16),
            shape((rows, kv_width), jnp.bfloat16),
            shape((heads + kv_heads, HEAD_DIM), jnp.float32),
            shape((tok, 2 * kv_width), jnp.float32),
        ]
        + [term] * (ctx - 1),
        in_specs=[VMEM] * (6 + ctx),
        out_specs=[VMEM] * (6 + ctx - 1),
        scratch_shapes=[
            pltpu.VMEM((rows, columns), jnp.float32),
            pltpu.VMEM((rows, columns), jnp.float32),
        ],
        compiler_params=params(24 if ctx < 8 else 48),
        cost_estimate=pl.CostEstimate(
            flops=8 * rows * tok * width,
            bytes_accessed=4 * rows * columns,
            transcendentals=rows * columns,
        ),
        name="attend",
    )(*prepared, *pairs)
    attn, q_grad = pl.pallas_call(
        finish_kernel,
        out_shape=[
            shape((tok, width), jnp.bfloat16),
            shape((tok, width), jnp.bfloat16),
        ],
        in_specs=[VMEM] * 4,
        out_specs=[VMEM] * 2,
        compiler_params=params(24),
        cost_estimate=pl.CostEstimate(
            flops=4 * rows * tok * width, bytes_accessed=4 * rows * columns, transcendentals=0
        ),
        name="finish",
    )(probs, dscore, all_keys, all_values)
    early = -(-len(terms) // 2)
    back = [send_back(term, shift) for shift, term in enumerate(terms[:early], 1)]
    sums, (back[0], *terms) = total_between(exchange("dp", sums), [back[0], *terms[early:]])
    back += [send_back(term, shift) for shift, term in enumerate(terms, early + 1)]
    sums = exchange("ctx", sums)
    k_grad, v_grad, q_sum, v_sum = pl.pallas_call(
        functools.partial(collect_kernel, batches, len(sums), len(back)),
        out_shape=[
            shape((tok, kv_width), jnp.bfloat16),
            shape((tok, kv_width), jnp.bfloat16),
            shape((heads, HEAD_DIM), jnp.float32),
            shape((kv_heads, HEAD_DIM), jnp.float32),
        ],
        in_specs=[VMEM] * (len(sums) + 1 + len(back)),
        out_specs=[VMEM] * 4,
        compiler_params=params(8),
        cost_estimate=pl.CostEstimate(
            flops=8 * tok * kv_width, bytes_accessed=16 * tok * kv_width, transcendentals=0
        ),
        name="collect",
    )(*sums, own, *back)
    return (
        attn[None],
        q_grad[None],
        k_grad[None],
        v_grad[None],
        q_sum.reshape(width),
        v_sum.reshape(kv_width),
    )


def solution(mesh):
    tokens = P("dp", "ctx", "tp")
    return jax.shard_map(
        shards,
        mesh=mesh,
        in_specs=(tokens, P("tp"), tokens, tokens, P("tp"), tokens, P("dp", None)),
        out_specs=(tokens, tokens, tokens, tokens, P("tp"), P("tp")),
        check_vma=False,
    )
```

```python
import functools

import jax
import jax.numpy as jnp
from jax import lax
from jax.experimental import pallas as pl
from jax.experimental.pallas import tpu as pltpu
from jax.sharding import PartitionSpec as P

HEAD_DIM = 128
HEADS = 32
KV_HEADS = 4
GROUP = HEADS // KV_HEADS
PAIR = 2
BLOCK = 64
SCALE = HEAD_DIM ** (-0.5)
LOG2E = 1.4426950408889634
NEGATIVE = -1e30
VMEM = pl.BlockSpec(memory_space=pltpu.VMEM)
ANY = pl.BlockSpec(memory_space=pl.ANY)
SMEM = pl.BlockSpec(memory_space=pltpu.SMEM)


def dot(left, right, left_dim, right_dim):
    return lax.dot_general(
        left, right, (((left_dim,), (right_dim,)), ((), ())), preferred_element_type=jnp.float32
    )


def head_cols(head):
    return slice(head * HEAD_DIM, (head + 1) * HEAD_DIM)


def shape(dims, dtype):
    return jax.ShapeDtypeStruct(dims, dtype)


def params(mebibytes):
    return pltpu.CompilerParams(vmem_limit_bytes=mebibytes * 1024 * 1024)


def biased(values, bias):
    return (values.astype(jnp.float32) + bias.astype(jnp.float32)).astype(jnp.bfloat16)


def prepare_kernel(
    slots, len_ref, pair_ref, qb_ref, vb_ref, q_ref, g_ref, bias_ref, queries_ref, grads_ref,
    score_ref, dprob_ref, live_ref,
):
    tok = q_ref.shape[0]
    kv_heads = vb_ref.shape[0]
    rank = lax.axis_index("ctx")
    query_pos = rank * tok + lax.broadcasted_iota(jnp.int32, (1, tok), 1)
    start = jnp.zeros((1, tok), jnp.int32)
    end = jnp.int32(0)
    for doc in range(len_ref.shape[1]):
        length = len_ref[0, doc]
        end = end + length
        start = start + jnp.where(query_pos >= end, length, 0)
    offsets = lax.broadcasted_iota(jnp.int32, (tok, tok), 0)
    for slot in range(slots):
        key_pos = (rank - slot) * tok + offsets
        live = (key_pos >= start) & (key_pos <= query_pos)
        live_ref[slot * tok : (slot + 1) * tok, :] = jnp.where(live, 0.0, NEGATIVE)
    bias_ref[...] = vb_ref[...]
    column = lax.broadcasted_iota(jnp.int32, (tok, HEAD_DIM), 1)
    for kv_head in range(kv_heads):
        keys = pair_ref[:, head_cols(kv_head)]
        values = biased(pair_ref[:, head_cols(kv_heads + kv_head)], vb_ref[kv_head : kv_head + 1, :])
        for head in range(kv_head * GROUP, (kv_head + 1) * GROUP):
            at = slice(head * tok, (head + 1) * tok)
            queries_ref[at, :HEAD_DIM] = biased(q_ref[:, head_cols(head)], qb_ref[head : head + 1, :])
            queries_ref[at, HEAD_DIM:] = (column == head).astype(jnp.bfloat16)
            grads_ref[at, :] = g_ref[:, head_cols(head)]
        rows = slice(kv_head * GROUP * tok, (kv_head + 1) * GROUP * tok)
        score_ref[:, rows] = dot(keys, queries_ref[rows, :HEAD_DIM], 1, 1)
        dprob_ref[:, rows] = dot(values, grads_ref[rows, :], 1, 1)


def attend_kernel(slots, *refs):
    bias_ref, queries_ref, grads_ref, score_ref, dprob_ref, live_ref = refs[:6]
    pair_refs = refs[6 : 6 + slots][::-1]
    refs = refs[6 + slots :]
    probs_ref, dscore_ref, keys_ref, values_ref, sums_ref, own_ref = refs[:6]
    out_refs = refs[6 : 6 + slots - 1]
    weights_ref, all_dprob_ref = refs[6 + slots - 1 :]
    tok = pair_refs[0].shape[0]
    kv_heads = bias_ref.shape[0]
    kv_width = kv_heads * HEAD_DIM
    heads = kv_heads * GROUP
    for slot in range(slots):
        rows = slice(slot * tok, (slot + 1) * tok)
        keys_ref[rows, :] = pair_refs[slot][:, :kv_width]
        for kv_head in range(kv_heads):
            values_ref[rows, head_cols(kv_head)] = biased(
                pair_refs[slot][:, head_cols(kv_heads + kv_head)], bias_ref[kv_head : kv_head + 1, :]
            )
    blocks = [slice(row, row + BLOCK) for row in range(0, slots * tok, BLOCK)]
    for kv_head in range(kv_heads):
        cols = head_cols(kv_head)
        group = slice(kv_head * GROUP * tok, (kv_head + 1) * GROUP * tok)
        weights_ref[tok:, group] = dot(keys_ref[tok:, cols], queries_ref[group, :HEAD_DIM], 1, 1)
        all_dprob_ref[tok:, group] = dot(values_ref[tok:, cols], grads_ref[group, :], 1, 1)
        for pair in range(GROUP // PAIR):
            first = kv_head * GROUP + pair * PAIR
            at = slice(first * tok, (first + PAIR) * tok)
            row_max = None
            for block in blocks:
                score = (score_ref if block.start < tok else weights_ref)[block, at]
                score = score + jnp.concatenate([live_ref[block, :]] * PAIR, axis=1)
                weights_ref[block, at] = score
                part = jnp.max(score.reshape(-1, 8, PAIR * tok), axis=0)
                row_max = part if row_max is None else jnp.maximum(row_max, part)
            row_max = jnp.max(row_max, axis=0, keepdims=True)
            total = jnp.zeros((8, PAIR * tok), jnp.float32)
            delta = jnp.zeros((8, PAIR * tok), jnp.float32)
            for block in blocks:
                dprob = (dprob_ref if block.start < tok else all_dprob_ref)[block, at]
                weights = jnp.exp2((weights_ref[block, at] - row_max) * (SCALE * LOG2E))
                weights_ref[block, at] = weights
                total = total + jnp.sum(weights.reshape(-1, 8, PAIR * tok), axis=0)
                delta = delta + jnp.sum((weights * dprob).reshape(-1, 8, PAIR * tok), axis=0)
            inverse = 1.0 / jnp.sum(total, axis=0, keepdims=True)
            delta = jnp.sum(delta, axis=0, keepdims=True) * inverse
            for block in blocks:
                dprob = (dprob_ref if block.start < tok else all_dprob_ref)[block, at]
                probs = weights_ref[block, at] * inverse
                probs_ref[block, at] = probs.astype(jnp.bfloat16)
                dscore_ref[block, at] = (probs * (dprob - delta)).astype(jnp.bfloat16)
        value_term = dot(probs_ref[:, group], grads_ref[group, :], 1, 0)
        key_term = dot(dscore_ref[:, group], queries_ref[group, :], 1, 0)
        over_queries = key_term[:, HEAD_DIM:]
        key_term = key_term[:, :HEAD_DIM] * SCALE
        high = over_queries.astype(jnp.bfloat16)
        low = (over_queries - high.astype(jnp.float32)).astype(jnp.bfloat16)
        all_keys = keys_ref[:, cols]
        query_sums = (dot(high, all_keys, 0, 0) + dot(low, all_keys, 0, 0)) * SCALE
        of_group = slice(kv_head * GROUP, (kv_head + 1) * GROUP)
        sums_ref[of_group, :] = query_sums[of_group]
        sums_ref[heads + kv_head : heads + kv_head + 1, :] = jnp.sum(
            value_term, axis=0, keepdims=True
        )
        value_cols = head_cols(kv_heads + kv_head)
        own_ref[:, cols] = key_term[:tok]
        own_ref[:, value_cols] = value_term[:tok]
        for slot in range(1, slots):
            rows = slice(slot * tok, (slot + 1) * tok)
            out_refs[slot - 1][:, cols] = key_term[rows].astype(jnp.bfloat16)
            out_refs[slot - 1][:, value_cols] = value_term[rows].astype(jnp.bfloat16)


def finish_kernel(probs_ref, dscore_ref, keys_ref, values_ref, _, attn_ref, qg_ref, __):
    tok = attn_ref.shape[0]
    kv_heads = keys_ref.shape[1] // HEAD_DIM
    for kv_head in range(kv_heads):
        cols = head_cols(kv_head)
        keys_t = keys_ref[:, cols].T
        values_t = values_ref[:, cols].T
        for pair in range(GROUP // PAIR):
            first = kv_head * GROUP + pair * PAIR
            at = slice(first * tok, (first + PAIR) * tok)
            attn = dot(values_t, probs_ref[:, at], 1, 0).T
            query_grad = (dot(keys_t, dscore_ref[:, at], 1, 0) * SCALE).T
            for n in range(PAIR):
                head = first + n
                rows = slice(n * tok, (n + 1) * tok)
                attn_ref[:, head_cols(head)] = attn[rows].astype(jnp.bfloat16)
                qg_ref[:, head_cols(head)] = query_grad[rows].astype(jnp.bfloat16)


def collect_kernel(batches, messages, *refs):
    sum_refs, refs = refs[:2], refs[2:]
    own_ref, early_ref, refs = refs[0], refs[1], refs[2:]
    message_refs, (kg_ref, vg_ref, qb_ref, vb_ref) = refs[:messages], refs[messages:]
    heads, kv_heads = qb_ref.shape[0], vb_ref.shape[0]
    tok, kv_width = kg_ref.shape
    total = sum_refs[0][...] + sum_refs[1][...]
    term = own_ref[...] + early_ref[...].astype(jnp.float32)
    for ref in message_refs:
        sums = ref[tok:, :].astype(jnp.float32)
        sums = sums[:, :HEAD_DIM] + sums[:, HEAD_DIM : 2 * HEAD_DIM]
        total = total + sums[: heads + kv_heads]
        term = term + ref[:tok, :].astype(jnp.float32)
    total = total * (1.0 / batches)
    qb_ref[...] = total[:heads]
    vb_ref[...] = total[heads:]
    term = term.astype(jnp.bfloat16)
    kg_ref[...] = term[:, :kv_width]
    vg_ref[...] = term[:, kv_width:]


def total_kernel(count, *refs):
    parts, refs = refs[:count], refs[count:]
    sent = (len(refs) - 1) // 2
    term_refs, total_ref, message_refs = refs[:sent], refs[sent], refs[sent + 1 :]
    total = parts[0][...]
    for ref in parts[1:]:
        total = total + ref[...]
    total_ref[...] = total
    for term_ref, message_ref in zip(term_refs, message_refs):
        tok = term_ref.shape[0]
        rows = message_ref.shape[0] - tok
        high = jnp.concatenate([total, jnp.zeros((rows - total.shape[0], HEAD_DIM), jnp.float32)])
        message_ref[:tok, :] = term_ref[...]
        message_ref[tok:, :] = jnp.zeros((rows, term_ref.shape[1]), jnp.bfloat16)
        message_ref[tok:, :HEAD_DIM] = high.astype(jnp.bfloat16)
        low = high - high.astype(jnp.bfloat16).astype(jnp.float32)
        message_ref[tok:, HEAD_DIM : 2 * HEAD_DIM] = low.astype(jnp.bfloat16)


def total_with(parts, terms):
    rows = -(-parts[0].shape[0] // 16) * 16
    total, *messages = pl.pallas_call(
        functools.partial(total_kernel, len(parts)),
        out_shape=[shape(parts[0].shape, parts[0].dtype)]
        + [shape((term.shape[0] + rows, term.shape[1]), term.dtype) for term in terms],
        in_specs=[VMEM] * (len(parts) + len(terms)),
        out_specs=[VMEM] * (1 + len(terms)),
        compiler_params=params(8),
        cost_estimate=pl.CostEstimate(flops=parts[0].size, bytes_accessed=0, transcendentals=0),
        name="total",
    )(*parts, *terms)
    return total, messages


def send_back(term, shift):
    size = lax.axis_size("ctx")
    return lax.ppermute(term, "ctx", [(i, (i - shift) % size) for i in range(size)])


def exchange(axis, part):
    size = lax.axis_size(axis)
    return [part] + [
        lax.ppermute(part, axis, [(i, (i + shift) % size) for i in range(size)])
        for shift in range(1, size)
    ]


def shards(q_proj, q_bias, k_proj, v_proj, v_bias, dout, lengths):
    _, tok, width = q_proj.shape
    kv_width = k_proj.shape[2]
    heads = width // HEAD_DIM
    kv_heads = kv_width // HEAD_DIM
    ctx = lax.axis_size("ctx")
    batches = lax.axis_size("dp")
    rows = ctx * tok
    columns = heads * tok
    pair = jnp.concatenate([k_proj[0], v_proj[0]], axis=1)
    pairs = [
        lax.ppermute(pair, "ctx", [(i, (i + shift) % ctx) for i in range(ctx)])
        for shift in range(ctx - 1, 0, -1)
    ] + [pair]
    prepared = pl.pallas_call(
        functools.partial(prepare_kernel, ctx),
        out_shape=[
            shape((kv_heads, HEAD_DIM), jnp.bfloat16),
            shape((columns, 2 * HEAD_DIM), jnp.bfloat16),
            shape((columns, HEAD_DIM), jnp.bfloat16),
            shape((tok, columns), jnp.float32),
            shape((tok, columns), jnp.float32),
            shape((rows, tok), jnp.float32),
        ],
        in_specs=[SMEM] + [VMEM] * 5,
        out_specs=[VMEM] * 6,
        compiler_params=params(16),
        cost_estimate=pl.CostEstimate(
            flops=4 * tok * tok * width, bytes_accessed=16 * tok * width, transcendentals=0
        ),
        name="prepare",
    )(
        lengths,
        pair,
        q_bias.reshape(heads, HEAD_DIM),
        v_bias.reshape(kv_heads, HEAD_DIM),
        q_proj[0],
        dout[0],
    )
    term = shape((tok, 2 * kv_width), jnp.bfloat16)
    probs, dscore, all_keys, all_values, sums, own, *terms = pl.pallas_call(
        functools.partial(attend_kernel, ctx),
        out_shape=[
            shape((rows, columns), jnp.bfloat16),
            shape((rows, columns), jnp.bfloat16),
            shape((rows, kv_width), jnp.bfloat16),
            shape((rows, kv_width), jnp.bfloat16),
            shape((heads + kv_heads, HEAD_DIM), jnp.float32),
            shape((tok, 2 * kv_width), jnp.float32),
        ]
        + [term] * (ctx - 1),
        in_specs=[VMEM] * (6 + ctx),
        out_specs=[VMEM] * (6 + ctx - 1),
        scratch_shapes=[
            pltpu.VMEM((rows, columns), jnp.float32),
            pltpu.VMEM((rows, columns), jnp.float32),
        ],
        compiler_params=params(24 if ctx < 8 else 48),
        cost_estimate=pl.CostEstimate(
            flops=8 * rows * tok * width,
            bytes_accessed=4 * rows * columns,
            transcendentals=rows * columns,
        ),
        name="attend",
    )(*prepared, *pairs)
    half = ctx // 2
    early = send_back(terms.pop(half - 1), half)
    attn, q_grad, early = pl.pallas_call(
        finish_kernel,
        out_shape=[
            shape((tok, width), jnp.bfloat16),
            shape((tok, width), jnp.bfloat16),
            shape(early.shape, early.dtype),
        ],
        in_specs=[VMEM] * 4 + [ANY],
        out_specs=[VMEM] * 2 + [ANY],
        input_output_aliases={4: 2},
        compiler_params=params(24),
        cost_estimate=pl.CostEstimate(
            flops=4 * rows * tok * width, bytes_accessed=4 * rows * columns, transcendentals=0
        ),
        name="finish",
    )(probs, dscore, all_keys, all_values, early)
    sums, messages = total_with(exchange("dp", sums), terms)
    shifts = [shift for shift in range(1, ctx) if shift != half]
    back = [send_back(message, shift) for shift, message in zip(shifts, messages)]
    sums = [sums, send_back(sums, half)]
    k_grad, v_grad, q_sum, v_sum = pl.pallas_call(
        functools.partial(collect_kernel, batches, len(back)),
        out_shape=[
            shape((tok, kv_width), jnp.bfloat16),
            shape((tok, kv_width), jnp.bfloat16),
            shape((heads, HEAD_DIM), jnp.float32),
            shape((kv_heads, HEAD_DIM), jnp.float32),
        ],
        in_specs=[VMEM] * (4 + len(back)),
        out_specs=[VMEM] * 4,
        compiler_params=params(8),
        cost_estimate=pl.CostEstimate(
            flops=8 * tok * kv_width, bytes_accessed=16 * tok * kv_width, transcendentals=0
        ),
        name="collect",
    )(*sums, own, early, *back)
    return (
        attn[None],
        q_grad[None],
        k_grad[None],
        v_grad[None],
        q_sum.reshape(width),
        v_sum.reshape(kv_width),
    )


def solution(mesh):
    tokens = P("dp", "ctx", "tp")
    return jax.shard_map(
        shards,
        mesh=mesh,
        in_specs=(tokens, P("tp"), tokens, tokens, P("tp"), tokens, P("dp", None)),
        out_specs=(tokens, tokens, tokens, tokens, P("tp"), P("tp")),
        check_vma=False,
    )
```

```python
import functools

import jax
import jax.numpy as jnp
from jax import lax
from jax.experimental import pallas as pl
from jax.experimental.pallas import tpu as pltpu
from jax.sharding import PartitionSpec as P

HEAD_DIM = 128
HEADS = 32
KV_HEADS = 4
GROUP = HEADS // KV_HEADS
PAIR = 2
BLOCK = 64
SCALE = HEAD_DIM ** (-0.5)
LOG2E = 1.4426950408889634
NEGATIVE = -1e30
VMEM = pl.BlockSpec(memory_space=pltpu.VMEM)
ANY = pl.BlockSpec(memory_space=pl.ANY)
SMEM = pl.BlockSpec(memory_space=pltpu.SMEM)


def dot(left, right, left_dim, right_dim):
    return lax.dot_general(
        left, right, (((left_dim,), (right_dim,)), ((), ())), preferred_element_type=jnp.float32
    )


def head_cols(head):
    return slice(head * HEAD_DIM, (head + 1) * HEAD_DIM)


def shape(dims, dtype):
    return jax.ShapeDtypeStruct(dims, dtype)


def params(mebibytes):
    return pltpu.CompilerParams(vmem_limit_bytes=mebibytes * 1024 * 1024)


def biased(values, bias):
    return (values.astype(jnp.float32) + bias.astype(jnp.float32)).astype(jnp.bfloat16)


def source_of(rank, slot, size):
    if size & (size - 1):
        return (rank + size - slot) % size
    return rank ^ slot


def fetch(array, axis, slot):
    size = lax.axis_size(axis)
    return lax.ppermute(array, axis, [(source_of(i, slot, size), i) for i in range(size)])


def send_back(array, slot):
    size = lax.axis_size("ctx")
    return lax.ppermute(array, "ctx", [(i, source_of(i, slot, size)) for i in range(size)])


def prepare_kernel(
    slots, len_ref, pair_ref, qb_ref, vb_ref, q_ref, g_ref, bias_ref, queries_ref, grads_ref,
    score_ref, dprob_ref, live_ref,
):
    tok = q_ref.shape[0]
    kv_heads = vb_ref.shape[0]
    rank = lax.axis_index("ctx")
    query_pos = rank * tok + lax.broadcasted_iota(jnp.int32, (1, tok), 1)
    start = jnp.zeros((1, tok), jnp.int32)
    end = jnp.int32(0)
    for doc in range(len_ref.shape[1]):
        length = len_ref[0, doc]
        end = end + length
        start = start + jnp.where(query_pos >= end, length, 0)
    offsets = lax.broadcasted_iota(jnp.int32, (tok, tok), 0)
    for slot in range(slots):
        key_pos = source_of(rank, slot, slots) * tok + offsets
        live = (key_pos >= start) & (key_pos <= query_pos)
        live_ref[slot * tok : (slot + 1) * tok, :] = jnp.where(live, 0.0, NEGATIVE)
    bias_ref[...] = vb_ref[...]
    column = lax.broadcasted_iota(jnp.int32, (tok, HEAD_DIM), 1)
    for kv_head in range(kv_heads):
        keys = pair_ref[:, head_cols(kv_head)]
        values = biased(pair_ref[:, head_cols(kv_heads + kv_head)], vb_ref[kv_head : kv_head + 1, :])
        for head in range(kv_head * GROUP, (kv_head + 1) * GROUP):
            at = slice(head * tok, (head + 1) * tok)
            queries_ref[at, :HEAD_DIM] = biased(q_ref[:, head_cols(head)], qb_ref[head : head + 1, :])
            queries_ref[at, HEAD_DIM:] = (column == head).astype(jnp.bfloat16)
            grads_ref[at, :] = g_ref[:, head_cols(head)]
        rows = slice(kv_head * GROUP * tok, (kv_head + 1) * GROUP * tok)
        score_ref[:, rows] = dot(keys, queries_ref[rows, :HEAD_DIM], 1, 1)
        dprob_ref[:, rows] = dot(values, grads_ref[rows, :], 1, 1)


def attend_kernel(slots, *refs):
    bias_ref, queries_ref, grads_ref, score_ref, dprob_ref, live_ref = refs[:6]
    pair_refs = refs[6 : 6 + slots]
    refs = refs[6 + slots :]
    probs_ref, dscore_ref, keys_ref, values_ref, sums_ref, own_ref = refs[:6]
    out_refs = refs[6 : 6 + slots - 1]
    weights_ref, all_dprob_ref = refs[6 + slots - 1 :]
    tok = pair_refs[0].shape[0]
    kv_heads = bias_ref.shape[0]
    kv_width = kv_heads * HEAD_DIM
    heads = kv_heads * GROUP
    for slot in range(slots):
        rows = slice(slot * tok, (slot + 1) * tok)
        keys_ref[rows, :] = pair_refs[slot][:, :kv_width]
        for kv_head in range(kv_heads):
            values_ref[rows, head_cols(kv_head)] = biased(
                pair_refs[slot][:, head_cols(kv_heads + kv_head)], bias_ref[kv_head : kv_head + 1, :]
            )
    blocks = [slice(row, row + BLOCK) for row in range(0, slots * tok, BLOCK)]
    for kv_head in range(kv_heads):
        cols = head_cols(kv_head)
        group = slice(kv_head * GROUP * tok, (kv_head + 1) * GROUP * tok)
        weights_ref[tok:, group] = dot(keys_ref[tok:, cols], queries_ref[group, :HEAD_DIM], 1, 1)
        all_dprob_ref[tok:, group] = dot(values_ref[tok:, cols], grads_ref[group, :], 1, 1)
        for pair in range(GROUP // PAIR):
            first = kv_head * GROUP + pair * PAIR
            at = slice(first * tok, (first + PAIR) * tok)
            row_max = None
            for block in blocks:
                score = (score_ref if block.start < tok else weights_ref)[block, at]
                score = score + jnp.concatenate([live_ref[block, :]] * PAIR, axis=1)
                weights_ref[block, at] = score
                part = jnp.max(score.reshape(-1, 8, PAIR * tok), axis=0)
                row_max = part if row_max is None else jnp.maximum(row_max, part)
            row_max = jnp.max(row_max, axis=0, keepdims=True)
            total = jnp.zeros((8, PAIR * tok), jnp.float32)
            delta = jnp.zeros((8, PAIR * tok), jnp.float32)
            for block in blocks:
                dprob = (dprob_ref if block.start < tok else all_dprob_ref)[block, at]
                weights = jnp.exp2((weights_ref[block, at] - row_max) * (SCALE * LOG2E))
                weights_ref[block, at] = weights
                total = total + jnp.sum(weights.reshape(-1, 8, PAIR * tok), axis=0)
                delta = delta + jnp.sum((weights * dprob).reshape(-1, 8, PAIR * tok), axis=0)
            inverse = 1.0 / jnp.sum(total, axis=0, keepdims=True)
            delta = jnp.sum(delta, axis=0, keepdims=True) * inverse
            for block in blocks:
                dprob = (dprob_ref if block.start < tok else all_dprob_ref)[block, at]
                probs = weights_ref[block, at] * inverse
                probs_ref[block, at] = probs.astype(jnp.bfloat16)
                dscore_ref[block, at] = (probs * (dprob - delta)).astype(jnp.bfloat16)
        value_term = dot(probs_ref[:, group], grads_ref[group, :], 1, 0)
        key_term = dot(dscore_ref[:, group], queries_ref[group, :], 1, 0)
        over_queries = key_term[:, HEAD_DIM:]
        key_term = key_term[:, :HEAD_DIM] * SCALE
        high = over_queries.astype(jnp.bfloat16)
        low = (over_queries - high.astype(jnp.float32)).astype(jnp.bfloat16)
        all_keys = keys_ref[:, cols]
        query_sums = (dot(high, all_keys, 0, 0) + dot(low, all_keys, 0, 0)) * SCALE
        of_group = slice(kv_head * GROUP, (kv_head + 1) * GROUP)
        sums_ref[of_group, :] = query_sums[of_group]
        sums_ref[heads + kv_head : heads + kv_head + 1, :] = jnp.sum(
            value_term, axis=0, keepdims=True
        )
        value_cols = head_cols(kv_heads + kv_head)
        own_ref[:, cols] = key_term[:tok]
        own_ref[:, value_cols] = value_term[:tok]
        for slot in range(1, slots):
            rows = slice(slot * tok, (slot + 1) * tok)
            out_refs[slot - 1][:, cols] = key_term[rows].astype(jnp.bfloat16)
            out_refs[slot - 1][:, value_cols] = value_term[rows].astype(jnp.bfloat16)


def finish_kernel(probs_ref, dscore_ref, keys_ref, values_ref, _, attn_ref, qg_ref, __):
    tok = attn_ref.shape[0]
    kv_heads = keys_ref.shape[1] // HEAD_DIM
    for kv_head in range(kv_heads):
        cols = head_cols(kv_head)
        keys_t = keys_ref[:, cols].T
        values_t = values_ref[:, cols].T
        for pair in range(GROUP // PAIR):
            first = kv_head * GROUP + pair * PAIR
            at = slice(first * tok, (first + PAIR) * tok)
            attn = dot(values_t, probs_ref[:, at], 1, 0).T
            query_grad = (dot(keys_t, dscore_ref[:, at], 1, 0) * SCALE).T
            for n in range(PAIR):
                head = first + n
                rows = slice(n * tok, (n + 1) * tok)
                attn_ref[:, head_cols(head)] = attn[rows].astype(jnp.bfloat16)
                qg_ref[:, head_cols(head)] = query_grad[rows].astype(jnp.bfloat16)


def collect_kernel(batches, messages, *refs):
    sum_refs, refs = refs[:2], refs[2:]
    own_ref, early_ref, refs = refs[0], refs[1], refs[2:]
    message_refs, (kg_ref, vg_ref, qb_ref, vb_ref) = refs[:messages], refs[messages:]
    heads, kv_heads = qb_ref.shape[0], vb_ref.shape[0]
    tok, kv_width = kg_ref.shape
    total = sum_refs[0][...] + sum_refs[1][...]
    term = own_ref[...] + early_ref[...].astype(jnp.float32)
    for ref in message_refs:
        sums = ref[tok:, :].astype(jnp.float32)
        sums = sums[:, :HEAD_DIM] + sums[:, HEAD_DIM : 2 * HEAD_DIM]
        total = total + sums[: heads + kv_heads]
        term = term + ref[:tok, :].astype(jnp.float32)
    total = total * (1.0 / batches)
    qb_ref[...] = total[:heads]
    vb_ref[...] = total[heads:]
    term = term.astype(jnp.bfloat16)
    kg_ref[...] = term[:, :kv_width]
    vg_ref[...] = term[:, kv_width:]


def total_kernel(count, *refs):
    parts, refs = refs[:count], refs[count:]
    sent = (len(refs) - 1) // 2
    term_refs, total_ref, message_refs = refs[:sent], refs[sent], refs[sent + 1 :]
    total = parts[0][...]
    for ref in parts[1:]:
        total = total + ref[...]
    total_ref[...] = total
    for term_ref, message_ref in zip(term_refs, message_refs):
        tok = term_ref.shape[0]
        rows = message_ref.shape[0] - tok
        high = jnp.concatenate([total, jnp.zeros((rows - total.shape[0], HEAD_DIM), jnp.float32)])
        message_ref[:tok, :] = term_ref[...]
        message_ref[tok:, :] = jnp.zeros((rows, term_ref.shape[1]), jnp.bfloat16)
        message_ref[tok:, :HEAD_DIM] = high.astype(jnp.bfloat16)
        low = high - high.astype(jnp.bfloat16).astype(jnp.float32)
        message_ref[tok:, HEAD_DIM : 2 * HEAD_DIM] = low.astype(jnp.bfloat16)


def total_with(parts, terms):
    rows = -(-parts[0].shape[0] // 16) * 16
    total, *messages = pl.pallas_call(
        functools.partial(total_kernel, len(parts)),
        out_shape=[shape(parts[0].shape, parts[0].dtype)]
        + [shape((term.shape[0] + rows, term.shape[1]), term.dtype) for term in terms],
        in_specs=[VMEM] * (len(parts) + len(terms)),
        out_specs=[VMEM] * (1 + len(terms)),
        compiler_params=params(8),
        cost_estimate=pl.CostEstimate(flops=parts[0].size, bytes_accessed=0, transcendentals=0),
        name="total",
    )(*parts, *terms)
    return total, messages


def exchange(axis, part):
    return [part] + [fetch(part, axis, slot) for slot in range(1, lax.axis_size(axis))]


def shards(q_proj, q_bias, k_proj, v_proj, v_bias, dout, lengths):
    _, tok, width = q_proj.shape
    kv_width = k_proj.shape[2]
    heads = width // HEAD_DIM
    kv_heads = kv_width // HEAD_DIM
    ctx = lax.axis_size("ctx")
    batches = lax.axis_size("dp")
    rows = ctx * tok
    columns = heads * tok
    pair = jnp.concatenate([k_proj[0], v_proj[0]], axis=1)
    pairs = [pair] + [fetch(pair, "ctx", slot) for slot in range(1, ctx)]
    prepared = pl.pallas_call(
        functools.partial(prepare_kernel, ctx),
        out_shape=[
            shape((kv_heads, HEAD_DIM), jnp.bfloat16),
            shape((columns, 2 * HEAD_DIM), jnp.bfloat16),
            shape((columns, HEAD_DIM), jnp.bfloat16),
            shape((tok, columns), jnp.float32),
            shape((tok, columns), jnp.float32),
            shape((rows, tok), jnp.float32),
        ],
        in_specs=[SMEM] + [VMEM] * 5,
        out_specs=[VMEM] * 6,
        compiler_params=params(16),
        cost_estimate=pl.CostEstimate(
            flops=4 * tok * tok * width, bytes_accessed=16 * tok * width, transcendentals=0
        ),
        name="prepare",
    )(
        lengths,
        pair,
        q_bias.reshape(heads, HEAD_DIM),
        v_bias.reshape(kv_heads, HEAD_DIM),
        q_proj[0],
        dout[0],
    )
    term = shape((tok, 2 * kv_width), jnp.bfloat16)
    probs, dscore, all_keys, all_values, sums, own, *terms = pl.pallas_call(
        functools.partial(attend_kernel, ctx),
        out_shape=[
            shape((rows, columns), jnp.bfloat16),
            shape((rows, columns), jnp.bfloat16),
            shape((rows, kv_width), jnp.bfloat16),
            shape((rows, kv_width), jnp.bfloat16),
            shape((heads + kv_heads, HEAD_DIM), jnp.float32),
            shape((tok, 2 * kv_width), jnp.float32),
        ]
        + [term] * (ctx - 1),
        in_specs=[VMEM] * (6 + ctx),
        out_specs=[VMEM] * (6 + ctx - 1),
        scratch_shapes=[
            pltpu.VMEM((rows, columns), jnp.float32),
            pltpu.VMEM((rows, columns), jnp.float32),
        ],
        compiler_params=params(24 if ctx < 8 else 48),
        cost_estimate=pl.CostEstimate(
            flops=8 * rows * tok * width,
            bytes_accessed=4 * rows * columns,
            transcendentals=rows * columns,
        ),
        name="attend",
    )(*prepared, *pairs)
    half = ctx // 2
    early = send_back(terms.pop(half - 1), half)
    attn, q_grad, early = pl.pallas_call(
        finish_kernel,
        out_shape=[
            shape((tok, width), jnp.bfloat16),
            shape((tok, width), jnp.bfloat16),
            shape(early.shape, early.dtype),
        ],
        in_specs=[VMEM] * 4 + [ANY],
        out_specs=[VMEM] * 2 + [ANY],
        input_output_aliases={4: 2},
        compiler_params=params(24),
        cost_estimate=pl.CostEstimate(
            flops=4 * rows * tok * width, bytes_accessed=4 * rows * columns, transcendentals=0
        ),
        name="finish",
    )(probs, dscore, all_keys, all_values, early)
    sums, messages = total_with(exchange("dp", sums), terms)
    slots = [slot for slot in range(1, ctx) if slot != half]
    back = [send_back(message, slot) for slot, message in zip(slots, messages)][::-1]
    sums = [sums, send_back(sums, half)]
    k_grad, v_grad, q_sum, v_sum = pl.pallas_call(
        functools.partial(collect_kernel, batches, len(back)),
        out_shape=[
            shape((tok, kv_width), jnp.bfloat16),
            shape((tok, kv_width), jnp.bfloat16),
            shape((heads, HEAD_DIM), jnp.float32),
            shape((kv_heads, HEAD_DIM), jnp.float32),
        ],
        in_specs=[VMEM] * (4 + len(back)),
        out_specs=[VMEM] * 4,
        compiler_params=params(8),
        cost_estimate=pl.CostEstimate(
            flops=8 * tok * kv_width, bytes_accessed=16 * tok * kv_width, transcendentals=0
        ),
        name="collect",
    )(*sums, own, early, *back)
    return (
        attn[None],
        q_grad[None],
        k_grad[None],
        v_grad[None],
        q_sum.reshape(width),
        v_sum.reshape(kv_width),
    )


def solution(mesh):
    tokens = P("dp", "ctx", "tp")
    return jax.shard_map(
        shards,
        mesh=mesh,
        in_specs=(tokens, P("tp"), tokens, tokens, P("tp"), tokens, P("dp", None)),
        out_specs=(tokens, tokens, tokens, tokens, P("tp"), P("tp")),
        check_vma=False,
    )
```

```python
import functools

import jax
import jax.numpy as jnp
from jax import lax
from jax.experimental import pallas as pl
from jax.experimental.pallas import tpu as pltpu
from jax.sharding import PartitionSpec as P

HEAD_DIM = 128
HEADS = 32
KV_HEADS = 4
GROUP = HEADS // KV_HEADS
PAIR = 2
BLOCK = 64
SCALE = HEAD_DIM ** (-0.5)
LOG2E = 1.4426950408889634
NEGATIVE = -1e30
VMEM = pl.BlockSpec(memory_space=pltpu.VMEM)
ANY = pl.BlockSpec(memory_space=pl.ANY)
SMEM = pl.BlockSpec(memory_space=pltpu.SMEM)


def dot(left, right, left_dim, right_dim):
    return lax.dot_general(
        left, right, (((left_dim,), (right_dim,)), ((), ())), preferred_element_type=jnp.float32
    )


def head_cols(head):
    return slice(head * HEAD_DIM, (head + 1) * HEAD_DIM)


def shape(dims, dtype):
    return jax.ShapeDtypeStruct(dims, dtype)


def params(mebibytes):
    return pltpu.CompilerParams(vmem_limit_bytes=mebibytes * 1024 * 1024)


def biased(values, bias):
    return (values.astype(jnp.float32) + bias.astype(jnp.float32)).astype(jnp.bfloat16)


def source_of(rank, slot, size):
    if size & (size - 1):
        return (rank + size - slot) % size
    return rank ^ slot


def fetch(array, axis, slot):
    size = lax.axis_size(axis)
    return lax.ppermute(array, axis, [(source_of(i, slot, size), i) for i in range(size)])


def send_back(array, slot):
    size = lax.axis_size("ctx")
    return lax.ppermute(array, "ctx", [(i, source_of(i, slot, size)) for i in range(size)])


def prepare_kernel(
    slots, len_ref, pair_ref, qb_ref, vb_ref, q_ref, g_ref, bias_ref, queries_ref, grads_ref,
    score_ref, dprob_ref, live_ref,
):
    tok = q_ref.shape[0]
    kv_heads = vb_ref.shape[0]
    rank = lax.axis_index("ctx")
    query_pos = rank * tok + lax.broadcasted_iota(jnp.int32, (1, tok), 1)
    start = jnp.zeros((1, tok), jnp.int32)
    end = jnp.int32(0)
    for doc in range(len_ref.shape[1]):
        length = len_ref[0, doc]
        end = end + length
        start = start + jnp.where(query_pos >= end, length, 0)
    offsets = lax.broadcasted_iota(jnp.int32, (tok, tok), 0)
    for slot in range(slots):
        key_pos = source_of(rank, slot, slots) * tok + offsets
        live = (key_pos >= start) & (key_pos <= query_pos)
        live_ref[slot * tok : (slot + 1) * tok, :] = jnp.where(live, 0.0, NEGATIVE)
    bias_ref[...] = vb_ref[...]
    column = lax.broadcasted_iota(jnp.int32, (tok, HEAD_DIM), 1)
    for kv_head in range(kv_heads):
        keys = pair_ref[:, head_cols(kv_head)]
        values = biased(pair_ref[:, head_cols(kv_heads + kv_head)], vb_ref[kv_head : kv_head + 1, :])
        for head in range(kv_head * GROUP, (kv_head + 1) * GROUP):
            at = slice(head * tok, (head + 1) * tok)
            queries_ref[at, :HEAD_DIM] = biased(q_ref[:, head_cols(head)], qb_ref[head : head + 1, :])
            queries_ref[at, HEAD_DIM:] = (column == head).astype(jnp.bfloat16)
            grads_ref[at, :] = g_ref[:, head_cols(head)]
        rows = slice(kv_head * GROUP * tok, (kv_head + 1) * GROUP * tok)
        score_ref[:, rows] = dot(keys, queries_ref[rows, :HEAD_DIM], 1, 1)
        dprob_ref[:, rows] = dot(values, grads_ref[rows, :], 1, 1)


def attend_kernel(slots, *refs):
    bias_ref, queries_ref, grads_ref, score_ref, dprob_ref, live_ref = refs[:6]
    pair_refs = refs[6 : 6 + slots]
    refs = refs[6 + slots :]
    probs_ref, dscore_ref, keys_ref, values_ref, sums_ref, own_ref = refs[:6]
    out_refs = refs[6 : 6 + slots - 1]
    weights_ref, all_dprob_ref = refs[6 + slots - 1 :]
    tok = pair_refs[0].shape[0]
    kv_heads = bias_ref.shape[0]
    kv_width = kv_heads * HEAD_DIM
    heads = kv_heads * GROUP
    for slot in range(slots):
        rows = slice(slot * tok, (slot + 1) * tok)
        keys_ref[rows, :] = pair_refs[slot][:, :kv_width]
        for kv_head in range(kv_heads):
            values_ref[rows, head_cols(kv_head)] = biased(
                pair_refs[slot][:, head_cols(kv_heads + kv_head)], bias_ref[kv_head : kv_head + 1, :]
            )
    blocks = [slice(row, row + BLOCK) for row in range(0, slots * tok, BLOCK)]
    for kv_head in range(kv_heads):
        cols = head_cols(kv_head)
        group = slice(kv_head * GROUP * tok, (kv_head + 1) * GROUP * tok)
        weights_ref[tok:, group] = dot(keys_ref[tok:, cols], queries_ref[group, :HEAD_DIM], 1, 1)
        all_dprob_ref[tok:, group] = dot(values_ref[tok:, cols], grads_ref[group, :], 1, 1)
        for pair in range(GROUP // PAIR):
            first = kv_head * GROUP + pair * PAIR
            at = slice(first * tok, (first + PAIR) * tok)
            row_max = None
            for block in blocks:
                score = (score_ref if block.start < tok else weights_ref)[block, at]
                score = score + jnp.concatenate([live_ref[block, :]] * PAIR, axis=1)
                weights_ref[block, at] = score
                part = jnp.max(score.reshape(-1, 8, PAIR * tok), axis=0)
                row_max = part if row_max is None else jnp.maximum(row_max, part)
            row_max = jnp.max(row_max, axis=0, keepdims=True)
            total = jnp.zeros((8, PAIR * tok), jnp.float32)
            delta = jnp.zeros((8, PAIR * tok), jnp.float32)
            for block in blocks:
                dprob = (dprob_ref if block.start < tok else all_dprob_ref)[block, at]
                weights = jnp.exp2((weights_ref[block, at] - row_max) * (SCALE * LOG2E))
                weights_ref[block, at] = weights
                total = total + jnp.sum(weights.reshape(-1, 8, PAIR * tok), axis=0)
                delta = delta + jnp.sum((weights * dprob).reshape(-1, 8, PAIR * tok), axis=0)
            inverse = 1.0 / jnp.sum(total, axis=0, keepdims=True)
            delta = jnp.sum(delta, axis=0, keepdims=True) * inverse
            for block in blocks:
                dprob = (dprob_ref if block.start < tok else all_dprob_ref)[block, at]
                probs = weights_ref[block, at] * inverse
                probs_ref[block, at] = probs.astype(jnp.bfloat16)
                dscore_ref[block, at] = (probs * (dprob - delta)).astype(jnp.bfloat16)
        value_term = dot(probs_ref[:, group], grads_ref[group, :], 1, 0)
        key_term = dot(dscore_ref[:, group], queries_ref[group, :], 1, 0)
        over_queries = key_term[:, HEAD_DIM:]
        key_term = key_term[:, :HEAD_DIM] * SCALE
        high = over_queries.astype(jnp.bfloat16)
        low = (over_queries - high.astype(jnp.float32)).astype(jnp.bfloat16)
        all_keys = keys_ref[:, cols]
        query_sums = (dot(high, all_keys, 0, 0) + dot(low, all_keys, 0, 0)) * SCALE
        of_group = slice(kv_head * GROUP, (kv_head + 1) * GROUP)
        sums_ref[of_group, :] = query_sums[of_group]
        sums_ref[heads + kv_head : heads + kv_head + 1, :] = jnp.sum(
            value_term, axis=0, keepdims=True
        )
        value_cols = head_cols(kv_heads + kv_head)
        own_ref[:, cols] = key_term[:tok]
        own_ref[:, value_cols] = value_term[:tok]
        for slot in range(1, slots):
            rows = slice(slot * tok, (slot + 1) * tok)
            out_refs[slot - 1][:, cols] = key_term[rows].astype(jnp.bfloat16)
            out_refs[slot - 1][:, value_cols] = value_term[rows].astype(jnp.bfloat16)


def finish_kernel(probs_ref, dscore_ref, keys_ref, values_ref, attn_ref, qg_ref):
    tok = attn_ref.shape[0]
    kv_heads = keys_ref.shape[1] // HEAD_DIM
    for kv_head in range(kv_heads):
        cols = head_cols(kv_head)
        keys_t = keys_ref[:, cols].T
        values_t = values_ref[:, cols].T
        for pair in range(GROUP // PAIR):
            first = kv_head * GROUP + pair * PAIR
            at = slice(first * tok, (first + PAIR) * tok)
            attn = dot(values_t, probs_ref[:, at], 1, 0).T
            query_grad = (dot(keys_t, dscore_ref[:, at], 1, 0) * SCALE).T
            for n in range(PAIR):
                head = first + n
                rows = slice(n * tok, (n + 1) * tok)
                attn_ref[:, head_cols(head)] = attn[rows].astype(jnp.bfloat16)
                qg_ref[:, head_cols(head)] = query_grad[rows].astype(jnp.bfloat16)


def collect_kernel(batches, parts, kv_parts, *refs):
    sum_refs, refs = refs[:parts], refs[parts:]
    own_ref, refs = refs[0], refs[1:]
    back_refs, refs = refs[:kv_parts], refs[kv_parts:]
    kg_ref, vg_ref, qb_ref, vb_ref = refs
    heads = qb_ref.shape[0]
    kv_width = kg_ref.shape[1]
    total = sum_refs[0][...]
    for ref in sum_refs[1:]:
        total = total + ref[...]
    total = total * (1.0 / batches)
    qb_ref[...] = total[:heads]
    vb_ref[...] = total[heads:]
    term = own_ref[...]
    for ref in back_refs:
        term = term + ref[...].astype(jnp.float32)
    term = term.astype(jnp.bfloat16)
    kg_ref[...] = term[:, :kv_width]
    vg_ref[...] = term[:, kv_width:]


def total_kernel(count, *refs):
    total = refs[0][...]
    for ref in refs[1:count]:
        total = total + ref[...]
    refs[count + (len(refs) - count - 1) // 2][...] = total


def total_between(parts, passed):
    count = len(parts)
    total, *passed = pl.pallas_call(
        functools.partial(total_kernel, count),
        out_shape=[shape(array.shape, array.dtype) for array in (parts[0], *passed)],
        in_specs=[VMEM] * count + [ANY] * len(passed),
        out_specs=[VMEM] + [ANY] * len(passed),
        input_output_aliases={count + n: 1 + n for n in range(len(passed))},
        compiler_params=params(4),
        cost_estimate=pl.CostEstimate(flops=parts[0].size, bytes_accessed=0, transcendentals=0),
        name="total",
    )(*parts, *passed)
    return total, passed


def exchange(axis, part):
    return [part] + [fetch(part, axis, slot) for slot in range(1, lax.axis_size(axis))]


def shards(q_proj, q_bias, k_proj, v_proj, v_bias, dout, lengths):
    _, tok, width = q_proj.shape
    kv_width = k_proj.shape[2]
    heads = width // HEAD_DIM
    kv_heads = kv_width // HEAD_DIM
    ctx = lax.axis_size("ctx")
    batches = lax.axis_size("dp")
    rows = ctx * tok
    columns = heads * tok
    pair = jnp.concatenate([k_proj[0], v_proj[0]], axis=1)
    pairs = [pair] + [fetch(pair, "ctx", slot) for slot in range(1, ctx)]
    prepared = pl.pallas_call(
        functools.partial(prepare_kernel, ctx),
        out_shape=[
            shape((kv_heads, HEAD_DIM), jnp.bfloat16),
            shape((columns, 2 * HEAD_DIM), jnp.bfloat16),
            shape((columns, HEAD_DIM), jnp.bfloat16),
            shape((tok, columns), jnp.float32),
            shape((tok, columns), jnp.float32),
            shape((rows, tok), jnp.float32),
        ],
        in_specs=[SMEM] + [VMEM] * 5,
        out_specs=[VMEM] * 6,
        compiler_params=params(16),
        cost_estimate=pl.CostEstimate(
            flops=4 * tok * tok * width, bytes_accessed=16 * tok * width, transcendentals=0
        ),
        name="prepare",
    )(
        lengths,
        pair,
        q_bias.reshape(heads, HEAD_DIM),
        v_bias.reshape(kv_heads, HEAD_DIM),
        q_proj[0],
        dout[0],
    )
    term = shape((tok, 2 * kv_width), jnp.bfloat16)
    probs, dscore, all_keys, all_values, sums, own, *terms = pl.pallas_call(
        functools.partial(attend_kernel, ctx),
        out_shape=[
            shape((rows, columns), jnp.bfloat16),
            shape((rows, columns), jnp.bfloat16),
            shape((rows, kv_width), jnp.bfloat16),
            shape((rows, kv_width), jnp.bfloat16),
            shape((heads + kv_heads, HEAD_DIM), jnp.float32),
            shape((tok, 2 * kv_width), jnp.float32),
        ]
        + [term] * (ctx - 1),
        in_specs=[VMEM] * (6 + ctx),
        out_specs=[VMEM] * (6 + ctx - 1),
        scratch_shapes=[
            pltpu.VMEM((rows, columns), jnp.float32),
            pltpu.VMEM((rows, columns), jnp.float32),
        ],
        compiler_params=params(24 if ctx < 8 else 48),
        cost_estimate=pl.CostEstimate(
            flops=8 * rows * tok * width,
            bytes_accessed=4 * rows * columns,
            transcendentals=rows * columns,
        ),
        name="attend",
    )(*prepared, *pairs)
    attn, q_grad = pl.pallas_call(
        finish_kernel,
        out_shape=[
            shape((tok, width), jnp.bfloat16),
            shape((tok, width), jnp.bfloat16),
        ],
        in_specs=[VMEM] * 4,
        out_specs=[VMEM] * 2,
        compiler_params=params(24),
        cost_estimate=pl.CostEstimate(
            flops=4 * rows * tok * width, bytes_accessed=4 * rows * columns, transcendentals=0
        ),
        name="finish",
    )(probs, dscore, all_keys, all_values)
    half = ctx // 2
    back = {slot: send_back(terms[slot - 1], slot) for slot in range(half, ctx)}
    sums, (back[half], *terms) = total_between(
        exchange("dp", sums), [back[half], *terms[: half - 1]]
    )
    back.update({slot: send_back(term, slot) for slot, term in enumerate(terms, 1)})
    back = [back[slot] for slot in sorted(back)]
    sums = exchange("ctx", sums)
    k_grad, v_grad, q_sum, v_sum = pl.pallas_call(
        functools.partial(collect_kernel, batches, len(sums), len(back)),
        out_shape=[
            shape((tok, kv_width), jnp.bfloat16),
            shape((tok, kv_width), jnp.bfloat16),
            shape((heads, HEAD_DIM), jnp.float32),
            shape((kv_heads, HEAD_DIM), jnp.float32),
        ],
        in_specs=[VMEM] * (len(sums) + 1 + len(back)),
        out_specs=[VMEM] * 4,
        compiler_params=params(8),
        cost_estimate=pl.CostEstimate(
            flops=8 * tok * kv_width, bytes_accessed=16 * tok * kv_width, transcendentals=0
        ),
        name="collect",
    )(*sums, own, *back)
    return (
        attn[None],
        q_grad[None],
        k_grad[None],
        v_grad[None],
        q_sum.reshape(width),
        v_sum.reshape(kv_width),
    )


def solution(mesh):
    tokens = P("dp", "ctx", "tp")
    return jax.shard_map(
        shards,
        mesh=mesh,
        in_specs=(tokens, P("tp"), tokens, tokens, P("tp"), tokens, P("dp", None)),
        out_specs=(tokens, tokens, tokens, tokens, P("tp"), P("tp")),
        check_vma=False,
    )
```

```python
import functools

import jax
import jax.numpy as jnp
from jax import lax
from jax.experimental import pallas as pl
from jax.experimental.pallas import tpu as pltpu
from jax.sharding import PartitionSpec as P

HEAD_DIM = 128
HEADS = 32
KV_HEADS = 4
GROUP = HEADS // KV_HEADS
PAIR = 2
BLOCK = 64
SCALE = HEAD_DIM ** (-0.5)
LOG2E = 1.4426950408889634
NEGATIVE = -1e30
VMEM = pl.BlockSpec(memory_space=pltpu.VMEM)
ANY = pl.BlockSpec(memory_space=pl.ANY)
SMEM = pl.BlockSpec(memory_space=pltpu.SMEM)


def dot(left, right, left_dim, right_dim):
    return lax.dot_general(
        left, right, (((left_dim,), (right_dim,)), ((), ())), preferred_element_type=jnp.float32
    )


def head_cols(head):
    return slice(head * HEAD_DIM, (head + 1) * HEAD_DIM)


def shape(dims, dtype):
    return jax.ShapeDtypeStruct(dims, dtype)


def params(mebibytes):
    return pltpu.CompilerParams(vmem_limit_bytes=mebibytes * 1024 * 1024)


def biased(values, bias):
    return (values.astype(jnp.float32) + bias.astype(jnp.float32)).astype(jnp.bfloat16)


def source_of(rank, slot, size):
    if size & (size - 1):
        return (rank + size - slot) % size
    return rank ^ slot


def slot_order(size):
    return [slot for slot in range(size) if slot != size // 2] + [size // 2]


def fetch(array, axis, slot):
    size = lax.axis_size(axis)
    return lax.ppermute(array, axis, [(source_of(i, slot, size), i) for i in range(size)])


def send_back(array, slot):
    size = lax.axis_size("ctx")
    return lax.ppermute(array, "ctx", [(i, source_of(i, slot, size)) for i in range(size)])


def prepare_kernel(
    slots, len_ref, pair_ref, qb_ref, vb_ref, q_ref, g_ref, bias_ref, queries_ref, grads_ref,
    score_ref, dprob_ref, live_ref,
):
    tok = q_ref.shape[0]
    kv_heads = vb_ref.shape[0]
    rank = lax.axis_index("ctx")
    query_pos = rank * tok + lax.broadcasted_iota(jnp.int32, (1, tok), 1)
    start = jnp.zeros((1, tok), jnp.int32)
    end = jnp.int32(0)
    for doc in range(len_ref.shape[1]):
        length = len_ref[0, doc]
        end = end + length
        start = start + jnp.where(query_pos >= end, length, 0)
    offsets = lax.broadcasted_iota(jnp.int32, (tok, tok), 0)
    for index, slot in enumerate(slot_order(slots)):
        key_pos = source_of(rank, slot, slots) * tok + offsets
        live = (key_pos >= start) & (key_pos <= query_pos)
        live_ref[index * tok : (index + 1) * tok, :] = jnp.where(live, 0.0, NEGATIVE)
    bias_ref[...] = vb_ref[...]
    column = lax.broadcasted_iota(jnp.int32, (tok, HEAD_DIM), 1)
    for kv_head in range(kv_heads):
        keys = pair_ref[:, head_cols(kv_head)]
        values = biased(pair_ref[:, head_cols(kv_heads + kv_head)], vb_ref[kv_head : kv_head + 1, :])
        for head in range(kv_head * GROUP, (kv_head + 1) * GROUP):
            at = slice(head * tok, (head + 1) * tok)
            queries_ref[at, :HEAD_DIM] = biased(q_ref[:, head_cols(head)], qb_ref[head : head + 1, :])
            queries_ref[at, HEAD_DIM:] = (column == head).astype(jnp.bfloat16)
            grads_ref[at, :] = g_ref[:, head_cols(head)]
        rows = slice(kv_head * GROUP * tok, (kv_head + 1) * GROUP * tok)
        score_ref[:, rows] = dot(keys, queries_ref[rows, :HEAD_DIM], 1, 1)
        dprob_ref[:, rows] = dot(values, grads_ref[rows, :], 1, 1)


def over_rows(array, reduce):
    return reduce(array.reshape(-1, 8, array.shape[-1]), axis=0)


def unpack(pair_ref, bias_ref, keys_ref, values_ref, rows):
    kv_heads = bias_ref.shape[0]
    keys_ref[rows, :] = pair_ref[:, : kv_heads * HEAD_DIM]
    for kv_head in range(kv_heads):
        values_ref[rows, head_cols(kv_head)] = biased(
            pair_ref[:, head_cols(kv_heads + kv_head)], bias_ref[kv_head : kv_head + 1, :]
        )


def near_kernel(
    bias_ref, queries_ref, grads_ref, score_ref, own_dprob_ref, live_ref, *refs
):
    pair_refs, (weights_ref, dprob_ref, stats_ref, keys_ref, values_ref) = refs[:-5], refs[-5:]
    tok = pair_refs[0].shape[0]
    for index, pair_ref in enumerate(pair_refs):
        unpack(pair_ref, bias_ref, keys_ref, values_ref, slice(index * tok, (index + 1) * tok))
    blocks = [slice(row, row + BLOCK) for row in range(0, len(pair_refs) * tok, BLOCK)]
    for kv_head in range(bias_ref.shape[0]):
        cols = head_cols(kv_head)
        group = slice(kv_head * GROUP * tok, (kv_head + 1) * GROUP * tok)
        weights_ref[tok:, group] = dot(keys_ref[tok:, cols], queries_ref[group, :HEAD_DIM], 1, 1)
        dprob_ref[tok:, group] = dot(values_ref[tok:, cols], grads_ref[group, :], 1, 1)
        for first in range(group.start, group.stop, PAIR * tok):
            at = slice(first, first + PAIR * tok)
            row_max = None
            for block in blocks:
                score = (score_ref if block.start < tok else weights_ref)[block, at]
                score = score + jnp.concatenate([live_ref[block, :]] * PAIR, axis=1)
                weights_ref[block, at] = score
                part = over_rows(score, jnp.max)
                row_max = part if row_max is None else jnp.maximum(row_max, part)
            row_max = jnp.max(row_max, axis=0, keepdims=True)
            total = jnp.zeros((8, PAIR * tok), jnp.float32)
            delta = jnp.zeros((8, PAIR * tok), jnp.float32)
            for block in blocks:
                dprob = (own_dprob_ref if block.start < tok else dprob_ref)[block, at]
                weights = jnp.exp2((weights_ref[block, at] - row_max) * (SCALE * LOG2E))
                weights_ref[block, at] = weights
                if block.start < tok:
                    dprob_ref[block, at] = dprob
                total = total + over_rows(weights, jnp.sum)
                delta = delta + over_rows(weights * dprob, jnp.sum)
            stats_ref[0:1, at] = row_max
            stats_ref[1:2, at] = jnp.sum(total, axis=0, keepdims=True)
            stats_ref[2:3, at] = jnp.sum(delta, axis=0, keepdims=True)


def last_kernel(slots, first_head, *refs):
    bias_ref, queries_ref, grads_ref, live_ref = refs[:4]
    weights_ref, dprob_ref, stats_ref, near_keys_ref, near_values_ref, pair_ref = refs[4:10]
    probs_ref, dscore_ref, keys_ref, values_ref, sums_ref, own_ref = refs[10:16]
    out_refs = refs[16 : 16 + slots - 1]
    last_weights_ref, last_dprob_ref = refs[16 + slots - 1 :]
    tok = pair_ref.shape[0]
    near = (slots - 1) * tok
    kv_heads = bias_ref.shape[0]
    kv_width = kv_heads * HEAD_DIM
    heads = kv_heads * GROUP
    keys_ref[:near, :] = near_keys_ref[...]
    values_ref[:near, :] = near_values_ref[...]
    unpack(pair_ref, bias_ref, keys_ref, values_ref, slice(near, near + tok))
    near_blocks = [slice(row, row + BLOCK) for row in range(0, near, BLOCK)]
    blocks = [slice(row, row + BLOCK) for row in range(0, tok, BLOCK)]
    for kv_head in range(kv_heads):
        cols = head_cols(kv_head)
        group = slice(kv_head * GROUP * tok, (kv_head + 1) * GROUP * tok)
        last_weights_ref[:, group] = dot(
            keys_ref[near:, cols], queries_ref[group, :HEAD_DIM], 1, 1
        )
        last_dprob_ref[:, group] = dot(values_ref[near:, cols], grads_ref[group, :], 1, 1)
        for first in range(group.start, group.stop, PAIR * tok):
            at = slice(first, first + PAIR * tok)
            near_max = stats_ref[0:1, at]
            row_max = jnp.broadcast_to(near_max, (8, PAIR * tok))
            for block in blocks:
                live = live_ref[near + block.start : near + block.stop, :]
                score = last_weights_ref[block, at] + jnp.concatenate([live] * PAIR, axis=1)
                last_weights_ref[block, at] = score
                row_max = jnp.maximum(row_max, over_rows(score, jnp.max))
            row_max = jnp.max(row_max, axis=0, keepdims=True)
            total = jnp.zeros((8, PAIR * tok), jnp.float32)
            delta = jnp.zeros((8, PAIR * tok), jnp.float32)
            for block in blocks:
                weights = jnp.exp2((last_weights_ref[block, at] - row_max) * (SCALE * LOG2E))
                last_weights_ref[block, at] = weights
                total = total + over_rows(weights, jnp.sum)
                delta = delta + over_rows(weights * last_dprob_ref[block, at], jnp.sum)
            factor = jnp.exp2((near_max - row_max) * (SCALE * LOG2E))
            total = jnp.sum(total, axis=0, keepdims=True) + stats_ref[1:2, at] * factor
            delta = jnp.sum(delta, axis=0, keepdims=True) + stats_ref[2:3, at] * factor
            inverse = 1.0 / total
            delta = delta * inverse
            factor = factor * inverse
            for block in near_blocks:
                probs = weights_ref[block, at] * factor
                probs_ref[block, at] = probs.astype(jnp.bfloat16)
                dscore_ref[block, at] = (probs * (dprob_ref[block, at] - delta)).astype(jnp.bfloat16)
            for block in blocks:
                to = slice(near + block.start, near + block.stop)
                probs = last_weights_ref[block, at] * inverse
                probs_ref[to, at] = probs.astype(jnp.bfloat16)
                dscore = probs * (last_dprob_ref[block, at] - delta)
                dscore_ref[to, at] = dscore.astype(jnp.bfloat16)
        value_term = dot(probs_ref[:, group], grads_ref[group, :], 1, 0)
        key_term = dot(dscore_ref[:, group], queries_ref[group, :], 1, 0)
        over_queries = key_term[:, HEAD_DIM:]
        key_term = key_term[:, :HEAD_DIM] * SCALE
        high = over_queries.astype(jnp.bfloat16)
        low = (over_queries - high.astype(jnp.float32)).astype(jnp.bfloat16)
        all_keys = keys_ref[:, cols]
        query_sums = (dot(high, all_keys, 0, 0) + dot(low, all_keys, 0, 0)) * SCALE
        of_group = slice(kv_head * GROUP, (kv_head + 1) * GROUP)
        sums_ref[of_group, :] = query_sums[first_head + of_group.start : first_head + of_group.stop]
        sums_ref[heads + kv_head : heads + kv_head + 1, :] = jnp.sum(
            value_term, axis=0, keepdims=True
        )
        value_cols = head_cols(kv_heads + kv_head)
        own_ref[:, cols] = key_term[:tok]
        own_ref[:, value_cols] = value_term[:tok]
        for index, slot in enumerate(slot_order(slots)):
            if slot == 0:
                continue
            rows = slice(index * tok, (index + 1) * tok)
            out_refs[slot - 1][:, cols] = key_term[rows].astype(jnp.bfloat16)
            out_refs[slot - 1][:, value_cols] = value_term[rows].astype(jnp.bfloat16)


def finish_kernel(probs_ref, dscore_ref, keys_ref, values_ref, _, attn_ref, qg_ref, __):
    tok = attn_ref.shape[0]
    kv_heads = keys_ref.shape[1] // HEAD_DIM
    for kv_head in range(kv_heads):
        cols = head_cols(kv_head)
        keys_t = keys_ref[:, cols].T
        values_t = values_ref[:, cols].T
        for pair in range(GROUP // PAIR):
            first = kv_head * GROUP + pair * PAIR
            at = slice(first * tok, (first + PAIR) * tok)
            attn = dot(values_t, probs_ref[:, at], 1, 0).T
            query_grad = (dot(keys_t, dscore_ref[:, at], 1, 0) * SCALE).T
            for n in range(PAIR):
                head = first + n
                rows = slice(n * tok, (n + 1) * tok)
                attn_ref[:, head_cols(head)] = attn[rows].astype(jnp.bfloat16)
                qg_ref[:, head_cols(head)] = query_grad[rows].astype(jnp.bfloat16)


def collect_kernel(batches, messages, *refs):
    sum_refs, refs = refs[:2], refs[2:]
    own_ref, early_ref, refs = refs[0], refs[1], refs[2:]
    message_refs, (kg_ref, vg_ref, qb_ref, vb_ref) = refs[:messages], refs[messages:]
    heads, kv_heads = qb_ref.shape[0], vb_ref.shape[0]
    tok, kv_width = kg_ref.shape
    total = sum_refs[0][...] + sum_refs[1][...]
    term = own_ref[...] + early_ref[...].astype(jnp.float32)
    for ref in message_refs:
        sums = ref[tok:, :].astype(jnp.float32)
        sums = sums[:, :HEAD_DIM] + sums[:, HEAD_DIM : 2 * HEAD_DIM]
        total = total + sums[: heads + kv_heads]
        term = term + ref[:tok, :].astype(jnp.float32)
    total = total * (1.0 / batches)
    qb_ref[...] = total[:heads]
    vb_ref[...] = total[heads:]
    term = term.astype(jnp.bfloat16)
    kg_ref[...] = term[:, :kv_width]
    vg_ref[...] = term[:, kv_width:]


def total_kernel(count, *refs):
    parts, refs = refs[:count], refs[count:]
    sent = (len(refs) - 1) // 2
    term_refs, total_ref, message_refs = refs[:sent], refs[sent], refs[sent + 1 :]
    total = parts[0][...]
    for ref in parts[1:]:
        total = total + ref[...]
    total_ref[...] = total
    for term_ref, message_ref in zip(term_refs, message_refs):
        tok = term_ref.shape[0]
        rows = message_ref.shape[0] - tok
        high = jnp.concatenate([total, jnp.zeros((rows - total.shape[0], HEAD_DIM), jnp.float32)])
        message_ref[:tok, :] = term_ref[...]
        message_ref[tok:, :] = jnp.zeros((rows, term_ref.shape[1]), jnp.bfloat16)
        message_ref[tok:, :HEAD_DIM] = high.astype(jnp.bfloat16)
        low = high - high.astype(jnp.bfloat16).astype(jnp.float32)
        message_ref[tok:, HEAD_DIM : 2 * HEAD_DIM] = low.astype(jnp.bfloat16)


def total_with(parts, terms):
    rows = -(-parts[0].shape[0] // 16) * 16
    total, *messages = pl.pallas_call(
        functools.partial(total_kernel, len(parts)),
        out_shape=[shape(parts[0].shape, parts[0].dtype)]
        + [shape((term.shape[0] + rows, term.shape[1]), term.dtype) for term in terms],
        in_specs=[VMEM] * (len(parts) + len(terms)),
        out_specs=[VMEM] * (1 + len(terms)),
        compiler_params=params(8),
        cost_estimate=pl.CostEstimate(flops=parts[0].size, bytes_accessed=0, transcendentals=0),
        name="total",
    )(*parts, *terms)
    return total, messages


def exchange(axis, part):
    return [part] + [fetch(part, axis, slot) for slot in range(1, lax.axis_size(axis))]


def attend(first_head, bias, queries, grads, score, own_dprob, live, pairs):
    ctx = len(pairs)
    tok = pairs[0].shape[0]
    kv_width = bias.shape[0] * HEAD_DIM
    columns = queries.shape[0]
    rows = ctx * tok
    near = rows - tok
    near_slots = slot_order(ctx)[:-1]
    weights, dprob, stats, near_keys, near_values = pl.pallas_call(
        near_kernel,
        out_shape=[
            shape((near, columns), jnp.float32),
            shape((near, columns), jnp.float32),
            shape((8, columns), jnp.float32),
            shape((near, kv_width), jnp.bfloat16),
            shape((near, kv_width), jnp.bfloat16),
        ],
        in_specs=[VMEM] * (6 + len(near_slots)),
        out_specs=[VMEM] * 5,
        compiler_params=params(20 if ctx < 8 else 48),
        cost_estimate=pl.CostEstimate(
            flops=4 * near * columns * HEAD_DIM,
            bytes_accessed=8 * near * columns,
            transcendentals=near * columns,
        ),
        name="near",
    )(bias, queries, grads, score, own_dprob, live, *[pairs[slot] for slot in near_slots])
    term = shape((tok, 2 * kv_width), jnp.bfloat16)
    return pl.pallas_call(
        functools.partial(last_kernel, ctx, first_head),
        out_shape=[
            shape((rows, columns), jnp.bfloat16),
            shape((rows, columns), jnp.bfloat16),
            shape((rows, kv_width), jnp.bfloat16),
            shape((rows, kv_width), jnp.bfloat16),
            shape((bias.shape[0] * (GROUP + 1), HEAD_DIM), jnp.float32),
            shape((tok, 2 * kv_width), jnp.float32),
        ]
        + [term] * (ctx - 1),
        in_specs=[VMEM] * 10,
        out_specs=[VMEM] * (6 + ctx - 1),
        scratch_shapes=[pltpu.VMEM((tok, columns), jnp.float32)] * 2,
        compiler_params=params(24 if ctx < 8 else 48),
        cost_estimate=pl.CostEstimate(
            flops=4 * rows * columns * HEAD_DIM,
            bytes_accessed=4 * rows * columns,
            transcendentals=tok * columns,
        ),
        name="last",
    )(bias, queries, grads, live, weights, dprob, stats, near_keys, near_values, pairs[ctx // 2])


def joined(place, parts):
    if place < 4:
        return jnp.concatenate(parts, axis=1)
    cut, axis = (GROUP, 0) if place == 4 else (HEAD_DIM, 1)
    pieces = [jnp.split(part, [cut], axis=axis) for part in parts]
    return jnp.concatenate([piece[n] for n in range(2) for piece in pieces], axis=axis)


def shards(q_proj, q_bias, k_proj, v_proj, v_bias, dout, lengths):
    _, tok, width = q_proj.shape
    kv_width = k_proj.shape[2]
    heads = width // HEAD_DIM
    kv_heads = kv_width // HEAD_DIM
    ctx = lax.axis_size("ctx")
    batches = lax.axis_size("dp")
    rows = ctx * tok
    columns = heads * tok
    pair = jnp.concatenate([k_proj[0], v_proj[0]], axis=1)
    pairs = [pair] + [fetch(pair, "ctx", slot) for slot in range(1, ctx)]
    prepared = pl.pallas_call(
        functools.partial(prepare_kernel, ctx),
        out_shape=[
            shape((kv_heads, HEAD_DIM), jnp.bfloat16),
            shape((columns, 2 * HEAD_DIM), jnp.bfloat16),
            shape((columns, HEAD_DIM), jnp.bfloat16),
            shape((tok, columns), jnp.float32),
            shape((tok, columns), jnp.float32),
            shape((rows, tok), jnp.float32),
        ],
        in_specs=[SMEM] + [VMEM] * 5,
        out_specs=[VMEM] * 6,
        compiler_params=params(16),
        cost_estimate=pl.CostEstimate(
            flops=4 * tok * tok * width, bytes_accessed=16 * tok * width, transcendentals=0
        ),
        name="prepare",
    )(
        lengths,
        pair,
        q_bias.reshape(heads, HEAD_DIM),
        v_bias.reshape(kv_heads, HEAD_DIM),
        q_proj[0],
        dout[0],
    )
    bias, queries, grads, score, own_dprob, live = prepared
    if ctx < 8:
        made = attend(0, bias, queries, grads, score, own_dprob, live, pairs)
    else:
        made = [
            attend(
                kv_head * GROUP,
                bias[kv_head : kv_head + 1],
                *(part[at] for part in (queries, grads)),
                *(part[:, at] for part in (score, own_dprob)),
                live,
                [
                    jnp.concatenate(
                        [part[:, head_cols(kv_head)], part[:, head_cols(kv_heads + kv_head)]], axis=1
                    )
                    for part in pairs
                ],
            )
            for kv_head in range(kv_heads)
            for at in [slice(kv_head * GROUP * tok, (kv_head + 1) * GROUP * tok)]
        ]
        made = [joined(n, parts) for n, parts in enumerate(zip(*made))]
    probs, dscore, all_keys, all_values, sums, own, *terms = made
    term = shape((tok, 2 * kv_width), jnp.bfloat16)
    half = ctx // 2
    early = send_back(terms.pop(half - 1), half)
    attn, q_grad, early = pl.pallas_call(
        finish_kernel,
        out_shape=[
            shape((tok, width), jnp.bfloat16),
            shape((tok, width), jnp.bfloat16),
            shape(early.shape, early.dtype),
        ],
        in_specs=[VMEM] * 4 + [ANY],
        out_specs=[VMEM] * 2 + [ANY],
        input_output_aliases={4: 2},
        compiler_params=params(24),
        cost_estimate=pl.CostEstimate(
            flops=4 * rows * tok * width, bytes_accessed=4 * rows * columns, transcendentals=0
        ),
        name="finish",
    )(probs, dscore, all_keys, all_values, early)
    sums, messages = total_with(exchange("dp", sums), terms)
    slots = [slot for slot in range(1, ctx) if slot != half]
    back = [send_back(message, slot) for slot, message in zip(slots, messages)][::-1]
    sums = [sums, send_back(sums, half)]
    k_grad, v_grad, q_sum, v_sum = pl.pallas_call(
        functools.partial(collect_kernel, batches, len(back)),
        out_shape=[
            shape((tok, kv_width), jnp.bfloat16),
            shape((tok, kv_width), jnp.bfloat16),
            shape((heads, HEAD_DIM), jnp.float32),
            shape((kv_heads, HEAD_DIM), jnp.float32),
        ],
        in_specs=[VMEM] * (4 + len(back)),
        out_specs=[VMEM] * 4,
        compiler_params=params(8),
        cost_estimate=pl.CostEstimate(
            flops=8 * tok * kv_width, bytes_accessed=16 * tok * kv_width, transcendentals=0
        ),
        name="collect",
    )(*sums, own, early, *back)
    return (
        attn[None],
        q_grad[None],
        k_grad[None],
        v_grad[None],
        q_sum.reshape(width),
        v_sum.reshape(kv_width),
    )


def solution(mesh):
    tokens = P("dp", "ctx", "tp")
    return jax.shard_map(
        shards,
        mesh=mesh,
        in_specs=(tokens, P("tp"), tokens, tokens, P("tp"), tokens, P("dp", None)),
        out_specs=(tokens, tokens, tokens, tokens, P("tp"), P("tp")),
        check_vma=False,
    )
```

```python
import functools

import jax
import jax.numpy as jnp
from jax import lax
from jax.experimental import pallas as pl
from jax.experimental.pallas import tpu as pltpu
from jax.sharding import PartitionSpec as P

HEAD_DIM = 128
HEADS = 32
KV_HEADS = 4
GROUP = HEADS // KV_HEADS
PAIR = 2
BLOCK = 64
SCALE = HEAD_DIM ** (-0.5)
LOG2E = 1.4426950408889634
NEGATIVE = -1e30
VMEM = pl.BlockSpec(memory_space=pltpu.VMEM)
HBM = pl.BlockSpec(memory_space=pltpu.HBM)
ANY = pl.BlockSpec(memory_space=pl.ANY)
SMEM = pl.BlockSpec(memory_space=pltpu.SMEM)


def dot(left, right, left_dim, right_dim):
    return lax.dot_general(
        left, right, (((left_dim,), (right_dim,)), ((), ())), preferred_element_type=jnp.float32
    )


def head_cols(head):
    return slice(head * HEAD_DIM, (head + 1) * HEAD_DIM)


def shape(dims, dtype):
    return jax.ShapeDtypeStruct(dims, dtype)


def params(mebibytes):
    return pltpu.CompilerParams(vmem_limit_bytes=mebibytes * 1024 * 1024)


def biased(values, bias):
    return (values.astype(jnp.float32) + bias.astype(jnp.float32)).astype(jnp.bfloat16)


def source_of(rank, slot, size):
    if size & (size - 1):
        return (rank + size - slot) % size
    return rank ^ slot


def slot_order(size):
    return [slot for slot in range(size) if slot != size // 2] + [size // 2]


def fetch(array, axis, slot):
    size = lax.axis_size(axis)
    return lax.ppermute(array, axis, [(source_of(i, slot, size), i) for i in range(size)])


def send_back(array, slot):
    size = lax.axis_size("ctx")
    return lax.ppermute(array, "ctx", [(i, source_of(i, slot, size)) for i in range(size)])


def pack_kernel(k_ref, v_ref, pair_ref, sems):
    kv_width = k_ref.shape[1]
    copies = [
        pltpu.make_async_copy(
            part_ref, pair_ref.at[:, pl.ds(n * kv_width, kv_width)], sems.at[n]
        )
        for n, part_ref in enumerate([k_ref, v_ref])
    ]
    for copy in copies:
        copy.start()
    for copy in copies:
        copy.wait()


def prepare_kernel(
    slots, len_ref, pair_ref, qb_ref, vb_ref, q_ref, g_ref, bias_ref, queries_ref, grads_ref,
    score_ref, dprob_ref, live_ref,
):
    tok = q_ref.shape[0]
    kv_heads = vb_ref.shape[0]
    rank = lax.axis_index("ctx")
    query_pos = rank * tok + lax.broadcasted_iota(jnp.int32, (1, tok), 1)
    start = jnp.zeros((1, tok), jnp.int32)
    end = jnp.int32(0)
    for doc in range(len_ref.shape[1]):
        length = len_ref[0, doc]
        end = end + length
        start = start + jnp.where(query_pos >= end, length, 0)
    offsets = lax.broadcasted_iota(jnp.int32, (tok, tok), 0)
    for index, slot in enumerate(slot_order(slots)):
        key_pos = source_of(rank, slot, slots) * tok + offsets
        live = (key_pos >= start) & (key_pos <= query_pos)
        live_ref[index * tok : (index + 1) * tok, :] = jnp.where(live, 0.0, NEGATIVE)
    bias_ref[...] = vb_ref[...]
    column = lax.broadcasted_iota(jnp.int32, (tok, HEAD_DIM), 1)
    for kv_head in range(kv_heads):
        keys = pair_ref[:, head_cols(kv_head)]
        values = biased(pair_ref[:, head_cols(kv_heads + kv_head)], vb_ref[kv_head : kv_head + 1, :])
        for head in range(kv_head * GROUP, (kv_head + 1) * GROUP):
            at = slice(head * tok, (head + 1) * tok)
            queries_ref[at, :HEAD_DIM] = biased(q_ref[:, head_cols(head)], qb_ref[head : head + 1, :])
            queries_ref[at, HEAD_DIM:] = (column == head).astype(jnp.bfloat16)
            grads_ref[at, :] = g_ref[:, head_cols(head)]
        rows = slice(kv_head * GROUP * tok, (kv_head + 1) * GROUP * tok)
        score_ref[:, rows] = dot(keys, queries_ref[rows, :HEAD_DIM], 1, 1)
        dprob_ref[:, rows] = dot(values, grads_ref[rows, :], 1, 1)


def over_rows(array, reduce):
    return reduce(array.reshape(-1, 8, array.shape[-1]), axis=0)


def unpack(pair_ref, bias_ref, keys_ref, values_ref, rows):
    kv_heads = bias_ref.shape[0]
    keys_ref[rows, :] = pair_ref[:, : kv_heads * HEAD_DIM]
    for kv_head in range(kv_heads):
        values_ref[rows, head_cols(kv_head)] = biased(
            pair_ref[:, head_cols(kv_heads + kv_head)], bias_ref[kv_head : kv_head + 1, :]
        )


def near_kernel(
    bias_ref, queries_ref, grads_ref, score_ref, own_dprob_ref, live_ref, *refs
):
    pair_refs, (weights_ref, dprob_ref, stats_ref, keys_ref, values_ref) = refs[:-5], refs[-5:]
    tok = pair_refs[0].shape[0]
    for index, pair_ref in enumerate(pair_refs):
        unpack(pair_ref, bias_ref, keys_ref, values_ref, slice(index * tok, (index + 1) * tok))
    blocks = [slice(row, row + BLOCK) for row in range(0, len(pair_refs) * tok, BLOCK)]
    for kv_head in range(bias_ref.shape[0]):
        cols = head_cols(kv_head)
        group = slice(kv_head * GROUP * tok, (kv_head + 1) * GROUP * tok)
        weights_ref[tok:, group] = dot(keys_ref[tok:, cols], queries_ref[group, :HEAD_DIM], 1, 1)
        dprob_ref[tok:, group] = dot(values_ref[tok:, cols], grads_ref[group, :], 1, 1)
        for first in range(group.start, group.stop, PAIR * tok):
            at = slice(first, first + PAIR * tok)
            row_max = None
            for block in blocks:
                score = (score_ref if block.start < tok else weights_ref)[block, at]
                score = score + jnp.concatenate([live_ref[block, :]] * PAIR, axis=1)
                weights_ref[block, at] = score
                part = over_rows(score, jnp.max)
                row_max = part if row_max is None else jnp.maximum(row_max, part)
            row_max = jnp.max(row_max, axis=0, keepdims=True)
            total = jnp.zeros((8, PAIR * tok), jnp.float32)
            delta = jnp.zeros((8, PAIR * tok), jnp.float32)
            for block in blocks:
                dprob = (own_dprob_ref if block.start < tok else dprob_ref)[block, at]
                weights = jnp.exp2((weights_ref[block, at] - row_max) * (SCALE * LOG2E))
                weights_ref[block, at] = weights
                if block.start < tok:
                    dprob_ref[block, at] = dprob
                total = total + over_rows(weights, jnp.sum)
                delta = delta + over_rows(weights * dprob, jnp.sum)
            stats_ref[0:1, at] = row_max
            stats_ref[1:2, at] = jnp.sum(total, axis=0, keepdims=True)
            stats_ref[2:3, at] = jnp.sum(delta, axis=0, keepdims=True)


def last_kernel(slots, first_head, *refs):
    bias_ref, queries_ref, grads_ref, live_ref = refs[:4]
    weights_ref, dprob_ref, stats_ref, near_keys_ref, near_values_ref, pair_ref = refs[4:10]
    probs_ref, dscore_ref, keys_ref, values_ref, sums_ref, own_ref = refs[10:16]
    out_refs, (last_weights_ref, last_dprob_ref) = refs[16:-2], refs[-2:]
    tok = pair_ref.shape[0]
    near = (slots - 1) * tok
    kv_heads = bias_ref.shape[0]
    kv_width = kv_heads * HEAD_DIM
    heads = kv_heads * GROUP
    keys_ref[:near, :] = near_keys_ref[...]
    values_ref[:near, :] = near_values_ref[...]
    unpack(pair_ref, bias_ref, keys_ref, values_ref, slice(near, near + tok))
    near_blocks = [slice(row, row + BLOCK) for row in range(0, near, BLOCK)]
    blocks = [slice(row, row + BLOCK) for row in range(0, tok, BLOCK)]
    for kv_head in range(kv_heads):
        cols = head_cols(kv_head)
        group = slice(kv_head * GROUP * tok, (kv_head + 1) * GROUP * tok)
        last_weights_ref[:, group] = dot(
            keys_ref[near:, cols], queries_ref[group, :HEAD_DIM], 1, 1
        )
        last_dprob_ref[:, group] = dot(values_ref[near:, cols], grads_ref[group, :], 1, 1)
        for first in range(group.start, group.stop, PAIR * tok):
            at = slice(first, first + PAIR * tok)
            near_max = stats_ref[0:1, at]
            row_max = jnp.broadcast_to(near_max, (8, PAIR * tok))
            for block in blocks:
                live = live_ref[near + block.start : near + block.stop, :]
                score = last_weights_ref[block, at] + jnp.concatenate([live] * PAIR, axis=1)
                last_weights_ref[block, at] = score
                row_max = jnp.maximum(row_max, over_rows(score, jnp.max))
            row_max = jnp.max(row_max, axis=0, keepdims=True)
            total = jnp.zeros((8, PAIR * tok), jnp.float32)
            delta = jnp.zeros((8, PAIR * tok), jnp.float32)
            for block in blocks:
                weights = jnp.exp2((last_weights_ref[block, at] - row_max) * (SCALE * LOG2E))
                last_weights_ref[block, at] = weights
                total = total + over_rows(weights, jnp.sum)
                delta = delta + over_rows(weights * last_dprob_ref[block, at], jnp.sum)
            factor = jnp.exp2((near_max - row_max) * (SCALE * LOG2E))
            total = jnp.sum(total, axis=0, keepdims=True) + stats_ref[1:2, at] * factor
            delta = jnp.sum(delta, axis=0, keepdims=True) + stats_ref[2:3, at] * factor
            inverse = 1.0 / total
            delta = delta * inverse
            factor = factor * inverse
            for block in near_blocks:
                probs = weights_ref[block, at] * factor
                probs_ref[block, at] = probs.astype(jnp.bfloat16)
                dscore_ref[block, at] = (probs * (dprob_ref[block, at] - delta)).astype(jnp.bfloat16)
            for block in blocks:
                to = slice(near + block.start, near + block.stop)
                probs = last_weights_ref[block, at] * inverse
                probs_ref[to, at] = probs.astype(jnp.bfloat16)
                dscore = probs * (last_dprob_ref[block, at] - delta)
                dscore_ref[to, at] = dscore.astype(jnp.bfloat16)
        value_term = dot(probs_ref[:, group], grads_ref[group, :], 1, 0)
        key_term = dot(dscore_ref[:, group], queries_ref[group, :], 1, 0)
        over_queries = key_term[:, HEAD_DIM:]
        key_term = key_term[:, :HEAD_DIM] * SCALE
        high = over_queries.astype(jnp.bfloat16)
        low = (over_queries - high.astype(jnp.float32)).astype(jnp.bfloat16)
        all_keys = keys_ref[:, cols]
        query_sums = (dot(high, all_keys, 0, 0) + dot(low, all_keys, 0, 0)) * SCALE
        of_group = slice(kv_head * GROUP, (kv_head + 1) * GROUP)
        sums_ref[of_group, :] = query_sums[first_head + of_group.start : first_head + of_group.stop]
        sums_ref[heads + kv_head : heads + kv_head + 1, :] = jnp.sum(
            value_term, axis=0, keepdims=True
        )
        value_cols = head_cols(kv_heads + kv_head)
        own_ref[:, cols] = key_term[:tok]
        own_ref[:, value_cols] = value_term[:tok]
        for index, slot in enumerate(slot_order(slots)):
            rows = slice(index * tok, (index + 1) * tok)
            if slot:
                out_refs[slot - 1][:, cols] = key_term[rows].astype(jnp.bfloat16)
                out_refs[slot - 1][:, value_cols] = value_term[rows].astype(jnp.bfloat16)


def finish_kernel(probs_ref, dscore_ref, keys_ref, values_ref, *refs):
    passed = (len(refs) - 2) // 2
    attn_ref, qg_ref = refs[passed : passed + 2]
    tok = attn_ref.shape[0]
    kv_heads = keys_ref.shape[1] // HEAD_DIM
    for kv_head in range(kv_heads):
        cols = head_cols(kv_head)
        keys_t = keys_ref[:, cols].T
        values_t = values_ref[:, cols].T
        for pair in range(GROUP // PAIR):
            first = kv_head * GROUP + pair * PAIR
            at = slice(first * tok, (first + PAIR) * tok)
            attn = dot(values_t, probs_ref[:, at], 1, 0).T
            query_grad = (dot(keys_t, dscore_ref[:, at], 1, 0) * SCALE).T
            for n in range(PAIR):
                head = first + n
                rows = slice(n * tok, (n + 1) * tok)
                attn_ref[:, head_cols(head)] = attn[rows].astype(jnp.bfloat16)
                qg_ref[:, head_cols(head)] = query_grad[rows].astype(jnp.bfloat16)


def collect_kernel(batches, parts, whole, *refs):
    sum_refs, own_ref, refs = refs[:parts], refs[parts], refs[parts + 1 :]
    whole_refs, message_refs, (kg_ref, vg_ref, qb_ref, vb_ref) = (
        refs[:whole],
        refs[whole:-4],
        refs[-4:],
    )
    heads, kv_heads = qb_ref.shape[0], vb_ref.shape[0]
    tok, kv_width = kg_ref.shape
    total = sum_refs[0][...]
    for ref in sum_refs[1:]:
        total = total + ref[...]
    query_sums, value_sums = total[:heads], total[heads:]
    term = own_ref[...]
    for ref in whole_refs:
        term = term + ref[...].astype(jnp.float32)
    for ref in message_refs:
        added = ref[tok:, :].astype(jnp.float32)
        high_and_low = added[:, : 2 * HEAD_DIM], added[:, 2 * HEAD_DIM : 4 * HEAD_DIM]
        of_queries, of_values = (both[:, :HEAD_DIM] + both[:, HEAD_DIM:] for both in high_and_low)
        query_sums = query_sums + of_queries[:heads]
        value_sums = value_sums + of_values[:kv_heads]
        term = term + ref[:tok, :].astype(jnp.float32)
    qb_ref[...] = query_sums * (1.0 / batches)
    vb_ref[...] = value_sums * (1.0 / batches)
    term = term.astype(jnp.bfloat16)
    kg_ref[...] = term[:, :kv_width]
    vg_ref[...] = term[:, kv_width:]


def total_kernel(count, *refs):
    parts, refs = refs[:count], refs[count:]
    sent = (len(refs) - 1) // 2
    term_refs, total_ref, message_refs = refs[:sent], refs[sent], refs[sent + 1 :]
    total = parts[0][...]
    for ref in parts[1:]:
        total = total + ref[...]
    total_ref[...] = total
    for term_ref, message_ref in zip(term_refs, message_refs):
        tok = term_ref.shape[0]
        kv_heads = term_ref.shape[1] // (2 * HEAD_DIM)
        rows = message_ref.shape[0] - tok
        message_ref[:tok, :] = term_ref[...]
        message_ref[tok:, : 4 * HEAD_DIM] = added_rows(total, total.shape[0] - kv_heads, rows)


def added_rows(total, heads, rows):
    high = total.astype(jnp.bfloat16).astype(jnp.float32)
    both = jnp.concatenate([high, total - high], axis=1)
    blocks = [both[:heads], both[heads:]]
    blocks = [
        jnp.concatenate([block, jnp.zeros((rows - block.shape[0], 2 * HEAD_DIM), jnp.float32)])
        if block.shape[0] < rows
        else block
        for block in blocks
    ]
    return jnp.concatenate(blocks, axis=1).astype(jnp.bfloat16)


def total_with(parts, terms):
    rows = -(-parts[0].shape[0] * GROUP // (GROUP + 1) // 16) * 16
    total, *messages = pl.pallas_call(
        functools.partial(total_kernel, len(parts)),
        out_shape=[shape(parts[0].shape, parts[0].dtype)]
        + [shape((term.shape[0] + rows, term.shape[1]), term.dtype) for term in terms],
        in_specs=[VMEM] * (len(parts) + len(terms)),
        out_specs=[VMEM] * (1 + len(terms)),
        compiler_params=params(8),
        cost_estimate=pl.CostEstimate(flops=parts[0].size, bytes_accessed=0, transcendentals=0),
        name="total",
    )(*parts, *terms)
    return total, messages


def exchange(axis, part):
    return [part] + [fetch(part, axis, slot) for slot in range(1, lax.axis_size(axis))]


def attend(first_head, bias, queries, grads, score, own_dprob, live, pairs):
    ctx = len(pairs)
    tok = pairs[0].shape[0]
    kv_width = bias.shape[0] * HEAD_DIM
    columns = queries.shape[0]
    rows = ctx * tok
    near = rows - tok
    near_slots = slot_order(ctx)[:-1]
    weights, dprob, stats, near_keys, near_values = pl.pallas_call(
        near_kernel,
        out_shape=[
            shape((near, columns), jnp.float32),
            shape((near, columns), jnp.float32),
            shape((8, columns), jnp.float32),
            shape((near, kv_width), jnp.bfloat16),
            shape((near, kv_width), jnp.bfloat16),
        ],
        in_specs=[VMEM] * (6 + len(near_slots)),
        out_specs=[VMEM] * 5,
        compiler_params=params(20 if ctx < 8 else 48),
        cost_estimate=pl.CostEstimate(
            flops=4 * near * columns * HEAD_DIM,
            bytes_accessed=8 * near * columns,
            transcendentals=near * columns,
        ),
        name="near",
    )(bias, queries, grads, score, own_dprob, live, *[pairs[slot] for slot in near_slots])
    terms = [shape((tok, 2 * kv_width), jnp.bfloat16)] * (ctx - 1)
    return pl.pallas_call(
        functools.partial(last_kernel, ctx, first_head),
        out_shape=[
            shape((rows, columns), jnp.bfloat16),
            shape((rows, columns), jnp.bfloat16),
            shape((rows, kv_width), jnp.bfloat16),
            shape((rows, kv_width), jnp.bfloat16),
            shape((bias.shape[0] * (GROUP + 1), HEAD_DIM), jnp.float32),
            shape((tok, 2 * kv_width), jnp.float32),
        ]
        + terms,
        in_specs=[VMEM] * 10,
        out_specs=[VMEM] * (6 + len(terms)),
        scratch_shapes=[pltpu.VMEM((tok, columns), jnp.float32)] * 2,
        compiler_params=params(24 if ctx < 8 else 48),
        cost_estimate=pl.CostEstimate(
            flops=4 * rows * columns * HEAD_DIM,
            bytes_accessed=4 * rows * columns,
            transcendentals=tok * columns,
        ),
        name="last",
    )(bias, queries, grads, live, weights, dprob, stats, near_keys, near_values, pairs[ctx // 2])


def joined(place, parts):
    if place < 4:
        return jnp.concatenate(parts, axis=1)
    cut, axis = (GROUP, 0) if place == 4 else (HEAD_DIM, 1)
    pieces = [jnp.split(part, [cut], axis=axis) for part in parts]
    return jnp.concatenate([piece[n] for n in range(2) for piece in pieces], axis=axis)


def shards(q_proj, q_bias, k_proj, v_proj, v_bias, dout, lengths):
    _, tok, width = q_proj.shape
    kv_width = k_proj.shape[2]
    heads = width // HEAD_DIM
    kv_heads = kv_width // HEAD_DIM
    ctx = lax.axis_size("ctx")
    batches = lax.axis_size("dp")
    rows = ctx * tok
    columns = heads * tok
    pair = pl.pallas_call(
        pack_kernel,
        out_shape=shape((tok, 2 * kv_width), jnp.bfloat16),
        in_specs=[HBM] * 2,
        out_specs=VMEM,
        scratch_shapes=[pltpu.SemaphoreType.DMA((2,))],
        compiler_params=params(2),
        cost_estimate=pl.CostEstimate(
            flops=0, bytes_accessed=8 * tok * kv_width, transcendentals=0
        ),
        name="pack",
    )(*[pltpu.with_memory_space_constraint(part[0], pltpu.HBM) for part in (k_proj, v_proj)])
    pairs = [pair] + [fetch(pair, "ctx", slot) for slot in range(1, ctx)]
    prepared = pl.pallas_call(
        functools.partial(prepare_kernel, ctx),
        out_shape=[
            shape((kv_heads, HEAD_DIM), jnp.bfloat16),
            shape((columns, 2 * HEAD_DIM), jnp.bfloat16),
            shape((columns, HEAD_DIM), jnp.bfloat16),
            shape((tok, columns), jnp.float32),
            shape((tok, columns), jnp.float32),
            shape((rows, tok), jnp.float32),
        ],
        in_specs=[SMEM] + [VMEM] * 5,
        out_specs=[VMEM] * 6,
        compiler_params=params(16),
        cost_estimate=pl.CostEstimate(
            flops=4 * tok * tok * width, bytes_accessed=16 * tok * width, transcendentals=0
        ),
        name="prepare",
    )(
        lengths,
        pair,
        q_bias.reshape(heads, HEAD_DIM),
        v_bias.reshape(kv_heads, HEAD_DIM),
        q_proj[0],
        dout[0],
    )
    bias, queries, grads, score, own_dprob, live = prepared
    if ctx < 8:
        made = attend(0, bias, queries, grads, score, own_dprob, live, pairs)
    else:
        made = [
            attend(
                kv_head * GROUP,
                bias[kv_head : kv_head + 1],
                *(part[at] for part in (queries, grads)),
                *(part[:, at] for part in (score, own_dprob)),
                live,
                [
                    jnp.concatenate(
                        [part[:, head_cols(kv_head)], part[:, head_cols(kv_heads + kv_head)]], axis=1
                    )
                    for part in pairs
                ],
            )
            for kv_head in range(kv_heads)
            for at in [slice(kv_head * GROUP * tok, (kv_head + 1) * GROUP * tok)]
        ]
        made = [joined(n, parts) for n, parts in enumerate(zip(*made))]
    probs, dscore, all_keys, all_values, sums, own, *terms = made
    half = ctx // 2
    far = range(half, ctx)
    early = [send_back(terms[slot - 1], slot) for slot in far]
    attn, q_grad, *early = pl.pallas_call(
        finish_kernel,
        out_shape=[
            shape((tok, width), jnp.bfloat16),
            shape((tok, width), jnp.bfloat16),
        ]
        + [shape(part.shape, part.dtype) for part in early],
        in_specs=[VMEM] * 4 + [ANY] * len(early),
        out_specs=[VMEM] * 2 + [ANY] * len(early),
        input_output_aliases={4 + n: 2 + n for n in range(len(early))},
        compiler_params=params(24),
        cost_estimate=pl.CostEstimate(
            flops=4 * rows * tok * width, bytes_accessed=4 * rows * columns, transcendentals=0
        ),
        name="finish",
    )(probs, dscore, all_keys, all_values, *early)
    sums, messages = total_with(exchange("dp", sums), terms[: half - 1])
    late = [send_back(message, slot) for slot, message in enumerate(messages, 1)]
    sums = [sums] + [send_back(sums, slot) for slot in far]
    k_grad, v_grad, q_sum, v_sum = pl.pallas_call(
        functools.partial(collect_kernel, batches, len(sums), len(early)),
        out_shape=[
            shape((tok, kv_width), jnp.bfloat16),
            shape((tok, kv_width), jnp.bfloat16),
            shape((heads, HEAD_DIM), jnp.float32),
            shape((kv_heads, HEAD_DIM), jnp.float32),
        ],
        in_specs=[VMEM] * (len(sums) + 1 + len(early) + len(late)),
        out_specs=[VMEM] * 4,
        compiler_params=params(8),
        cost_estimate=pl.CostEstimate(
            flops=8 * tok * kv_width, bytes_accessed=16 * tok * kv_width, transcendentals=0
        ),
        name="collect",
    )(*sums, own, *early, *late)
    return (
        attn[None],
        q_grad[None],
        k_grad[None],
        v_grad[None],
        q_sum.reshape(width),
        v_sum.reshape(kv_width),
    )


def solution(mesh):
    tokens = P("dp", "ctx", "tp")
    return jax.shard_map(
        shards,
        mesh=mesh,
        in_specs=(tokens, P("tp"), tokens, tokens, P("tp"), tokens, P("dp", None)),
        out_specs=(tokens, tokens, tokens, tokens, P("tp"), P("tp")),
        check_vma=False,
    )
```

```python
import functools

import jax
import jax.numpy as jnp
from jax import lax
from jax.experimental import pallas as pl
from jax.experimental.pallas import tpu as pltpu
from jax.sharding import PartitionSpec as P

HEAD_DIM = 128
HEADS = 32
KV_HEADS = 4
GROUP = HEADS // KV_HEADS
PAIR = 2
BLOCK = 32
SCALE = HEAD_DIM ** (-0.5)
LOG2E = 1.4426950408889634
NEGATIVE = -1e30
VMEM = pl.BlockSpec(memory_space=pltpu.VMEM)
ANY = pl.BlockSpec(memory_space=pl.ANY)
SMEM = pl.BlockSpec(memory_space=pltpu.SMEM)


def dot(left, right, left_dim, right_dim):
    return lax.dot_general(
        left, right, (((left_dim,), (right_dim,)), ((), ())), preferred_element_type=jnp.float32
    )


def head_cols(head):
    return slice(head * HEAD_DIM, (head + 1) * HEAD_DIM)


def shape(dims, dtype):
    return jax.ShapeDtypeStruct(dims, dtype)


def params(mebibytes):
    return pltpu.CompilerParams(vmem_limit_bytes=mebibytes * 1024 * 1024)


def biased(values, bias):
    return (values.astype(jnp.float32) + bias.astype(jnp.float32)).astype(jnp.bfloat16)


def source_of(rank, slot, size):
    if size & (size - 1):
        return (rank + size - slot) % size
    return rank ^ slot


def slot_order(size):
    return [slot for slot in range(size) if slot != size // 2] + [size // 2]


def fetch(array, axis, slot):
    size = lax.axis_size(axis)
    return lax.ppermute(array, axis, [(source_of(i, slot, size), i) for i in range(size)])


def send_back(array, slot):
    size = lax.axis_size("ctx")
    return lax.ppermute(array, "ctx", [(i, source_of(i, slot, size)) for i in range(size)])


def prepare_kernel(
    slots, len_ref, pair_ref, qb_ref, vb_ref, q_ref, g_ref, bias_ref, queries_ref, grads_ref,
    score_ref, dprob_ref, live_ref,
):
    tok = q_ref.shape[0]
    kv_heads = vb_ref.shape[0]
    rank = lax.axis_index("ctx")
    query_pos = rank * tok + lax.broadcasted_iota(jnp.int32, (1, tok), 1)
    start = jnp.zeros((1, tok), jnp.int32)
    end = jnp.int32(0)
    for doc in range(len_ref.shape[1]):
        length = len_ref[0, doc]
        end = end + length
        start = start + jnp.where(query_pos >= end, length, 0)
    offsets = lax.broadcasted_iota(jnp.int32, (tok, tok), 0)
    for index, slot in enumerate(slot_order(slots)):
        key_pos = source_of(rank, slot, slots) * tok + offsets
        live = (key_pos >= start) & (key_pos <= query_pos)
        live_ref[index * tok : (index + 1) * tok, :] = jnp.where(live, 0.0, NEGATIVE)
    bias_ref[...] = vb_ref[...]
    column = lax.broadcasted_iota(jnp.int32, (tok, HEAD_DIM), 1)
    for kv_head in range(kv_heads):
        keys = pair_ref[:, head_cols(kv_head)]
        values = biased(pair_ref[:, head_cols(kv_heads + kv_head)], vb_ref[kv_head : kv_head + 1, :])
        for head in range(kv_head * GROUP, (kv_head + 1) * GROUP):
            at = slice(head * tok, (head + 1) * tok)
            queries_ref[at, :HEAD_DIM] = biased(q_ref[:, head_cols(head)], qb_ref[head : head + 1, :])
            queries_ref[at, HEAD_DIM:] = (column == head).astype(jnp.bfloat16)
            grads_ref[at, :] = g_ref[:, head_cols(head)]
        rows = slice(kv_head * GROUP * tok, (kv_head + 1) * GROUP * tok)
        score_ref[:, rows] = dot(keys, queries_ref[rows, :HEAD_DIM], 1, 1)
        dprob_ref[:, rows] = dot(values, grads_ref[rows, :], 1, 1)


def over_rows(array, reduce):
    return reduce(array.reshape(-1, 8, array.shape[-1]), axis=0)


def unpack(pair_ref, bias_ref, keys_ref, values_ref, rows):
    kv_heads = bias_ref.shape[0]
    keys_ref[rows, :] = pair_ref[:, : kv_heads * HEAD_DIM]
    for kv_head in range(kv_heads):
        values_ref[rows, head_cols(kv_head)] = biased(
            pair_ref[:, head_cols(kv_heads + kv_head)], bias_ref[kv_head : kv_head + 1, :]
        )


def near_kernel(
    bias_ref, queries_ref, grads_ref, score_ref, own_dprob_ref, live_ref, *refs
):
    pair_refs, (weights_ref, dprob_ref, stats_ref, keys_ref, values_ref) = refs[:-5], refs[-5:]
    tok = pair_refs[0].shape[0]
    for index, pair_ref in enumerate(pair_refs):
        unpack(pair_ref, bias_ref, keys_ref, values_ref, slice(index * tok, (index + 1) * tok))
    blocks = [slice(row, row + BLOCK) for row in range(0, len(pair_refs) * tok, BLOCK)]
    for kv_head in range(bias_ref.shape[0]):
        cols = head_cols(kv_head)
        group = slice(kv_head * GROUP * tok, (kv_head + 1) * GROUP * tok)
        weights_ref[tok:, group] = dot(keys_ref[tok:, cols], queries_ref[group, :HEAD_DIM], 1, 1)
        dprob_ref[tok:, group] = dot(values_ref[tok:, cols], grads_ref[group, :], 1, 1)
        for first in range(group.start, group.stop, PAIR * tok):
            at = slice(first, first + PAIR * tok)
            row_max = None
            for block in blocks:
                score = (score_ref if block.start < tok else weights_ref)[block, at]
                score = score + jnp.concatenate([live_ref[block, :]] * PAIR, axis=1)
                weights_ref[block, at] = score
                part = over_rows(score, jnp.max)
                row_max = part if row_max is None else jnp.maximum(row_max, part)
            row_max = jnp.max(row_max, axis=0, keepdims=True)
            total = jnp.zeros((8, PAIR * tok), jnp.float32)
            delta = jnp.zeros((8, PAIR * tok), jnp.float32)
            for block in blocks:
                dprob = (own_dprob_ref if block.start < tok else dprob_ref)[block, at]
                weights = jnp.exp2((weights_ref[block, at] - row_max) * (SCALE * LOG2E))
                weights_ref[block, at] = weights
                if block.start < tok:
                    dprob_ref[block, at] = dprob
                total = total + over_rows(weights, jnp.sum)
                delta = delta + over_rows(weights * dprob, jnp.sum)
            stats_ref[0:1, at] = row_max
            stats_ref[1:2, at] = jnp.sum(total, axis=0, keepdims=True)
            stats_ref[2:3, at] = jnp.sum(delta, axis=0, keepdims=True)


def last_kernel(slots, first_head, *refs):
    bias_ref, queries_ref, grads_ref, live_ref = refs[:4]
    weights_ref, dprob_ref, stats_ref, near_keys_ref, near_values_ref, pair_ref = refs[4:10]
    probs_ref, dscore_ref, keys_ref, values_ref, sums_ref, own_ref = refs[10:16]
    out_refs = refs[16 : 16 + slots - 1]
    last_weights_ref, last_dprob_ref = refs[16 + slots - 1 :]
    tok = pair_ref.shape[0]
    near = (slots - 1) * tok
    kv_heads = bias_ref.shape[0]
    kv_width = kv_heads * HEAD_DIM
    heads = kv_heads * GROUP
    keys_ref[:near, :] = near_keys_ref[...]
    values_ref[:near, :] = near_values_ref[...]
    unpack(pair_ref, bias_ref, keys_ref, values_ref, slice(near, near + tok))
    near_blocks = [slice(row, row + BLOCK) for row in range(0, near, BLOCK)]
    blocks = [slice(row, row + BLOCK) for row in range(0, tok, BLOCK)]
    for kv_head in range(kv_heads):
        cols = head_cols(kv_head)
        group = slice(kv_head * GROUP * tok, (kv_head + 1) * GROUP * tok)
        last_weights_ref[:, group] = dot(
            keys_ref[near:, cols], queries_ref[group, :HEAD_DIM], 1, 1
        )
        last_dprob_ref[:, group] = dot(values_ref[near:, cols], grads_ref[group, :], 1, 1)
        for first in range(group.start, group.stop, PAIR * tok):
            at = slice(first, first + PAIR * tok)
            near_max = stats_ref[0:1, at]
            row_max = jnp.broadcast_to(near_max, (8, PAIR * tok))
            for block in blocks:
                live = live_ref[near + block.start : near + block.stop, :]
                score = last_weights_ref[block, at] + jnp.concatenate([live] * PAIR, axis=1)
                last_weights_ref[block, at] = score
                row_max = jnp.maximum(row_max, over_rows(score, jnp.max))
            row_max = jnp.max(row_max, axis=0, keepdims=True)
            total = jnp.zeros((8, PAIR * tok), jnp.float32)
            delta = jnp.zeros((8, PAIR * tok), jnp.float32)
            for block in blocks:
                weights = jnp.exp2((last_weights_ref[block, at] - row_max) * (SCALE * LOG2E))
                last_weights_ref[block, at] = weights
                total = total + over_rows(weights, jnp.sum)
                delta = delta + over_rows(weights * last_dprob_ref[block, at], jnp.sum)
            factor = jnp.exp2((near_max - row_max) * (SCALE * LOG2E))
            total = jnp.sum(total, axis=0, keepdims=True) + stats_ref[1:2, at] * factor
            delta = jnp.sum(delta, axis=0, keepdims=True) + stats_ref[2:3, at] * factor
            inverse = 1.0 / total
            delta = delta * inverse
            factor = factor * inverse
            for block in near_blocks:
                probs = weights_ref[block, at] * factor
                probs_ref[block, at] = probs.astype(jnp.bfloat16)
                dscore_ref[block, at] = (probs * (dprob_ref[block, at] - delta)).astype(jnp.bfloat16)
            for block in blocks:
                to = slice(near + block.start, near + block.stop)
                probs = last_weights_ref[block, at] * inverse
                probs_ref[to, at] = probs.astype(jnp.bfloat16)
                dscore = probs * (last_dprob_ref[block, at] - delta)
                dscore_ref[to, at] = dscore.astype(jnp.bfloat16)
        value_term = dot(probs_ref[:, group], grads_ref[group, :], 1, 0)
        key_term = dot(dscore_ref[:, group], queries_ref[group, :], 1, 0)
        over_queries = key_term[:, HEAD_DIM:]
        key_term = key_term[:, :HEAD_DIM] * SCALE
        high = over_queries.astype(jnp.bfloat16)
        low = (over_queries - high.astype(jnp.float32)).astype(jnp.bfloat16)
        all_keys = keys_ref[:, cols]
        query_sums = (dot(high, all_keys, 0, 0) + dot(low, all_keys, 0, 0)) * SCALE
        of_group = slice(kv_head * GROUP, (kv_head + 1) * GROUP)
        sums_ref[of_group, :] = query_sums[first_head + of_group.start : first_head + of_group.stop]
        sums_ref[heads + kv_head : heads + kv_head + 1, :] = jnp.sum(
            value_term, axis=0, keepdims=True
        )
        value_cols = head_cols(kv_heads + kv_head)
        own_ref[:, cols] = key_term[:tok]
        own_ref[:, value_cols] = value_term[:tok]
        for index, slot in enumerate(slot_order(slots)):
            if slot == 0:
                continue
            rows = slice(index * tok, (index + 1) * tok)
            out_refs[slot - 1][:, cols] = key_term[rows].astype(jnp.bfloat16)
            out_refs[slot - 1][:, value_cols] = value_term[rows].astype(jnp.bfloat16)


def finish_kernel(probs_ref, dscore_ref, keys_ref, values_ref, _, attn_ref, qg_ref, __):
    tok = attn_ref.shape[0]
    kv_heads = keys_ref.shape[1] // HEAD_DIM
    for kv_head in range(kv_heads):
        cols = head_cols(kv_head)
        keys_t = keys_ref[:, cols].T
        values_t = values_ref[:, cols].T
        for pair in range(GROUP // PAIR):
            first = kv_head * GROUP + pair * PAIR
            at = slice(first * tok, (first + PAIR) * tok)
            attn = dot(values_t, probs_ref[:, at], 1, 0).T
            query_grad = (dot(keys_t, dscore_ref[:, at], 1, 0) * SCALE).T
            for n in range(PAIR):
                head = first + n
                rows = slice(n * tok, (n + 1) * tok)
                attn_ref[:, head_cols(head)] = attn[rows].astype(jnp.bfloat16)
                qg_ref[:, head_cols(head)] = query_grad[rows].astype(jnp.bfloat16)


def collect_kernel(batches, messages, *refs):
    sum_refs, (own_ref, early_ref), refs = refs[:2], refs[2:4], refs[4:]
    message_refs, (kg_ref, vg_ref, qb_ref, vb_ref) = refs[:messages], refs[messages:]
    heads, kv_heads = qb_ref.shape[0], vb_ref.shape[0]
    tok, kv_width = kg_ref.shape
    total = sum_refs[0][...] + sum_refs[1][...]
    query_sums, value_sums = total[:heads], total[heads:]
    term = own_ref[...] + early_ref[...].astype(jnp.float32)
    for ref in message_refs:
        added = ref[tok:, :].astype(jnp.float32)
        high_and_low = added[:, : 2 * HEAD_DIM], added[:, 2 * HEAD_DIM : 4 * HEAD_DIM]
        of_queries, of_values = (both[:, :HEAD_DIM] + both[:, HEAD_DIM:] for both in high_and_low)
        query_sums = query_sums + of_queries[:heads]
        value_sums = value_sums + of_values[:kv_heads]
        term = term + ref[:tok, :].astype(jnp.float32)
    qb_ref[...] = query_sums * (1.0 / batches)
    vb_ref[...] = value_sums * (1.0 / batches)
    term = term.astype(jnp.bfloat16)
    kg_ref[...] = term[:, :kv_width]
    vg_ref[...] = term[:, kv_width:]


def total_kernel(count, *refs):
    parts, refs = refs[:count], refs[count:]
    sent = (len(refs) - 1) // 2
    term_refs, total_ref, message_refs = refs[:sent], refs[sent], refs[sent + 1 :]
    total = parts[0][...]
    for ref in parts[1:]:
        total = total + ref[...]
    total_ref[...] = total
    for term_ref, message_ref in zip(term_refs, message_refs):
        tok, kv_heads = term_ref.shape[0], term_ref.shape[1] // (2 * HEAD_DIM)
        message_ref[:tok, :] = term_ref[...]
        message_ref[tok:, : 4 * HEAD_DIM] = added_rows(
            total, total.shape[0] - kv_heads, message_ref.shape[0] - tok
        )


def added_rows(total, heads, rows):
    high = total.astype(jnp.bfloat16).astype(jnp.float32)
    both = jnp.concatenate([high, total - high], axis=1)
    blocks = [
        jnp.concatenate([block, jnp.zeros((rows - block.shape[0], 2 * HEAD_DIM), jnp.float32)])
        if block.shape[0] < rows
        else block
        for block in (both[:heads], both[heads:])
    ]
    return jnp.concatenate(blocks, axis=1).astype(jnp.bfloat16)


def total_with(parts, terms):
    rows = -(-parts[0].shape[0] * GROUP // (GROUP + 1) // 16) * 16
    total, *messages = pl.pallas_call(
        functools.partial(total_kernel, len(parts)),
        out_shape=[shape(parts[0].shape, parts[0].dtype)]
        + [shape((term.shape[0] + rows, term.shape[1]), term.dtype) for term in terms],
        in_specs=[VMEM] * (len(parts) + len(terms)),
        out_specs=[VMEM] * (1 + len(terms)),
        compiler_params=params(8),
        cost_estimate=pl.CostEstimate(flops=parts[0].size, bytes_accessed=0, transcendentals=0),
        name="total",
    )(*parts, *terms)
    return total, messages


def exchange(axis, part):
    return [part] + [fetch(part, axis, slot) for slot in range(1, lax.axis_size(axis))]


def attend(first_head, bias, queries, grads, score, own_dprob, live, pairs):
    ctx = len(pairs)
    tok = pairs[0].shape[0]
    kv_width = bias.shape[0] * HEAD_DIM
    columns = queries.shape[0]
    rows = ctx * tok
    near = rows - tok
    near_slots = slot_order(ctx)[:-1]
    weights, dprob, stats, near_keys, near_values = pl.pallas_call(
        near_kernel,
        out_shape=[
            shape((near, columns), jnp.float32),
            shape((near, columns), jnp.float32),
            shape((8, columns), jnp.float32),
            shape((near, kv_width), jnp.bfloat16),
            shape((near, kv_width), jnp.bfloat16),
        ],
        in_specs=[VMEM] * (6 + len(near_slots)),
        out_specs=[VMEM] * 5,
        compiler_params=params(20 if ctx < 8 else 48),
        cost_estimate=pl.CostEstimate(
            flops=4 * near * columns * HEAD_DIM,
            bytes_accessed=8 * near * columns,
            transcendentals=near * columns,
        ),
        name="near",
    )(bias, queries, grads, score, own_dprob, live, *[pairs[slot] for slot in near_slots])
    term = shape((tok, 2 * kv_width), jnp.bfloat16)
    return pl.pallas_call(
        functools.partial(last_kernel, ctx, first_head),
        out_shape=[
            shape((rows, columns), jnp.bfloat16),
            shape((rows, columns), jnp.bfloat16),
            shape((rows, kv_width), jnp.bfloat16),
            shape((rows, kv_width), jnp.bfloat16),
            shape((bias.shape[0] * (GROUP + 1), HEAD_DIM), jnp.float32),
            shape((tok, 2 * kv_width), jnp.float32),
        ]
        + [term] * (ctx - 1),
        in_specs=[VMEM] * 10,
        out_specs=[VMEM] * (6 + ctx - 1),
        scratch_shapes=[pltpu.VMEM((tok, columns), jnp.float32)] * 2,
        compiler_params=params(24 if ctx < 8 else 48),
        cost_estimate=pl.CostEstimate(
            flops=4 * rows * columns * HEAD_DIM,
            bytes_accessed=4 * rows * columns,
            transcendentals=tok * columns,
        ),
        name="last",
    )(bias, queries, grads, live, weights, dprob, stats, near_keys, near_values, pairs[ctx // 2])


def joined(place, parts):
    if place < 4:
        return jnp.concatenate(parts, axis=1)
    cut, axis = (GROUP, 0) if place == 4 else (HEAD_DIM, 1)
    pieces = [jnp.split(part, [cut], axis=axis) for part in parts]
    return jnp.concatenate([piece[n] for n in range(2) for piece in pieces], axis=axis)


def shards(q_proj, q_bias, k_proj, v_proj, v_bias, dout, lengths):
    _, tok, width = q_proj.shape
    kv_width = k_proj.shape[2]
    heads = width // HEAD_DIM
    kv_heads = kv_width // HEAD_DIM
    ctx = lax.axis_size("ctx")
    batches = lax.axis_size("dp")
    rows = ctx * tok
    columns = heads * tok
    pair = jnp.concatenate([k_proj[0], v_proj[0]], axis=1)
    pairs = [pair] + [fetch(pair, "ctx", slot) for slot in range(1, ctx)]
    prepared = pl.pallas_call(
        functools.partial(prepare_kernel, ctx),
        out_shape=[
            shape((kv_heads, HEAD_DIM), jnp.bfloat16),
            shape((columns, 2 * HEAD_DIM), jnp.bfloat16),
            shape((columns, HEAD_DIM), jnp.bfloat16),
            shape((tok, columns), jnp.float32),
            shape((tok, columns), jnp.float32),
            shape((rows, tok), jnp.float32),
        ],
        in_specs=[SMEM] + [VMEM] * 5,
        out_specs=[VMEM] * 6,
        compiler_params=params(16),
        cost_estimate=pl.CostEstimate(
            flops=4 * tok * tok * width, bytes_accessed=16 * tok * width, transcendentals=0
        ),
        name="prepare",
    )(
        lengths,
        pair,
        q_bias.reshape(heads, HEAD_DIM),
        v_bias.reshape(kv_heads, HEAD_DIM),
        q_proj[0],
        dout[0],
    )
    bias, queries, grads, score, own_dprob, live = prepared
    if ctx < 8:
        made = attend(0, bias, queries, grads, score, own_dprob, live, pairs)
    else:
        made = [
            attend(
                kv_head * GROUP,
                bias[kv_head : kv_head + 1],
                *(part[at] for part in (queries, grads)),
                *(part[:, at] for part in (score, own_dprob)),
                live,
                [
                    jnp.concatenate(
                        [part[:, head_cols(kv_head)], part[:, head_cols(kv_heads + kv_head)]], axis=1
                    )
                    for part in pairs
                ],
            )
            for kv_head in range(kv_heads)
            for at in [slice(kv_head * GROUP * tok, (kv_head + 1) * GROUP * tok)]
        ]
        made = [joined(n, parts) for n, parts in enumerate(zip(*made))]
    probs, dscore, all_keys, all_values, sums, own, *terms = made
    term = shape((tok, 2 * kv_width), jnp.bfloat16)
    half = ctx // 2
    early = send_back(terms.pop(half - 1), half)
    attn, q_grad, early = pl.pallas_call(
        finish_kernel,
        out_shape=[
            shape((tok, width), jnp.bfloat16),
            shape((tok, width), jnp.bfloat16),
            shape(early.shape, early.dtype),
        ],
        in_specs=[VMEM] * 4 + [ANY],
        out_specs=[VMEM] * 2 + [ANY],
        input_output_aliases={4: 2},
        compiler_params=params(24),
        cost_estimate=pl.CostEstimate(
            flops=4 * rows * tok * width, bytes_accessed=4 * rows * columns, transcendentals=0
        ),
        name="finish",
    )(probs, dscore, all_keys, all_values, early)
    sums, messages = total_with(exchange("dp", sums), terms)
    slots = [slot for slot in range(1, ctx) if slot != half]
    back = [send_back(message, slot) for slot, message in zip(slots, messages)][::-1]
    sums = [sums, send_back(sums, half)]
    k_grad, v_grad, q_sum, v_sum = pl.pallas_call(
        functools.partial(collect_kernel, batches, len(back)),
        out_shape=[
            shape((tok, kv_width), jnp.bfloat16),
            shape((tok, kv_width), jnp.bfloat16),
            shape((heads, HEAD_DIM), jnp.float32),
            shape((kv_heads, HEAD_DIM), jnp.float32),
        ],
        in_specs=[VMEM] * (4 + len(back)),
        out_specs=[VMEM] * 4,
        compiler_params=params(8),
        cost_estimate=pl.CostEstimate(
            flops=8 * tok * kv_width, bytes_accessed=16 * tok * kv_width, transcendentals=0
        ),
        name="collect",
    )(*sums, own, early, *back)
    return (
        attn[None],
        q_grad[None],
        k_grad[None],
        v_grad[None],
        q_sum.reshape(width),
        v_sum.reshape(kv_width),
    )


def solution(mesh):
    tokens = P("dp", "ctx", "tp")
    return jax.shard_map(
        shards,
        mesh=mesh,
        in_specs=(tokens, P("tp"), tokens, tokens, P("tp"), tokens, P("dp", None)),
        out_specs=(tokens, tokens, tokens, tokens, P("tp"), P("tp")),
        check_vma=False,
    )
```

```python
import functools

import jax
import jax.numpy as jnp
from jax import lax
from jax.experimental import pallas as pl
from jax.experimental.pallas import tpu as pltpu
from jax.sharding import PartitionSpec as P

HEAD_DIM = 128
HEADS = 32
KV_HEADS = 4
GROUP = HEADS // KV_HEADS
PAIR = 2
BLOCK = 32
SCALE = HEAD_DIM ** (-0.5)
LOG2E = 1.4426950408889634
NEGATIVE = -1e30
VMEM = pl.BlockSpec(memory_space=pltpu.VMEM)
ANY = pl.BlockSpec(memory_space=pl.ANY)
SMEM = pl.BlockSpec(memory_space=pltpu.SMEM)


def dot(left, right, left_dim, right_dim):
    return lax.dot_general(
        left, right, (((left_dim,), (right_dim,)), ((), ())), preferred_element_type=jnp.float32
    )


def head_cols(head):
    return slice(head * HEAD_DIM, (head + 1) * HEAD_DIM)


def shape(dims, dtype):
    return jax.ShapeDtypeStruct(dims, dtype)


def params(mebibytes):
    return pltpu.CompilerParams(vmem_limit_bytes=mebibytes * 1024 * 1024)


def biased(values, bias):
    return (values.astype(jnp.float32) + bias.astype(jnp.float32)).astype(jnp.bfloat16)


def source_of(rank, slot, size):
    if size & (size - 1):
        return (rank + size - slot) % size
    return rank ^ slot


def slot_order(size):
    return [slot for slot in range(size) if slot != size // 2] + [size // 2]


def fetch(array, axis, slot):
    size = lax.axis_size(axis)
    return lax.ppermute(array, axis, [(source_of(i, slot, size), i) for i in range(size)])


def send_back(array, slot):
    size = lax.axis_size("ctx")
    return lax.ppermute(array, "ctx", [(i, source_of(i, slot, size)) for i in range(size)])


def prepare_kernel(
    slots, len_ref, pair_ref, qb_ref, vb_ref, q_ref, g_ref, bias_ref, queries_ref, grads_ref,
    score_ref, dprob_ref, live_ref,
):
    tok = q_ref.shape[0]
    kv_heads = vb_ref.shape[0]
    rank = lax.axis_index("ctx")
    query_pos = rank * tok + lax.broadcasted_iota(jnp.int32, (1, tok), 1)
    start = jnp.zeros((1, tok), jnp.int32)
    end = jnp.int32(0)
    for doc in range(len_ref.shape[1]):
        length = len_ref[0, doc]
        end = end + length
        start = start + jnp.where(query_pos >= end, length, 0)
    offsets = lax.broadcasted_iota(jnp.int32, (tok, tok), 0)
    for index, slot in enumerate(slot_order(slots)):
        key_pos = source_of(rank, slot, slots) * tok + offsets
        live = (key_pos >= start) & (key_pos <= query_pos)
        live_ref[index * tok : (index + 1) * tok, :] = jnp.where(live, 0.0, NEGATIVE)
    bias_ref[...] = vb_ref[...]
    column = lax.broadcasted_iota(jnp.int32, (tok, HEAD_DIM), 1)
    for kv_head in range(kv_heads):
        keys = pair_ref[:, head_cols(kv_head)]
        values = biased(pair_ref[:, head_cols(kv_heads + kv_head)], vb_ref[kv_head : kv_head + 1, :])
        for head in range(kv_head * GROUP, (kv_head + 1) * GROUP):
            at = slice(head * tok, (head + 1) * tok)
            queries_ref[at, :HEAD_DIM] = biased(q_ref[:, head_cols(head)], qb_ref[head : head + 1, :])
            queries_ref[at, HEAD_DIM:] = (column == head).astype(jnp.bfloat16)
            grads_ref[at, :] = g_ref[:, head_cols(head)]
        rows = slice(kv_head * GROUP * tok, (kv_head + 1) * GROUP * tok)
        score_ref[:, rows] = dot(keys, queries_ref[rows, :HEAD_DIM], 1, 1)
        dprob_ref[:, rows] = dot(values, grads_ref[rows, :], 1, 1)


def over_rows(array, reduce):
    return reduce(array.reshape(-1, 8, array.shape[-1]), axis=0)


def unpack(pair_ref, bias_ref, keys_ref, values_ref, rows):
    kv_heads = bias_ref.shape[0]
    keys_ref[rows, :] = pair_ref[:, : kv_heads * HEAD_DIM]
    for kv_head in range(kv_heads):
        values_ref[rows, head_cols(kv_head)] = biased(
            pair_ref[:, head_cols(kv_heads + kv_head)], bias_ref[kv_head : kv_head + 1, :]
        )


def near_kernel(
    bias_ref, queries_ref, grads_ref, score_ref, own_dprob_ref, live_ref, *refs
):
    pair_refs, (weights_ref, dprob_ref, stats_ref, keys_ref, values_ref) = refs[:-5], refs[-5:]
    tok = pair_refs[0].shape[0]
    for index, pair_ref in enumerate(pair_refs):
        unpack(pair_ref, bias_ref, keys_ref, values_ref, slice(index * tok, (index + 1) * tok))
    blocks = [slice(row, row + BLOCK) for row in range(0, len(pair_refs) * tok, BLOCK)]
    for kv_head in range(bias_ref.shape[0]):
        cols = head_cols(kv_head)
        group = slice(kv_head * GROUP * tok, (kv_head + 1) * GROUP * tok)
        weights_ref[tok:, group] = dot(keys_ref[tok:, cols], queries_ref[group, :HEAD_DIM], 1, 1)
        dprob_ref[tok:, group] = dot(values_ref[tok:, cols], grads_ref[group, :], 1, 1)
        for first in range(group.start, group.stop, PAIR * tok):
            at = slice(first, first + PAIR * tok)
            row_max = None
            for block in blocks:
                score = (score_ref if block.start < tok else weights_ref)[block, at]
                score = score + jnp.concatenate([live_ref[block, :]] * PAIR, axis=1)
                weights_ref[block, at] = score
                part = over_rows(score, jnp.max)
                row_max = part if row_max is None else jnp.maximum(row_max, part)
            row_max = jnp.max(row_max, axis=0, keepdims=True)
            total = jnp.zeros((8, PAIR * tok), jnp.float32)
            delta = jnp.zeros((8, PAIR * tok), jnp.float32)
            for block in blocks:
                dprob = (own_dprob_ref if block.start < tok else dprob_ref)[block, at]
                weights = jnp.exp2((weights_ref[block, at] - row_max) * (SCALE * LOG2E))
                weights_ref[block, at] = weights
                if block.start < tok:
                    dprob_ref[block, at] = dprob
                total = total + over_rows(weights, jnp.sum)
                delta = delta + over_rows(weights * dprob, jnp.sum)
            stats_ref[0:1, at] = row_max
            stats_ref[1:2, at] = jnp.sum(total, axis=0, keepdims=True)
            stats_ref[2:3, at] = jnp.sum(delta, axis=0, keepdims=True)


def last_kernel(slots, first_head, *refs):
    bias_ref, queries_ref, grads_ref, live_ref = refs[:4]
    weights_ref, dprob_ref, stats_ref, near_keys_ref, near_values_ref, pair_ref = refs[4:10]
    probs_ref, dscore_ref, keys_ref, values_ref, sums_ref, own_ref = refs[10:16]
    out_refs = refs[16 : 16 + slots - 1]
    last_weights_ref, last_dprob_ref = refs[16 + slots - 1 :]
    tok = pair_ref.shape[0]
    near = (slots - 1) * tok
    kv_heads = bias_ref.shape[0]
    kv_width = kv_heads * HEAD_DIM
    heads = kv_heads * GROUP
    keys_ref[:near, :] = near_keys_ref[...]
    values_ref[:near, :] = near_values_ref[...]
    unpack(pair_ref, bias_ref, keys_ref, values_ref, slice(near, near + tok))
    near_blocks = [slice(row, row + BLOCK) for row in range(0, near, BLOCK)]
    blocks = [slice(row, row + BLOCK) for row in range(0, tok, BLOCK)]
    for kv_head in range(kv_heads):
        cols = head_cols(kv_head)
        group = slice(kv_head * GROUP * tok, (kv_head + 1) * GROUP * tok)
        last_weights_ref[:, group] = dot(
            keys_ref[near:, cols], queries_ref[group, :HEAD_DIM], 1, 1
        )
        last_dprob_ref[:, group] = dot(values_ref[near:, cols], grads_ref[group, :], 1, 1)
        for first in range(group.start, group.stop, PAIR * tok):
            at = slice(first, first + PAIR * tok)
            near_max = stats_ref[0:1, at]
            row_max = jnp.broadcast_to(near_max, (8, PAIR * tok))
            for block in blocks:
                live = live_ref[near + block.start : near + block.stop, :]
                score = last_weights_ref[block, at] + jnp.concatenate([live] * PAIR, axis=1)
                last_weights_ref[block, at] = score
                row_max = jnp.maximum(row_max, over_rows(score, jnp.max))
            row_max = jnp.max(row_max, axis=0, keepdims=True)
            total = jnp.zeros((8, PAIR * tok), jnp.float32)
            delta = jnp.zeros((8, PAIR * tok), jnp.float32)
            for block in blocks:
                weights = jnp.exp2((last_weights_ref[block, at] - row_max) * (SCALE * LOG2E))
                last_weights_ref[block, at] = weights
                total = total + over_rows(weights, jnp.sum)
                delta = delta + over_rows(weights * last_dprob_ref[block, at], jnp.sum)
            factor = jnp.exp2((near_max - row_max) * (SCALE * LOG2E))
            total = jnp.sum(total, axis=0, keepdims=True) + stats_ref[1:2, at] * factor
            delta = jnp.sum(delta, axis=0, keepdims=True) + stats_ref[2:3, at] * factor
            inverse = 1.0 / total
            delta = delta * inverse
            factor = factor * inverse
            for block in near_blocks:
                probs = weights_ref[block, at] * factor
                probs_ref[block, at] = probs.astype(jnp.bfloat16)
                dscore_ref[block, at] = (probs * (dprob_ref[block, at] - delta)).astype(jnp.bfloat16)
            for block in blocks:
                to = slice(near + block.start, near + block.stop)
                probs = last_weights_ref[block, at] * inverse
                probs_ref[to, at] = probs.astype(jnp.bfloat16)
                dscore = probs * (last_dprob_ref[block, at] - delta)
                dscore_ref[to, at] = dscore.astype(jnp.bfloat16)
        value_term = dot(probs_ref[:, group], grads_ref[group, :], 1, 0)
        key_term = dot(dscore_ref[:, group], queries_ref[group, :], 1, 0)
        over_queries = key_term[:, HEAD_DIM:]
        key_term = key_term[:, :HEAD_DIM] * SCALE
        high = over_queries.astype(jnp.bfloat16)
        low = (over_queries - high.astype(jnp.float32)).astype(jnp.bfloat16)
        all_keys = keys_ref[:, cols]
        query_sums = (dot(high, all_keys, 0, 0) + dot(low, all_keys, 0, 0)) * SCALE
        of_group = slice(kv_head * GROUP, (kv_head + 1) * GROUP)
        sums_ref[of_group, :] = query_sums[first_head + of_group.start : first_head + of_group.stop]
        sums_ref[heads + kv_head : heads + kv_head + 1, :] = jnp.sum(
            value_term, axis=0, keepdims=True
        )
        value_cols = head_cols(kv_heads + kv_head)
        own_ref[:, cols] = key_term[:tok]
        own_ref[:, value_cols] = value_term[:tok]
        for index, slot in enumerate(slot_order(slots)):
            if slot == 0:
                continue
            rows = slice(index * tok, (index + 1) * tok)
            out_refs[slot - 1][:, cols] = key_term[rows].astype(jnp.bfloat16)
            out_refs[slot - 1][:, value_cols] = value_term[rows].astype(jnp.bfloat16)


def finish_kernel(probs_ref, dscore_ref, keys_ref, values_ref, _, attn_ref, qg_ref, __):
    tok = attn_ref.shape[0]
    kv_heads = keys_ref.shape[1] // HEAD_DIM
    for kv_head in range(kv_heads):
        cols = head_cols(kv_head)
        keys_t = keys_ref[:, cols].T
        values_t = values_ref[:, cols].T
        for pair in range(GROUP // PAIR):
            first = kv_head * GROUP + pair * PAIR
            at = slice(first * tok, (first + PAIR) * tok)
            attn = dot(values_t, probs_ref[:, at], 1, 0).T
            query_grad = (dot(keys_t, dscore_ref[:, at], 1, 0) * SCALE).T
            for n in range(PAIR):
                head = first + n
                rows = slice(n * tok, (n + 1) * tok)
                attn_ref[:, head_cols(head)] = attn[rows].astype(jnp.bfloat16)
                qg_ref[:, head_cols(head)] = query_grad[rows].astype(jnp.bfloat16)


def collect_kernel(batches, parts, *refs):
    sum_refs, term_refs, (kg_ref, vg_ref, qb_ref, vb_ref) = refs[:parts], refs[parts:-4], refs[-4:]
    heads = qb_ref.shape[0]
    kv_width = kg_ref.shape[1]
    total = sum_refs[0][...]
    for ref in sum_refs[1:]:
        total = total + ref[...]
    total = total * (1.0 / batches)
    qb_ref[...] = total[:heads]
    vb_ref[...] = total[heads:]
    term = term_refs[0][...]
    for ref in term_refs[1:]:
        term = term + ref[...].astype(jnp.float32)
    term = term.astype(jnp.bfloat16)
    kg_ref[...] = term[:, :kv_width]
    vg_ref[...] = term[:, kv_width:]


def exchange(axis, part):
    return [part] + [fetch(part, axis, slot) for slot in range(1, lax.axis_size(axis))]


def attend(first_head, bias, queries, grads, score, own_dprob, live, pairs):
    ctx = len(pairs)
    tok = pairs[0].shape[0]
    kv_width = bias.shape[0] * HEAD_DIM
    columns = queries.shape[0]
    rows = ctx * tok
    near = rows - tok
    near_slots = slot_order(ctx)[:-1]
    weights, dprob, stats, near_keys, near_values = pl.pallas_call(
        near_kernel,
        out_shape=[
            shape((near, columns), jnp.float32),
            shape((near, columns), jnp.float32),
            shape((8, columns), jnp.float32),
            shape((near, kv_width), jnp.bfloat16),
            shape((near, kv_width), jnp.bfloat16),
        ],
        in_specs=[VMEM] * (6 + len(near_slots)),
        out_specs=[VMEM] * 5,
        compiler_params=params(20 if ctx < 8 else 48),
        cost_estimate=pl.CostEstimate(
            flops=4 * near * columns * HEAD_DIM,
            bytes_accessed=8 * near * columns,
            transcendentals=near * columns,
        ),
        name="near",
    )(bias, queries, grads, score, own_dprob, live, *[pairs[slot] for slot in near_slots])
    term = shape((tok, 2 * kv_width), jnp.bfloat16)
    return pl.pallas_call(
        functools.partial(last_kernel, ctx, first_head),
        out_shape=[
            shape((rows, columns), jnp.bfloat16),
            shape((rows, columns), jnp.bfloat16),
            shape((rows, kv_width), jnp.bfloat16),
            shape((rows, kv_width), jnp.bfloat16),
            shape((bias.shape[0] * (GROUP + 1), HEAD_DIM), jnp.float32),
            shape((tok, 2 * kv_width), jnp.float32),
        ]
        + [term] * (ctx - 1),
        in_specs=[VMEM] * 10,
        out_specs=[VMEM] * (6 + ctx - 1),
        scratch_shapes=[pltpu.VMEM((tok, columns), jnp.float32)] * 2,
        compiler_params=params(24 if ctx < 8 else 48),
        cost_estimate=pl.CostEstimate(
            flops=4 * rows * columns * HEAD_DIM,
            bytes_accessed=4 * rows * columns,
            transcendentals=tok * columns,
        ),
        name="last",
    )(bias, queries, grads, live, weights, dprob, stats, near_keys, near_values, pairs[ctx // 2])


def joined(place, parts):
    if place < 4:
        return jnp.concatenate(parts, axis=1)
    cut, axis = (GROUP, 0) if place == 4 else (HEAD_DIM, 1)
    pieces = [jnp.split(part, [cut], axis=axis) for part in parts]
    return jnp.concatenate([piece[n] for n in range(2) for piece in pieces], axis=axis)


def shards(q_proj, q_bias, k_proj, v_proj, v_bias, dout, lengths):
    _, tok, width = q_proj.shape
    kv_width = k_proj.shape[2]
    heads = width // HEAD_DIM
    kv_heads = kv_width // HEAD_DIM
    ctx = lax.axis_size("ctx")
    batches = lax.axis_size("dp")
    rows = ctx * tok
    columns = heads * tok
    pair = jnp.concatenate([k_proj[0], v_proj[0]], axis=1)
    pairs = [pair] + [fetch(pair, "ctx", slot) for slot in range(1, ctx)]
    prepared = pl.pallas_call(
        functools.partial(prepare_kernel, ctx),
        out_shape=[
            shape((kv_heads, HEAD_DIM), jnp.bfloat16),
            shape((columns, 2 * HEAD_DIM), jnp.bfloat16),
            shape((columns, HEAD_DIM), jnp.bfloat16),
            shape((tok, columns), jnp.float32),
            shape((tok, columns), jnp.float32),
            shape((rows, tok), jnp.float32),
        ],
        in_specs=[SMEM] + [VMEM] * 5,
        out_specs=[VMEM] * 6,
        compiler_params=params(16),
        cost_estimate=pl.CostEstimate(
            flops=4 * tok * tok * width, bytes_accessed=16 * tok * width, transcendentals=0
        ),
        name="prepare",
    )(
        lengths,
        pair,
        q_bias.reshape(heads, HEAD_DIM),
        v_bias.reshape(kv_heads, HEAD_DIM),
        q_proj[0],
        dout[0],
    )
    bias, queries, grads, score, own_dprob, live = prepared
    if ctx < 8:
        made = attend(0, bias, queries, grads, score, own_dprob, live, pairs)
    else:
        made = [
            attend(
                kv_head * GROUP,
                bias[kv_head : kv_head + 1],
                *(part[at] for part in (queries, grads)),
                *(part[:, at] for part in (score, own_dprob)),
                live,
                [
                    jnp.concatenate(
                        [part[:, head_cols(kv_head)], part[:, head_cols(kv_heads + kv_head)]], axis=1
                    )
                    for part in pairs
                ],
            )
            for kv_head in range(kv_heads)
            for at in [slice(kv_head * GROUP * tok, (kv_head + 1) * GROUP * tok)]
        ]
        made = [joined(n, parts) for n, parts in enumerate(zip(*made))]
    probs, dscore, all_keys, all_values, sums, own, *terms = made
    term = shape((tok, 2 * kv_width), jnp.bfloat16)
    half = ctx // 2
    early = send_back(terms[half - 1], half)
    attn, q_grad, early = pl.pallas_call(
        finish_kernel,
        out_shape=[
            shape((tok, width), jnp.bfloat16),
            shape((tok, width), jnp.bfloat16),
            shape(early.shape, early.dtype),
        ],
        in_specs=[VMEM] * 4 + [ANY],
        out_specs=[VMEM] * 2 + [ANY],
        input_output_aliases={4: 2},
        compiler_params=params(24),
        cost_estimate=pl.CostEstimate(
            flops=4 * rows * tok * width, bytes_accessed=4 * rows * columns, transcendentals=0
        ),
        name="finish",
    )(probs, dscore, all_keys, all_values, early)
    sums = functools.reduce(lambda left, right: left + right, exchange("dp", sums))
    sums = exchange("ctx", sums)
    back = [send_back(terms[slot - 1], slot) for slot in range(ctx - 1, 0, -1) if slot != half]
    k_grad, v_grad, q_sum, v_sum = pl.pallas_call(
        functools.partial(collect_kernel, batches, len(sums)),
        out_shape=[
            shape((tok, kv_width), jnp.bfloat16),
            shape((tok, kv_width), jnp.bfloat16),
            shape((heads, HEAD_DIM), jnp.float32),
            shape((kv_heads, HEAD_DIM), jnp.float32),
        ],
        in_specs=[VMEM] * (len(sums) + 2 + len(back)),
        out_specs=[VMEM] * 4,
        compiler_params=params(8),
        cost_estimate=pl.CostEstimate(
            flops=8 * tok * kv_width, bytes_accessed=16 * tok * kv_width, transcendentals=0
        ),
        name="collect",
    )(*sums, own, early, *back)
    return (
        attn[None],
        q_grad[None],
        k_grad[None],
        v_grad[None],
        q_sum.reshape(width),
        v_sum.reshape(kv_width),
    )


def solution(mesh):
    tokens = P("dp", "ctx", "tp")
    return jax.shard_map(
        shards,
        mesh=mesh,
        in_specs=(tokens, P("tp"), tokens, tokens, P("tp"), tokens, P("dp", None)),
        out_specs=(tokens, tokens, tokens, tokens, P("tp"), P("tp")),
        check_vma=False,
    )
```

```python
import functools

import jax
import jax.numpy as jnp
from jax import lax
from jax.experimental import pallas as pl
from jax.experimental.pallas import tpu as pltpu
from jax.sharding import PartitionSpec as P

HEAD_DIM = 128
HEADS = 32
KV_HEADS = 4
GROUP = HEADS // KV_HEADS
PAIR = 2
BLOCK = 32
SCALE = HEAD_DIM ** (-0.5)
LOG2E = 1.4426950408889634
NEGATIVE = -1e30
VMEM = pl.BlockSpec(memory_space=pltpu.VMEM)
ANY = pl.BlockSpec(memory_space=pl.ANY)
SMEM = pl.BlockSpec(memory_space=pltpu.SMEM)


def dot(left, right, left_dim, right_dim):
    return lax.dot_general(
        left, right, (((left_dim,), (right_dim,)), ((), ())), preferred_element_type=jnp.float32
    )


def head_cols(head):
    return slice(head * HEAD_DIM, (head + 1) * HEAD_DIM)


def shape(dims, dtype):
    return jax.ShapeDtypeStruct(dims, dtype)


def params(mebibytes):
    return pltpu.CompilerParams(vmem_limit_bytes=mebibytes * 1024 * 1024)


def biased(values, bias):
    return (values.astype(jnp.float32) + bias.astype(jnp.float32)).astype(jnp.bfloat16)


def source_of(rank, slot, size):
    if size & (size - 1):
        return (rank + size - slot) % size
    return rank ^ slot


def slot_order(size):
    return [slot for slot in range(size) if slot != size // 2] + [size // 2]


def fetch(array, axis, slot):
    size = lax.axis_size(axis)
    return lax.ppermute(array, axis, [(source_of(i, slot, size), i) for i in range(size)])


def send_back(array, slot):
    size = lax.axis_size("ctx")
    return lax.ppermute(array, "ctx", [(i, source_of(i, slot, size)) for i in range(size)])


def prepare_kernel(
    slots, len_ref, pair_ref, qb_ref, vb_ref, q_ref, g_ref, bias_ref, queries_ref, grads_ref,
    score_ref, dprob_ref, live_ref,
):
    tok = q_ref.shape[0]
    kv_heads = vb_ref.shape[0]
    rank = lax.axis_index("ctx")
    query_pos = rank * tok + lax.broadcasted_iota(jnp.int32, (1, tok), 1)
    start = jnp.zeros((1, tok), jnp.int32)
    end = jnp.int32(0)
    for doc in range(len_ref.shape[1]):
        length = len_ref[0, doc]
        end = end + length
        start = start + jnp.where(query_pos >= end, length, 0)
    offsets = lax.broadcasted_iota(jnp.int32, (tok, tok), 0)
    for index, slot in enumerate(slot_order(slots)):
        key_pos = source_of(rank, slot, slots) * tok + offsets
        live = (key_pos >= start) & (key_pos <= query_pos)
        live_ref[index * tok : (index + 1) * tok, :] = jnp.where(live, 0.0, NEGATIVE)
    bias_ref[...] = vb_ref[...]
    column = lax.broadcasted_iota(jnp.int32, (tok, HEAD_DIM), 1)
    for kv_head in range(kv_heads):
        keys = pair_ref[:, head_cols(kv_head)]
        values = biased(pair_ref[:, head_cols(kv_heads + kv_head)], vb_ref[kv_head : kv_head + 1, :])
        for head in range(kv_head * GROUP, (kv_head + 1) * GROUP):
            at = slice(head * tok, (head + 1) * tok)
            queries_ref[at, :HEAD_DIM] = biased(q_ref[:, head_cols(head)], qb_ref[head : head + 1, :])
            queries_ref[at, HEAD_DIM:] = (column == head).astype(jnp.bfloat16)
            grads_ref[at, :] = g_ref[:, head_cols(head)]
        rows = slice(kv_head * GROUP * tok, (kv_head + 1) * GROUP * tok)
        score_ref[:, rows] = dot(keys, queries_ref[rows, :HEAD_DIM], 1, 1)
        dprob_ref[:, rows] = dot(values, grads_ref[rows, :], 1, 1)


def over_rows(array, reduce):
    return reduce(array.reshape(-1, 8, array.shape[-1]), axis=0)


def unpack(pair_ref, bias_ref, keys_ref, values_ref, rows):
    kv_heads = bias_ref.shape[0]
    keys_ref[rows, :] = pair_ref[:, : kv_heads * HEAD_DIM]
    for kv_head in range(kv_heads):
        values_ref[rows, head_cols(kv_head)] = biased(
            pair_ref[:, head_cols(kv_heads + kv_head)], bias_ref[kv_head : kv_head + 1, :]
        )


def near_kernel(
    bias_ref, queries_ref, grads_ref, score_ref, own_dprob_ref, live_ref, *refs
):
    pair_refs, (weights_ref, dprob_ref, stats_ref, keys_ref, values_ref) = refs[:-5], refs[-5:]
    tok = pair_refs[0].shape[0]
    for index, pair_ref in enumerate(pair_refs):
        unpack(pair_ref, bias_ref, keys_ref, values_ref, slice(index * tok, (index + 1) * tok))
    blocks = [slice(row, row + BLOCK) for row in range(0, len(pair_refs) * tok, BLOCK)]
    for kv_head in range(bias_ref.shape[0]):
        cols = head_cols(kv_head)
        group = slice(kv_head * GROUP * tok, (kv_head + 1) * GROUP * tok)
        weights_ref[tok:, group] = dot(keys_ref[tok:, cols], queries_ref[group, :HEAD_DIM], 1, 1)
        dprob_ref[tok:, group] = dot(values_ref[tok:, cols], grads_ref[group, :], 1, 1)
        for first in range(group.start, group.stop, PAIR * tok):
            at = slice(first, first + PAIR * tok)
            row_max = None
            for block in blocks:
                score = (score_ref if block.start < tok else weights_ref)[block, at]
                score = score + jnp.concatenate([live_ref[block, :]] * PAIR, axis=1)
                weights_ref[block, at] = score
                part = over_rows(score, jnp.max)
                row_max = part if row_max is None else jnp.maximum(row_max, part)
            row_max = jnp.max(row_max, axis=0, keepdims=True)
            total = jnp.zeros((8, PAIR * tok), jnp.float32)
            delta = jnp.zeros((8, PAIR * tok), jnp.float32)
            for block in blocks:
                dprob = (own_dprob_ref if block.start < tok else dprob_ref)[block, at]
                weights = jnp.exp2((weights_ref[block, at] - row_max) * (SCALE * LOG2E))
                weights_ref[block, at] = weights
                if block.start < tok:
                    dprob_ref[block, at] = dprob
                total = total + over_rows(weights, jnp.sum)
                delta = delta + over_rows(weights * dprob, jnp.sum)
            stats_ref[0:1, at] = row_max
            stats_ref[1:2, at] = jnp.sum(total, axis=0, keepdims=True)
            stats_ref[2:3, at] = jnp.sum(delta, axis=0, keepdims=True)


def last_kernel(slots, first_head, *refs):
    bias_ref, queries_ref, grads_ref, live_ref = refs[:4]
    weights_ref, dprob_ref, stats_ref, near_keys_ref, near_values_ref, pair_ref = refs[4:10]
    probs_ref, dscore_ref, keys_ref, values_ref, sums_ref, own_ref = refs[10:16]
    out_refs, (last_weights_ref, last_dprob_ref) = refs[16:-2], refs[-2:]
    tok = pair_ref.shape[0]
    near = (slots - 1) * tok
    kv_heads = bias_ref.shape[0]
    kv_width = kv_heads * HEAD_DIM
    heads = kv_heads * GROUP
    keys_ref[:near, :] = near_keys_ref[...]
    values_ref[:near, :] = near_values_ref[...]
    unpack(pair_ref, bias_ref, keys_ref, values_ref, slice(near, near + tok))
    near_blocks = [slice(row, row + BLOCK) for row in range(0, near, BLOCK)]
    blocks = [slice(row, row + BLOCK) for row in range(0, tok, BLOCK)]
    for kv_head in range(kv_heads):
        cols = head_cols(kv_head)
        group = slice(kv_head * GROUP * tok, (kv_head + 1) * GROUP * tok)
        last_weights_ref[:, group] = dot(
            keys_ref[near:, cols], queries_ref[group, :HEAD_DIM], 1, 1
        )
        last_dprob_ref[:, group] = dot(values_ref[near:, cols], grads_ref[group, :], 1, 1)
        for first in range(group.start, group.stop, PAIR * tok):
            at = slice(first, first + PAIR * tok)
            near_max = stats_ref[0:1, at]
            row_max = jnp.broadcast_to(near_max, (8, PAIR * tok))
            for block in blocks:
                live = live_ref[near + block.start : near + block.stop, :]
                score = last_weights_ref[block, at] + jnp.concatenate([live] * PAIR, axis=1)
                last_weights_ref[block, at] = score
                row_max = jnp.maximum(row_max, over_rows(score, jnp.max))
            row_max = jnp.max(row_max, axis=0, keepdims=True)
            total = jnp.zeros((8, PAIR * tok), jnp.float32)
            delta = jnp.zeros((8, PAIR * tok), jnp.float32)
            for block in blocks:
                weights = jnp.exp2((last_weights_ref[block, at] - row_max) * (SCALE * LOG2E))
                last_weights_ref[block, at] = weights
                total = total + over_rows(weights, jnp.sum)
                delta = delta + over_rows(weights * last_dprob_ref[block, at], jnp.sum)
            factor = jnp.exp2((near_max - row_max) * (SCALE * LOG2E))
            total = jnp.sum(total, axis=0, keepdims=True) + stats_ref[1:2, at] * factor
            delta = jnp.sum(delta, axis=0, keepdims=True) + stats_ref[2:3, at] * factor
            inverse = 1.0 / total
            delta = delta * inverse
            factor = factor * inverse
            for block in near_blocks:
                probs = weights_ref[block, at] * factor
                probs_ref[block, at] = probs.astype(jnp.bfloat16)
                dscore_ref[block, at] = (probs * (dprob_ref[block, at] - delta)).astype(jnp.bfloat16)
            for block in blocks:
                to = slice(near + block.start, near + block.stop)
                probs = last_weights_ref[block, at] * inverse
                probs_ref[to, at] = probs.astype(jnp.bfloat16)
                dscore = probs * (last_dprob_ref[block, at] - delta)
                dscore_ref[to, at] = dscore.astype(jnp.bfloat16)
        value_term = dot(probs_ref[:, group], grads_ref[group, :], 1, 0)
        key_term = dot(dscore_ref[:, group], queries_ref[group, :], 1, 0)
        over_queries = key_term[:, HEAD_DIM:]
        key_term = key_term[:, :HEAD_DIM] * SCALE
        high = over_queries.astype(jnp.bfloat16)
        low = (over_queries - high.astype(jnp.float32)).astype(jnp.bfloat16)
        all_keys = keys_ref[:, cols]
        query_sums = (dot(high, all_keys, 0, 0) + dot(low, all_keys, 0, 0)) * SCALE
        of_group = slice(kv_head * GROUP, (kv_head + 1) * GROUP)
        sums_ref[of_group, :] = query_sums[first_head + of_group.start : first_head + of_group.stop]
        sums_ref[heads + kv_head : heads + kv_head + 1, :] = jnp.sum(
            value_term, axis=0, keepdims=True
        )
        value_cols = head_cols(kv_heads + kv_head)
        own_ref[:, cols] = key_term[:tok]
        own_ref[:, value_cols] = value_term[:tok]
        for index, slot in enumerate(slot_order(slots)):
            rows = slice(index * tok, (index + 1) * tok)
            if slot:
                out_refs[slot - 1][:, cols] = key_term[rows].astype(jnp.bfloat16)
                out_refs[slot - 1][:, value_cols] = value_term[rows].astype(jnp.bfloat16)


def finish_kernel(probs_ref, dscore_ref, keys_ref, values_ref, *refs):
    passed = (len(refs) - 2) // 2
    attn_ref, qg_ref = refs[passed : passed + 2]
    tok = attn_ref.shape[0]
    kv_heads = keys_ref.shape[1] // HEAD_DIM
    for kv_head in range(kv_heads):
        cols = head_cols(kv_head)
        keys_t = keys_ref[:, cols].T
        values_t = values_ref[:, cols].T
        for pair in range(GROUP // PAIR):
            first = kv_head * GROUP + pair * PAIR
            at = slice(first * tok, (first + PAIR) * tok)
            attn = dot(values_t, probs_ref[:, at], 1, 0).T
            query_grad = (dot(keys_t, dscore_ref[:, at], 1, 0) * SCALE).T
            for n in range(PAIR):
                head = first + n
                rows = slice(n * tok, (n + 1) * tok)
                attn_ref[:, head_cols(head)] = attn[rows].astype(jnp.bfloat16)
                qg_ref[:, head_cols(head)] = query_grad[rows].astype(jnp.bfloat16)


def collect_kernel(batches, parts, whole, *refs):
    sum_refs, own_ref, refs = refs[:parts], refs[parts], refs[parts + 1 :]
    whole_refs, message_refs, (kg_ref, vg_ref, qb_ref, vb_ref) = (
        refs[:whole],
        refs[whole:-4],
        refs[-4:],
    )
    heads, kv_heads = qb_ref.shape[0], vb_ref.shape[0]
    tok, kv_width = kg_ref.shape
    total = sum_refs[0][...]
    for ref in sum_refs[1:]:
        total = total + ref[...]
    query_sums, value_sums = total[:heads], total[heads:]
    term = own_ref[...]
    for ref in whole_refs:
        term = term + ref[...].astype(jnp.float32)
    for ref in message_refs:
        added = ref[tok:, :].astype(jnp.float32)
        high_and_low = added[:, : 2 * HEAD_DIM], added[:, 2 * HEAD_DIM : 4 * HEAD_DIM]
        of_queries, of_values = (both[:, :HEAD_DIM] + both[:, HEAD_DIM:] for both in high_and_low)
        query_sums = query_sums + of_queries[:heads]
        value_sums = value_sums + of_values[:kv_heads]
        term = term + ref[:tok, :].astype(jnp.float32)
    qb_ref[...] = query_sums * (1.0 / batches)
    vb_ref[...] = value_sums * (1.0 / batches)
    term = term.astype(jnp.bfloat16)
    kg_ref[...] = term[:, :kv_width]
    vg_ref[...] = term[:, kv_width:]


def total_kernel(count, *refs):
    parts, refs = refs[:count], refs[count:]
    sent = (len(refs) - 1) // 2
    term_refs, total_ref, message_refs = refs[:sent], refs[sent], refs[sent + 1 :]
    total = parts[0][...]
    for ref in parts[1:]:
        total = total + ref[...]
    total_ref[...] = total
    for term_ref, message_ref in zip(term_refs, message_refs):
        tok = term_ref.shape[0]
        kv_heads = term_ref.shape[1] // (2 * HEAD_DIM)
        rows = message_ref.shape[0] - tok
        message_ref[:tok, :] = term_ref[...]
        message_ref[tok:, : 4 * HEAD_DIM] = added_rows(total, total.shape[0] - kv_heads, rows)


def added_rows(total, heads, rows):
    high = total.astype(jnp.bfloat16).astype(jnp.float32)
    both = jnp.concatenate([high, total - high], axis=1)
    blocks = [both[:heads], both[heads:]]
    blocks = [
        jnp.concatenate([block, jnp.zeros((rows - block.shape[0], 2 * HEAD_DIM), jnp.float32)])
        if block.shape[0] < rows
        else block
        for block in blocks
    ]
    return jnp.concatenate(blocks, axis=1).astype(jnp.bfloat16)


def total_with(parts, terms):
    rows = -(-parts[0].shape[0] * GROUP // (GROUP + 1) // 16) * 16
    total, *messages = pl.pallas_call(
        functools.partial(total_kernel, len(parts)),
        out_shape=[shape(parts[0].shape, parts[0].dtype)]
        + [shape((term.shape[0] + rows, term.shape[1]), term.dtype) for term in terms],
        in_specs=[VMEM] * (len(parts) + len(terms)),
        out_specs=[VMEM] * (1 + len(terms)),
        compiler_params=params(8),
        cost_estimate=pl.CostEstimate(flops=parts[0].size, bytes_accessed=0, transcendentals=0),
        name="total",
    )(*parts, *terms)
    return total, messages


def exchange(axis, part):
    return [part] + [fetch(part, axis, slot) for slot in range(1, lax.axis_size(axis))]


def attend(first_head, bias, queries, grads, score, own_dprob, live, pairs):
    ctx = len(pairs)
    tok = pairs[0].shape[0]
    kv_width = bias.shape[0] * HEAD_DIM
    columns = queries.shape[0]
    rows = ctx * tok
    near = rows - tok
    near_slots = slot_order(ctx)[:-1]
    weights, dprob, stats, near_keys, near_values = pl.pallas_call(
        near_kernel,
        out_shape=[
            shape((near, columns), jnp.float32),
            shape((near, columns), jnp.float32),
            shape((8, columns), jnp.float32),
            shape((near, kv_width), jnp.bfloat16),
            shape((near, kv_width), jnp.bfloat16),
        ],
        in_specs=[VMEM] * (6 + len(near_slots)),
        out_specs=[VMEM] * 5,
        compiler_params=params(20 if ctx < 8 else 48),
        cost_estimate=pl.CostEstimate(
            flops=4 * near * columns * HEAD_DIM,
            bytes_accessed=8 * near * columns,
            transcendentals=near * columns,
        ),
        name="near",
    )(bias, queries, grads, score, own_dprob, live, *[pairs[slot] for slot in near_slots])
    terms = [shape((tok, 2 * kv_width), jnp.bfloat16)] * (ctx - 1)
    return pl.pallas_call(
        functools.partial(last_kernel, ctx, first_head),
        out_shape=[
            shape((rows, columns), jnp.bfloat16),
            shape((rows, columns), jnp.bfloat16),
            shape((rows, kv_width), jnp.bfloat16),
            shape((rows, kv_width), jnp.bfloat16),
            shape((bias.shape[0] * (GROUP + 1), HEAD_DIM), jnp.float32),
            shape((tok, 2 * kv_width), jnp.float32),
        ]
        + terms,
        in_specs=[VMEM] * 10,
        out_specs=[VMEM] * (6 + len(terms)),
        scratch_shapes=[pltpu.VMEM((tok, columns), jnp.float32)] * 2,
        compiler_params=params(24 if ctx < 8 else 48),
        cost_estimate=pl.CostEstimate(
            flops=4 * rows * columns * HEAD_DIM,
            bytes_accessed=4 * rows * columns,
            transcendentals=tok * columns,
        ),
        name="last",
    )(bias, queries, grads, live, weights, dprob, stats, near_keys, near_values, pairs[ctx // 2])


def joined(place, parts):
    if place < 4:
        return jnp.concatenate(parts, axis=1)
    cut, axis = (GROUP, 0) if place == 4 else (HEAD_DIM, 1)
    pieces = [jnp.split(part, [cut], axis=axis) for part in parts]
    return jnp.concatenate([piece[n] for n in range(2) for piece in pieces], axis=axis)


def shards(q_proj, q_bias, k_proj, v_proj, v_bias, dout, lengths):
    _, tok, width = q_proj.shape
    kv_width = k_proj.shape[2]
    heads = width // HEAD_DIM
    kv_heads = kv_width // HEAD_DIM
    ctx = lax.axis_size("ctx")
    batches = lax.axis_size("dp")
    rows = ctx * tok
    columns = heads * tok
    pair = jnp.concatenate([k_proj[0], v_proj[0]], axis=1)
    pairs = [pair] + [fetch(pair, "ctx", slot) for slot in range(1, ctx)]
    prepared = pl.pallas_call(
        functools.partial(prepare_kernel, ctx),
        out_shape=[
            shape((kv_heads, HEAD_DIM), jnp.bfloat16),
            shape((columns, 2 * HEAD_DIM), jnp.bfloat16),
            shape((columns, HEAD_DIM), jnp.bfloat16),
            shape((tok, columns), jnp.float32),
            shape((tok, columns), jnp.float32),
            shape((rows, tok), jnp.float32),
        ],
        in_specs=[SMEM] + [VMEM] * 5,
        out_specs=[VMEM] * 6,
        compiler_params=params(16),
        cost_estimate=pl.CostEstimate(
            flops=4 * tok * tok * width, bytes_accessed=16 * tok * width, transcendentals=0
        ),
        name="prepare",
    )(
        lengths,
        pair,
        q_bias.reshape(heads, HEAD_DIM),
        v_bias.reshape(kv_heads, HEAD_DIM),
        q_proj[0],
        dout[0],
    )
    bias, queries, grads, score, own_dprob, live = prepared
    if ctx < 8:
        made = attend(0, bias, queries, grads, score, own_dprob, live, pairs)
    else:
        made = [
            attend(
                kv_head * GROUP,
                bias[kv_head : kv_head + 1],
                *(part[at] for part in (queries, grads)),
                *(part[:, at] for part in (score, own_dprob)),
                live,
                [
                    jnp.concatenate(
                        [part[:, head_cols(kv_head)], part[:, head_cols(kv_heads + kv_head)]], axis=1
                    )
                    for part in pairs
                ],
            )
            for kv_head in range(kv_heads)
            for at in [slice(kv_head * GROUP * tok, (kv_head + 1) * GROUP * tok)]
        ]
        made = [joined(n, parts) for n, parts in enumerate(zip(*made))]
    probs, dscore, all_keys, all_values, sums, own, *terms = made
    half = ctx // 2
    far = range(half, ctx)
    early = [send_back(terms[slot - 1], slot) for slot in far]
    attn, q_grad, early[0] = pl.pallas_call(
        finish_kernel,
        out_shape=[
            shape((tok, width), jnp.bfloat16),
            shape((tok, width), jnp.bfloat16),
        ]
        + [shape(early[0].shape, early[0].dtype)],
        in_specs=[VMEM] * 4 + [ANY],
        out_specs=[VMEM] * 2 + [ANY],
        input_output_aliases={4: 2},
        compiler_params=params(24),
        cost_estimate=pl.CostEstimate(
            flops=16 * rows * tok * width, bytes_accessed=0, transcendentals=0
        ),
        name="finish",
    )(probs, dscore, all_keys, all_values, early[0])
    sums, messages = total_with(exchange("dp", sums), terms[: half - 1])
    late = [send_back(message, slot) for slot, message in enumerate(messages, 1)]
    sums = [sums] + [send_back(sums, slot) for slot in far]
    k_grad, v_grad, q_sum, v_sum = pl.pallas_call(
        functools.partial(collect_kernel, batches, len(sums), len(early)),
        out_shape=[
            shape((tok, kv_width), jnp.bfloat16),
            shape((tok, kv_width), jnp.bfloat16),
            shape((heads, HEAD_DIM), jnp.float32),
            shape((kv_heads, HEAD_DIM), jnp.float32),
        ],
        in_specs=[VMEM] * (len(sums) + 1 + len(early) + len(late)),
        out_specs=[VMEM] * 4,
        compiler_params=params(8),
        cost_estimate=pl.CostEstimate(
            flops=8 * tok * kv_width, bytes_accessed=16 * tok * kv_width, transcendentals=0
        ),
        name="collect",
    )(*sums, own, *early, *late)
    return (
        attn[None],
        q_grad[None],
        k_grad[None],
        v_grad[None],
        q_sum.reshape(width),
        v_sum.reshape(kv_width),
    )


def solution(mesh):
    tokens = P("dp", "ctx", "tp")
    return jax.shard_map(
        shards,
        mesh=mesh,
        in_specs=(tokens, P("tp"), tokens, tokens, P("tp"), tokens, P("dp", None)),
        out_specs=(tokens, tokens, tokens, tokens, P("tp"), P("tp")),
        check_vma=False,
    )
```

```python
import functools

import jax
import jax.numpy as jnp
from jax import lax
from jax.experimental import pallas as pl
from jax.experimental.pallas import tpu as pltpu
from jax.sharding import PartitionSpec as P

HEAD_DIM = 128
HEADS = 32
KV_HEADS = 4
GROUP = HEADS // KV_HEADS
PAIR = 2
BLOCK = 32
SCALE = HEAD_DIM ** (-0.5)
LOG2E = 1.4426950408889634
NEGATIVE = -1e30
VMEM = pl.BlockSpec(memory_space=pltpu.VMEM)
ANY = pl.BlockSpec(memory_space=pl.ANY)
SMEM = pl.BlockSpec(memory_space=pltpu.SMEM)


def dot(left, right, left_dim, right_dim):
    return lax.dot_general(
        left, right, (((left_dim,), (right_dim,)), ((), ())), preferred_element_type=jnp.float32
    )


def head_cols(head):
    return slice(head * HEAD_DIM, (head + 1) * HEAD_DIM)


def shape(dims, dtype):
    return jax.ShapeDtypeStruct(dims, dtype)


def params(mebibytes):
    return pltpu.CompilerParams(vmem_limit_bytes=mebibytes * 1024 * 1024)


def biased(values, bias):
    return (values.astype(jnp.float32) + bias.astype(jnp.float32)).astype(jnp.bfloat16)


def source_of(rank, slot, size):
    if size & (size - 1):
        return (rank + size - slot) % size
    return rank ^ slot


def slot_order(size):
    return [slot for slot in range(size) if slot != size // 2] + [size // 2]


def fetch(array, axis, slot):
    size = lax.axis_size(axis)
    return lax.ppermute(array, axis, [(source_of(i, slot, size), i) for i in range(size)])


def send_back(array, slot):
    size = lax.axis_size("ctx")
    return lax.ppermute(array, "ctx", [(i, source_of(i, slot, size)) for i in range(size)])


def prepare_kernel(
    slots, len_ref, pair_ref, qb_ref, vb_ref, q_ref, g_ref, bias_ref, queries_ref, grads_ref,
    score_ref, dprob_ref, live_ref,
):
    tok = q_ref.shape[0]
    kv_heads = vb_ref.shape[0]
    rank = lax.axis_index("ctx")
    query_pos = rank * tok + lax.broadcasted_iota(jnp.int32, (1, tok), 1)
    start = jnp.zeros((1, tok), jnp.int32)
    end = jnp.int32(0)
    for doc in range(len_ref.shape[1]):
        length = len_ref[0, doc]
        end = end + length
        start = start + jnp.where(query_pos >= end, length, 0)
    offsets = lax.broadcasted_iota(jnp.int32, (tok, tok), 0)
    for index, slot in enumerate(slot_order(slots)):
        key_pos = source_of(rank, slot, slots) * tok + offsets
        live = (key_pos >= start) & (key_pos <= query_pos)
        live_ref[index * tok : (index + 1) * tok, :] = jnp.where(live, 0.0, NEGATIVE)
    bias_ref[...] = vb_ref[...]
    column = lax.broadcasted_iota(jnp.int32, (tok, HEAD_DIM), 1)
    for kv_head in range(kv_heads):
        keys = pair_ref[:, head_cols(kv_head)]
        values = biased(pair_ref[:, head_cols(kv_heads + kv_head)], vb_ref[kv_head : kv_head + 1, :])
        for head in range(kv_head * GROUP, (kv_head + 1) * GROUP):
            at = slice(head * tok, (head + 1) * tok)
            queries_ref[at, :HEAD_DIM] = biased(q_ref[:, head_cols(head)], qb_ref[head : head + 1, :])
            queries_ref[at, HEAD_DIM:] = (column == head).astype(jnp.bfloat16)
            grads_ref[at, :] = g_ref[:, head_cols(head)]
        rows = slice(kv_head * GROUP * tok, (kv_head + 1) * GROUP * tok)
        score_ref[:, rows] = dot(keys, queries_ref[rows, :HEAD_DIM], 1, 1)
        dprob_ref[:, rows] = dot(values, grads_ref[rows, :], 1, 1)


def over_rows(array, reduce):
    return reduce(array.reshape(-1, 8, array.shape[-1]), axis=0)


def unpack(pair_ref, bias_ref, keys_ref, values_ref, rows):
    kv_heads = bias_ref.shape[0]
    keys_ref[rows, :] = pair_ref[:, : kv_heads * HEAD_DIM]
    for kv_head in range(kv_heads):
        values_ref[rows, head_cols(kv_head)] = biased(
            pair_ref[:, head_cols(kv_heads + kv_head)], bias_ref[kv_head : kv_head + 1, :]
        )


def near_kernel(
    bias_ref, queries_ref, grads_ref, score_ref, own_dprob_ref, live_ref, *refs
):
    pair_refs, (weights_ref, dprob_ref, stats_ref, keys_ref, values_ref) = refs[:-5], refs[-5:]
    tok = pair_refs[0].shape[0]
    for index, pair_ref in enumerate(pair_refs):
        unpack(pair_ref, bias_ref, keys_ref, values_ref, slice(index * tok, (index + 1) * tok))
    blocks = [slice(row, row + BLOCK) for row in range(0, len(pair_refs) * tok, BLOCK)]
    for kv_head in range(bias_ref.shape[0]):
        cols = head_cols(kv_head)
        group = slice(kv_head * GROUP * tok, (kv_head + 1) * GROUP * tok)
        weights_ref[tok:, group] = dot(keys_ref[tok:, cols], queries_ref[group, :HEAD_DIM], 1, 1)
        dprob_ref[tok:, group] = dot(values_ref[tok:, cols], grads_ref[group, :], 1, 1)
        for first in range(group.start, group.stop, PAIR * tok):
            at = slice(first, first + PAIR * tok)
            row_max = None
            for block in blocks:
                score = (score_ref if block.start < tok else weights_ref)[block, at]
                score = score + jnp.concatenate([live_ref[block, :]] * PAIR, axis=1)
                weights_ref[block, at] = score
                part = over_rows(score, jnp.max)
                row_max = part if row_max is None else jnp.maximum(row_max, part)
            row_max = jnp.max(row_max, axis=0, keepdims=True)
            total = jnp.zeros((8, PAIR * tok), jnp.float32)
            delta = jnp.zeros((8, PAIR * tok), jnp.float32)
            for block in blocks:
                dprob = (own_dprob_ref if block.start < tok else dprob_ref)[block, at]
                weights = jnp.exp2((weights_ref[block, at] - row_max) * (SCALE * LOG2E))
                weights_ref[block, at] = weights
                if block.start < tok:
                    dprob_ref[block, at] = dprob
                total = total + over_rows(weights, jnp.sum)
                delta = delta + over_rows(weights * dprob, jnp.sum)
            stats_ref[0:1, at] = row_max
            stats_ref[1:2, at] = jnp.sum(total, axis=0, keepdims=True)
            stats_ref[2:3, at] = jnp.sum(delta, axis=0, keepdims=True)


def last_kernel(slots, first_head, *refs):
    bias_ref, queries_ref, grads_ref, live_ref = refs[:4]
    weights_ref, dprob_ref, stats_ref, near_keys_ref, near_values_ref, pair_ref = refs[4:10]
    probs_ref, dscore_ref, keys_ref, values_ref, sums_ref, own_ref = refs[10:16]
    out_refs = refs[16 : 16 + slots - 1]
    last_weights_ref, last_dprob_ref = refs[16 + slots - 1 :]
    tok = pair_ref.shape[0]
    near = (slots - 1) * tok
    kv_heads = bias_ref.shape[0]
    kv_width = kv_heads * HEAD_DIM
    heads = kv_heads * GROUP
    keys_ref[:near, :] = near_keys_ref[...]
    values_ref[:near, :] = near_values_ref[...]
    unpack(pair_ref, bias_ref, keys_ref, values_ref, slice(near, near + tok))
    near_blocks = [slice(row, row + BLOCK) for row in range(0, near, BLOCK)]
    blocks = [slice(row, row + BLOCK) for row in range(0, tok, BLOCK)]
    for kv_head in range(kv_heads):
        cols = head_cols(kv_head)
        group = slice(kv_head * GROUP * tok, (kv_head + 1) * GROUP * tok)
        last_weights_ref[:, group] = dot(
            keys_ref[near:, cols], queries_ref[group, :HEAD_DIM], 1, 1
        )
        last_dprob_ref[:, group] = dot(values_ref[near:, cols], grads_ref[group, :], 1, 1)
        for first in range(group.start, group.stop, PAIR * tok):
            at = slice(first, first + PAIR * tok)
            near_max = stats_ref[0:1, at]
            row_max = jnp.broadcast_to(near_max, (8, PAIR * tok))
            for block in blocks:
                live = live_ref[near + block.start : near + block.stop, :]
                score = last_weights_ref[block, at] + jnp.concatenate([live] * PAIR, axis=1)
                last_weights_ref[block, at] = score
                row_max = jnp.maximum(row_max, over_rows(score, jnp.max))
            row_max = jnp.max(row_max, axis=0, keepdims=True)
            total = jnp.zeros((8, PAIR * tok), jnp.float32)
            delta = jnp.zeros((8, PAIR * tok), jnp.float32)
            for block in blocks:
                weights = jnp.exp2((last_weights_ref[block, at] - row_max) * (SCALE * LOG2E))
                last_weights_ref[block, at] = weights
                total = total + over_rows(weights, jnp.sum)
                delta = delta + over_rows(weights * last_dprob_ref[block, at], jnp.sum)
            factor = jnp.exp2((near_max - row_max) * (SCALE * LOG2E))
            total = jnp.sum(total, axis=0, keepdims=True) + stats_ref[1:2, at] * factor
            delta = jnp.sum(delta, axis=0, keepdims=True) + stats_ref[2:3, at] * factor
            inverse = 1.0 / total
            delta = delta * inverse
            factor = factor * inverse
            for block in near_blocks:
                probs = weights_ref[block, at] * factor
                probs_ref[block, at] = probs.astype(jnp.bfloat16)
                dscore_ref[block, at] = (probs * (dprob_ref[block, at] - delta)).astype(jnp.bfloat16)
            for block in blocks:
                to = slice(near + block.start, near + block.stop)
                probs = last_weights_ref[block, at] * inverse
                probs_ref[to, at] = probs.astype(jnp.bfloat16)
                dscore = probs * (last_dprob_ref[block, at] - delta)
                dscore_ref[to, at] = dscore.astype(jnp.bfloat16)
        value_term = dot(probs_ref[:, group], grads_ref[group, :], 1, 0)
        key_term = dot(dscore_ref[:, group], queries_ref[group, :], 1, 0)
        over_queries = key_term[:, HEAD_DIM:]
        key_term = key_term[:, :HEAD_DIM] * SCALE
        high = over_queries.astype(jnp.bfloat16)
        low = (over_queries - high.astype(jnp.float32)).astype(jnp.bfloat16)
        all_keys = keys_ref[:, cols]
        query_sums = (dot(high, all_keys, 0, 0) + dot(low, all_keys, 0, 0)) * SCALE
        of_group = slice(kv_head * GROUP, (kv_head + 1) * GROUP)
        sums_ref[of_group, :] = query_sums[first_head + of_group.start : first_head + of_group.stop]
        sums_ref[heads + kv_head : heads + kv_head + 1, :] = jnp.sum(
            value_term, axis=0, keepdims=True
        )
        value_cols = head_cols(kv_heads + kv_head)
        own_ref[:, cols] = key_term[:tok]
        own_ref[:, value_cols] = value_term[:tok]
        for index, slot in enumerate(slot_order(slots)):
            if slot == 0:
                continue
            rows = slice(index * tok, (index + 1) * tok)
            out_refs[slot - 1][:, cols] = key_term[rows].astype(jnp.bfloat16)
            out_refs[slot - 1][:, value_cols] = value_term[rows].astype(jnp.bfloat16)


def finish_kernel(probs_ref, dscore_ref, keys_ref, values_ref, *refs):
    passed = (len(refs) - 2) // 2
    attn_ref, qg_ref = refs[passed : passed + 2]
    tok = attn_ref.shape[0]
    kv_heads = keys_ref.shape[1] // HEAD_DIM
    for kv_head in range(kv_heads):
        cols = head_cols(kv_head)
        keys_t = keys_ref[:, cols].T
        values_t = values_ref[:, cols].T
        for pair in range(GROUP // PAIR):
            first = kv_head * GROUP + pair * PAIR
            at = slice(first * tok, (first + PAIR) * tok)
            attn = dot(values_t, probs_ref[:, at], 1, 0).T
            query_grad = (dot(keys_t, dscore_ref[:, at], 1, 0) * SCALE).T
            for n in range(PAIR):
                head = first + n
                rows = slice(n * tok, (n + 1) * tok)
                attn_ref[:, head_cols(head)] = attn[rows].astype(jnp.bfloat16)
                qg_ref[:, head_cols(head)] = query_grad[rows].astype(jnp.bfloat16)


def collect_kernel(batches, parts, *refs):
    sum_refs, term_refs, (kg_ref, vg_ref, qb_ref, vb_ref) = refs[:parts], refs[parts:-4], refs[-4:]
    heads = qb_ref.shape[0]
    kv_width = kg_ref.shape[1]
    total = sum_refs[0][...]
    for ref in sum_refs[1:]:
        total = total + ref[...]
    total = total * (1.0 / batches)
    qb_ref[...] = total[:heads]
    vb_ref[...] = total[heads:]
    term = term_refs[0][...]
    for ref in term_refs[1:]:
        term = term + ref[...].astype(jnp.float32)
    term = term.astype(jnp.bfloat16)
    kg_ref[...] = term[:, :kv_width]
    vg_ref[...] = term[:, kv_width:]


def total_kernel(*refs):
    total = refs[0][...]
    for ref in refs[1:-1]:
        total = total + ref[...]
    refs[-1][...] = total


def exchange(axis, part):
    return [part] + [fetch(part, axis, slot) for slot in range(1, lax.axis_size(axis))]


def attend(first_head, bias, queries, grads, score, own_dprob, live, pairs):
    ctx = len(pairs)
    tok = pairs[0].shape[0]
    kv_width = bias.shape[0] * HEAD_DIM
    columns = queries.shape[0]
    rows = ctx * tok
    near = rows - tok
    near_slots = slot_order(ctx)[:-1]
    weights, dprob, stats, near_keys, near_values = pl.pallas_call(
        near_kernel,
        out_shape=[
            shape((near, columns), jnp.float32),
            shape((near, columns), jnp.float32),
            shape((8, columns), jnp.float32),
            shape((near, kv_width), jnp.bfloat16),
            shape((near, kv_width), jnp.bfloat16),
        ],
        in_specs=[VMEM] * (6 + len(near_slots)),
        out_specs=[VMEM] * 5,
        compiler_params=params(20 if ctx < 8 else 48),
        cost_estimate=pl.CostEstimate(
            flops=4 * near * columns * HEAD_DIM,
            bytes_accessed=8 * near * columns,
            transcendentals=near * columns,
        ),
        name="near",
    )(bias, queries, grads, score, own_dprob, live, *[pairs[slot] for slot in near_slots])
    term = shape((tok, 2 * kv_width), jnp.bfloat16)
    return pl.pallas_call(
        functools.partial(last_kernel, ctx, first_head),
        out_shape=[
            shape((rows, columns), jnp.bfloat16),
            shape((rows, columns), jnp.bfloat16),
            shape((rows, kv_width), jnp.bfloat16),
            shape((rows, kv_width), jnp.bfloat16),
            shape((bias.shape[0] * (GROUP + 1), HEAD_DIM), jnp.float32),
            shape((tok, 2 * kv_width), jnp.float32),
        ]
        + [term] * (ctx - 1),
        in_specs=[VMEM] * 10,
        out_specs=[VMEM] * (6 + ctx - 1),
        scratch_shapes=[pltpu.VMEM((tok, columns), jnp.float32)] * 2,
        compiler_params=params(24 if ctx < 8 else 48),
        cost_estimate=pl.CostEstimate(
            flops=4 * rows * columns * HEAD_DIM,
            bytes_accessed=4 * rows * columns,
            transcendentals=tok * columns,
        ),
        name="last",
    )(bias, queries, grads, live, weights, dprob, stats, near_keys, near_values, pairs[ctx // 2])


def joined(place, parts):
    if place < 4:
        return jnp.concatenate(parts, axis=1)
    cut, axis = (GROUP, 0) if place == 4 else (HEAD_DIM, 1)
    pieces = [jnp.split(part, [cut], axis=axis) for part in parts]
    return jnp.concatenate([piece[n] for n in range(2) for piece in pieces], axis=axis)


def shards(q_proj, q_bias, k_proj, v_proj, v_bias, dout, lengths):
    _, tok, width = q_proj.shape
    kv_width = k_proj.shape[2]
    heads = width // HEAD_DIM
    kv_heads = kv_width // HEAD_DIM
    ctx = lax.axis_size("ctx")
    batches = lax.axis_size("dp")
    rows = ctx * tok
    columns = heads * tok
    pair = jnp.concatenate([k_proj[0], v_proj[0]], axis=1)
    pairs = [pair] + [fetch(pair, "ctx", slot) for slot in range(1, ctx)]
    prepared = pl.pallas_call(
        functools.partial(prepare_kernel, ctx),
        out_shape=[
            shape((kv_heads, HEAD_DIM), jnp.bfloat16),
            shape((columns, 2 * HEAD_DIM), jnp.bfloat16),
            shape((columns, HEAD_DIM), jnp.bfloat16),
            shape((tok, columns), jnp.float32),
            shape((tok, columns), jnp.float32),
            shape((rows, tok), jnp.float32),
        ],
        in_specs=[SMEM] + [VMEM] * 5,
        out_specs=[VMEM] * 6,
        compiler_params=params(16),
        cost_estimate=pl.CostEstimate(
            flops=4 * tok * tok * width, bytes_accessed=16 * tok * width, transcendentals=0
        ),
        name="prepare",
    )(
        lengths,
        pair,
        q_bias.reshape(heads, HEAD_DIM),
        v_bias.reshape(kv_heads, HEAD_DIM),
        q_proj[0],
        dout[0],
    )
    bias, queries, grads, score, own_dprob, live = prepared
    if ctx < 8:
        made = attend(0, bias, queries, grads, score, own_dprob, live, pairs)
    else:
        made = [
            attend(
                kv_head * GROUP,
                bias[kv_head : kv_head + 1],
                *(part[at] for part in (queries, grads)),
                *(part[:, at] for part in (score, own_dprob)),
                live,
                [
                    jnp.concatenate(
                        [part[:, head_cols(kv_head)], part[:, head_cols(kv_heads + kv_head)]], axis=1
                    )
                    for part in pairs
                ],
            )
            for kv_head in range(kv_heads)
            for at in [slice(kv_head * GROUP * tok, (kv_head + 1) * GROUP * tok)]
        ]
        made = [joined(n, parts) for n, parts in enumerate(zip(*made))]
    probs, dscore, all_keys, all_values, sums, own, *terms = made
    term = shape((tok, 2 * kv_width), jnp.bfloat16)
    half = ctx // 2
    back = {slot: send_back(terms[slot - 1], slot) for slot in range(1, ctx)}
    tied = [half]
    attn, q_grad, *passed = pl.pallas_call(
        finish_kernel,
        out_shape=[
            shape((tok, width), jnp.bfloat16),
            shape((tok, width), jnp.bfloat16),
        ]
        + [shape((tok, 2 * kv_width), jnp.bfloat16)] * len(tied),
        in_specs=[VMEM] * 4 + [ANY] * len(tied),
        out_specs=[VMEM] * 2 + [ANY] * len(tied),
        input_output_aliases={4 + n: 2 + n for n in range(len(tied))},
        compiler_params=params(24),
        cost_estimate=pl.CostEstimate(
            flops=16 * rows * tok * width, bytes_accessed=0, transcendentals=0
        ),
        name="finish",
    )(probs, dscore, all_keys, all_values, *[back[slot] for slot in tied])
    parts = exchange("dp", sums)
    sums = pl.pallas_call(
        total_kernel,
        out_shape=shape(sums.shape, sums.dtype),
        in_specs=[VMEM] * len(parts),
        out_specs=VMEM,
        compiler_params=params(4),
        cost_estimate=pl.CostEstimate(flops=sums.size, bytes_accessed=0, transcendentals=0),
        name="total",
    )(*parts)
    sums = exchange("ctx", sums)
    back.update(zip(tied, passed))
    k_grad, v_grad, q_sum, v_sum = pl.pallas_call(
        functools.partial(collect_kernel, batches, len(sums)),
        out_shape=[
            shape((tok, kv_width), jnp.bfloat16),
            shape((tok, kv_width), jnp.bfloat16),
            shape((heads, HEAD_DIM), jnp.float32),
            shape((kv_heads, HEAD_DIM), jnp.float32),
        ],
        in_specs=[VMEM] * (len(sums) + 1 + len(back)),
        out_specs=[VMEM] * 4,
        compiler_params=params(8),
        cost_estimate=pl.CostEstimate(
            flops=8 * tok * kv_width, bytes_accessed=16 * tok * kv_width, transcendentals=0
        ),
        name="collect",
    )(*sums, own, *[back[slot] for slot in sorted(back, reverse=True)])
    return (
        attn[None],
        q_grad[None],
        k_grad[None],
        v_grad[None],
        q_sum.reshape(width),
        v_sum.reshape(kv_width),
    )


def solution(mesh):
    tokens = P("dp", "ctx", "tp")
    return jax.shard_map(
        shards,
        mesh=mesh,
        in_specs=(tokens, P("tp"), tokens, tokens, P("tp"), tokens, P("dp", None)),
        out_specs=(tokens, tokens, tokens, tokens, P("tp"), P("tp")),
        check_vma=False,
    )
```

```python
import functools

import jax
import jax.numpy as jnp
from jax import lax
from jax.experimental import pallas as pl
from jax.experimental.pallas import tpu as pltpu
from jax.sharding import PartitionSpec as P

HEAD_DIM = 128
HEADS = 32
KV_HEADS = 4
GROUP = HEADS // KV_HEADS
PAIR = 2
BLOCK = 32
SCALE = HEAD_DIM ** (-0.5)
LOG2E = 1.4426950408889634
NEGATIVE = -1e30
VMEM = pl.BlockSpec(memory_space=pltpu.VMEM)
ANY = pl.BlockSpec(memory_space=pl.ANY)
SMEM = pl.BlockSpec(memory_space=pltpu.SMEM)


def dot(left, right, left_dim, right_dim):
    return lax.dot_general(
        left, right, (((left_dim,), (right_dim,)), ((), ())), preferred_element_type=jnp.float32
    )


def head_cols(head):
    return slice(head * HEAD_DIM, (head + 1) * HEAD_DIM)


def shape(dims, dtype):
    return jax.ShapeDtypeStruct(dims, dtype)


def params(mebibytes):
    return pltpu.CompilerParams(vmem_limit_bytes=mebibytes * 1024 * 1024)


def biased(values, bias):
    return (values.astype(jnp.float32) + bias.astype(jnp.float32)).astype(jnp.bfloat16)


def source_of(rank, slot, size):
    if size & (size - 1):
        return (rank + size - slot) % size
    return rank ^ slot


def slot_order(size):
    return [slot for slot in range(size) if slot != size // 2] + [size // 2]


def fetch(array, axis, slot):
    size = lax.axis_size(axis)
    return lax.ppermute(array, axis, [(source_of(i, slot, size), i) for i in range(size)])


def send_back(array, slot):
    size = lax.axis_size("ctx")
    return lax.ppermute(array, "ctx", [(i, source_of(i, slot, size)) for i in range(size)])


def prepare_kernel(
    slots, len_ref, pair_ref, qb_ref, vb_ref, q_ref, g_ref, bias_ref, queries_ref, grads_ref,
    score_ref, dprob_ref, live_ref,
):
    tok = q_ref.shape[0]
    kv_heads = vb_ref.shape[0]
    rank = lax.axis_index("ctx")
    query_pos = rank * tok + lax.broadcasted_iota(jnp.int32, (1, tok), 1)
    start = jnp.zeros((1, tok), jnp.int32)
    end = jnp.int32(0)
    for doc in range(len_ref.shape[1]):
        length = len_ref[0, doc]
        end = end + length
        start = start + jnp.where(query_pos >= end, length, 0)
    offsets = lax.broadcasted_iota(jnp.int32, (tok, tok), 0)
    for index, slot in enumerate(slot_order(slots)):
        key_pos = source_of(rank, slot, slots) * tok + offsets
        live = (key_pos >= start) & (key_pos <= query_pos)
        live_ref[index * tok : (index + 1) * tok, :] = jnp.where(live, 0.0, NEGATIVE)
    bias_ref[...] = vb_ref[...]
    column = lax.broadcasted_iota(jnp.int32, (tok, HEAD_DIM), 1)
    for kv_head in range(kv_heads):
        keys = pair_ref[:, head_cols(kv_head)]
        values = biased(pair_ref[:, head_cols(kv_heads + kv_head)], vb_ref[kv_head : kv_head + 1, :])
        for head in range(kv_head * GROUP, (kv_head + 1) * GROUP):
            at = slice(head * tok, (head + 1) * tok)
            queries_ref[at, :HEAD_DIM] = biased(q_ref[:, head_cols(head)], qb_ref[head : head + 1, :])
            queries_ref[at, HEAD_DIM:] = (column == head).astype(jnp.bfloat16)
            grads_ref[at, :] = g_ref[:, head_cols(head)]
        rows = slice(kv_head * GROUP * tok, (kv_head + 1) * GROUP * tok)
        score_ref[:, rows] = dot(keys, queries_ref[rows, :HEAD_DIM], 1, 1)
        dprob_ref[:, rows] = dot(values, grads_ref[rows, :], 1, 1)


def over_rows(array, reduce):
    return reduce(array.reshape(-1, 8, array.shape[-1]), axis=0)


def unpack(pair_ref, bias_ref, keys_ref, values_ref, rows):
    kv_heads = bias_ref.shape[0]
    keys_ref[rows, :] = pair_ref[:, : kv_heads * HEAD_DIM]
    for kv_head in range(kv_heads):
        values_ref[rows, head_cols(kv_head)] = biased(
            pair_ref[:, head_cols(kv_heads + kv_head)], bias_ref[kv_head : kv_head + 1, :]
        )


def near_kernel(
    bias_ref, queries_ref, grads_ref, score_ref, own_dprob_ref, live_ref, *refs
):
    pair_refs, (weights_ref, dprob_ref, stats_ref, keys_ref, values_ref) = refs[:-5], refs[-5:]
    tok = pair_refs[0].shape[0]
    for index, pair_ref in enumerate(pair_refs):
        unpack(pair_ref, bias_ref, keys_ref, values_ref, slice(index * tok, (index + 1) * tok))
    blocks = [slice(row, row + BLOCK) for row in range(0, len(pair_refs) * tok, BLOCK)]
    for kv_head in range(bias_ref.shape[0]):
        cols = head_cols(kv_head)
        group = slice(kv_head * GROUP * tok, (kv_head + 1) * GROUP * tok)
        weights_ref[tok:, group] = dot(keys_ref[tok:, cols], queries_ref[group, :HEAD_DIM], 1, 1)
        dprob_ref[tok:, group] = dot(values_ref[tok:, cols], grads_ref[group, :], 1, 1)
        for first in range(group.start, group.stop, PAIR * tok):
            at = slice(first, first + PAIR * tok)
            row_max = None
            for block in blocks:
                score = (score_ref if block.start < tok else weights_ref)[block, at]
                score = score + jnp.concatenate([live_ref[block, :]] * PAIR, axis=1)
                weights_ref[block, at] = score
                part = over_rows(score, jnp.max)
                row_max = part if row_max is None else jnp.maximum(row_max, part)
            row_max = jnp.max(row_max, axis=0, keepdims=True)
            total = jnp.zeros((8, PAIR * tok), jnp.float32)
            delta = jnp.zeros((8, PAIR * tok), jnp.float32)
            for block in blocks:
                dprob = (own_dprob_ref if block.start < tok else dprob_ref)[block, at]
                weights = jnp.exp2((weights_ref[block, at] - row_max) * (SCALE * LOG2E))
                weights_ref[block, at] = weights
                if block.start < tok:
                    dprob_ref[block, at] = dprob
                total = total + over_rows(weights, jnp.sum)
                delta = delta + over_rows(weights * dprob, jnp.sum)
            stats_ref[0:1, at] = row_max
            stats_ref[1:2, at] = jnp.sum(total, axis=0, keepdims=True)
            stats_ref[2:3, at] = jnp.sum(delta, axis=0, keepdims=True)


def last_kernel(slots, first_head, *refs):
    bias_ref, queries_ref, grads_ref, live_ref = refs[:4]
    weights_ref, dprob_ref, stats_ref, near_keys_ref, near_values_ref, pair_ref = refs[4:10]
    probs_ref, dscore_ref, keys_ref, values_ref, sums_ref, own_ref = refs[10:16]
    out_refs = refs[16 : 16 + slots - 1]
    last_weights_ref, last_dprob_ref = refs[16 + slots - 1 :]
    tok = pair_ref.shape[0]
    near = (slots - 1) * tok
    kv_heads = bias_ref.shape[0]
    kv_width = kv_heads * HEAD_DIM
    heads = kv_heads * GROUP
    keys_ref[:near, :] = near_keys_ref[...]
    values_ref[:near, :] = near_values_ref[...]
    unpack(pair_ref, bias_ref, keys_ref, values_ref, slice(near, near + tok))
    near_blocks = [slice(row, row + BLOCK) for row in range(0, near, BLOCK)]
    blocks = [slice(row, row + BLOCK) for row in range(0, tok, BLOCK)]
    for kv_head in range(kv_heads):
        cols = head_cols(kv_head)
        group = slice(kv_head * GROUP * tok, (kv_head + 1) * GROUP * tok)
        last_weights_ref[:, group] = dot(
            keys_ref[near:, cols], queries_ref[group, :HEAD_DIM], 1, 1
        )
        last_dprob_ref[:, group] = dot(values_ref[near:, cols], grads_ref[group, :], 1, 1)
        for first in range(group.start, group.stop, PAIR * tok):
            at = slice(first, first + PAIR * tok)
            near_max = stats_ref[0:1, at]
            row_max = jnp.broadcast_to(near_max, (8, PAIR * tok))
            for block in blocks:
                live = live_ref[near + block.start : near + block.stop, :]
                score = last_weights_ref[block, at] + jnp.concatenate([live] * PAIR, axis=1)
                last_weights_ref[block, at] = score
                row_max = jnp.maximum(row_max, over_rows(score, jnp.max))
            row_max = jnp.max(row_max, axis=0, keepdims=True)
            total = jnp.zeros((8, PAIR * tok), jnp.float32)
            delta = jnp.zeros((8, PAIR * tok), jnp.float32)
            for block in blocks:
                weights = jnp.exp2((last_weights_ref[block, at] - row_max) * (SCALE * LOG2E))
                last_weights_ref[block, at] = weights
                total = total + over_rows(weights, jnp.sum)
                delta = delta + over_rows(weights * last_dprob_ref[block, at], jnp.sum)
            factor = jnp.exp2((near_max - row_max) * (SCALE * LOG2E))
            total = jnp.sum(total, axis=0, keepdims=True) + stats_ref[1:2, at] * factor
            delta = jnp.sum(delta, axis=0, keepdims=True) + stats_ref[2:3, at] * factor
            inverse = 1.0 / total
            delta = delta * inverse
            factor = factor * inverse
            for block in near_blocks:
                probs = weights_ref[block, at] * factor
                probs_ref[block, at] = probs.astype(jnp.bfloat16)
                dscore_ref[block, at] = (probs * (dprob_ref[block, at] - delta)).astype(jnp.bfloat16)
            for block in blocks:
                to = slice(near + block.start, near + block.stop)
                probs = last_weights_ref[block, at] * inverse
                probs_ref[to, at] = probs.astype(jnp.bfloat16)
                dscore = probs * (last_dprob_ref[block, at] - delta)
                dscore_ref[to, at] = dscore.astype(jnp.bfloat16)
        value_term = dot(probs_ref[:, group], grads_ref[group, :], 1, 0)
        key_term = dot(dscore_ref[:, group], queries_ref[group, :], 1, 0)
        over_queries = key_term[:, HEAD_DIM:]
        key_term = key_term[:, :HEAD_DIM] * SCALE
        high = over_queries.astype(jnp.bfloat16)
        low = (over_queries - high.astype(jnp.float32)).astype(jnp.bfloat16)
        all_keys = keys_ref[:, cols]
        query_sums = (dot(high, all_keys, 0, 0) + dot(low, all_keys, 0, 0)) * SCALE
        of_group = slice(kv_head * GROUP, (kv_head + 1) * GROUP)
        sums_ref[of_group, :] = query_sums[first_head + of_group.start : first_head + of_group.stop]
        sums_ref[heads + kv_head : heads + kv_head + 1, :] = jnp.sum(
            value_term, axis=0, keepdims=True
        )
        value_cols = head_cols(kv_heads + kv_head)
        own_ref[:, cols] = key_term[:tok]
        own_ref[:, value_cols] = value_term[:tok]
        for index, slot in enumerate(slot_order(slots)):
            if slot == 0:
                continue
            rows = slice(index * tok, (index + 1) * tok)
            out_refs[slot - 1][:, cols] = key_term[rows].astype(jnp.bfloat16)
            out_refs[slot - 1][:, value_cols] = value_term[rows].astype(jnp.bfloat16)


def finish_kernel(probs_ref, dscore_ref, keys_ref, values_ref, *refs):
    passed = (len(refs) - 2) // 2
    attn_ref, qg_ref = refs[passed : passed + 2]
    tok = attn_ref.shape[0]
    kv_heads = keys_ref.shape[1] // HEAD_DIM
    for kv_head in range(kv_heads):
        cols = head_cols(kv_head)
        keys_t = keys_ref[:, cols].T
        values_t = values_ref[:, cols].T
        for pair in range(GROUP // PAIR):
            first = kv_head * GROUP + pair * PAIR
            at = slice(first * tok, (first + PAIR) * tok)
            attn = dot(values_t, probs_ref[:, at], 1, 0).T
            query_grad = (dot(keys_t, dscore_ref[:, at], 1, 0) * SCALE).T
            for n in range(PAIR):
                head = first + n
                rows = slice(n * tok, (n + 1) * tok)
                attn_ref[:, head_cols(head)] = attn[rows].astype(jnp.bfloat16)
                qg_ref[:, head_cols(head)] = query_grad[rows].astype(jnp.bfloat16)


def collect_kernel(batches, parts, *refs):
    sum_refs, term_refs, (kg_ref, vg_ref, qb_ref, vb_ref) = refs[:parts], refs[parts:-4], refs[-4:]
    heads = qb_ref.shape[0]
    kv_width = kg_ref.shape[1]
    total = sum_refs[0][...]
    for ref in sum_refs[1:]:
        total = total + ref[...]
    total = total * (1.0 / batches)
    qb_ref[...] = total[:heads]
    vb_ref[...] = total[heads:]
    term = term_refs[0][...]
    for ref in term_refs[1:]:
        term = term + ref[...].astype(jnp.float32)
    term = term.astype(jnp.bfloat16)
    kg_ref[...] = term[:, :kv_width]
    vg_ref[...] = term[:, kv_width:]


def total_kernel(*refs):
    total = refs[0][...]
    for ref in refs[1:-1]:
        total = total + ref[...]
    refs[-1][...] = total


def exchange(axis, part):
    return [part] + [fetch(part, axis, slot) for slot in range(1, lax.axis_size(axis))]


def attend(first_head, bias, queries, grads, score, own_dprob, live, pairs):
    ctx = len(pairs)
    tok = pairs[0].shape[0]
    kv_width = bias.shape[0] * HEAD_DIM
    columns = queries.shape[0]
    rows = ctx * tok
    near = rows - tok
    near_slots = slot_order(ctx)[:-1]
    weights, dprob, stats, near_keys, near_values = pl.pallas_call(
        near_kernel,
        out_shape=[
            shape((near, columns), jnp.float32),
            shape((near, columns), jnp.float32),
            shape((8, columns), jnp.float32),
            shape((near, kv_width), jnp.bfloat16),
            shape((near, kv_width), jnp.bfloat16),
        ],
        in_specs=[VMEM] * (6 + len(near_slots)),
        out_specs=[VMEM] * 5,
        compiler_params=params(20 if ctx < 8 else 48),
        cost_estimate=pl.CostEstimate(
            flops=4 * near * columns * HEAD_DIM,
            bytes_accessed=8 * near * columns,
            transcendentals=near * columns,
        ),
        name="near",
    )(bias, queries, grads, score, own_dprob, live, *[pairs[slot] for slot in near_slots])
    term = shape((tok, 2 * kv_width), jnp.bfloat16)
    return pl.pallas_call(
        functools.partial(last_kernel, ctx, first_head),
        out_shape=[
            shape((rows, columns), jnp.bfloat16),
            shape((rows, columns), jnp.bfloat16),
            shape((rows, kv_width), jnp.bfloat16),
            shape((rows, kv_width), jnp.bfloat16),
            shape((bias.shape[0] * (GROUP + 1), HEAD_DIM), jnp.float32),
            shape((tok, 2 * kv_width), jnp.float32),
        ]
        + [term] * (ctx - 1),
        in_specs=[VMEM] * 10,
        out_specs=[VMEM] * (6 + ctx - 1),
        scratch_shapes=[pltpu.VMEM((tok, columns), jnp.float32)] * 2,
        compiler_params=params(24 if ctx < 8 else 48),
        cost_estimate=pl.CostEstimate(
            flops=4 * rows * columns * HEAD_DIM,
            bytes_accessed=4 * rows * columns,
            transcendentals=tok * columns,
        ),
        name="last",
    )(bias, queries, grads, live, weights, dprob, stats, near_keys, near_values, pairs[ctx // 2])


def joined(place, parts):
    if place < 4:
        return jnp.concatenate(parts, axis=1)
    cut, axis = (GROUP, 0) if place == 4 else (HEAD_DIM, 1)
    pieces = [jnp.split(part, [cut], axis=axis) for part in parts]
    return jnp.concatenate([piece[n] for n in range(2) for piece in pieces], axis=axis)


def shards(q_proj, q_bias, k_proj, v_proj, v_bias, dout, lengths):
    _, tok, width = q_proj.shape
    kv_width = k_proj.shape[2]
    heads = width // HEAD_DIM
    kv_heads = kv_width // HEAD_DIM
    ctx = lax.axis_size("ctx")
    batches = lax.axis_size("dp")
    rows = ctx * tok
    columns = heads * tok
    pair = jnp.concatenate([k_proj[0], v_proj[0]], axis=1)
    pairs = [pair] + [fetch(pair, "ctx", slot) for slot in range(1, ctx)]
    prepared = pl.pallas_call(
        functools.partial(prepare_kernel, ctx),
        out_shape=[
            shape((kv_heads, HEAD_DIM), jnp.bfloat16),
            shape((columns, 2 * HEAD_DIM), jnp.bfloat16),
            shape((columns, HEAD_DIM), jnp.bfloat16),
            shape((tok, columns), jnp.float32),
            shape((tok, columns), jnp.float32),
            shape((rows, tok), jnp.float32),
        ],
        in_specs=[SMEM] + [VMEM] * 5,
        out_specs=[VMEM] * 6,
        compiler_params=params(16),
        cost_estimate=pl.CostEstimate(
            flops=4 * tok * tok * width, bytes_accessed=16 * tok * width, transcendentals=0
        ),
        name="prepare",
    )(
        lengths,
        pair,
        q_bias.reshape(heads, HEAD_DIM),
        v_bias.reshape(kv_heads, HEAD_DIM),
        q_proj[0],
        dout[0],
    )
    bias, queries, grads, score, own_dprob, live = prepared
    if ctx < 8:
        made = attend(0, bias, queries, grads, score, own_dprob, live, pairs)
    else:
        made = [
            attend(
                kv_head * GROUP,
                bias[kv_head : kv_head + 1],
                *(part[at] for part in (queries, grads)),
                *(part[:, at] for part in (score, own_dprob)),
                live,
                [
                    jnp.concatenate(
                        [part[:, head_cols(kv_head)], part[:, head_cols(kv_heads + kv_head)]], axis=1
                    )
                    for part in pairs
                ],
            )
            for kv_head in range(kv_heads)
            for at in [slice(kv_head * GROUP * tok, (kv_head + 1) * GROUP * tok)]
        ]
        made = [joined(n, parts) for n, parts in enumerate(zip(*made))]
    probs, dscore, all_keys, all_values, sums, own, *terms = made
    term = shape((tok, 2 * kv_width), jnp.bfloat16)
    half = ctx // 2
    back = {slot: send_back(terms[slot - 1], slot) for slot in range(1, ctx)}
    tied = [half]
    attn, q_grad, *passed = pl.pallas_call(
        finish_kernel,
        out_shape=[
            shape((tok, width), jnp.bfloat16),
            shape((tok, width), jnp.bfloat16),
        ]
        + [shape((tok, 2 * kv_width), jnp.bfloat16)] * len(tied),
        in_specs=[VMEM] * 4 + [ANY] * len(tied),
        out_specs=[VMEM] * 2 + [ANY] * len(tied),
        input_output_aliases={4 + n: 2 + n for n in range(len(tied))},
        compiler_params=params(24),
        cost_estimate=pl.CostEstimate(
            flops=16 * rows * tok * width, bytes_accessed=0, transcendentals=0
        ),
        name="finish",
    )(probs, dscore, all_keys, all_values, *[back[slot] for slot in tied])
    parts = exchange("dp", sums)[::-1]
    sums = pl.pallas_call(
        total_kernel,
        out_shape=shape(sums.shape, sums.dtype),
        in_specs=[VMEM] * len(parts),
        out_specs=VMEM,
        compiler_params=params(4),
        cost_estimate=pl.CostEstimate(flops=sums.size, bytes_accessed=0, transcendentals=0),
        name="total",
    )(*parts)
    sums = exchange("ctx", sums)
    back.update(zip(tied, passed))
    k_grad, v_grad, q_sum, v_sum = pl.pallas_call(
        functools.partial(collect_kernel, batches, len(sums)),
        out_shape=[
            shape((tok, kv_width), jnp.bfloat16),
            shape((tok, kv_width), jnp.bfloat16),
            shape((heads, HEAD_DIM), jnp.float32),
            shape((kv_heads, HEAD_DIM), jnp.float32),
        ],
        in_specs=[VMEM] * (len(sums) + 1 + len(back)),
        out_specs=[VMEM] * 4,
        compiler_params=params(8),
        cost_estimate=pl.CostEstimate(
            flops=8 * tok * kv_width, bytes_accessed=16 * tok * kv_width, transcendentals=0
        ),
        name="collect",
    )(*sums, own, *[back[slot] for slot in sorted(back, reverse=True)])
    return (
        attn[None],
        q_grad[None],
        k_grad[None],
        v_grad[None],
        q_sum.reshape(width),
        v_sum.reshape(kv_width),
    )


def solution(mesh):
    tokens = P("dp", "ctx", "tp")
    return jax.shard_map(
        shards,
        mesh=mesh,
        in_specs=(tokens, P("tp"), tokens, tokens, P("tp"), tokens, P("dp", None)),
        out_specs=(tokens, tokens, tokens, tokens, P("tp"), P("tp")),
        check_vma=False,
    )
```

```python
import functools

import jax
import jax.numpy as jnp
from jax import lax
from jax.experimental import pallas as pl
from jax.experimental.pallas import tpu as pltpu
from jax.sharding import PartitionSpec as P

HEAD_DIM = 128
HEADS = 32
KV_HEADS = 4
GROUP = HEADS // KV_HEADS
PAIR = 4
BLOCK = 32
SCALE = HEAD_DIM ** (-0.5)
LOG2E = 1.4426950408889634
NEGATIVE = -1e30
VMEM = pl.BlockSpec(memory_space=pltpu.VMEM)
ANY = pl.BlockSpec(memory_space=pl.ANY)
SMEM = pl.BlockSpec(memory_space=pltpu.SMEM)


def dot(left, right, left_dim, right_dim):
    return lax.dot_general(
        left, right, (((left_dim,), (right_dim,)), ((), ())), preferred_element_type=jnp.float32
    )


def head_cols(head):
    return slice(head * HEAD_DIM, (head + 1) * HEAD_DIM)


def shape(dims, dtype):
    return jax.ShapeDtypeStruct(dims, dtype)


def params(mebibytes):
    return pltpu.CompilerParams(vmem_limit_bytes=mebibytes * 1024 * 1024)


def biased(values, bias):
    return (values.astype(jnp.float32) + bias.astype(jnp.float32)).astype(jnp.bfloat16)


def source_of(rank, slot, size):
    if size & (size - 1):
        return (rank + size - slot) % size
    return rank ^ slot


def slot_order(size):
    return [slot for slot in range(size) if slot != size // 2] + [size // 2]


def fetch(array, axis, slot):
    size = lax.axis_size(axis)
    return lax.ppermute(array, axis, [(source_of(i, slot, size), i) for i in range(size)])


def send_back(array, slot):
    size = lax.axis_size("ctx")
    return lax.ppermute(array, "ctx", [(i, source_of(i, slot, size)) for i in range(size)])


def prepare_kernel(
    slots, len_ref, pair_ref, qb_ref, vb_ref, q_ref, g_ref, bias_ref, queries_ref, grads_ref,
    score_ref, dprob_ref, live_ref,
):
    tok = q_ref.shape[0]
    kv_heads = vb_ref.shape[0]
    rank = lax.axis_index("ctx")
    query_pos = rank * tok + lax.broadcasted_iota(jnp.int32, (1, tok), 1)
    start = jnp.zeros((1, tok), jnp.int32)
    end = jnp.int32(0)
    for doc in range(len_ref.shape[1]):
        length = len_ref[0, doc]
        end = end + length
        start = start + jnp.where(query_pos >= end, length, 0)
    offsets = lax.broadcasted_iota(jnp.int32, (tok, tok), 0)
    for index, slot in enumerate(slot_order(slots)):
        key_pos = source_of(rank, slot, slots) * tok + offsets
        live = (key_pos >= start) & (key_pos <= query_pos)
        live_ref[index * tok : (index + 1) * tok, :] = jnp.where(live, 0.0, NEGATIVE)
    bias_ref[...] = vb_ref[...]
    column = lax.broadcasted_iota(jnp.int32, (tok, HEAD_DIM), 1)
    for kv_head in range(kv_heads):
        keys = pair_ref[:, head_cols(kv_head)]
        values = biased(pair_ref[:, head_cols(kv_heads + kv_head)], vb_ref[kv_head : kv_head + 1, :])
        for head in range(kv_head * GROUP, (kv_head + 1) * GROUP):
            at = slice(head * tok, (head + 1) * tok)
            queries_ref[at, :HEAD_DIM] = biased(q_ref[:, head_cols(head)], qb_ref[head : head + 1, :])
            queries_ref[at, HEAD_DIM:] = (column == head).astype(jnp.bfloat16)
            grads_ref[at, :] = g_ref[:, head_cols(head)]
        rows = slice(kv_head * GROUP * tok, (kv_head + 1) * GROUP * tok)
        score_ref[:, rows] = dot(keys, queries_ref[rows, :HEAD_DIM], 1, 1)
        dprob_ref[:, rows] = dot(values, grads_ref[rows, :], 1, 1)


def over_rows(array, reduce):
    return reduce(array.reshape(-1, 8, array.shape[-1]), axis=0)


def unpack(pair_ref, bias_ref, keys_ref, values_ref, rows):
    kv_heads = bias_ref.shape[0]
    keys_ref[rows, :] = pair_ref[:, : kv_heads * HEAD_DIM]
    for kv_head in range(kv_heads):
        values_ref[rows, head_cols(kv_head)] = biased(
            pair_ref[:, head_cols(kv_heads + kv_head)], bias_ref[kv_head : kv_head + 1, :]
        )


def near_kernel(
    bias_ref, queries_ref, grads_ref, score_ref, own_dprob_ref, live_ref, *refs
):
    pair_refs, (weights_ref, dprob_ref, stats_ref, keys_ref, values_ref) = refs[:-5], refs[-5:]
    tok = pair_refs[0].shape[0]
    for index, pair_ref in enumerate(pair_refs):
        unpack(pair_ref, bias_ref, keys_ref, values_ref, slice(index * tok, (index + 1) * tok))
    blocks = [slice(row, row + BLOCK) for row in range(0, len(pair_refs) * tok, BLOCK)]
    for kv_head in range(bias_ref.shape[0]):
        cols = head_cols(kv_head)
        group = slice(kv_head * GROUP * tok, (kv_head + 1) * GROUP * tok)
        weights_ref[tok:, group] = dot(keys_ref[tok:, cols], queries_ref[group, :HEAD_DIM], 1, 1)
        dprob_ref[tok:, group] = dot(values_ref[tok:, cols], grads_ref[group, :], 1, 1)
        for first in range(group.start, group.stop, PAIR * tok):
            at = slice(first, first + PAIR * tok)
            row_max = None
            for block in blocks:
                score = (score_ref if block.start < tok else weights_ref)[block, at]
                score = score + jnp.concatenate([live_ref[block, :]] * PAIR, axis=1)
                weights_ref[block, at] = score
                part = over_rows(score, jnp.max)
                row_max = part if row_max is None else jnp.maximum(row_max, part)
            row_max = jnp.max(row_max, axis=0, keepdims=True)
            total = jnp.zeros((8, PAIR * tok), jnp.float32)
            delta = jnp.zeros((8, PAIR * tok), jnp.float32)
            for block in blocks:
                dprob = (own_dprob_ref if block.start < tok else dprob_ref)[block, at]
                weights = jnp.exp2((weights_ref[block, at] - row_max) * (SCALE * LOG2E))
                weights_ref[block, at] = weights
                if block.start < tok:
                    dprob_ref[block, at] = dprob
                total = total + over_rows(weights, jnp.sum)
                delta = delta + over_rows(weights * dprob, jnp.sum)
            stats_ref[0:1, at] = row_max
            stats_ref[1:2, at] = jnp.sum(total, axis=0, keepdims=True)
            stats_ref[2:3, at] = jnp.sum(delta, axis=0, keepdims=True)


def last_kernel(slots, first_head, *refs):
    bias_ref, queries_ref, grads_ref, live_ref = refs[:4]
    weights_ref, dprob_ref, stats_ref, near_keys_ref, near_values_ref, pair_ref = refs[4:10]
    probs_ref, dscore_ref, keys_ref, values_ref, sums_ref, own_ref = refs[10:16]
    out_refs = refs[16 : 16 + slots - 1]
    last_weights_ref, last_dprob_ref = refs[16 + slots - 1 :]
    tok = pair_ref.shape[0]
    near = (slots - 1) * tok
    kv_heads = bias_ref.shape[0]
    kv_width = kv_heads * HEAD_DIM
    heads = kv_heads * GROUP
    keys_ref[:near, :] = near_keys_ref[...]
    values_ref[:near, :] = near_values_ref[...]
    unpack(pair_ref, bias_ref, keys_ref, values_ref, slice(near, near + tok))
    near_blocks = [slice(row, row + BLOCK) for row in range(0, near, BLOCK)]
    blocks = [slice(row, row + BLOCK) for row in range(0, tok, BLOCK)]
    for kv_head in range(kv_heads):
        cols = head_cols(kv_head)
        group = slice(kv_head * GROUP * tok, (kv_head + 1) * GROUP * tok)
        last_weights_ref[:, group] = dot(
            keys_ref[near:, cols], queries_ref[group, :HEAD_DIM], 1, 1
        )
        last_dprob_ref[:, group] = dot(values_ref[near:, cols], grads_ref[group, :], 1, 1)
        for first in range(group.start, group.stop, PAIR * tok):
            at = slice(first, first + PAIR * tok)
            near_max = stats_ref[0:1, at]
            row_max = jnp.broadcast_to(near_max, (8, PAIR * tok))
            for block in blocks:
                live = live_ref[near + block.start : near + block.stop, :]
                score = last_weights_ref[block, at] + jnp.concatenate([live] * PAIR, axis=1)
                last_weights_ref[block, at] = score
                row_max = jnp.maximum(row_max, over_rows(score, jnp.max))
            row_max = jnp.max(row_max, axis=0, keepdims=True)
            total = jnp.zeros((8, PAIR * tok), jnp.float32)
            delta = jnp.zeros((8, PAIR * tok), jnp.float32)
            for block in blocks:
                weights = jnp.exp2((last_weights_ref[block, at] - row_max) * (SCALE * LOG2E))
                last_weights_ref[block, at] = weights
                total = total + over_rows(weights, jnp.sum)
                delta = delta + over_rows(weights * last_dprob_ref[block, at], jnp.sum)
            factor = jnp.exp2((near_max - row_max) * (SCALE * LOG2E))
            total = jnp.sum(total, axis=0, keepdims=True) + stats_ref[1:2, at] * factor
            delta = jnp.sum(delta, axis=0, keepdims=True) + stats_ref[2:3, at] * factor
            inverse = 1.0 / total
            delta = delta * inverse
            factor = factor * inverse
            for block in near_blocks:
                probs = weights_ref[block, at] * factor
                probs_ref[block, at] = probs.astype(jnp.bfloat16)
                dscore_ref[block, at] = (probs * (dprob_ref[block, at] - delta)).astype(jnp.bfloat16)
            for block in blocks:
                to = slice(near + block.start, near + block.stop)
                probs = last_weights_ref[block, at] * inverse
                probs_ref[to, at] = probs.astype(jnp.bfloat16)
                dscore = probs * (last_dprob_ref[block, at] - delta)
                dscore_ref[to, at] = dscore.astype(jnp.bfloat16)
        value_term = dot(probs_ref[:, group], grads_ref[group, :], 1, 0)
        key_term = dot(dscore_ref[:, group], queries_ref[group, :], 1, 0)
        over_queries = key_term[:, HEAD_DIM:]
        key_term = key_term[:, :HEAD_DIM] * SCALE
        high = over_queries.astype(jnp.bfloat16)
        low = (over_queries - high.astype(jnp.float32)).astype(jnp.bfloat16)
        all_keys = keys_ref[:, cols]
        query_sums = (dot(high, all_keys, 0, 0) + dot(low, all_keys, 0, 0)) * SCALE
        of_group = slice(kv_head * GROUP, (kv_head + 1) * GROUP)
        sums_ref[of_group, :] = query_sums[first_head + of_group.start : first_head + of_group.stop]
        sums_ref[heads + kv_head : heads + kv_head + 1, :] = jnp.sum(
            value_term, axis=0, keepdims=True
        )
        value_cols = head_cols(kv_heads + kv_head)
        own_ref[:, cols] = key_term[:tok]
        own_ref[:, value_cols] = value_term[:tok]
        for index, slot in enumerate(slot_order(slots)):
            if slot == 0:
                continue
            rows = slice(index * tok, (index + 1) * tok)
            out_refs[slot - 1][:, cols] = key_term[rows].astype(jnp.bfloat16)
            out_refs[slot - 1][:, value_cols] = value_term[rows].astype(jnp.bfloat16)


def finish_kernel(probs_ref, dscore_ref, keys_ref, values_ref, *refs):
    passed = (len(refs) - 2) // 2
    attn_ref, qg_ref = refs[passed : passed + 2]
    tok = attn_ref.shape[0]
    kv_heads = keys_ref.shape[1] // HEAD_DIM
    for kv_head in range(kv_heads):
        cols = head_cols(kv_head)
        keys_t = keys_ref[:, cols].T
        values_t = values_ref[:, cols].T
        for pair in range(GROUP // PAIR):
            first = kv_head * GROUP + pair * PAIR
            at = slice(first * tok, (first + PAIR) * tok)
            attn = dot(values_t, probs_ref[:, at], 1, 0).T
            query_grad = (dot(keys_t, dscore_ref[:, at], 1, 0) * SCALE).T
            for n in range(PAIR):
                head = first + n
                rows = slice(n * tok, (n + 1) * tok)
                attn_ref[:, head_cols(head)] = attn[rows].astype(jnp.bfloat16)
                qg_ref[:, head_cols(head)] = query_grad[rows].astype(jnp.bfloat16)


def collect_kernel(batches, parts, *refs):
    sum_refs, term_refs, (kg_ref, vg_ref, qb_ref, vb_ref) = refs[:parts], refs[parts:-4], refs[-4:]
    heads = qb_ref.shape[0]
    kv_width = kg_ref.shape[1]
    total = sum_refs[0][...]
    for ref in sum_refs[1:]:
        total = total + ref[...]
    total = total * (1.0 / batches)
    qb_ref[...] = total[:heads]
    vb_ref[...] = total[heads:]
    term = term_refs[0][...]
    for ref in term_refs[1:]:
        term = term + ref[...].astype(jnp.float32)
    term = term.astype(jnp.bfloat16)
    kg_ref[...] = term[:, :kv_width]
    vg_ref[...] = term[:, kv_width:]


def total_kernel(*refs):
    total = refs[0][...]
    for ref in refs[1:-1]:
        total = total + ref[...]
    refs[-1][...] = total


def exchange(axis, part):
    return [part] + [fetch(part, axis, slot) for slot in range(1, lax.axis_size(axis))]


def attend(first_head, bias, queries, grads, score, own_dprob, live, pairs):
    ctx = len(pairs)
    tok = pairs[0].shape[0]
    kv_width = bias.shape[0] * HEAD_DIM
    columns = queries.shape[0]
    rows = ctx * tok
    near = rows - tok
    near_slots = slot_order(ctx)[:-1]
    weights, dprob, stats, near_keys, near_values = pl.pallas_call(
        near_kernel,
        out_shape=[
            shape((near, columns), jnp.float32),
            shape((near, columns), jnp.float32),
            shape((8, columns), jnp.float32),
            shape((near, kv_width), jnp.bfloat16),
            shape((near, kv_width), jnp.bfloat16),
        ],
        in_specs=[VMEM] * (6 + len(near_slots)),
        out_specs=[VMEM] * 5,
        compiler_params=params(20 if ctx < 8 else 48),
        cost_estimate=pl.CostEstimate(
            flops=4 * near * columns * HEAD_DIM,
            bytes_accessed=8 * near * columns,
            transcendentals=near * columns,
        ),
        name="near",
    )(bias, queries, grads, score, own_dprob, live, *[pairs[slot] for slot in near_slots])
    term = shape((tok, 2 * kv_width), jnp.bfloat16)
    return pl.pallas_call(
        functools.partial(last_kernel, ctx, first_head),
        out_shape=[
            shape((rows, columns), jnp.bfloat16),
            shape((rows, columns), jnp.bfloat16),
            shape((rows, kv_width), jnp.bfloat16),
            shape((rows, kv_width), jnp.bfloat16),
            shape((bias.shape[0] * (GROUP + 1), HEAD_DIM), jnp.float32),
            shape((tok, 2 * kv_width), jnp.float32),
        ]
        + [term] * (ctx - 1),
        in_specs=[VMEM] * 10,
        out_specs=[VMEM] * (6 + ctx - 1),
        scratch_shapes=[pltpu.VMEM((tok, columns), jnp.float32)] * 2,
        compiler_params=params(24 if ctx < 8 else 48),
        cost_estimate=pl.CostEstimate(
            flops=4 * rows * columns * HEAD_DIM,
            bytes_accessed=4 * rows * columns,
            transcendentals=tok * columns,
        ),
        name="last",
    )(bias, queries, grads, live, weights, dprob, stats, near_keys, near_values, pairs[ctx // 2])


def joined(place, parts):
    if place < 4:
        return jnp.concatenate(parts, axis=1)
    cut, axis = (GROUP, 0) if place == 4 else (HEAD_DIM, 1)
    pieces = [jnp.split(part, [cut], axis=axis) for part in parts]
    return jnp.concatenate([piece[n] for n in range(2) for piece in pieces], axis=axis)


def shards(q_proj, q_bias, k_proj, v_proj, v_bias, dout, lengths):
    _, tok, width = q_proj.shape
    kv_width = k_proj.shape[2]
    heads = width // HEAD_DIM
    kv_heads = kv_width // HEAD_DIM
    ctx = lax.axis_size("ctx")
    batches = lax.axis_size("dp")
    rows = ctx * tok
    columns = heads * tok
    pair = jnp.concatenate([k_proj[0], v_proj[0]], axis=1)
    pairs = [pair] + [fetch(pair, "ctx", slot) for slot in range(1, ctx)]
    prepared = pl.pallas_call(
        functools.partial(prepare_kernel, ctx),
        out_shape=[
            shape((kv_heads, HEAD_DIM), jnp.bfloat16),
            shape((columns, 2 * HEAD_DIM), jnp.bfloat16),
            shape((columns, HEAD_DIM), jnp.bfloat16),
            shape((tok, columns), jnp.float32),
            shape((tok, columns), jnp.float32),
            shape((rows, tok), jnp.float32),
        ],
        in_specs=[SMEM] + [VMEM] * 5,
        out_specs=[VMEM] * 6,
        compiler_params=params(16),
        cost_estimate=pl.CostEstimate(
            flops=4 * tok * tok * width, bytes_accessed=16 * tok * width, transcendentals=0
        ),
        name="prepare",
    )(
        lengths,
        pair,
        q_bias.reshape(heads, HEAD_DIM),
        v_bias.reshape(kv_heads, HEAD_DIM),
        q_proj[0],
        dout[0],
    )
    bias, queries, grads, score, own_dprob, live = prepared
    if ctx < 8:
        made = attend(0, bias, queries, grads, score, own_dprob, live, pairs)
    else:
        made = [
            attend(
                kv_head * GROUP,
                bias[kv_head : kv_head + 1],
                *(part[at] for part in (queries, grads)),
                *(part[:, at] for part in (score, own_dprob)),
                live,
                [
                    jnp.concatenate(
                        [part[:, head_cols(kv_head)], part[:, head_cols(kv_heads + kv_head)]], axis=1
                    )
                    for part in pairs
                ],
            )
            for kv_head in range(kv_heads)
            for at in [slice(kv_head * GROUP * tok, (kv_head + 1) * GROUP * tok)]
        ]
        made = [joined(n, parts) for n, parts in enumerate(zip(*made))]
    probs, dscore, all_keys, all_values, sums, own, *terms = made
    term = shape((tok, 2 * kv_width), jnp.bfloat16)
    half = ctx // 2
    back = {slot: send_back(terms[slot - 1], slot) for slot in range(1, ctx)}
    tied = [half]
    attn, q_grad, *passed = pl.pallas_call(
        finish_kernel,
        out_shape=[
            shape((tok, width), jnp.bfloat16),
            shape((tok, width), jnp.bfloat16),
        ]
        + [shape((tok, 2 * kv_width), jnp.bfloat16)] * len(tied),
        in_specs=[VMEM] * 4 + [ANY] * len(tied),
        out_specs=[VMEM] * 2 + [ANY] * len(tied),
        input_output_aliases={4 + n: 2 + n for n in range(len(tied))},
        compiler_params=params(24),
        cost_estimate=pl.CostEstimate(
            flops=16 * rows * tok * width, bytes_accessed=0, transcendentals=0
        ),
        name="finish",
    )(probs, dscore, all_keys, all_values, *[back[slot] for slot in tied])
    parts = exchange("dp", sums)
    sums = pl.pallas_call(
        total_kernel,
        out_shape=shape(sums.shape, sums.dtype),
        in_specs=[VMEM] * len(parts),
        out_specs=VMEM,
        compiler_params=params(4),
        cost_estimate=pl.CostEstimate(flops=sums.size, bytes_accessed=0, transcendentals=0),
        name="total",
    )(*parts)
    sums = exchange("ctx", sums)
    back.update(zip(tied, passed))
    k_grad, v_grad, q_sum, v_sum = pl.pallas_call(
        functools.partial(collect_kernel, batches, len(sums)),
        out_shape=[
            shape((tok, kv_width), jnp.bfloat16),
            shape((tok, kv_width), jnp.bfloat16),
            shape((heads, HEAD_DIM), jnp.float32),
            shape((kv_heads, HEAD_DIM), jnp.float32),
        ],
        in_specs=[VMEM] * (len(sums) + 1 + len(back)),
        out_specs=[VMEM] * 4,
        compiler_params=params(8),
        cost_estimate=pl.CostEstimate(
            flops=8 * tok * kv_width, bytes_accessed=16 * tok * kv_width, transcendentals=0
        ),
        name="collect",
    )(*sums, own, *[back[slot] for slot in sorted(back, reverse=True)])
    return (
        attn[None],
        q_grad[None],
        k_grad[None],
        v_grad[None],
        q_sum.reshape(width),
        v_sum.reshape(kv_width),
    )


def solution(mesh):
    tokens = P("dp", "ctx", "tp")
    return jax.shard_map(
        shards,
        mesh=mesh,
        in_specs=(tokens, P("tp"), tokens, tokens, P("tp"), tokens, P("dp", None)),
        out_specs=(tokens, tokens, tokens, tokens, P("tp"), P("tp")),
        check_vma=False,
    )
```

```python
import functools

import jax
import jax.numpy as jnp
from jax import lax
from jax.experimental import pallas as pl
from jax.experimental.pallas import tpu as pltpu
from jax.sharding import PartitionSpec as P

HEAD_DIM = 128
HEADS = 32
KV_HEADS = 4
GROUP = HEADS // KV_HEADS
PAIR = 4
BLOCK = 32
SCALE = HEAD_DIM ** (-0.5)
LOG2E = 1.4426950408889634
NEGATIVE = -1e30
VMEM = pl.BlockSpec(memory_space=pltpu.VMEM)
ANY = pl.BlockSpec(memory_space=pl.ANY)
SMEM = pl.BlockSpec(memory_space=pltpu.SMEM)


def dot(left, right, left_dim, right_dim):
    return lax.dot_general(
        left, right, (((left_dim,), (right_dim,)), ((), ())), preferred_element_type=jnp.float32
    )


def head_cols(head):
    return slice(head * HEAD_DIM, (head + 1) * HEAD_DIM)


def shape(dims, dtype):
    return jax.ShapeDtypeStruct(dims, dtype)


def params(mebibytes):
    return pltpu.CompilerParams(vmem_limit_bytes=mebibytes * 1024 * 1024)


def biased(values, bias):
    return (values.astype(jnp.float32) + bias.astype(jnp.float32)).astype(jnp.bfloat16)


def source_of(rank, slot, size):
    if size & (size - 1):
        return (rank + size - slot) % size
    return rank ^ slot


def slot_order(size):
    return [slot for slot in range(size) if slot != size // 2] + [size // 2]


def fetch(array, axis, slot):
    size = lax.axis_size(axis)
    return lax.ppermute(array, axis, [(source_of(i, slot, size), i) for i in range(size)])


def send_back(array, slot):
    size = lax.axis_size("ctx")
    return lax.ppermute(array, "ctx", [(i, source_of(i, slot, size)) for i in range(size)])


def prepare_kernel(
    slots, len_ref, pair_ref, qb_ref, vb_ref, q_ref, g_ref, bias_ref, queries_ref, grads_ref,
    score_ref, dprob_ref, live_ref,
):
    tok = q_ref.shape[0]
    kv_heads = vb_ref.shape[0]
    rank = lax.axis_index("ctx")
    query_pos = rank * tok + lax.broadcasted_iota(jnp.int32, (1, tok), 1)
    start = jnp.zeros((1, tok), jnp.int32)
    end = jnp.int32(0)
    for doc in range(len_ref.shape[1]):
        length = len_ref[0, doc]
        end = end + length
        start = start + jnp.where(query_pos >= end, length, 0)
    offsets = lax.broadcasted_iota(jnp.int32, (tok, tok), 0)
    for index, slot in enumerate(slot_order(slots)):
        key_pos = source_of(rank, slot, slots) * tok + offsets
        live = (key_pos >= start) & (key_pos <= query_pos)
        live_ref[index * tok : (index + 1) * tok, :] = jnp.where(live, 0.0, NEGATIVE)
    bias_ref[...] = vb_ref[...]
    column = lax.broadcasted_iota(jnp.int32, (tok, HEAD_DIM), 1)
    for kv_head in range(kv_heads):
        keys = pair_ref[:, head_cols(kv_head)]
        values = biased(pair_ref[:, head_cols(kv_heads + kv_head)], vb_ref[kv_head : kv_head + 1, :])
        for head in range(kv_head * GROUP, (kv_head + 1) * GROUP):
            at = slice(head * tok, (head + 1) * tok)
            queries_ref[at, :HEAD_DIM] = biased(q_ref[:, head_cols(head)], qb_ref[head : head + 1, :])
            queries_ref[at, HEAD_DIM:] = (column == head).astype(jnp.bfloat16)
            grads_ref[at, :] = g_ref[:, head_cols(head)]
        rows = slice(kv_head * GROUP * tok, (kv_head + 1) * GROUP * tok)
        score_ref[:, rows] = dot(keys, queries_ref[rows, :HEAD_DIM], 1, 1)
        dprob_ref[:, rows] = dot(values, grads_ref[rows, :], 1, 1)


def over_rows(array, reduce):
    return reduce(array.reshape(-1, 8, array.shape[-1]), axis=0)


def unpack(pair_ref, bias_ref, keys_ref, values_ref, rows):
    kv_heads = bias_ref.shape[0]
    keys_ref[rows, :] = pair_ref[:, : kv_heads * HEAD_DIM]
    for kv_head in range(kv_heads):
        values_ref[rows, head_cols(kv_head)] = biased(
            pair_ref[:, head_cols(kv_heads + kv_head)], bias_ref[kv_head : kv_head + 1, :]
        )


def near_kernel(
    bias_ref, queries_ref, grads_ref, score_ref, own_dprob_ref, live_ref, *refs
):
    pair_refs, (weights_ref, dprob_ref, stats_ref, keys_ref, values_ref) = refs[:-5], refs[-5:]
    tok = pair_refs[0].shape[0]
    for index, pair_ref in enumerate(pair_refs):
        unpack(pair_ref, bias_ref, keys_ref, values_ref, slice(index * tok, (index + 1) * tok))
    blocks = [slice(row, row + BLOCK) for row in range(0, len(pair_refs) * tok, BLOCK)]
    for kv_head in range(bias_ref.shape[0]):
        cols = head_cols(kv_head)
        group = slice(kv_head * GROUP * tok, (kv_head + 1) * GROUP * tok)
        weights_ref[tok:, group] = dot(keys_ref[tok:, cols], queries_ref[group, :HEAD_DIM], 1, 1)
        dprob_ref[tok:, group] = dot(values_ref[tok:, cols], grads_ref[group, :], 1, 1)
        for first in range(group.start, group.stop, PAIR * tok):
            at = slice(first, first + PAIR * tok)
            row_max = None
            for block in blocks:
                score = (score_ref if block.start < tok else weights_ref)[block, at]
                score = score + jnp.concatenate([live_ref[block, :]] * PAIR, axis=1)
                weights_ref[block, at] = score
                part = over_rows(score, jnp.max)
                row_max = part if row_max is None else jnp.maximum(row_max, part)
            row_max = jnp.max(row_max, axis=0, keepdims=True)
            total = jnp.zeros((8, PAIR * tok), jnp.float32)
            delta = jnp.zeros((8, PAIR * tok), jnp.float32)
            for block in blocks:
                dprob = (own_dprob_ref if block.start < tok else dprob_ref)[block, at]
                weights = jnp.exp2((weights_ref[block, at] - row_max) * (SCALE * LOG2E))
                weights_ref[block, at] = weights
                if block.start < tok:
                    dprob_ref[block, at] = dprob
                total = total + over_rows(weights, jnp.sum)
                delta = delta + over_rows(weights * dprob, jnp.sum)
            stats_ref[0:1, at] = row_max
            stats_ref[1:2, at] = jnp.sum(total, axis=0, keepdims=True)
            stats_ref[2:3, at] = jnp.sum(delta, axis=0, keepdims=True)


def last_kernel(slots, first_head, *refs):
    bias_ref, queries_ref, grads_ref, live_ref = refs[:4]
    weights_ref, dprob_ref, stats_ref, near_keys_ref, near_values_ref, pair_ref = refs[4:10]
    probs_ref, dscore_ref, keys_ref, values_ref, sums_ref, own_ref = refs[10:16]
    out_refs = refs[16 : 16 + slots - 1]
    last_weights_ref, last_dprob_ref = refs[16 + slots - 1 :]
    tok = pair_ref.shape[0]
    near = (slots - 1) * tok
    kv_heads = bias_ref.shape[0]
    kv_width = kv_heads * HEAD_DIM
    heads = kv_heads * GROUP
    keys_ref[:near, :] = near_keys_ref[...]
    values_ref[:near, :] = near_values_ref[...]
    unpack(pair_ref, bias_ref, keys_ref, values_ref, slice(near, near + tok))
    near_blocks = [slice(row, row + BLOCK) for row in range(0, near, BLOCK)]
    blocks = [slice(row, row + BLOCK) for row in range(0, tok, BLOCK)]
    for kv_head in range(kv_heads):
        cols = head_cols(kv_head)
        group = slice(kv_head * GROUP * tok, (kv_head + 1) * GROUP * tok)
        last_weights_ref[:, group] = dot(
            keys_ref[near:, cols], queries_ref[group, :HEAD_DIM], 1, 1
        )
        last_dprob_ref[:, group] = dot(values_ref[near:, cols], grads_ref[group, :], 1, 1)
        for first in range(group.start, group.stop, PAIR * tok):
            at = slice(first, first + PAIR * tok)
            near_max = stats_ref[0:1, at]
            row_max = jnp.broadcast_to(near_max, (8, PAIR * tok))
            for block in blocks:
                live = live_ref[near + block.start : near + block.stop, :]
                score = last_weights_ref[block, at] + jnp.concatenate([live] * PAIR, axis=1)
                last_weights_ref[block, at] = score
                row_max = jnp.maximum(row_max, over_rows(score, jnp.max))
            row_max = jnp.max(row_max, axis=0, keepdims=True)
            total = jnp.zeros((8, PAIR * tok), jnp.float32)
            delta = jnp.zeros((8, PAIR * tok), jnp.float32)
            for block in blocks:
                weights = jnp.exp2((last_weights_ref[block, at] - row_max) * (SCALE * LOG2E))
                last_weights_ref[block, at] = weights
                total = total + over_rows(weights, jnp.sum)
                delta = delta + over_rows(weights * last_dprob_ref[block, at], jnp.sum)
            factor = jnp.exp2((near_max - row_max) * (SCALE * LOG2E))
            total = jnp.sum(total, axis=0, keepdims=True) + stats_ref[1:2, at] * factor
            delta = jnp.sum(delta, axis=0, keepdims=True) + stats_ref[2:3, at] * factor
            inverse = 1.0 / total
            delta = delta * inverse
            factor = factor * inverse
            for block in near_blocks:
                probs = weights_ref[block, at] * factor
                probs_ref[block, at] = probs.astype(jnp.bfloat16)
                dscore_ref[block, at] = (probs * (dprob_ref[block, at] - delta)).astype(jnp.bfloat16)
            for block in blocks:
                to = slice(near + block.start, near + block.stop)
                probs = last_weights_ref[block, at] * inverse
                probs_ref[to, at] = probs.astype(jnp.bfloat16)
                dscore = probs * (last_dprob_ref[block, at] - delta)
                dscore_ref[to, at] = dscore.astype(jnp.bfloat16)
        value_term = dot(probs_ref[:, group], grads_ref[group, :], 1, 0)
        key_term = dot(dscore_ref[:, group], queries_ref[group, :], 1, 0)
        over_queries = key_term[:, HEAD_DIM:]
        key_term = key_term[:, :HEAD_DIM] * SCALE
        high = over_queries.astype(jnp.bfloat16)
        low = (over_queries - high.astype(jnp.float32)).astype(jnp.bfloat16)
        all_keys = keys_ref[:, cols]
        query_sums = (dot(high, all_keys, 0, 0) + dot(low, all_keys, 0, 0)) * SCALE
        of_group = slice(kv_head * GROUP, (kv_head + 1) * GROUP)
        sums_ref[of_group, :] = query_sums[first_head + of_group.start : first_head + of_group.stop]
        sums_ref[heads + kv_head : heads + kv_head + 1, :] = jnp.sum(
            value_term, axis=0, keepdims=True
        )
        value_cols = head_cols(kv_heads + kv_head)
        own_ref[:, cols] = key_term[:tok]
        own_ref[:, value_cols] = value_term[:tok]
        for index, slot in enumerate(slot_order(slots)):
            if slot == 0:
                continue
            rows = slice(index * tok, (index + 1) * tok)
            out_refs[slot - 1][:, cols] = key_term[rows].astype(jnp.bfloat16)
            out_refs[slot - 1][:, value_cols] = value_term[rows].astype(jnp.bfloat16)


def finish_kernel(probs_ref, dscore_ref, keys_ref, values_ref, *refs):
    passed = (len(refs) - 2) // 2
    attn_ref, qg_ref = refs[passed : passed + 2]
    tok = attn_ref.shape[0]
    kv_heads = keys_ref.shape[1] // HEAD_DIM
    for kv_head in range(kv_heads):
        cols = head_cols(kv_head)
        keys_t = keys_ref[:, cols].T
        values_t = values_ref[:, cols].T
        for pair in range(GROUP // PAIR):
            first = kv_head * GROUP + pair * PAIR
            at = slice(first * tok, (first + PAIR) * tok)
            attn = dot(values_t, probs_ref[:, at], 1, 0).T
            query_grad = (dot(keys_t, dscore_ref[:, at], 1, 0) * SCALE).T
            for n in range(PAIR):
                head = first + n
                rows = slice(n * tok, (n + 1) * tok)
                attn_ref[:, head_cols(head)] = attn[rows].astype(jnp.bfloat16)
                qg_ref[:, head_cols(head)] = query_grad[rows].astype(jnp.bfloat16)


def collect_kernel(batches, parts, *refs):
    sum_refs, term_refs, (kg_ref, vg_ref, qb_ref, vb_ref) = refs[:parts], refs[parts:-4], refs[-4:]
    heads = qb_ref.shape[0]
    kv_width = kg_ref.shape[1]
    total = sum_refs[0][...]
    for ref in sum_refs[1:]:
        total = total + ref[...]
    total = total * (1.0 / batches)
    qb_ref[...] = total[:heads]
    vb_ref[...] = total[heads:]
    term = term_refs[0][...]
    for ref in term_refs[1:]:
        term = term + ref[...].astype(jnp.float32)
    term = term.astype(jnp.bfloat16)
    kg_ref[...] = term[:, :kv_width]
    vg_ref[...] = term[:, kv_width:]


def total_kernel(*refs):
    total = refs[0][...]
    for ref in refs[1:-1]:
        total = total + ref[...]
    refs[-1][...] = total


def exchange(axis, part):
    return [part] + [fetch(part, axis, slot) for slot in range(1, lax.axis_size(axis))]


def attend(first_head, bias, queries, grads, score, own_dprob, live, pairs):
    ctx = len(pairs)
    tok = pairs[0].shape[0]
    kv_width = bias.shape[0] * HEAD_DIM
    columns = queries.shape[0]
    rows = ctx * tok
    near = rows - tok
    near_slots = slot_order(ctx)[:-1]
    weights, dprob, stats, near_keys, near_values = pl.pallas_call(
        near_kernel,
        out_shape=[
            shape((near, columns), jnp.float32),
            shape((near, columns), jnp.float32),
            shape((8, columns), jnp.float32),
            shape((near, kv_width), jnp.bfloat16),
            shape((near, kv_width), jnp.bfloat16),
        ],
        in_specs=[VMEM] * (6 + len(near_slots)),
        out_specs=[VMEM] * 5,
        compiler_params=params(20 if ctx < 8 else 48),
        cost_estimate=pl.CostEstimate(
            flops=4 * near * columns * HEAD_DIM,
            bytes_accessed=8 * near * columns,
            transcendentals=near * columns,
        ),
        name="near",
    )(bias, queries, grads, score, own_dprob, live, *[pairs[slot] for slot in near_slots])
    term = shape((tok, 2 * kv_width), jnp.bfloat16)
    return pl.pallas_call(
        functools.partial(last_kernel, ctx, first_head),
        out_shape=[
            shape((rows, columns), jnp.bfloat16),
            shape((rows, columns), jnp.bfloat16),
            shape((rows, kv_width), jnp.bfloat16),
            shape((rows, kv_width), jnp.bfloat16),
            shape((bias.shape[0] * (GROUP + 1), HEAD_DIM), jnp.float32),
            shape((tok, 2 * kv_width), jnp.float32),
        ]
        + [term] * (ctx - 1),
        in_specs=[VMEM] * 10,
        out_specs=[VMEM] * (6 + ctx - 1),
        scratch_shapes=[pltpu.VMEM((tok, columns), jnp.float32)] * 2,
        compiler_params=params(24 if ctx < 8 else 48),
        cost_estimate=pl.CostEstimate(
            flops=4 * rows * columns * HEAD_DIM,
            bytes_accessed=4 * rows * columns,
            transcendentals=tok * columns,
        ),
        name="last",
    )(bias, queries, grads, live, weights, dprob, stats, near_keys, near_values, pairs[ctx // 2])


def joined(place, parts):
    if place < 4:
        return jnp.concatenate(parts, axis=1)
    cut, axis = (GROUP, 0) if place == 4 else (HEAD_DIM, 1)
    pieces = [jnp.split(part, [cut], axis=axis) for part in parts]
    return jnp.concatenate([piece[n] for n in range(2) for piece in pieces], axis=axis)


def shards(q_proj, q_bias, k_proj, v_proj, v_bias, dout, lengths):
    _, tok, width = q_proj.shape
    kv_width = k_proj.shape[2]
    heads = width // HEAD_DIM
    kv_heads = kv_width // HEAD_DIM
    ctx = lax.axis_size("ctx")
    batches = lax.axis_size("dp")
    rows = ctx * tok
    columns = heads * tok
    pair = jnp.concatenate([k_proj[0], v_proj[0]], axis=1)
    pairs = [pair] + [fetch(pair, "ctx", slot) for slot in range(1, ctx)]
    prepared = pl.pallas_call(
        functools.partial(prepare_kernel, ctx),
        out_shape=[
            shape((kv_heads, HEAD_DIM), jnp.bfloat16),
            shape((columns, 2 * HEAD_DIM), jnp.bfloat16),
            shape((columns, HEAD_DIM), jnp.bfloat16),
            shape((tok, columns), jnp.float32),
            shape((tok, columns), jnp.float32),
            shape((rows, tok), jnp.float32),
        ],
        in_specs=[SMEM] + [VMEM] * 5,
        out_specs=[VMEM] * 6,
        compiler_params=params(16),
        cost_estimate=pl.CostEstimate(
            flops=4 * tok * tok * width, bytes_accessed=16 * tok * width, transcendentals=0
        ),
        name="prepare",
    )(
        lengths,
        pair,
        q_bias.reshape(heads, HEAD_DIM),
        v_bias.reshape(kv_heads, HEAD_DIM),
        q_proj[0],
        dout[0],
    )
    bias, queries, grads, score, own_dprob, live = prepared
    if ctx < 8:
        made = attend(0, bias, queries, grads, score, own_dprob, live, pairs)
    else:
        made = [
            attend(
                kv_head * GROUP,
                bias[kv_head : kv_head + 1],
                *(part[at] for part in (queries, grads)),
                *(part[:, at] for part in (score, own_dprob)),
                live,
                [
                    jnp.concatenate(
                        [part[:, head_cols(kv_head)], part[:, head_cols(kv_heads + kv_head)]], axis=1
                    )
                    for part in pairs
                ],
            )
            for kv_head in range(kv_heads)
            for at in [slice(kv_head * GROUP * tok, (kv_head + 1) * GROUP * tok)]
        ]
        made = [joined(n, parts) for n, parts in enumerate(zip(*made))]
    probs, dscore, all_keys, all_values, sums, own, *terms = made
    term = shape((tok, 2 * kv_width), jnp.bfloat16)
    half = ctx // 2
    back = {slot: send_back(terms[slot - 1], slot) for slot in range(1, ctx)}
    tied = [half]
    attn, q_grad, *passed = pl.pallas_call(
        finish_kernel,
        out_shape=[
            shape((tok, width), jnp.bfloat16),
            shape((tok, width), jnp.bfloat16),
        ]
        + [shape((tok, 2 * kv_width), jnp.bfloat16)] * len(tied),
        in_specs=[VMEM] * 4 + [ANY] * len(tied),
        out_specs=[VMEM] * 2 + [ANY] * len(tied),
        input_output_aliases={4 + n: 2 + n for n in range(len(tied))},
        compiler_params=params(24),
        cost_estimate=pl.CostEstimate(
            flops=16 * rows * tok * width, bytes_accessed=0, transcendentals=0
        ),
        name="finish",
    )(probs, dscore, all_keys, all_values, *[back[slot] for slot in tied])
    parts = exchange("dp", sums)
    sums = pl.pallas_call(
        total_kernel,
        out_shape=shape(sums.shape, sums.dtype),
        in_specs=[VMEM] * len(parts),
        out_specs=VMEM,
        compiler_params=params(4),
        cost_estimate=pl.CostEstimate(flops=sums.size, bytes_accessed=0, transcendentals=0),
        name="total",
    )(*parts)
    sums = exchange("ctx", sums)
    sums = [sums[0], *sums[2:], *sums[1:2]]
    back.update(zip(tied, passed))
    k_grad, v_grad, q_sum, v_sum = pl.pallas_call(
        functools.partial(collect_kernel, batches, len(sums)),
        out_shape=[
            shape((tok, kv_width), jnp.bfloat16),
            shape((tok, kv_width), jnp.bfloat16),
            shape((heads, HEAD_DIM), jnp.float32),
            shape((kv_heads, HEAD_DIM), jnp.float32),
        ],
        in_specs=[VMEM] * (len(sums) + 1 + len(back)),
        out_specs=[VMEM] * 4,
        compiler_params=params(8),
        cost_estimate=pl.CostEstimate(
            flops=8 * tok * kv_width, bytes_accessed=16 * tok * kv_width, transcendentals=0
        ),
        name="collect",
    )(*sums, own, *[back[slot] for slot in sorted(back, reverse=True)])
    return (
        attn[None],
        q_grad[None],
        k_grad[None],
        v_grad[None],
        q_sum.reshape(width),
        v_sum.reshape(kv_width),
    )


def solution(mesh):
    tokens = P("dp", "ctx", "tp")
    return jax.shard_map(
        shards,
        mesh=mesh,
        in_specs=(tokens, P("tp"), tokens, tokens, P("tp"), tokens, P("dp", None)),
        out_specs=(tokens, tokens, tokens, tokens, P("tp"), P("tp")),
        check_vma=False,
    )
```

```python
import functools

import jax
import jax.numpy as jnp
from jax import lax
from jax.experimental import pallas as pl
from jax.experimental.pallas import tpu as pltpu
from jax.sharding import PartitionSpec as P

HEAD_DIM = 128
HEADS = 32
KV_HEADS = 4
GROUP = HEADS // KV_HEADS
PAIR = 4
BLOCK = 32
SCALE = HEAD_DIM ** (-0.5)
LOG2E = 1.4426950408889634
NEGATIVE = -1e30
VMEM = pl.BlockSpec(memory_space=pltpu.VMEM)
ANY = pl.BlockSpec(memory_space=pl.ANY)
SMEM = pl.BlockSpec(memory_space=pltpu.SMEM)


def dot(left, right, left_dim, right_dim):
    return lax.dot_general(
        left, right, (((left_dim,), (right_dim,)), ((), ())), preferred_element_type=jnp.float32
    )


def head_cols(head):
    return slice(head * HEAD_DIM, (head + 1) * HEAD_DIM)


def shape(dims, dtype):
    return jax.ShapeDtypeStruct(dims, dtype)


def params(mebibytes):
    return pltpu.CompilerParams(vmem_limit_bytes=mebibytes * 1024 * 1024)


def biased(values, bias):
    return (values.astype(jnp.float32) + bias.astype(jnp.float32)).astype(jnp.bfloat16)


def source_of(rank, slot, size):
    if size & (size - 1):
        return (rank + size - slot) % size
    return rank ^ slot


def slot_order(size):
    return [slot for slot in range(size) if slot != size // 2] + [size // 2]


def fetch(array, axis, slot):
    size = lax.axis_size(axis)
    return lax.ppermute(array, axis, [(source_of(i, slot, size), i) for i in range(size)])


def send_back(array, slot):
    size = lax.axis_size("ctx")
    return lax.ppermute(array, "ctx", [(i, source_of(i, slot, size)) for i in range(size)])


def prepare_kernel(
    slots, len_ref, pair_ref, qb_ref, vb_ref, q_ref, g_ref, bias_ref, queries_ref, grads_ref,
    score_ref, dprob_ref, live_ref,
):
    tok = q_ref.shape[0]
    kv_heads = vb_ref.shape[0]
    rank = lax.axis_index("ctx")
    query_pos = rank * tok + lax.broadcasted_iota(jnp.int32, (1, tok), 1)
    start = jnp.zeros((1, tok), jnp.int32)
    end = jnp.int32(0)
    for doc in range(len_ref.shape[1]):
        length = len_ref[0, doc]
        end = end + length
        start = start + jnp.where(query_pos >= end, length, 0)
    offsets = lax.broadcasted_iota(jnp.int32, (tok, tok), 0)
    for index, slot in enumerate(slot_order(slots)):
        key_pos = source_of(rank, slot, slots) * tok + offsets
        live = (key_pos >= start) & (key_pos <= query_pos)
        live_ref[index * tok : (index + 1) * tok, :] = jnp.where(live, 0.0, NEGATIVE)
    bias_ref[...] = vb_ref[...]
    column = lax.broadcasted_iota(jnp.int32, (tok, HEAD_DIM), 1)
    for kv_head in range(kv_heads):
        keys = pair_ref[:, head_cols(kv_head)]
        values = biased(pair_ref[:, head_cols(kv_heads + kv_head)], vb_ref[kv_head : kv_head + 1, :])
        for head in range(kv_head * GROUP, (kv_head + 1) * GROUP):
            at = slice(head * tok, (head + 1) * tok)
            queries_ref[at, :HEAD_DIM] = biased(q_ref[:, head_cols(head)], qb_ref[head : head + 1, :])
            queries_ref[at, HEAD_DIM:] = (column == head).astype(jnp.bfloat16)
            grads_ref[at, :] = g_ref[:, head_cols(head)]
        rows = slice(kv_head * GROUP * tok, (kv_head + 1) * GROUP * tok)
        score_ref[:, rows] = dot(keys, queries_ref[rows, :HEAD_DIM], 1, 1)
        dprob_ref[:, rows] = dot(values, grads_ref[rows, :], 1, 1)


def over_rows(array, reduce):
    return reduce(array.reshape(-1, 8, array.shape[-1]), axis=0)


def unpack(pair_ref, bias_ref, keys_ref, values_ref, rows):
    kv_heads = bias_ref.shape[0]
    keys_ref[rows, :] = pair_ref[:, : kv_heads * HEAD_DIM]
    for kv_head in range(kv_heads):
        values_ref[rows, head_cols(kv_head)] = biased(
            pair_ref[:, head_cols(kv_heads + kv_head)], bias_ref[kv_head : kv_head + 1, :]
        )


def near_kernel(
    bias_ref, queries_ref, grads_ref, score_ref, own_dprob_ref, live_ref, *refs
):
    pair_refs, (weights_ref, dprob_ref, stats_ref, keys_ref, values_ref) = refs[:-5], refs[-5:]
    tok = pair_refs[0].shape[0]
    for index, pair_ref in enumerate(pair_refs):
        unpack(pair_ref, bias_ref, keys_ref, values_ref, slice(index * tok, (index + 1) * tok))
    blocks = [slice(row, row + BLOCK) for row in range(0, len(pair_refs) * tok, BLOCK)]
    for kv_head in range(bias_ref.shape[0]):
        cols = head_cols(kv_head)
        group = slice(kv_head * GROUP * tok, (kv_head + 1) * GROUP * tok)
        weights_ref[tok:, group] = dot(keys_ref[tok:, cols], queries_ref[group, :HEAD_DIM], 1, 1)
        dprob_ref[tok:, group] = dot(values_ref[tok:, cols], grads_ref[group, :], 1, 1)
        for first in range(group.start, group.stop, PAIR * tok):
            at = slice(first, first + PAIR * tok)
            row_max = None
            for block in blocks:
                score = (score_ref if block.start < tok else weights_ref)[block, at]
                score = score + jnp.concatenate([live_ref[block, :]] * PAIR, axis=1)
                weights_ref[block, at] = score
                part = over_rows(score, jnp.max)
                row_max = part if row_max is None else jnp.maximum(row_max, part)
            row_max = jnp.max(row_max, axis=0, keepdims=True)
            total = jnp.zeros((8, PAIR * tok), jnp.float32)
            delta = jnp.zeros((8, PAIR * tok), jnp.float32)
            for block in blocks:
                dprob = (own_dprob_ref if block.start < tok else dprob_ref)[block, at]
                weights = jnp.exp2((weights_ref[block, at] - row_max) * (SCALE * LOG2E))
                weights_ref[block, at] = weights
                if block.start < tok:
                    dprob_ref[block, at] = dprob
                total = total + over_rows(weights, jnp.sum)
                delta = delta + over_rows(weights * dprob, jnp.sum)
            stats_ref[0:1, at] = row_max
            stats_ref[1:2, at] = jnp.sum(total, axis=0, keepdims=True)
            stats_ref[2:3, at] = jnp.sum(delta, axis=0, keepdims=True)


def last_kernel(slots, first_head, *refs):
    bias_ref, queries_ref, grads_ref, live_ref = refs[:4]
    weights_ref, dprob_ref, stats_ref, near_keys_ref, near_values_ref, pair_ref = refs[4:10]
    probs_ref, dscore_ref, keys_ref, values_ref, sums_ref, own_ref = refs[10:16]
    out_refs = refs[16 : 16 + slots - 1]
    last_weights_ref, last_dprob_ref = refs[16 + slots - 1 :]
    tok = pair_ref.shape[0]
    near = (slots - 1) * tok
    kv_heads = bias_ref.shape[0]
    kv_width = kv_heads * HEAD_DIM
    heads = kv_heads * GROUP
    keys_ref[:near, :] = near_keys_ref[...]
    values_ref[:near, :] = near_values_ref[...]
    unpack(pair_ref, bias_ref, keys_ref, values_ref, slice(near, near + tok))
    near_blocks = [slice(row, row + BLOCK) for row in range(0, near, BLOCK)]
    blocks = [slice(row, row + BLOCK) for row in range(0, tok, BLOCK)]
    for kv_head in range(kv_heads):
        cols = head_cols(kv_head)
        group = slice(kv_head * GROUP * tok, (kv_head + 1) * GROUP * tok)
        last_weights_ref[:, group] = dot(
            keys_ref[near:, cols], queries_ref[group, :HEAD_DIM], 1, 1
        )
        last_dprob_ref[:, group] = dot(values_ref[near:, cols], grads_ref[group, :], 1, 1)
        for first in range(group.start, group.stop, PAIR * tok):
            at = slice(first, first + PAIR * tok)
            near_max = stats_ref[0:1, at]
            row_max = jnp.broadcast_to(near_max, (8, PAIR * tok))
            for block in blocks:
                live = live_ref[near + block.start : near + block.stop, :]
                score = last_weights_ref[block, at] + jnp.concatenate([live] * PAIR, axis=1)
                last_weights_ref[block, at] = score
                row_max = jnp.maximum(row_max, over_rows(score, jnp.max))
            row_max = jnp.max(row_max, axis=0, keepdims=True)
            total = jnp.zeros((8, PAIR * tok), jnp.float32)
            delta = jnp.zeros((8, PAIR * tok), jnp.float32)
            for block in blocks:
                weights = jnp.exp2((last_weights_ref[block, at] - row_max) * (SCALE * LOG2E))
                last_weights_ref[block, at] = weights
                total = total + over_rows(weights, jnp.sum)
                delta = delta + over_rows(weights * last_dprob_ref[block, at], jnp.sum)
            factor = jnp.exp2((near_max - row_max) * (SCALE * LOG2E))
            total = jnp.sum(total, axis=0, keepdims=True) + stats_ref[1:2, at] * factor
            delta = jnp.sum(delta, axis=0, keepdims=True) + stats_ref[2:3, at] * factor
            inverse = 1.0 / total
            delta = delta * inverse
            factor = factor * inverse
            for block in near_blocks:
                probs = weights_ref[block, at] * factor
                probs_ref[block, at] = probs.astype(jnp.bfloat16)
                dscore_ref[block, at] = (probs * (dprob_ref[block, at] - delta)).astype(jnp.bfloat16)
            for block in blocks:
                to = slice(near + block.start, near + block.stop)
                probs = last_weights_ref[block, at] * inverse
                probs_ref[to, at] = probs.astype(jnp.bfloat16)
                dscore = probs * (last_dprob_ref[block, at] - delta)
                dscore_ref[to, at] = dscore.astype(jnp.bfloat16)
        value_term = dot(probs_ref[:, group], grads_ref[group, :], 1, 0)
        key_term = dot(dscore_ref[:, group], queries_ref[group, :], 1, 0)
        over_queries = key_term[:, HEAD_DIM:]
        key_term = key_term[:, :HEAD_DIM] * SCALE
        high = over_queries.astype(jnp.bfloat16)
        low = (over_queries - high.astype(jnp.float32)).astype(jnp.bfloat16)
        all_keys = keys_ref[:, cols]
        query_sums = (dot(high, all_keys, 0, 0) + dot(low, all_keys, 0, 0)) * SCALE
        of_group = slice(kv_head * GROUP, (kv_head + 1) * GROUP)
        sums_ref[of_group, :] = query_sums[first_head + of_group.start : first_head + of_group.stop]
        sums_ref[heads + kv_head : heads + kv_head + 1, :] = jnp.sum(
            value_term, axis=0, keepdims=True
        )
        value_cols = head_cols(kv_heads + kv_head)
        own_ref[:, cols] = key_term[:tok]
        own_ref[:, value_cols] = value_term[:tok]
        for index, slot in enumerate(slot_order(slots)):
            if slot == 0:
                continue
            rows = slice(index * tok, (index + 1) * tok)
            out_refs[slot - 1][:, cols] = key_term[rows].astype(jnp.bfloat16)
            out_refs[slot - 1][:, value_cols] = value_term[rows].astype(jnp.bfloat16)


def finish_kernel(probs_ref, dscore_ref, keys_ref, values_ref, *refs):
    passed = (len(refs) - 2) // 2
    attn_ref, qg_ref = refs[passed : passed + 2]
    tok = attn_ref.shape[0]
    kv_heads = keys_ref.shape[1] // HEAD_DIM
    for kv_head in range(kv_heads):
        cols = head_cols(kv_head)
        keys_t = keys_ref[:, cols].T
        values_t = values_ref[:, cols].T
        for pair in range(GROUP // PAIR):
            first = kv_head * GROUP + pair * PAIR
            at = slice(first * tok, (first + PAIR) * tok)
            attn = dot(values_t, probs_ref[:, at], 1, 0).T
            query_grad = (dot(keys_t, dscore_ref[:, at], 1, 0) * SCALE).T
            for n in range(PAIR):
                head = first + n
                rows = slice(n * tok, (n + 1) * tok)
                attn_ref[:, head_cols(head)] = attn[rows].astype(jnp.bfloat16)
                qg_ref[:, head_cols(head)] = query_grad[rows].astype(jnp.bfloat16)


def collect_kernel(batches, parts, *refs):
    sum_refs, term_refs, (kg_ref, vg_ref, qb_ref, vb_ref) = refs[:parts], refs[parts:-4], refs[-4:]
    heads = qb_ref.shape[0]
    kv_width = kg_ref.shape[1]
    total = sum_refs[0][...]
    for ref in sum_refs[1:]:
        total = total + ref[...]
    total = total * (1.0 / batches)
    qb_ref[...] = total[:heads]
    vb_ref[...] = total[heads:]
    term = term_refs[0][...]
    for ref in term_refs[1:]:
        term = term + ref[...].astype(jnp.float32)
    term = term.astype(jnp.bfloat16)
    kg_ref[...] = term[:, :kv_width]
    vg_ref[...] = term[:, kv_width:]


def total_kernel(*refs):
    total = refs[0][...]
    for ref in refs[1:-1]:
        total = total + ref[...]
    refs[-1][...] = total


def exchange(axis, part):
    return [part] + [fetch(part, axis, slot) for slot in range(1, lax.axis_size(axis))]


def attend(first_head, bias, queries, grads, score, own_dprob, live, pairs):
    ctx = len(pairs)
    tok = pairs[0].shape[0]
    kv_width = bias.shape[0] * HEAD_DIM
    columns = queries.shape[0]
    rows = ctx * tok
    near = rows - tok
    near_slots = slot_order(ctx)[:-1]
    weights, dprob, stats, near_keys, near_values = pl.pallas_call(
        near_kernel,
        out_shape=[
            shape((near, columns), jnp.float32),
            shape((near, columns), jnp.float32),
            shape((8, columns), jnp.float32),
            shape((near, kv_width), jnp.bfloat16),
            shape((near, kv_width), jnp.bfloat16),
        ],
        in_specs=[VMEM] * (6 + len(near_slots)),
        out_specs=[VMEM] * 5,
        compiler_params=params(20 if ctx < 8 else 48),
        cost_estimate=pl.CostEstimate(
            flops=4 * near * columns * HEAD_DIM,
            bytes_accessed=8 * near * columns,
            transcendentals=near * columns,
        ),
        name="near",
    )(bias, queries, grads, score, own_dprob, live, *[pairs[slot] for slot in near_slots])
    term = shape((tok, 2 * kv_width), jnp.bfloat16)
    return pl.pallas_call(
        functools.partial(last_kernel, ctx, first_head),
        out_shape=[
            shape((rows, columns), jnp.bfloat16),
            shape((rows, columns), jnp.bfloat16),
            shape((rows, kv_width), jnp.bfloat16),
            shape((rows, kv_width), jnp.bfloat16),
            shape((bias.shape[0] * (GROUP + 1), HEAD_DIM), jnp.float32),
            shape((tok, 2 * kv_width), jnp.float32),
        ]
        + [term] * (ctx - 1),
        in_specs=[VMEM] * 10,
        out_specs=[VMEM] * (6 + ctx - 1),
        scratch_shapes=[pltpu.VMEM((tok, columns), jnp.float32)] * 2,
        compiler_params=params(24 if ctx < 8 else 48),
        cost_estimate=pl.CostEstimate(
            flops=4 * rows * columns * HEAD_DIM,
            bytes_accessed=4 * rows * columns,
            transcendentals=tok * columns,
        ),
        name="last",
    )(bias, queries, grads, live, weights, dprob, stats, near_keys, near_values, pairs[ctx // 2])


def joined(place, parts):
    if place < 4:
        return jnp.concatenate(parts, axis=1)
    cut, axis = (GROUP, 0) if place == 4 else (HEAD_DIM, 1)
    pieces = [jnp.split(part, [cut], axis=axis) for part in parts]
    return jnp.concatenate([piece[n] for n in range(2) for piece in pieces], axis=axis)


def shards(q_proj, q_bias, k_proj, v_proj, v_bias, dout, lengths):
    _, tok, width = q_proj.shape
    kv_width = k_proj.shape[2]
    heads = width // HEAD_DIM
    kv_heads = kv_width // HEAD_DIM
    ctx = lax.axis_size("ctx")
    batches = lax.axis_size("dp")
    rows = ctx * tok
    columns = heads * tok
    pair = jnp.concatenate([k_proj[0], v_proj[0]], axis=1)
    pairs = [pair] + [fetch(pair, "ctx", slot) for slot in range(1, ctx)]
    prepared = pl.pallas_call(
        functools.partial(prepare_kernel, ctx),
        out_shape=[
            shape((kv_heads, HEAD_DIM), jnp.bfloat16),
            shape((columns, 2 * HEAD_DIM), jnp.bfloat16),
            shape((columns, HEAD_DIM), jnp.bfloat16),
            shape((tok, columns), jnp.float32),
            shape((tok, columns), jnp.float32),
            shape((rows, tok), jnp.float32),
        ],
        in_specs=[SMEM] + [VMEM] * 5,
        out_specs=[VMEM] * 6,
        compiler_params=params(16),
        cost_estimate=pl.CostEstimate(
            flops=4 * tok * tok * width, bytes_accessed=16 * tok * width, transcendentals=0
        ),
        name="prepare",
    )(
        lengths,
        pair,
        q_bias.reshape(heads, HEAD_DIM),
        v_bias.reshape(kv_heads, HEAD_DIM),
        q_proj[0],
        dout[0],
    )
    bias, queries, grads, score, own_dprob, live = prepared
    if ctx < 8:
        made = attend(0, bias, queries, grads, score, own_dprob, live, pairs)
    else:
        made = [
            attend(
                kv_head * GROUP,
                bias[kv_head : kv_head + 1],
                *(part[at] for part in (queries, grads)),
                *(part[:, at] for part in (score, own_dprob)),
                live,
                [
                    jnp.concatenate(
                        [part[:, head_cols(kv_head)], part[:, head_cols(kv_heads + kv_head)]], axis=1
                    )
                    for part in pairs
                ],
            )
            for kv_head in range(kv_heads)
            for at in [slice(kv_head * GROUP * tok, (kv_head + 1) * GROUP * tok)]
        ]
        made = [joined(n, parts) for n, parts in enumerate(zip(*made))]
    probs, dscore, all_keys, all_values, sums, own, *terms = made
    term = shape((tok, 2 * kv_width), jnp.bfloat16)
    half = ctx // 2
    back = {slot: send_back(terms[slot - 1], slot) for slot in range(1, ctx)}
    tied = [half]
    attn, q_grad, *passed = pl.pallas_call(
        finish_kernel,
        out_shape=[
            shape((tok, width), jnp.bfloat16),
            shape((tok, width), jnp.bfloat16),
        ]
        + [shape((tok, 2 * kv_width), jnp.bfloat16)] * len(tied),
        in_specs=[VMEM] * 4 + [ANY] * len(tied),
        out_specs=[VMEM] * 2 + [ANY] * len(tied),
        input_output_aliases={4 + n: 2 + n for n in range(len(tied))},
        compiler_params=params(24),
        cost_estimate=pl.CostEstimate(
            flops=16 * rows * tok * width, bytes_accessed=0, transcendentals=0
        ),
        name="finish",
    )(probs, dscore, all_keys, all_values, *[back[slot] for slot in tied])
    parts = exchange("dp", sums)
    sums = pl.pallas_call(
        total_kernel,
        out_shape=shape(sums.shape, sums.dtype),
        in_specs=[VMEM] * len(parts),
        out_specs=VMEM,
        compiler_params=params(4),
        cost_estimate=pl.CostEstimate(flops=sums.size, bytes_accessed=0, transcendentals=0),
        name="total",
    )(*parts)
    sums = exchange("ctx", sums)
    back.update(zip(tied, passed))
    k_grad, v_grad, q_sum, v_sum = pl.pallas_call(
        functools.partial(collect_kernel, batches, len(sums)),
        out_shape=[
            shape((tok, kv_width), jnp.bfloat16),
            shape((tok, kv_width), jnp.bfloat16),
            shape((heads, HEAD_DIM), jnp.float32),
            shape((kv_heads, HEAD_DIM), jnp.float32),
        ],
        in_specs=[VMEM] * (len(sums) + 1 + len(back)),
        out_specs=[VMEM] * 4,
        compiler_params=params(8),
        cost_estimate=pl.CostEstimate(
            flops=8 * tok * kv_width, bytes_accessed=16 * tok * kv_width, transcendentals=0
        ),
        name="collect",
    )(*sums, own, *[back[slot] for slot in sorted(back)])
    return (
        attn[None],
        q_grad[None],
        k_grad[None],
        v_grad[None],
        q_sum.reshape(width),
        v_sum.reshape(kv_width),
    )


def solution(mesh):
    tokens = P("dp", "ctx", "tp")
    return jax.shard_map(
        shards,
        mesh=mesh,
        in_specs=(tokens, P("tp"), tokens, tokens, P("tp"), tokens, P("dp", None)),
        out_specs=(tokens, tokens, tokens, tokens, P("tp"), P("tp")),
        check_vma=False,
    )
```
